32 devices in a mesh: row: 4 (over z), col: 8 (over y, x, core).
Axes of the slice: x: 2, y: 2, z: 4, core: 2. Of those that a mesh axis runs over, the one named last changes fastest.
Arguments:
- tiles: bfloat16 [4, 8, 32, 128, 128], P('row', 'col'), may hold values from 1.347065e-05 to 0.013427734
- tile_rows: int32 [4, 8, 32], P('row', 'col'), may hold values from 0 to 63, as said below
- tile_cols: int32 [4, 8, 32], P('row', 'col'), may hold values from 0 to 31, as said below
- start_vectors: float32 [64, 32768], P(None, ('row', 'col')), may hold values from -6 to 6
Outputs:
- ritz: float32 [64, 32768], P(None, ('row', 'col'))
- rayleigh: float32 [64, 64], replicated
The draws below stay inside these ranges and needn't reach their ends.
Inputs may be any that keep to these rules, and one draw needn't show every extreme that they name: `tile_rows`: tile row of each stored tile inside its block row; tile rows g * 8 to g * 8 + 7 belong to the block row's node group g. One block holds at most 4 tiles in the rows of any one node group, and exactly 4 in the rows of its own node group (group r * 8 + c of block r, c); in every block row one node group receives exactly 4 tiles from every block of that block row. The same position may repeat, and such tiles add. `tile_cols`: tile column of each stored tile inside its block column; tiles in the rows of the block's own node group lie in that group's columns.
All inputs are finite; a program needn't handle non-finite values.
Results may differ from the reference program's by a relative error of at most 0.00044.
Values may be sent and summed in bfloat16 or wider, within the bound.
No kernel may reach another device: no remote copies, remote signals or barrier semaphores. Data moves between devices by JAX's collectives and lax.ppermute only.
A program may use at most 64 MiB of HBM per device.

```python
import math
import jax
import jax.numpy as jnp
from jax import lax

K = 64
TB = 128
TILES_PER_BLOCK = 32
CAP = 4
GROUP_TILES = 8
ROW_TILES = 64
COL_TILES = 32
NN = 32768
N_ROW = 4
N_COL = 8


def tile_pattern(key):
    slot_total_count = N_COL * CAP
    owning_blocks = jnp.arange(slot_total_count, dtype=jnp.int32) // CAP
    grid_rows = jnp.repeat(jnp.arange(N_ROW, dtype=jnp.int32), N_COL)
    grid_cols = jnp.tile(jnp.arange(N_COL, dtype=jnp.int32), N_ROW)

    def one_block(block_row, block_column_index):
        block_key = jax.random.fold_in(key, block_row * N_COL + block_column_index)
        central_node = jax.random.randint(jax.random.fold_in(key, 100003 + block_row), (), 0, N_COL)
        first, second, third, fourth = jax.random.split(block_key, 4)
        sorted_indices = jax.random.permutation(first, slot_total_count).astype(jnp.int32)
        extra_weight = jnp.where((owning_blocks == block_column_index) | (owning_blocks == central_node), slot_total_count, 0).astype(jnp.int32)
        selected_nodes = jnp.argsort(-(sorted_indices + extra_weight), stable=True)[:TILES_PER_BLOCK].astype(jnp.int32)
        owner = selected_nodes // CAP
        offset = jax.random.randint(second, (TILES_PER_BLOCK,), 0, GROUP_TILES).astype(jnp.int32)
        rows_out = owner * GROUP_TILES + offset
        nearby = (offset + jax.random.randint(third, (TILES_PER_BLOCK,), 0, 2).astype(jnp.int32)) % GROUP_TILES
        spread = jax.random.randint(fourth, (TILES_PER_BLOCK,), 0, COL_TILES).astype(jnp.int32)
        cols_out = jnp.where(owner == block_column_index, block_row * GROUP_TILES + nearby, spread)
        return (rows_out, cols_out)
    rows_all, cols_all = jax.vmap(one_block)(grid_rows, grid_cols)
    return (rows_all.reshape(N_ROW, N_COL, TILES_PER_BLOCK).astype(jnp.int32), cols_all.reshape(N_ROW, N_COL, TILES_PER_BLOCK).astype(jnp.int32))


def draw_tile_rows(key, part):
    return tile_pattern(jax.random.fold_in(key, 4242))[0]


def draw_tile_cols(key, part):
    return tile_pattern(jax.random.fold_in(key, 4242))[1]


def levels(own_key, dims, shards, low, high):
    gain = 1.0
    for position, shards_of in shards:
        heights = jax.random.uniform(jax.random.fold_in(jax.random.fold_in(own_key, 6), position), (shards_of,), jnp.float32, low / len(shards), high / len(shards))
        gain = gain * jnp.repeat(jnp.exp(heights), dims[position] // shards_of).reshape((-1,) + (1,) * (len(dims) - 1 - position))
    return gain


def normal_values(rng, extent, scale, bound, cuts=(), kind=jnp.bfloat16):
    level = levels(rng, extent, cuts, -0.22, 0.18) if cuts else 1.0
    values = jax.random.normal(rng, extent, jnp.float32) * scale * level
    return jnp.minimum(jnp.maximum(values, -bound), bound).astype(kind)


def setup_inputs(seed: int = 0) -> dict:
    streams_of = jax.random.split(jax.random.key(seed), 5)
    tiles = jnp.clip(jnp.exp(math.log(0.013427734) - 6.9045644 * jax.random.uniform(streams_of[0], (N_ROW, N_COL, TILES_PER_BLOCK, TB, TB), jnp.float32) ** levels(streams_of[0], (N_ROW, N_COL, TILES_PER_BLOCK, TB, TB), ((0, 4), (1, 8)), -0.2, 0.2)), 1.3470649719238281e-05, 0.013427734).astype(jnp.bfloat16)
    tile_rows = draw_tile_rows(jax.random.fold_in(streams_of[4], 71), 0)
    tile_cols = draw_tile_cols(jax.random.fold_in(streams_of[4], 71), 0)
    start_vectors = normal_values(streams_of[3], (K, NN), 1.0, 6.0, ((1, 32),), jnp.float32)
    return {"tiles": tiles, "tile_rows": tile_rows, "tile_cols": tile_cols, "start_vectors": start_vectors}


CENTER = 1.0
HALF_WIDTH = 0.5

def tile_index(tile_rows, tile_cols):
    block_row = jnp.arange(N_ROW, dtype=jnp.int32)[:, None, None]
    block_column_index = jnp.arange(N_COL, dtype=jnp.int32)[None, :, None]
    row_index = block_row * ROW_TILES + tile_rows
    col_index = tile_cols // GROUP_TILES * (N_COL * GROUP_TILES) + block_column_index * GROUP_TILES + tile_cols % GROUP_TILES
    return (row_index.reshape(N_ROW * N_COL, TILES_PER_BLOCK).astype(jnp.int32), col_index.reshape(N_ROW * N_COL, TILES_PER_BLOCK).astype(jnp.int32))

def node_degree(blocks, row_index, col_index):

    def visit(totals, device):
        row_total, col_total = totals
        tile_float = blocks[device].astype(jnp.float32)
        row_total = row_total.at[row_index[device]].add(jnp.sum(tile_float, axis=2))
        col_total = col_total.at[col_index[device]].add(jnp.sum(tile_float, axis=1))
        return ((row_total, col_total), None)
    start = (jnp.zeros((NN // TB, TB), jnp.float32), jnp.zeros((NN // TB, TB), jnp.float32))
    (row_total, col_total), _ = lax.scan(visit, start, jnp.arange(N_ROW * N_COL, dtype=jnp.int32))
    return 0.5 * (row_total + col_total).reshape(NN)

def symmetric_part(vectors, blocks, row_index, col_index):
    rounded = lax.optimization_barrier(vectors.astype(jnp.bfloat16)).astype(jnp.float32)
    rounded = rounded.reshape(K, NN // TB, TB)

    def visit(totals, device):
        row_total, col_total = totals
        tile_float = blocks[device].astype(jnp.float32)
        picked_cols = jnp.take(rounded, col_index[device], axis=1)
        picked_rows = jnp.take(rounded, row_index[device], axis=1)
        row_term = jnp.einsum('tij,ktj->kti', tile_float, picked_cols)
        col_term = jnp.einsum('tij,kti->ktj', tile_float, picked_rows)
        row_total = row_total.at[:, row_index[device]].add(row_term)
        col_total = col_total.at[:, col_index[device]].add(col_term)
        return ((row_total, col_total), None)
    start = (jnp.zeros((K, NN // TB, TB), jnp.float32), jnp.zeros((K, NN // TB, TB), jnp.float32))
    (row_total, col_total), _ = lax.scan(visit, start, jnp.arange(N_ROW * N_COL, dtype=jnp.int32))
    return 0.5 * (row_total + col_total).reshape(K, NN)

def reference(tiles, tile_rows, tile_cols, start_vectors):
    blocks = tiles.reshape(N_ROW * N_COL, TILES_PER_BLOCK, TB, TB)
    row_index, col_index = tile_index(tile_rows, tile_cols)
    degree = node_degree(blocks, row_index, col_index)
    highest = lax.Precision.HIGHEST

    def laplace(vectors):
        return degree[None, :] * vectors - symmetric_part(vectors, blocks, row_index, col_index)
    first_step = (laplace(start_vectors) - CENTER * start_vectors) / HALF_WIDTH
    filtered = 2.0 * (laplace(first_step) - CENTER * first_step) / HALF_WIDTH - start_vectors
    gram_matrix = jnp.dot(filtered, filtered.T, precision=highest) / NN
    factor = jnp.linalg.cholesky(gram_matrix)
    inverse = jax.scipy.linalg.solve_triangular(factor, jnp.eye(K, dtype=jnp.float32), lower=True)
    block = jnp.dot(inverse, filtered, precision=highest)
    image = laplace(block)
    rayleigh = jnp.dot(block, image.T, precision=highest) / NN
    ritz = jnp.dot(rayleigh.T, block, precision=highest)
    return (ritz, rayleigh)
```

```python
import functools

import jax
import jax.numpy as jnp
from jax import lax
from jax.experimental import pallas as pl
from jax.experimental.pallas import tpu as pltpu
from jax.sharding import PartitionSpec as P

CENTER = 1.0
HALF_WIDTH = 0.5
HIGHEST = lax.Precision.HIGHEST
NT = (((1,), (1,)), ((), ()))
NN = (((1,), (0,)), ((), ()))
BF16 = jnp.bfloat16
F32 = jnp.float32
VMEM = pl.BlockSpec(memory_space=pltpu.VMEM)
SMEM = pl.BlockSpec(memory_space=pltpu.SMEM)
DEGREE_ROWS = 16


def call(kernel, out_shape, scratch, limit, args, flops=0, smem=0):
    moved = sum(x.size * x.dtype.itemsize for x in args)
    return pl.pallas_call(
        kernel,
        out_shape=out_shape,
        in_specs=[SMEM] * smem + [VMEM] * (len(args) - smem),
        out_specs=jax.tree.map(lambda _: VMEM, out_shape),
        scratch_shapes=scratch,
        compiler_params=pltpu.CompilerParams(vmem_limit_bytes=limit * 2**20),
        cost_estimate=pl.CostEstimate(flops=flops, bytes_accessed=moved, transcendentals=0),
    )(*args)


def exchange(parts, axis):
    n = lax.axis_size(axis)
    return [
        lax.ppermute(part, axis, [(i, i ^ d) for i in range(n)])
        for d, part in zip(range(1, n), parts)
    ]


def tiles_first(ref, width):
    return [ref[:, k * width : (k + 1) * width] for k in range(ref.shape[1] // width)]


def round_kernel(vec_ref, out_ref):
    for k, piece in enumerate(tiles_first(vec_ref, out_ref.shape[2])):
        out_ref[k] = piece.astype(BF16)


def product_kernel(parts_n, degree, dims, meta, in_rows, out_rows, tiles_ref, *refs):
    part_refs, refs = refs[:parts_n], refs[parts_n:]
    own_ref, send_refs, (panel, total) = refs[0], refs[1:-2], refs[-2:]
    group, vectors_n, width = part_refs[0].shape
    me_in, me_out = meta[0], meta[1]
    for d, part in enumerate(part_refs):
        panel[d * group : (d + 1) * group, :vectors_n, :] = part[...]
    if degree:
        panel[:, vectors_n:, :] = jnp.ones(
            (panel.shape[0], panel.shape[1] - vectors_n, width), BF16
        )
    total[...] = jnp.zeros_like(total)
    for t in range(tiles_ref.shape[0]):
        source, target = in_rows[t], out_rows[t]
        source = ((source // group) ^ me_in) * group + source % group
        target = ((target // group) ^ me_out) * group + target % group
        total[target] += lax.dot_general(
            panel[source], tiles_ref[t], dims, preferred_element_type=F32
        )
    own_ref[...] = total[:group]
    for d, send in enumerate(send_refs, 1):
        send[:group] = total[d * group : (d + 1) * group, :vectors_n, :].astype(BF16)
        if degree:
            sums = jnp.concatenate(
                [total[d * group + k, vectors_n : vectors_n + 1, :] for k in range(group)], 0
            )
            high = sums.astype(BF16).astype(F32)
            low = (sums - high).astype(BF16).astype(F32)
            rest = sums - high - low
            pad = jnp.zeros((vectors_n - 3 * group, width), F32)
            send[group] = jnp.concatenate([high, low, rest, pad], 0).astype(BF16)


def products(tiles, in_rows, out_rows, meta, parts, out_n, dims, degree):
    group, vectors_n, width = parts[0].shape
    height = vectors_n + (DEGREE_ROWS if degree else 0)
    blocks = group + (1 if degree else 0)
    out_shape = [jax.ShapeDtypeStruct((group, height, width), F32)]
    out_shape += [jax.ShapeDtypeStruct((blocks, vectors_n, width), BF16)] * (out_n - 1)
    scratch = [
        pltpu.VMEM((len(parts) * group, height, width), BF16),
        pltpu.VMEM((out_n * group, height, width), F32),
    ]
    kernel = functools.partial(product_kernel, len(parts), degree, dims)
    flops = 2 * tiles.size * height
    args = [meta, in_rows, out_rows, tiles, *parts]
    own, *send = call(kernel, out_shape, scratch, 24, args, flops, 3)
    return own, send


def gathered_sum(own, received, k, rows):
    total = own[k, rows, :]
    for part in received:
        total = total + part[k, rows, :].astype(F32)
    return total


def first_kernel(rows_n, cols_n, vec_ref, row_own, col_own, *refs):
    row_refs, refs = refs[: cols_n - 1], refs[cols_n - 1 :]
    col_refs, refs = refs[: rows_n - 1], refs[rows_n - 1 :]
    first_ref, rounded_ref, degree_ref = refs
    group, vectors_n, width = rounded_ref.shape
    degree = jnp.zeros((group, width), F32)
    for own, received in ((row_own, row_refs), (col_own, col_refs)):
        degree += jnp.concatenate(
            [own[k, vectors_n : vectors_n + 1, :] for k in range(group)], 0
        )
        for part in received:
            block = part[group].astype(F32)
            degree += (block[2 * group : 3 * group] + block[group : 2 * group]) + block[:group]
    degree = 0.5 * degree
    degree_ref[...] = degree
    every = slice(0, vectors_n)
    for k, vec in enumerate(tiles_first(vec_ref, width)):
        symmetric = 0.5 * (
            gathered_sum(row_own, row_refs, k, every) + gathered_sum(col_own, col_refs, k, every)
        )
        image = degree[k : k + 1, :] * vec - symmetric
        first = (image - CENTER * vec) / HALF_WIDTH
        first_ref[:, k * width : (k + 1) * width] = first
        rounded_ref[k] = first.astype(BF16)


def filter_kernel(rows_n, cols_n, start_ref, first_ref, degree_ref, row_own, col_own, *refs):
    row_refs, refs = refs[: cols_n - 1], refs[cols_n - 1 :]
    col_refs, refs = refs[: rows_n - 1], refs[rows_n - 1 :]
    filtered_ref, rounded_ref, gram_ref, both = refs
    group, vectors_n, width = rounded_ref.shape
    every = slice(0, vectors_n)
    for k, vec in enumerate(tiles_first(first_ref, width)):
        symmetric = 0.5 * (
            gathered_sum(row_own, row_refs, k, every) + gathered_sum(col_own, col_refs, k, every)
        )
        columns = slice(k * width, (k + 1) * width)
        image = degree_ref[k : k + 1, :] * vec - symmetric
        filtered = 2.0 * (image - CENTER * vec) / HALF_WIDTH - start_ref[:, columns]
        filtered_ref[:, columns] = filtered
        rounded_ref[k] = filtered.astype(BF16)
        both[:vectors_n, columns] = filtered
        both[vectors_n:, columns] = degree_ref[k : k + 1, :] * filtered
    gram_ref[...] = lax.dot_general(
        filtered_ref[...], both[...], NT, precision=HIGHEST, preferred_element_type=F32
    )


def form_kernel(cols_n, rows_n, meta, tile_rows, tile_cols, tiles_ref, *refs):
    row_refs, refs = refs[:cols_n], refs[cols_n:]
    col_refs, refs = refs[:rows_n], refs[rows_n:]
    out_ref, row_panel, col_panel, total = refs
    group, vectors_n, width = row_refs[0].shape
    for d, part in enumerate(row_refs):
        row_panel[d * group : (d + 1) * group] = part[...]
    for d, part in enumerate(col_refs):
        col_panel[d * group : (d + 1) * group] = part[...]
    total[...] = jnp.zeros_like(total)
    for t in range(tiles_ref.shape[0]):
        row, col = tile_rows[t], tile_cols[t]
        row = ((row // group) ^ meta[1]) * group + row % group
        col = ((col // group) ^ meta[0]) * group + col % group
        product = lax.dot_general(
            col_panel[col], tiles_ref[t], NT, preferred_element_type=F32
        )
        total[...] += lax.dot_general(
            row_panel[row], product.astype(BF16), NT, preferred_element_type=F32
        )
    out_ref[...] = total[...]


def tree_sum(parts):
    while len(parts) > 1:
        parts = [a + b for a, b in zip(parts[::2], parts[1::2])]
    return parts[0]


def all_sum(part):
    for axis in ("col", "row"):
        n = lax.axis_size(axis)
        part = tree_sum([part, *exchange([part] * (n - 1), axis)])
    return part


def local(tiles, tile_rows, tile_cols, start):
    tiles, tile_rows, tile_cols = tiles[0, 0], tile_rows[0, 0], tile_cols[0, 0]
    width = tiles.shape[-1]
    vectors_n, own_nodes = start.shape
    rows_n, cols_n = lax.axis_size("row"), lax.axis_size("col")
    total_nodes = own_nodes * rows_n * cols_n
    group = own_nodes // width
    row_me, col_me = lax.axis_index("row"), lax.axis_index("col")
    meta = jnp.stack([row_me, col_me]).astype(jnp.int32)
    swapped = jnp.stack([col_me, row_me]).astype(jnp.int32)

    rounded_shape = jax.ShapeDtypeStruct((group, vectors_n, width), BF16)
    vector_shape = jax.ShapeDtypeStruct((vectors_n, own_nodes), F32)

    def gather(rounded):
        col_parts = [rounded, *exchange([rounded] * (rows_n - 1), "row")]
        row_parts = [rounded, *exchange([rounded] * (cols_n - 1), "col")]
        return col_parts, row_parts

    def apply(rounded, degree):
        col_parts, row_parts = gather(rounded)
        col_own, col_send = products(
            tiles, tile_rows, tile_cols, swapped, row_parts, rows_n, NN, degree
        )
        col_got = exchange(col_send, "row")
        row_own, row_send = products(
            tiles, tile_cols, tile_rows, meta, col_parts, cols_n, NT, degree
        )
        row_got = exchange(row_send, "col")
        return [row_own, col_own, *row_got, *col_got]

    rounded = call(round_kernel, rounded_shape, [], 16, [start])
    sums = apply(rounded, True)
    first, rounded, degree = call(
        functools.partial(first_kernel, rows_n, cols_n),
        [vector_shape, rounded_shape, jax.ShapeDtypeStruct((group, width), F32)],
        [],
        24,
        [start, *sums],
    )
    sums = apply(rounded, False)
    filtered, rounded, gram = call(
        functools.partial(filter_kernel, rows_n, cols_n),
        [vector_shape, rounded_shape, jax.ShapeDtypeStruct((vectors_n, 2 * vectors_n), F32)],
        [pltpu.VMEM((2 * vectors_n, own_nodes), F32)],
        24,
        [start, first, degree, *sums],
    )
    col_parts, row_parts = gather(rounded)
    gram = all_sum(gram) / total_nodes
    factor = jnp.linalg.cholesky(gram[:, :vectors_n])
    inverse = jax.scipy.linalg.solve_triangular(
        factor, jnp.eye(vectors_n, dtype=F32), lower=True
    )
    form = call(
        functools.partial(form_kernel, cols_n, rows_n),
        jax.ShapeDtypeStruct((vectors_n, vectors_n), F32),
        [
            pltpu.VMEM((cols_n * group, vectors_n, width), BF16),
            pltpu.VMEM((rows_n * group, vectors_n, width), BF16),
            pltpu.VMEM((vectors_n, vectors_n), F32),
        ],
        24,
        [meta, tile_rows, tile_cols, tiles, *row_parts, *col_parts],
        2 * tiles.size * vectors_n,
        3,
    )
    form = all_sum(form) / total_nodes
    projected = gram[:, vectors_n:] - 0.5 * (form + form.T)
    rayleigh = jnp.dot(
        jnp.dot(inverse, projected, precision=HIGHEST), inverse.T, precision=HIGHEST
    )
    ritz = jnp.dot(
        jnp.dot(rayleigh.T, inverse, precision=HIGHEST), filtered, precision=HIGHEST
    )
    return (ritz, rayleigh)


def solution(mesh):
    placed = (
        P("row", "col", None, None, None),
        P("row", "col", None),
        P("row", "col", None),
        P(None, ("row", "col")),
    )
    return jax.shard_map(
        local, mesh=mesh, in_specs=placed, out_specs=(P(None, ("row", "col")), P()), check_vma=False
    )
```

```python
import functools

import jax
import jax.numpy as jnp
from jax import lax
from jax.experimental import pallas as pl
from jax.experimental.pallas import tpu as pltpu
from jax.sharding import PartitionSpec as P

CENTER = 1.0
HALF_WIDTH = 0.5
HIGHEST = lax.Precision.HIGHEST
NT = (((1,), (1,)), ((), ()))
NN = (((1,), (0,)), ((), ()))
BF16 = jnp.bfloat16
F32 = jnp.float32
VMEM = pl.BlockSpec(memory_space=pltpu.VMEM)
SMEM = pl.BlockSpec(memory_space=pltpu.SMEM)
DEGREE_ROWS = 16


def call(kernel, out_shape, scratch, limit, args, flops=0, smem=0):
    moved = sum(x.size * x.dtype.itemsize for x in args)
    return pl.pallas_call(
        kernel,
        out_shape=out_shape,
        in_specs=[SMEM] * smem + [VMEM] * (len(args) - smem),
        out_specs=jax.tree.map(lambda _: VMEM, out_shape),
        scratch_shapes=scratch,
        compiler_params=pltpu.CompilerParams(vmem_limit_bytes=limit * 2**20),
        cost_estimate=pl.CostEstimate(flops=flops, bytes_accessed=moved, transcendentals=0),
    )(*args)


def swap(parts, axis):
    return lax.all_to_all(parts, axis, 0, 0, tiled=True)


def exchange(parts, axis):
    n = lax.axis_size(axis)
    return [
        lax.ppermute(part, axis, [(i, i ^ d) for i in range(n)])
        for d, part in zip(range(1, n), parts)
    ]


def tiles_first(ref, width):
    return [ref[:, k * width : (k + 1) * width] for k in range(ref.shape[1] // width)]


def round_kernel(vec_ref, *out_refs):
    width = out_refs[0].shape[3]
    for k, piece in enumerate(tiles_first(vec_ref, width)):
        store_copies(out_refs, k, piece.astype(BF16))


def store_copies(out_refs, k, piece):
    for out in out_refs:
        for d in range(out.shape[0]):
            out[d, k] = piece


def product_kernel(degree, dims, meta, in_rows, out_rows, tiles_ref, parts_ref, own_ref, send_ref, panel, total):
    parts_n, group, vectors_n, width = parts_ref.shape
    for d in range(parts_n):
        panel[d * group : (d + 1) * group, :vectors_n, :] = parts_ref[d]
    if degree:
        panel[:, vectors_n:, :] = jnp.ones(
            (panel.shape[0], panel.shape[1] - vectors_n, width), BF16
        )
    total[...] = jnp.zeros_like(total)
    for t in range(tiles_ref.shape[0]):
        total[out_rows[t]] += lax.dot_general(
            panel[in_rows[t]], tiles_ref[t], dims, preferred_element_type=F32
        )
    own_ref[...] = total[pl.ds(meta[0] * group, group)]
    for d in range(send_ref.shape[0]):
        send_ref[d, :group] = total[d * group : (d + 1) * group, :vectors_n, :].astype(BF16)
        if degree:
            sums = jnp.concatenate(
                [total[d * group + k, vectors_n : vectors_n + 1, :] for k in range(group)], 0
            )
            high = sums.astype(BF16).astype(F32)
            low = (sums - high).astype(BF16).astype(F32)
            rest = sums - high - low
            pad = jnp.zeros((vectors_n - 3 * group, width), F32)
            send_ref[d, group] = jnp.concatenate([high, low, rest, pad], 0).astype(BF16)
    send_ref[meta[0]] = jnp.zeros(send_ref.shape[1:], BF16)


def products(tiles, in_rows, out_rows, meta, parts, out_n, dims, degree):
    parts_n, group, vectors_n, width = parts.shape
    height = vectors_n + (DEGREE_ROWS if degree else 0)
    blocks = group + (1 if degree else 0)
    out_shape = [
        jax.ShapeDtypeStruct((group, height, width), F32),
        jax.ShapeDtypeStruct((out_n, blocks, vectors_n, width), BF16),
    ]
    scratch = [
        pltpu.VMEM((parts_n * group, height, width), BF16),
        pltpu.VMEM((out_n * group, height, width), F32),
    ]
    kernel = functools.partial(product_kernel, degree, dims)
    flops = 2 * tiles.size * height
    args = [meta, in_rows, out_rows, tiles, parts]
    return call(kernel, out_shape, scratch, 24, args, flops, 3)


def gathered_sum(own, received, k, rows):
    total = own[k, rows, :]
    for d in range(received.shape[0]):
        total = total + received[d, k, rows, :].astype(F32)
    return total


def first_kernel(vec_ref, row_own, row_got, col_own, col_got, first_ref, degree_ref, *out_refs):
    group, vectors_n, width = out_refs[0].shape[1:]
    degree = jnp.zeros((group, width), F32)
    for own, received in ((row_own, row_got), (col_own, col_got)):
        degree += jnp.concatenate(
            [own[k, vectors_n : vectors_n + 1, :] for k in range(group)], 0
        )
        for d in range(received.shape[0]):
            block = received[d, group].astype(F32)
            degree += (block[2 * group : 3 * group] + block[group : 2 * group]) + block[:group]
    degree = 0.5 * degree
    degree_ref[...] = degree
    every = slice(0, vectors_n)
    for k, vec in enumerate(tiles_first(vec_ref, width)):
        symmetric = 0.5 * (
            gathered_sum(row_own, row_got, k, every) + gathered_sum(col_own, col_got, k, every)
        )
        image = degree[k : k + 1, :] * vec - symmetric
        first = (image - CENTER * vec) / HALF_WIDTH
        first_ref[:, k * width : (k + 1) * width] = first
        store_copies(out_refs, k, first.astype(BF16))


def filter_kernel(
    start_ref, first_ref, degree_ref, row_own, row_got, col_own, col_got, filtered_ref, gram_ref, *refs
):
    out_refs, both = refs[:-1], refs[-1]
    group, vectors_n, width = out_refs[0].shape[1:]
    every = slice(0, vectors_n)
    for k, vec in enumerate(tiles_first(first_ref, width)):
        symmetric = 0.5 * (
            gathered_sum(row_own, row_got, k, every) + gathered_sum(col_own, col_got, k, every)
        )
        columns = slice(k * width, (k + 1) * width)
        image = degree_ref[k : k + 1, :] * vec - symmetric
        filtered = 2.0 * (image - CENTER * vec) / HALF_WIDTH - start_ref[:, columns]
        filtered_ref[:, columns] = filtered
        store_copies(out_refs, k, filtered.astype(BF16))
        both[:vectors_n, columns] = filtered
        both[vectors_n:, columns] = degree_ref[k : k + 1, :] * filtered
    gram_ref[...] = lax.dot_general(
        filtered_ref[...], both[...], NT, precision=HIGHEST, preferred_element_type=F32
    )


def form_kernel(tile_rows, tile_cols, tiles_ref, row_parts, col_parts, out_ref, total):
    group = row_parts.shape[1]
    total[...] = jnp.zeros_like(total)
    for t in range(tiles_ref.shape[0]):
        row, col = tile_rows[t], tile_cols[t]
        product = lax.dot_general(
            col_parts[col // group, col % group], tiles_ref[t], NT, preferred_element_type=F32
        )
        total[...] += lax.dot_general(
            row_parts[row // group, row % group],
            product.astype(BF16),
            NT,
            preferred_element_type=F32,
        )
    out_ref[...] = total[...]


def tree_sum(parts):
    while len(parts) > 1:
        parts = [a + b for a, b in zip(parts[::2], parts[1::2])]
    return parts[0]


def all_sum(part):
    for axis in ("col", "row"):
        n = lax.axis_size(axis)
        part = tree_sum([part, *exchange([part] * (n - 1), axis)])
    return part


def local(tiles, tile_rows, tile_cols, start):
    tiles, tile_rows, tile_cols = tiles[0, 0], tile_rows[0, 0], tile_cols[0, 0]
    width = tiles.shape[-1]
    vectors_n, own_nodes = start.shape
    rows_n, cols_n = lax.axis_size("row"), lax.axis_size("col")
    total_nodes = own_nodes * rows_n * cols_n
    group = own_nodes // width
    row_me = lax.axis_index("row").astype(jnp.int32)[None]
    col_me = lax.axis_index("col").astype(jnp.int32)[None]

    rounded_shapes = [
        jax.ShapeDtypeStruct((n, group, vectors_n, width), BF16) for n in (rows_n, cols_n)
    ]
    vector_shape = jax.ShapeDtypeStruct((vectors_n, own_nodes), F32)

    def apply(to_rows, to_cols, degree):
        col_parts = swap(to_rows, "row")
        row_parts = swap(to_cols, "col")
        row_own, row_send = products(
            tiles, tile_cols, tile_rows, col_me, col_parts, cols_n, NT, degree
        )
        col_own, col_send = products(
            tiles, tile_rows, tile_cols, row_me, row_parts, rows_n, NN, degree
        )
        return [row_own, swap(row_send, "col"), col_own, swap(col_send, "row")]

    rounded = call(round_kernel, rounded_shapes, [], 16, [start])
    sums = apply(*rounded, True)
    first, degree, *rounded = call(
        first_kernel,
        [vector_shape, jax.ShapeDtypeStruct((group, width), F32), *rounded_shapes],
        [],
        24,
        [start, *sums],
    )
    sums = apply(*rounded, False)
    filtered, gram, *rounded = call(
        filter_kernel,
        [
            vector_shape,
            jax.ShapeDtypeStruct((vectors_n, 2 * vectors_n), F32),
            *rounded_shapes,
        ],
        [pltpu.VMEM((2 * vectors_n, own_nodes), F32)],
        24,
        [start, first, degree, *sums],
    )
    col_parts, row_parts = swap(rounded[0], "row"), swap(rounded[1], "col")
    gram = all_sum(gram) / total_nodes
    factor = jnp.linalg.cholesky(gram[:, :vectors_n])
    inverse = jax.scipy.linalg.solve_triangular(
        factor, jnp.eye(vectors_n, dtype=F32), lower=True
    )
    form = call(
        form_kernel,
        jax.ShapeDtypeStruct((vectors_n, vectors_n), F32),
        [pltpu.VMEM((vectors_n, vectors_n), F32)],
        24,
        [tile_rows, tile_cols, tiles, row_parts, col_parts],
        2 * tiles.size * vectors_n,
        2,
    )
    form = all_sum(form) / total_nodes
    projected = gram[:, vectors_n:] - 0.5 * (form + form.T)
    rayleigh = jnp.dot(
        jnp.dot(inverse, projected, precision=HIGHEST), inverse.T, precision=HIGHEST
    )
    ritz = jnp.dot(
        jnp.dot(rayleigh.T, inverse, precision=HIGHEST), filtered, precision=HIGHEST
    )
    return (ritz, rayleigh)


def solution(mesh):
    placed = (
        P("row", "col", None, None, None),
        P("row", "col", None),
        P("row", "col", None),
        P(None, ("row", "col")),
    )
    return jax.shard_map(
        local, mesh=mesh, in_specs=placed, out_specs=(P(None, ("row", "col")), P()), check_vma=False
    )
```

```python
import functools

import jax
import jax.numpy as jnp
from jax import lax
from jax.experimental import pallas as pl
from jax.experimental.pallas import tpu as pltpu
from jax.sharding import PartitionSpec as P

CENTER = 1.0
HALF_WIDTH = 0.5
HIGHEST = lax.Precision.HIGHEST
NT = (((1,), (1,)), ((), ()))
NN = (((1,), (0,)), ((), ()))
BF16 = jnp.bfloat16
F32 = jnp.float32
VMEM = pl.BlockSpec(memory_space=pltpu.VMEM)
SMEM = pl.BlockSpec(memory_space=pltpu.SMEM)
DEGREE_ROWS = 16


def call(kernel, out_shape, scratch, limit, args, flops=0, smem=0):
    moved = sum(x.size * x.dtype.itemsize for x in args)
    return pl.pallas_call(
        kernel,
        out_shape=out_shape,
        in_specs=[SMEM] * smem + [VMEM] * (len(args) - smem),
        out_specs=jax.tree.map(lambda _: VMEM, out_shape),
        scratch_shapes=scratch,
        compiler_params=pltpu.CompilerParams(vmem_limit_bytes=limit * 2**20),
        cost_estimate=pl.CostEstimate(flops=flops, bytes_accessed=moved, transcendentals=0),
    )(*args)


def trade(part, axis, d):
    n = lax.axis_size(axis)
    return lax.ppermute(part, axis, [(i, i ^ d) for i in range(n)])


def exchange(parts, axis, step=1):
    return [trade(part, axis, step * d) for d, part in enumerate(parts, 1)]


def tiles_first(ref, width):
    return [ref[:, k * width : (k + 1) * width] for k in range(ref.shape[1] // width)]


def round_kernel(vec_ref, out_ref):
    for k, piece in enumerate(tiles_first(vec_ref, out_ref.shape[2])):
        out_ref[k] = piece.astype(BF16)


def split_degree(sums, height):
    high = sums.astype(BF16).astype(F32)
    low = (sums - high).astype(BF16).astype(F32)
    rest = sums - high - low
    pad = jnp.zeros((height - 3 * sums.shape[0], sums.shape[1]), F32)
    return jnp.concatenate([high, low, rest, pad], 0).astype(BF16)


def join_degree(block, group):
    block = block.astype(F32)
    return (block[2 * group : 3 * group] + block[group : 2 * group]) + block[:group]


def degree_of(total, start, group, vectors_n):
    return jnp.concatenate(
        [total[start + k, vectors_n : vectors_n + 1, :] for k in range(group)], 0
    )


def place(tile, group, me, halves):
    apart = (tile // group) ^ me
    if halves:
        apart = (apart % 2) * halves + apart // 2
    return apart * group + tile % group


def product_kernel(parts_n, degree, dims, halves, meta, in_rows, out_rows, tiles_ref, *refs):
    part_refs, refs = refs[:parts_n], refs[parts_n:]
    own_ref, send_refs, (panel, total) = refs[0], refs[1:-2], refs[-2:]
    group, vectors_n, width = own_ref.shape[-3], part_refs[0].shape[-2], own_ref.shape[-1]
    place_at = 0
    for part in part_refs:
        blocks = part.reshape(-1, vectors_n, width)
        count = blocks.shape[0]
        panel[place_at : place_at + count, :vectors_n, :] = blocks[...]
        place_at += count
    if degree:
        panel[:, vectors_n:, :] = jnp.ones(
            (panel.shape[0], panel.shape[1] - vectors_n, width), BF16
        )
    total[...] = jnp.zeros_like(total)
    for t in range(tiles_ref.shape[0]):
        source = place(in_rows[t], group, meta[0], halves[0])
        target = place(out_rows[t], group, meta[1], halves[1])
        total[target] += lax.dot_general(
            panel[source], tiles_ref[t], dims, preferred_element_type=F32
        )
    kept = 1
    if halves[1]:
        kept = halves[1]
        for d in range(kept):
            own_ref[d] = total[d * group : (d + 1) * group]
        sends = [send_refs[0].at[d] for d in range(kept)]
    else:
        own_ref[...] = total[:group]
        sends = send_refs
    for d, send in enumerate(sends, kept):
        send[:group] = total[d * group : (d + 1) * group, :vectors_n, :].astype(BF16)
        if degree:
            send[group] = split_degree(degree_of(total, d * group, group, vectors_n), vectors_n)


def products(tiles, in_rows, out_rows, meta, parts, group, out_n, dims, halves, degree):
    vectors_n, width = parts[0].shape[-2:]
    height = vectors_n + (DEGREE_ROWS if degree else 0)
    blocks = group + (1 if degree else 0)
    half = halves[1]
    if half:
        out_shape = [
            jax.ShapeDtypeStruct((half, group, height, width), F32),
            jax.ShapeDtypeStruct((half, blocks, vectors_n, width), BF16),
        ]
    else:
        out_shape = [jax.ShapeDtypeStruct((group, height, width), F32)]
        out_shape += [jax.ShapeDtypeStruct((blocks, vectors_n, width), BF16)] * (out_n - 1)
    in_blocks = sum(part.size for part in parts) // (vectors_n * width)
    scratch = [
        pltpu.VMEM((in_blocks, height, width), BF16),
        pltpu.VMEM((out_n * group, height, width), F32),
    ]
    kernel = functools.partial(product_kernel, len(parts), degree, dims, halves)
    flops = 2 * tiles.size * height
    args = [meta, in_rows, out_rows, tiles, *parts]
    own, *send = call(kernel, out_shape, scratch, 24, args, flops, 3)
    return own, send


def merge_kernel(degree, kept, got, own_ref, *send_refs):
    _, group, height, width = kept.shape
    vectors_n = got.shape[2]
    for k in range(group):
        own_ref[k, :vectors_n, :] = kept[0, k, :vectors_n, :] + got[0, k].astype(F32)
        for d, send in enumerate(send_refs, 1):
            send[k] = (kept[d, k, :vectors_n, :] + got[d, k].astype(F32)).astype(BF16)
    if degree:
        sums = [
            degree_of(kept.at[d], 0, group, vectors_n) + join_degree(got[d, group], group)
            for d in range(kept.shape[0])
        ]
        for k in range(group):
            own_ref[k, vectors_n:, :] = jnp.broadcast_to(
                sums[0][k : k + 1], (height - vectors_n, width)
            )
        for d, send in enumerate(send_refs, 1):
            send[group] = split_degree(sums[d], vectors_n)


def merge(kept, got, degree):
    out_shape = [jax.ShapeDtypeStruct(kept.shape[1:], F32)]
    out_shape += [jax.ShapeDtypeStruct(got.shape[1:], BF16)] * (kept.shape[0] - 1)
    own, *send = call(functools.partial(merge_kernel, degree), out_shape, [], 24, [kept, got])
    return own, send


def gathered_sum(own, received, k, rows):
    total = own[k, rows, :]
    for part in received:
        total = total + part[k, rows, :].astype(F32)
    return total


def first_kernel(rows_n, chips_n, vec_ref, row_own, col_own, *refs):
    row_refs, refs = refs[: chips_n - 1], refs[chips_n - 1 :]
    col_refs, refs = refs[: rows_n - 1], refs[rows_n - 1 :]
    first_ref, rounded_ref, degree_ref = refs
    group, vectors_n, width = rounded_ref.shape
    degree = jnp.zeros((group, width), F32)
    for own, received in ((row_own, row_refs), (col_own, col_refs)):
        degree += degree_of(own, 0, group, vectors_n)
        for part in received:
            degree += join_degree(part[group], group)
    degree = 0.5 * degree
    degree_ref[...] = degree
    every = slice(0, vectors_n)
    for k, vec in enumerate(tiles_first(vec_ref, width)):
        symmetric = 0.5 * (
            gathered_sum(row_own, row_refs, k, every) + gathered_sum(col_own, col_refs, k, every)
        )
        image = degree[k : k + 1, :] * vec - symmetric
        first = (image - CENTER * vec) / HALF_WIDTH
        first_ref[:, k * width : (k + 1) * width] = first
        rounded_ref[k] = first.astype(BF16)


def filter_kernel(rows_n, chips_n, start_ref, first_ref, degree_ref, row_own, col_own, *refs):
    row_refs, refs = refs[: chips_n - 1], refs[chips_n - 1 :]
    col_refs, refs = refs[: rows_n - 1], refs[rows_n - 1 :]
    filtered_ref, rounded_ref, gram_ref, both = refs
    group, vectors_n, width = rounded_ref.shape
    every = slice(0, vectors_n)
    for k, vec in enumerate(tiles_first(first_ref, width)):
        symmetric = 0.5 * (
            gathered_sum(row_own, row_refs, k, every) + gathered_sum(col_own, col_refs, k, every)
        )
        columns = slice(k * width, (k + 1) * width)
        image = degree_ref[k : k + 1, :] * vec - symmetric
        filtered = 2.0 * (image - CENTER * vec) / HALF_WIDTH - start_ref[:, columns]
        filtered_ref[:, columns] = filtered
        rounded_ref[k] = filtered.astype(BF16)
        both[:vectors_n, columns] = filtered
        both[vectors_n:, columns] = degree_ref[k : k + 1, :] * filtered
    gram_ref[...] = lax.dot_general(
        filtered_ref[...], both[...], NT, precision=HIGHEST, preferred_element_type=F32
    )


def form_kernel(parts_n, halves, meta, tile_rows, tile_cols, tiles_ref, gram_ref, *refs):
    part_refs, (out_ref, panel, left, right) = refs[:parts_n], refs[parts_n:]
    group, (_, vectors_n, width) = part_refs[-1].shape[0], panel.shape
    place_at = 0
    for part in part_refs:
        blocks = part.reshape(-1, vectors_n, width)
        panel[place_at : place_at + blocks.shape[0]] = blocks[...]
        place_at += blocks.shape[0]
    cols_at = 2 * halves * group
    for t in range(tiles_ref.shape[0]):
        row = place(tile_rows[t], group, meta[1], halves)
        col = place(tile_cols[t], group, meta[0], 0) + cols_at
        columns = slice(t * width, (t + 1) * width)
        left[:, columns] = panel[row]
        right[:, columns] = lax.dot_general(
            panel[col], tiles_ref[t], NT, preferred_element_type=F32
        ).astype(BF16)
    form = lax.dot_general(left[...], right[...], NT, preferred_element_type=F32)
    out_ref[...] = jnp.concatenate([gram_ref[...], form], 1)


def all_sum(part):
    for axis in ("col", "row"):
        d = 1
        while d < lax.axis_size(axis):
            part = part + trade(part, axis, d)
            d *= 2
    return part


def local(tiles, tile_rows, tile_cols, start):
    tiles, tile_rows, tile_cols = tiles[0, 0], tile_rows[0, 0], tile_cols[0, 0]
    width = tiles.shape[-1]
    vectors_n, own_nodes = start.shape
    rows_n, cols_n = lax.axis_size("row"), lax.axis_size("col")
    total_nodes = own_nodes * rows_n * cols_n
    group = own_nodes // width
    row_me, col_me = lax.axis_index("row"), lax.axis_index("col")
    meta = jnp.stack([row_me, col_me]).astype(jnp.int32)
    swapped = jnp.stack([col_me, row_me]).astype(jnp.int32)

    rounded_shape = jax.ShapeDtypeStruct((group, vectors_n, width), BF16)
    vector_shape = jax.ShapeDtypeStruct((vectors_n, own_nodes), F32)

    chips_n = cols_n // 2

    def gather(rounded):
        chips = jnp.stack([rounded, *exchange([rounded] * (chips_n - 1), "col", 2)])
        col_parts = [rounded, *exchange([rounded] * (rows_n - 1), "row")]
        return col_parts, [chips, trade(chips, "col", 1)]

    def apply(rounded, degree):
        col_parts, row_parts = gather(rounded)
        col_own, col_send = products(
            tiles, tile_rows, tile_cols, swapped, row_parts, group, rows_n, NN, (chips_n, 0), degree
        )
        col_got = exchange(col_send, "row")
        kept, (send,) = products(
            tiles, tile_cols, tile_rows, meta, col_parts, group, cols_n, NT, (0, chips_n), degree
        )
        row_own, row_send = merge(kept, trade(send, "col", 1), degree)
        row_got = exchange(row_send, "col", 2)
        return [row_own, col_own, *row_got, *col_got]

    rounded = call(round_kernel, rounded_shape, [], 16, [start])
    sums = apply(rounded, True)
    first, rounded, degree = call(
        functools.partial(first_kernel, rows_n, chips_n),
        [vector_shape, rounded_shape, jax.ShapeDtypeStruct((group, width), F32)],
        [],
        24,
        [start, *sums],
    )
    sums = apply(rounded, False)
    filtered, rounded, gram = call(
        functools.partial(filter_kernel, rows_n, chips_n),
        [vector_shape, rounded_shape, jax.ShapeDtypeStruct((vectors_n, 2 * vectors_n), F32)],
        [pltpu.VMEM((2 * vectors_n, own_nodes), F32)],
        24,
        [start, first, degree, *sums],
    )
    col_parts, row_parts = gather(rounded)
    parts = [*row_parts, *col_parts]
    spread = (vectors_n, tiles.shape[0] * width)
    form = call(
        functools.partial(form_kernel, len(parts), chips_n),
        jax.ShapeDtypeStruct((vectors_n, 3 * vectors_n), F32),
        [
            pltpu.VMEM(((cols_n + rows_n) * group, vectors_n, width), BF16),
            pltpu.VMEM(spread, BF16),
            pltpu.VMEM(spread, BF16),
        ],
        24,
        [meta, tile_rows, tile_cols, tiles, gram, *parts],
        2 * tiles.size * vectors_n,
        3,
    )
    sums = all_sum(form) / total_nodes
    gram, scaled, form = (sums[:, i * vectors_n : (i + 1) * vectors_n] for i in range(3))
    factor = jnp.linalg.cholesky(gram)
    inverse = jax.scipy.linalg.solve_triangular(
        factor, jnp.eye(vectors_n, dtype=F32), lower=True
    )
    projected = scaled - 0.5 * (form + form.T)
    rayleigh = jnp.dot(
        jnp.dot(inverse, projected, precision=HIGHEST), inverse.T, precision=HIGHEST
    )
    ritz = jnp.dot(
        jnp.dot(rayleigh.T, inverse, precision=HIGHEST), filtered, precision=HIGHEST
    )
    return (ritz, rayleigh)


def solution(mesh):
    placed = (
        P("row", "col", None, None, None),
        P("row", "col", None),
        P("row", "col", None),
        P(None, ("row", "col")),
    )
    return jax.shard_map(
        local, mesh=mesh, in_specs=placed, out_specs=(P(None, ("row", "col")), P()), check_vma=False
    )
```

```python
import functools

import jax
import jax.numpy as jnp
from jax import lax
from jax.experimental import pallas as pl
from jax.experimental.pallas import tpu as pltpu
from jax.sharding import PartitionSpec as P

CENTER = 1.0
HALF_WIDTH = 0.5
HIGHEST = lax.Precision.HIGHEST
NT = (((1,), (1,)), ((), ()))
NN = (((1,), (0,)), ((), ()))
BF16 = jnp.bfloat16
F32 = jnp.float32
VMEM = pl.BlockSpec(memory_space=pltpu.VMEM)
SMEM = pl.BlockSpec(memory_space=pltpu.SMEM)
ANY = pl.BlockSpec(memory_space=pl.ANY)
DEGREE_ROWS = 16


def call(kernel, out_shape, scratch, limit, args, flops=0, smem=0, after=()):
    moved = sum(x.size * x.dtype.itemsize for x in args)
    return pl.pallas_call(
        lambda *refs: kernel(*refs[len(after) :]),
        out_shape=out_shape,
        in_specs=[ANY] * len(after) + [SMEM] * smem + [VMEM] * (len(args) - smem),
        out_specs=jax.tree.map(lambda _: VMEM, out_shape),
        scratch_shapes=scratch,
        compiler_params=pltpu.CompilerParams(vmem_limit_bytes=limit * 2**20),
        cost_estimate=pl.CostEstimate(flops=flops, bytes_accessed=moved, transcendentals=0),
    )(*after, *args)


def trade(part, axis, d):
    n = lax.axis_size(axis)
    return lax.ppermute(part, axis, [(i, i ^ d) for i in range(n)])


def exchange(parts, axis, step=1):
    return [trade(part, axis, step * d) for d, part in enumerate(parts, 1)]


def tiles_first(ref, width):
    return [ref[:, k * width : (k + 1) * width] for k in range(ref.shape[1] // width)]


def round_kernel(vec_ref, out_ref):
    for k, piece in enumerate(tiles_first(vec_ref, out_ref.shape[2])):
        out_ref[k] = piece.astype(BF16)


def split_degree(sums, height):
    high = sums.astype(BF16).astype(F32)
    low = (sums - high).astype(BF16).astype(F32)
    rest = sums - high - low
    pad = jnp.zeros((height - 3 * sums.shape[0], sums.shape[1]), F32)
    return jnp.concatenate([high, low, rest, pad], 0).astype(BF16)


def join_degree(block, group):
    block = block.astype(F32)
    return (block[2 * group : 3 * group] + block[group : 2 * group]) + block[:group]


def degree_of(total, start, group, vectors_n):
    return jnp.concatenate(
        [total[start + k, vectors_n : vectors_n + 1, :] for k in range(group)], 0
    )


def place(tile, group, me, halves):
    apart = (tile // group) ^ me
    if halves:
        apart = (apart % 2) * halves + apart // 2
    return apart * group + tile % group


def product_kernel(parts_n, degree, dims, halves, meta, in_rows, out_rows, tiles_ref, *refs):
    part_refs, refs = refs[:parts_n], refs[parts_n:]
    own_ref, send_refs, (panel, total) = refs[0], refs[1:-2], refs[-2:]
    group, vectors_n, width = own_ref.shape[-3], part_refs[0].shape[-2], own_ref.shape[-1]
    place_at = 0
    for part in part_refs:
        blocks = part.reshape(-1, vectors_n, width)
        count = blocks.shape[0]
        panel[place_at : place_at + count, :vectors_n, :] = blocks[...]
        place_at += count
    if degree:
        panel[:, vectors_n:, :] = jnp.ones(
            (panel.shape[0], panel.shape[1] - vectors_n, width), BF16
        )
    total[...] = jnp.zeros_like(total)
    for t in range(tiles_ref.shape[0]):
        source = place(in_rows[t], group, meta[0], halves[0])
        target = place(out_rows[t], group, meta[1], halves[1])
        total[target] += lax.dot_general(
            panel[source], tiles_ref[t], dims, preferred_element_type=F32
        )
    kept = 1
    if halves[1]:
        kept = halves[1]
        for d in range(kept):
            own_ref[d] = total[d * group : (d + 1) * group]
        sends = [send_refs[0].at[d] for d in range(kept)]
    else:
        own_ref[...] = total[:group]
        sends = send_refs
    for d, send in enumerate(sends, kept):
        send[:group] = total[d * group : (d + 1) * group, :vectors_n, :].astype(BF16)
        if degree:
            send[group] = split_degree(degree_of(total, d * group, group, vectors_n), vectors_n)


def products(tiles, in_rows, out_rows, meta, parts, group, out_n, dims, halves, degree, after=()):
    vectors_n, width = parts[0].shape[-2:]
    height = vectors_n + (DEGREE_ROWS if degree else 0)
    blocks = group + (1 if degree else 0)
    half = halves[1]
    if half:
        out_shape = [
            jax.ShapeDtypeStruct((half, group, height, width), F32),
            jax.ShapeDtypeStruct((half, blocks, vectors_n, width), BF16),
        ]
    else:
        out_shape = [jax.ShapeDtypeStruct((group, height, width), F32)]
        out_shape += [jax.ShapeDtypeStruct((blocks, vectors_n, width), BF16)] * (out_n - 1)
    in_blocks = sum(part.size for part in parts) // (vectors_n * width)
    scratch = [
        pltpu.VMEM((in_blocks, height, width), BF16),
        pltpu.VMEM((out_n * group, height, width), F32),
    ]
    kernel = functools.partial(product_kernel, len(parts), degree, dims, halves)
    flops = 2 * tiles.size * height
    args = [meta, in_rows, out_rows, tiles, *parts]
    own, *send = call(kernel, out_shape, scratch, 24, args, flops, 3, after)
    return own, send


def merge_kernel(degree, kept, got, own_ref, *send_refs):
    _, group, height, width = kept.shape
    vectors_n = got.shape[2]
    for k in range(group):
        own_ref[k, :vectors_n, :] = kept[0, k, :vectors_n, :] + got[0, k].astype(F32)
        for d, send in enumerate(send_refs, 1):
            send[k] = (kept[d, k, :vectors_n, :] + got[d, k].astype(F32)).astype(BF16)
    if degree:
        sums = [
            degree_of(kept.at[d], 0, group, vectors_n) + join_degree(got[d, group], group)
            for d in range(kept.shape[0])
        ]
        for k in range(group):
            own_ref[k, vectors_n:, :] = jnp.broadcast_to(
                sums[0][k : k + 1], (height - vectors_n, width)
            )
        for d, send in enumerate(send_refs, 1):
            send[group] = split_degree(sums[d], vectors_n)


def merge(kept, got, degree):
    out_shape = [jax.ShapeDtypeStruct(kept.shape[1:], F32)]
    out_shape += [jax.ShapeDtypeStruct(got.shape[1:], BF16)] * (kept.shape[0] - 1)
    own, *send = call(functools.partial(merge_kernel, degree), out_shape, [], 24, [kept, got])
    return own, send


def gathered_sum(own, received, k, rows):
    total = own[k, rows, :]
    for part in received:
        total = total + part[k, rows, :].astype(F32)
    return total


def first_kernel(rows_n, chips_n, vec_ref, row_own, col_own, *refs):
    row_refs, refs = refs[: chips_n - 1], refs[chips_n - 1 :]
    col_refs, refs = refs[: rows_n - 1], refs[rows_n - 1 :]
    first_ref, rounded_ref, degree_ref = refs
    group, vectors_n, width = rounded_ref.shape
    degree = jnp.zeros((group, width), F32)
    for own, received in ((row_own, row_refs), (col_own, col_refs)):
        degree += degree_of(own, 0, group, vectors_n)
        for part in received:
            degree += join_degree(part[group], group)
    degree = 0.5 * degree
    degree_ref[...] = degree
    every = slice(0, vectors_n)
    for k, vec in enumerate(tiles_first(vec_ref, width)):
        symmetric = 0.5 * (
            gathered_sum(row_own, row_refs, k, every) + gathered_sum(col_own, col_refs, k, every)
        )
        image = degree[k : k + 1, :] * vec - symmetric
        first = (image - CENTER * vec) / HALF_WIDTH
        first_ref[:, k * width : (k + 1) * width] = first
        rounded_ref[k] = first.astype(BF16)


def filter_kernel(rows_n, chips_n, start_ref, first_ref, degree_ref, row_own, col_own, *refs):
    row_refs, refs = refs[: chips_n - 1], refs[chips_n - 1 :]
    col_refs, refs = refs[: rows_n - 1], refs[rows_n - 1 :]
    filtered_ref, rounded_ref, gram_ref, both = refs
    group, vectors_n, width = rounded_ref.shape
    every = slice(0, vectors_n)
    for k, vec in enumerate(tiles_first(first_ref, width)):
        symmetric = 0.5 * (
            gathered_sum(row_own, row_refs, k, every) + gathered_sum(col_own, col_refs, k, every)
        )
        columns = slice(k * width, (k + 1) * width)
        image = degree_ref[k : k + 1, :] * vec - symmetric
        filtered = 2.0 * (image - CENTER * vec) / HALF_WIDTH - start_ref[:, columns]
        filtered_ref[:, columns] = filtered
        rounded_ref[k] = filtered.astype(BF16)
        both[:vectors_n, columns] = filtered
        both[vectors_n:, columns] = degree_ref[k : k + 1, :] * filtered
    gram_ref[...] = lax.dot_general(
        filtered_ref[...], both[...], NT, precision=HIGHEST, preferred_element_type=F32
    )


def half_form_kernel(halves, meta, tile_rows, tiles_ref, own_parts, other_parts, out_ref, panel):
    _, group, vectors_n, width = own_parts.shape
    for d in range(halves):
        panel[d * group : (d + 1) * group] = own_parts[d]
        panel[(halves + d) * group : (halves + d + 1) * group] = other_parts[d]
    for t in range(tiles_ref.shape[0]):
        row = place(tile_rows[t], group, meta[1], halves)
        out_ref[:, t * width : (t + 1) * width] = lax.dot_general(
            panel[row], tiles_ref[t], NN, preferred_element_type=F32
        ).astype(BF16)


def form_kernel(parts_n, meta, tile_cols, left, gram_ref, *refs):
    part_refs, (out_ref, panel, right) = refs[:parts_n], refs[parts_n:]
    group, vectors_n, width = part_refs[0].shape
    for d, part in enumerate(part_refs):
        panel[d * group : (d + 1) * group] = part[...]
    for t in range(right.shape[1] // width):
        right[:, t * width : (t + 1) * width] = panel[place(tile_cols[t], group, meta[0], 0)]
    form = lax.dot_general(left[...], right[...], NT, preferred_element_type=F32)
    swapped = lax.dot_general(right[...], left[...], NT, preferred_element_type=F32)
    projected = gram_ref[:, vectors_n:] - 0.5 * (form + swapped)
    row, col = square_index(vectors_n)
    packed = jnp.where(col >= row, gram_ref[:, :vectors_n], projected)
    diagonal = jnp.sum(jnp.where(row == col, projected, 0.0), 0, keepdims=True)
    half = vectors_n // 2
    out_ref[:half] = jnp.concatenate([packed[:half], packed[half:]], 1)
    diagonal = jnp.broadcast_to(diagonal, (8, vectors_n))
    out_ref[half:] = jnp.concatenate([diagonal, jnp.zeros_like(diagonal)], 1)


def square_index(n):
    return tuple(lax.broadcasted_iota(jnp.int32, (n, n), axis) for axis in (0, 1))


def inverse_factor(gram):
    n = gram.shape[0]
    row, col = square_index(n)
    table = jnp.concatenate([gram, jnp.where(row == col, 1.0, 0.0)], 1)
    bands = [table[i : i + 8] for i in range(0, n, 8)]
    below = lax.broadcasted_iota(jnp.int32, (8, 2 * n), 0)
    for j in range(n):
        at, line = j // 8, j % 8
        pivot_row = bands[at][line : line + 1, :]
        pivot_row = jnp.broadcast_to(pivot_row / pivot_row[:, j : j + 1], (8, 2 * n))
        for i in range(at, n // 8):
            update = bands[i][:, j : j + 1] * pivot_row
            if i == at:
                update = jnp.where(below > line, update, 0.0)
            bands[i] = bands[i] - update
    table = jnp.concatenate(bands, 0)
    pivots = jnp.sum(jnp.where(row == col, table[:, :n], 0.0), 1, keepdims=True)
    return table[:, n:] / jnp.sqrt(pivots)


def last_kernel(total_nodes, filtered_ref, *refs):
    parts, (ritz_ref, rayleigh_ref) = refs[:-2], refs[-2:]
    n = filtered_ref.shape[0]
    half = n // 2
    sums = tree_sum([part[...] for part in parts]) * (1.0 / total_nodes)
    packed = jnp.concatenate([sums[:half, :n], sums[:half, n:]], 0)
    row, col = square_index(n)
    upper = jnp.where(col > row, packed, 0.0)
    gram = jnp.where(col >= row, packed, 0.0) + upper.T
    lower = jnp.where(col < row, packed, 0.0)
    diagonal = jnp.broadcast_to(sums[half : half + 1, :n], (n, n))
    projected = lower + lower.T + jnp.where(row == col, diagonal, 0.0)
    inverse = inverse_factor(gram)

    def dot(a, b, dims):
        return lax.dot_general(a, b, dims, precision=HIGHEST, preferred_element_type=F32)

    half_way = dot(inverse, projected, NN)
    rayleigh_ref[...] = dot(half_way, inverse, NT)
    turned = dot(inverse, half_way, NT)
    ritz_ref[...] = dot(dot(turned, inverse, NN), filtered_ref[...], NN)


def tree_sum(parts):
    while len(parts) > 1:
        parts = [a + b for a, b in zip(parts[::2], parts[1::2])]
    return parts[0]


def local(tiles, tile_rows, tile_cols, start):
    tiles, tile_rows, tile_cols = tiles[0, 0], tile_rows[0, 0], tile_cols[0, 0]
    width = tiles.shape[-1]
    vectors_n, own_nodes = start.shape
    rows_n, cols_n = lax.axis_size("row"), lax.axis_size("col")
    total_nodes = own_nodes * rows_n * cols_n
    group = own_nodes // width
    row_me, col_me = lax.axis_index("row"), lax.axis_index("col")
    meta = jnp.stack([row_me, col_me]).astype(jnp.int32)
    swapped = jnp.stack([col_me, row_me]).astype(jnp.int32)

    rounded_shape = jax.ShapeDtypeStruct((group, vectors_n, width), BF16)
    vector_shape = jax.ShapeDtypeStruct((vectors_n, own_nodes), F32)

    chips_n = cols_n // 2

    def gather(rounded):
        chips = jnp.stack([rounded, *exchange([rounded] * (chips_n - 1), "col", 2)])
        col_parts = [rounded, *exchange([rounded] * (rows_n - 1), "row")]
        return col_parts, [chips, trade(chips, "col", 1)]

    def apply(rounded, degree):
        col_parts, row_parts = gather(rounded)
        col_own, col_send = products(
            tiles, tile_rows, tile_cols, swapped, row_parts, group, rows_n, NN, (chips_n, 0), degree
        )
        col_got = exchange(col_send, "row")
        kept, (send,) = products(
            tiles,
            tile_cols,
            tile_rows,
            meta,
            col_parts,
            group,
            cols_n,
            NT,
            (0, chips_n),
            degree,
            [col_own],
        )
        row_own, row_send = merge(kept, trade(send, "col", 1), degree)
        row_got = exchange(row_send, "col", 2)
        return [row_own, col_own, *row_got, *col_got]

    rounded = call(round_kernel, rounded_shape, [], 16, [start])
    sums = apply(rounded, True)
    first, rounded, degree = call(
        functools.partial(first_kernel, rows_n, chips_n),
        [vector_shape, rounded_shape, jax.ShapeDtypeStruct((group, width), F32)],
        [],
        24,
        [start, *sums],
    )
    sums = apply(rounded, False)
    filtered, rounded, gram = call(
        functools.partial(filter_kernel, rows_n, chips_n),
        [vector_shape, rounded_shape, jax.ShapeDtypeStruct((vectors_n, 2 * vectors_n), F32)],
        [pltpu.VMEM((2 * vectors_n, own_nodes), F32)],
        24,
        [start, first, degree, *sums],
    )
    col_parts, row_parts = gather(rounded)
    spread = (vectors_n, tiles.shape[0] * width)
    left = call(
        functools.partial(half_form_kernel, chips_n),
        jax.ShapeDtypeStruct(spread, BF16),
        [pltpu.VMEM((cols_n * group, vectors_n, width), BF16)],
        24,
        [meta, tile_rows, tiles, *row_parts],
        2 * tiles.size * vectors_n,
        2,
    )
    sums = call(
        functools.partial(form_kernel, rows_n),
        jax.ShapeDtypeStruct((vectors_n // 2 + 8, 2 * vectors_n), F32),
        [pltpu.VMEM((rows_n * group, vectors_n, width), BF16), pltpu.VMEM(spread, BF16)],
        24,
        [meta, tile_cols, left, gram, *col_parts],
        4 * vectors_n * tiles.size // width,
        2,
    )
    sums = sums + trade(sums, "col", 1)
    sums = tree_sum([sums, *exchange([sums] * (chips_n - 1), "col", 2)])
    return call(
        functools.partial(last_kernel, total_nodes),
        [vector_shape, jax.ShapeDtypeStruct((vectors_n, vectors_n), F32)],
        [],
        24,
        [filtered, sums, *exchange([sums] * (rows_n - 1), "row")],
    )


def solution(mesh):
    placed = (
        P("row", "col", None, None, None),
        P("row", "col", None),
        P("row", "col", None),
        P(None, ("row", "col")),
    )
    return jax.shard_map(
        local, mesh=mesh, in_specs=placed, out_specs=(P(None, ("row", "col")), P()), check_vma=False
    )
```

```python
import functools

import jax
import jax.numpy as jnp
from jax import lax
from jax.experimental import pallas as pl
from jax.experimental.pallas import tpu as pltpu
from jax.sharding import PartitionSpec as P

CENTER = 1.0
HALF_WIDTH = 0.5
HIGHEST = lax.Precision.HIGHEST
NT = (((1,), (1,)), ((), ()))
NN = (((1,), (0,)), ((), ()))
BF16 = jnp.bfloat16
F32 = jnp.float32
VMEM = pl.BlockSpec(memory_space=pltpu.VMEM)
SMEM = pl.BlockSpec(memory_space=pltpu.SMEM)
DEGREE_ROWS = 16


def call(kernel, out_shape, scratch, limit, args, flops=0, smem=0):
    moved = sum(x.size * x.dtype.itemsize for x in args)
    return pl.pallas_call(
        kernel,
        out_shape=out_shape,
        in_specs=[SMEM] * smem + [VMEM] * (len(args) - smem),
        out_specs=jax.tree.map(lambda _: VMEM, out_shape),
        scratch_shapes=scratch,
        compiler_params=pltpu.CompilerParams(vmem_limit_bytes=limit * 2**20),
        cost_estimate=pl.CostEstimate(flops=flops, bytes_accessed=moved, transcendentals=0),
    )(*args)


def trade(part, axis, d):
    n = lax.axis_size(axis)
    return lax.ppermute(part, axis, [(i, i ^ d) for i in range(n)])


def exchange(parts, axis, step=1):
    far_first = [trade(part, axis, step * d) for d, part in reversed(list(enumerate(parts, 1)))]
    return far_first[::-1]


def tiles_first(ref, width):
    return [ref[:, k * width : (k + 1) * width] for k in range(ref.shape[1] // width)]


def round_kernel(vec_ref, out_ref):
    for k, piece in enumerate(tiles_first(vec_ref, out_ref.shape[2])):
        out_ref[k] = piece.astype(BF16)


def split_degree(sums, height):
    high = sums.astype(BF16).astype(F32)
    low = (sums - high).astype(BF16).astype(F32)
    rest = sums - high - low
    pad = jnp.zeros((height - 3 * sums.shape[0], sums.shape[1]), F32)
    return jnp.concatenate([high, low, rest, pad], 0).astype(BF16)


def join_degree(block, group):
    block = block.astype(F32)
    return (block[2 * group : 3 * group] + block[group : 2 * group]) + block[:group]


def degree_of(total, start, group, vectors_n):
    return jnp.concatenate(
        [total[start + k, vectors_n : vectors_n + 1, :] for k in range(group)], 0
    )


def fill(panel, part_refs):
    place_at = 0
    for part in part_refs:
        blocks = part.reshape(-1, *part.shape[-2:])
        count = blocks.shape[0]
        panel[place_at : place_at + count, : part.shape[-2], :] = blocks[...]
        place_at += count


def place(tile, group, me, halves):
    apart = (tile // group) ^ me
    if halves:
        apart = (apart % 2) * halves + apart // 2
    return apart * group + tile % group


def product_kernel(counts, degree, meta, tile_rows, tile_cols, tiles_ref, *refs):
    cols_n, rows_n, half = counts
    col_parts, refs = refs[:cols_n], refs[cols_n:]
    row_parts, refs = refs[:rows_n], refs[rows_n:]
    kept_ref, swap_ref, own_ref, *send_refs = refs[:-4]
    col_panel, row_panel, row_total, col_total = refs[-4:]
    group, vectors_n, width = col_parts[0].shape
    for panel, parts in ((col_panel, col_parts), (row_panel, row_parts)):
        fill(panel, parts)
        if degree:
            panel[:, vectors_n:, :] = jnp.ones(
                (panel.shape[0], panel.shape[1] - vectors_n, width), BF16
            )
    row_total[...] = jnp.zeros_like(row_total)
    col_total[...] = jnp.zeros_like(col_total)
    for t in range(tiles_ref.shape[0]):
        tile = tiles_ref[t]
        row, col = tile_rows[t], tile_cols[t]
        here = place(col, group, meta[0], 0)
        row_total[place(row, group, meta[1], half)] += lax.dot_general(
            col_panel[here], tile, NT, preferred_element_type=F32
        )
        col_total[here] += lax.dot_general(
            row_panel[place(row, group, meta[1], 0)], tile, NN, preferred_element_type=F32
        )
    for d in range(half):
        kept_ref[d] = row_total[d * group : (d + 1) * group]
    own_ref[...] = col_total[:group]
    sends = [(row_total, half + d, swap_ref.at[d]) for d in range(half)]
    sends += [(col_total, d, send) for d, send in enumerate(send_refs, 1)]
    for total, d, send in sends:
        send[:group] = total[d * group : (d + 1) * group, :vectors_n, :].astype(BF16)
        if degree:
            send[group] = split_degree(degree_of(total, d * group, group, vectors_n), vectors_n)


def products(tiles, tile_rows, tile_cols, meta, col_parts, row_parts, degree):
    group, vectors_n, width = col_parts[0].shape
    rows_n, half = len(col_parts), len(row_parts)
    height = vectors_n + (DEGREE_ROWS if degree else 0)
    blocks = group + (1 if degree else 0)
    out_shape = [
        jax.ShapeDtypeStruct((half, group, height, width), F32),
        jax.ShapeDtypeStruct((half, blocks, vectors_n, width), BF16),
        jax.ShapeDtypeStruct((group, height, width), F32),
    ]
    out_shape += [jax.ShapeDtypeStruct((blocks, vectors_n, width), BF16)] * (rows_n - 1)
    scratch = [
        pltpu.VMEM((rows_n * group, height, width), BF16),
        pltpu.VMEM((2 * half * group, height, width), BF16),
        pltpu.VMEM((2 * half * group, height, width), F32),
        pltpu.VMEM((rows_n * group, height, width), F32),
    ]
    kernel = functools.partial(product_kernel, (rows_n, half, half), degree)
    args = [meta, tile_rows, tile_cols, tiles, *col_parts, *row_parts]
    kept, swap, own, *send = call(kernel, out_shape, scratch, 32, args, 4 * tiles.size * height, 3)
    return kept, swap, own, send


def merge_kernel(degree, kept, got, own_ref, *send_refs):
    _, group, height, width = kept.shape
    vectors_n = got.shape[2]
    for k in range(group):
        own_ref[k, :vectors_n, :] = kept[0, k, :vectors_n, :] + got[0, k].astype(F32)
        for d, send in enumerate(send_refs, 1):
            send[k] = (kept[d, k, :vectors_n, :] + got[d, k].astype(F32)).astype(BF16)
    if degree:
        sums = [
            degree_of(kept.at[d], 0, group, vectors_n) + join_degree(got[d, group], group)
            for d in range(kept.shape[0])
        ]
        for k in range(group):
            own_ref[k, vectors_n:, :] = jnp.broadcast_to(
                sums[0][k : k + 1], (height - vectors_n, width)
            )
        for d, send in enumerate(send_refs, 1):
            send[group] = split_degree(sums[d], vectors_n)


def merge(kept, got, degree):
    out_shape = [jax.ShapeDtypeStruct(kept.shape[1:], F32)]
    out_shape += [jax.ShapeDtypeStruct(got.shape[1:], BF16)] * (kept.shape[0] - 1)
    own, *send = call(functools.partial(merge_kernel, degree), out_shape, [], 24, [kept, got])
    return own, send


def gathered_sum(own, received, k, rows):
    total = own[k, rows, :]
    for part in received:
        total = total + part[k, rows, :].astype(F32)
    return total


def first_kernel(rows_n, chips_n, vec_ref, row_own, col_own, *refs):
    row_refs, refs = refs[: chips_n - 1], refs[chips_n - 1 :]
    col_refs, refs = refs[: rows_n - 1], refs[rows_n - 1 :]
    first_ref, rounded_ref, degree_ref = refs
    group, vectors_n, width = rounded_ref.shape
    degree = jnp.zeros((group, width), F32)
    for own, received in ((row_own, row_refs), (col_own, col_refs)):
        degree += degree_of(own, 0, group, vectors_n)
        for part in received:
            degree += join_degree(part[group], group)
    degree = 0.5 * degree
    degree_ref[...] = degree
    every = slice(0, vectors_n)
    for k, vec in enumerate(tiles_first(vec_ref, width)):
        symmetric = 0.5 * (
            gathered_sum(row_own, row_refs, k, every) + gathered_sum(col_own, col_refs, k, every)
        )
        image = degree[k : k + 1, :] * vec - symmetric
        first = (image - CENTER * vec) / HALF_WIDTH
        first_ref[:, k * width : (k + 1) * width] = first
        rounded_ref[k] = first.astype(BF16)


def filter_kernel(rows_n, chips_n, start_ref, first_ref, degree_ref, row_own, col_own, *refs):
    row_refs, refs = refs[: chips_n - 1], refs[chips_n - 1 :]
    col_refs, refs = refs[: rows_n - 1], refs[rows_n - 1 :]
    filtered_ref, rounded_ref, gram_ref, both = refs
    group, vectors_n, width = rounded_ref.shape
    every = slice(0, vectors_n)
    for k, vec in enumerate(tiles_first(first_ref, width)):
        symmetric = 0.5 * (
            gathered_sum(row_own, row_refs, k, every) + gathered_sum(col_own, col_refs, k, every)
        )
        columns = slice(k * width, (k + 1) * width)
        image = degree_ref[k : k + 1, :] * vec - symmetric
        filtered = 2.0 * (image - CENTER * vec) / HALF_WIDTH - start_ref[:, columns]
        filtered_ref[:, columns] = filtered
        rounded_ref[k] = filtered.astype(BF16)
        both[:vectors_n, columns] = filtered
        both[vectors_n:, columns] = degree_ref[k : k + 1, :] * filtered
    gram_ref[...] = lax.dot_general(
        filtered_ref[...], both[...], NT, precision=HIGHEST, preferred_element_type=F32
    )


def form_kernel(counts, meta, tile_rows, tile_cols, tiles_ref, gram_ref, *refs):
    cols_n, rows_n = counts
    col_parts, refs = refs[:cols_n], refs[cols_n:]
    row_parts, (out_ref, col_panel, row_panel, left, right) = refs[:rows_n], refs[rows_n:]
    group, vectors_n, width = col_parts[0].shape
    fill(col_panel, col_parts)
    fill(row_panel, row_parts)
    for t in range(tiles_ref.shape[0]):
        columns = slice(t * width, (t + 1) * width)
        left[:, columns] = row_panel[place(tile_rows[t], group, meta[1], 0)]
        right[:, columns] = lax.dot_general(
            col_panel[place(tile_cols[t], group, meta[0], 0)],
            tiles_ref[t],
            NT,
            preferred_element_type=F32,
        ).astype(BF16)
    form = lax.dot_general(left[...], right[...], NT, preferred_element_type=F32)
    swapped = lax.dot_general(right[...], left[...], NT, preferred_element_type=F32)
    projected = gram_ref[:, vectors_n:] - 0.5 * (form + swapped)
    row, col = square_index(vectors_n)
    packed = jnp.where(col >= row, gram_ref[:, :vectors_n], projected)
    diagonal = jnp.sum(jnp.where(row == col, projected, 0.0), 0, keepdims=True)
    half = vectors_n // 2
    out_ref[:half] = jnp.concatenate([packed[:half], packed[half:]], 1)
    diagonal = jnp.broadcast_to(diagonal, (8, vectors_n))
    out_ref[half:] = jnp.concatenate([diagonal, jnp.zeros_like(diagonal)], 1)


def square_index(n):
    return tuple(lax.broadcasted_iota(jnp.int32, (n, n), axis) for axis in (0, 1))


def inverse_factor(gram):
    n = gram.shape[0]
    row, col = square_index(n)
    table = jnp.concatenate([gram, jnp.where(row == col, 1.0, 0.0)], 1)
    bands = [table[i : i + 8] for i in range(0, n, 8)]
    below = lax.broadcasted_iota(jnp.int32, (8, 2 * n), 0)
    for j in range(n):
        at, line = j // 8, j % 8
        pivot_row = bands[at][line : line + 1, :]
        pivot_row = jnp.broadcast_to(pivot_row / pivot_row[:, j : j + 1], (8, 2 * n))
        for i in range(at, n // 8):
            update = bands[i][:, j : j + 1] * pivot_row
            if i == at:
                update = jnp.where(below > line, update, 0.0)
            bands[i] = bands[i] - update
    table = jnp.concatenate(bands, 0)
    pivots = jnp.sum(jnp.where(row == col, table[:, :n], 0.0), 1, keepdims=True)
    return table[:, n:] / jnp.sqrt(pivots)


def last_kernel(total_nodes, filtered_ref, *refs):
    parts, (ritz_ref, rayleigh_ref) = refs[:-2], refs[-2:]
    n = filtered_ref.shape[0]
    half = n // 2
    sums = tree_sum([part[...] for part in parts]) * (1.0 / total_nodes)
    packed = jnp.concatenate([sums[:half, :n], sums[:half, n:]], 0)
    row, col = square_index(n)
    upper = jnp.where(col > row, packed, 0.0)
    gram = jnp.where(col >= row, packed, 0.0) + upper.T
    lower = jnp.where(col < row, packed, 0.0)
    diagonal = jnp.broadcast_to(sums[half : half + 1, :n], (n, n))
    projected = lower + lower.T + jnp.where(row == col, diagonal, 0.0)
    inverse = inverse_factor(gram)

    def dot(a, b, dims):
        return lax.dot_general(a, b, dims, precision=HIGHEST, preferred_element_type=F32)

    half_way = dot(inverse, projected, NN)
    rayleigh_ref[...] = dot(half_way, inverse, NT)
    turned = dot(inverse, half_way, NT)
    ritz_ref[...] = dot(dot(turned, inverse, NN), filtered_ref[...], NN)


def tree_sum(parts):
    while len(parts) > 1:
        parts = [a + b for a, b in zip(parts[::2], parts[1::2])]
    return parts[0]


def local(tiles, tile_rows, tile_cols, start):
    tiles, tile_rows, tile_cols = tiles[0, 0], tile_rows[0, 0], tile_cols[0, 0]
    width = tiles.shape[-1]
    vectors_n, own_nodes = start.shape
    rows_n, cols_n = lax.axis_size("row"), lax.axis_size("col")
    total_nodes = own_nodes * rows_n * cols_n
    group = own_nodes // width
    row_me, col_me = lax.axis_index("row"), lax.axis_index("col")
    meta = jnp.stack([row_me, col_me]).astype(jnp.int32)

    rounded_shape = jax.ShapeDtypeStruct((group, vectors_n, width), BF16)
    vector_shape = jax.ShapeDtypeStruct((vectors_n, own_nodes), F32)

    chips_n = cols_n // 2

    def gather(rounded):
        col_parts = [rounded, *exchange([rounded] * (rows_n - 1), "row")]
        pair = jnp.stack([rounded, trade(rounded, "col", 1)])
        return col_parts, [pair, *exchange([pair] * (chips_n - 1), "col", 2)]

    def apply(rounded, degree):
        col_parts, row_parts = gather(rounded)
        kept, send, col_own, col_send = products(
            tiles, tile_rows, tile_cols, meta, col_parts, row_parts, degree
        )
        col_got = exchange(col_send, "row")
        row_own, row_send = merge(kept, trade(send, "col", 1), degree)
        row_got = exchange(row_send, "col", 2)
        return [row_own, col_own, *row_got, *col_got]

    rounded = call(round_kernel, rounded_shape, [], 16, [start])
    sums = apply(rounded, True)
    first, rounded, degree = call(
        functools.partial(first_kernel, rows_n, chips_n),
        [vector_shape, rounded_shape, jax.ShapeDtypeStruct((group, width), F32)],
        [],
        24,
        [start, *sums],
    )
    sums = apply(rounded, False)
    filtered, rounded, gram = call(
        functools.partial(filter_kernel, rows_n, chips_n),
        [vector_shape, rounded_shape, jax.ShapeDtypeStruct((vectors_n, 2 * vectors_n), F32)],
        [pltpu.VMEM((2 * vectors_n, own_nodes), F32)],
        24,
        [start, first, degree, *sums],
    )
    col_parts, row_parts = gather(rounded)
    spread = (vectors_n, tiles.shape[0] * width)
    sums = call(
        functools.partial(form_kernel, (len(col_parts), len(row_parts))),
        jax.ShapeDtypeStruct((vectors_n // 2 + 8, 2 * vectors_n), F32),
        [
            pltpu.VMEM((rows_n * group, vectors_n, width), BF16),
            pltpu.VMEM((cols_n * group, vectors_n, width), BF16),
            pltpu.VMEM(spread, BF16),
            pltpu.VMEM(spread, BF16),
        ],
        24,
        [meta, tile_rows, tile_cols, tiles, gram, *col_parts, *row_parts],
        4 * tiles.size * vectors_n,
        3,
    )
    sums = sums + trade(sums, "col", 1)
    sums = tree_sum([sums, *exchange([sums] * (chips_n - 1), "col", 2)])
    return call(
        functools.partial(last_kernel, total_nodes),
        [vector_shape, jax.ShapeDtypeStruct((vectors_n, vectors_n), F32)],
        [],
        24,
        [filtered, sums, *exchange([sums] * (rows_n - 1), "row")],
    )


def solution(mesh):
    placed = (
        P("row", "col", None, None, None),
        P("row", "col", None),
        P("row", "col", None),
        P(None, ("row", "col")),
    )
    return jax.shard_map(
        local, mesh=mesh, in_specs=placed, out_specs=(P(None, ("row", "col")), P()), check_vma=False
    )
```

```python
import functools

import jax
import jax.numpy as jnp
from jax import lax
from jax.experimental import pallas as pl
from jax.experimental.pallas import tpu as pltpu
from jax.sharding import PartitionSpec as P

CENTER = 1.0
HALF_WIDTH = 0.5
HIGHEST = lax.Precision.HIGHEST
NT = (((1,), (1,)), ((), ()))
NN = (((1,), (0,)), ((), ()))
BF16 = jnp.bfloat16
F32 = jnp.float32
VMEM = pl.BlockSpec(memory_space=pltpu.VMEM)
SMEM = pl.BlockSpec(memory_space=pltpu.SMEM)
DEGREE_ROWS = 16


def call(kernel, out_shape, scratch, limit, args, flops=0, smem=0):
    moved = sum(x.size * x.dtype.itemsize for x in args)
    return pl.pallas_call(
        kernel,
        out_shape=out_shape,
        in_specs=[SMEM] * smem + [VMEM] * (len(args) - smem),
        out_specs=jax.tree.map(lambda _: VMEM, out_shape),
        scratch_shapes=scratch,
        compiler_params=pltpu.CompilerParams(vmem_limit_bytes=limit * 2**20),
        cost_estimate=pl.CostEstimate(flops=flops, bytes_accessed=moved, transcendentals=0),
    )(*args)


def trade(part, axis, d):
    n = lax.axis_size(axis)
    return lax.ppermute(part, axis, [(i, i ^ d) for i in range(n)])


def exchange(parts, axis, step=1):
    far_first = [trade(part, axis, step * d) for d, part in reversed(list(enumerate(parts, 1)))]
    return far_first[::-1]


def tiles_first(ref, width):
    return [ref[:, k * width : (k + 1) * width] for k in range(ref.shape[1] // width)]


def round_kernel(vec_ref, out_ref):
    for k, piece in enumerate(tiles_first(vec_ref, out_ref.shape[2])):
        out_ref[k] = piece.astype(BF16)


def split_degree(sums, height):
    high = sums.astype(BF16).astype(F32)
    low = (sums - high).astype(BF16).astype(F32)
    rest = sums - high - low
    pad = jnp.zeros((height - 3 * sums.shape[0], sums.shape[1]), F32)
    return jnp.concatenate([high, low, rest, pad], 0).astype(BF16)


def join_degree(block, group):
    block = block.astype(F32)
    return (block[2 * group : 3 * group] + block[group : 2 * group]) + block[:group]


def degree_of(total, start, group, vectors_n):
    return jnp.concatenate(
        [total[start + k, vectors_n : vectors_n + 1, :] for k in range(group)], 0
    )


def fill(panel, parts, offsets):
    blocks = [part.at[d] for part in parts for d in range(part.shape[0])]
    for block, offset in zip(blocks, offsets):
        group, height, _ = block.shape
        panel[offset * group : (offset + 1) * group, :height, :] = block[...]


def place(tile, group, me, halves):
    apart = (tile // group) ^ me
    if halves:
        apart = (apart % 2) * halves + apart // 2
    return apart * group + tile % group


def product_kernel(offsets, degree, meta, tile_rows, tile_cols, tiles_ref, *refs):
    col_offsets, row_offsets = offsets
    half = len(row_offsets) // 2
    row_end = 2 + len(row_offsets)
    col_parts, row_parts, refs = refs[:2], refs[2:row_end], refs[row_end:]
    kept_ref, swap_ref, own_ref, *send_refs = refs[:-4]
    col_panel, row_panel, row_total, col_total = refs[-4:]
    group, vectors_n, width = col_parts[0].shape[1:]
    panels = ((col_panel, col_parts, col_offsets), (row_panel, row_parts, row_offsets))
    for panel, parts, places in panels:
        fill(panel, parts, places)
        if degree:
            panel[:, vectors_n:, :] = jnp.ones(
                (panel.shape[0], panel.shape[1] - vectors_n, width), BF16
            )
    row_total[...] = jnp.zeros_like(row_total)
    col_total[...] = jnp.zeros_like(col_total)
    for t in range(tiles_ref.shape[0]):
        tile = tiles_ref[t]
        row, col = tile_rows[t], tile_cols[t]
        here = place(col, group, meta[0], 0)
        row_total[place(row, group, meta[1], half)] += lax.dot_general(
            col_panel[here], tile, NT, preferred_element_type=F32
        )
        col_total[here] += lax.dot_general(
            row_panel[place(row, group, meta[1], 0)], tile, NN, preferred_element_type=F32
        )
    for d in range(half):
        kept_ref[d] = row_total[d * group : (d + 1) * group]
    own_ref[...] = col_total[:group]
    sends = [(row_total, half + d, swap_ref.at[d]) for d in range(half)]
    sends += [(col_total, d, send) for d, send in enumerate(send_refs, 1)]
    for total, d, send in sends:
        send[:group] = total[d * group : (d + 1) * group, :vectors_n, :].astype(BF16)
        if degree:
            send[group] = split_degree(degree_of(total, d * group, group, vectors_n), vectors_n)


def products(tiles, tile_rows, tile_cols, meta, col_parts, row_parts, offsets, degree):
    group, vectors_n, width = col_parts[0].shape[1:]
    rows_n, half = len(offsets[0]), len(offsets[1]) // 2
    height = vectors_n + (DEGREE_ROWS if degree else 0)
    blocks = group + (1 if degree else 0)
    out_shape = [
        jax.ShapeDtypeStruct((half, group, height, width), F32),
        jax.ShapeDtypeStruct((half, blocks, vectors_n, width), BF16),
        jax.ShapeDtypeStruct((group, height, width), F32),
    ]
    out_shape += [jax.ShapeDtypeStruct((blocks, vectors_n, width), BF16)] * (rows_n - 1)
    scratch = [
        pltpu.VMEM((rows_n * group, height, width), BF16),
        pltpu.VMEM((2 * half * group, height, width), BF16),
        pltpu.VMEM((2 * half * group, height, width), F32),
        pltpu.VMEM((rows_n * group, height, width), F32),
    ]
    kernel = functools.partial(product_kernel, offsets, degree)
    args = [meta, tile_rows, tile_cols, tiles, *col_parts, *row_parts]
    kept, swap, own, *send = call(kernel, out_shape, scratch, 32, args, 4 * tiles.size * height, 3)
    return kept, swap, own, send


def merge_kernel(degree, kept, got, own_ref, *send_refs):
    _, group, height, width = kept.shape
    vectors_n = got.shape[2]
    for k in range(group):
        own_ref[k, :vectors_n, :] = kept[0, k, :vectors_n, :] + got[0, k].astype(F32)
        for d, send in enumerate(send_refs, 1):
            send[k] = (kept[d, k, :vectors_n, :] + got[d, k].astype(F32)).astype(BF16)
    if degree:
        sums = [
            degree_of(kept.at[d], 0, group, vectors_n) + join_degree(got[d, group], group)
            for d in range(kept.shape[0])
        ]
        for k in range(group):
            own_ref[k, vectors_n:, :] = jnp.broadcast_to(
                sums[0][k : k + 1], (height - vectors_n, width)
            )
        for d, send in enumerate(send_refs, 1):
            send[group] = split_degree(sums[d], vectors_n)


def merge(kept, got, degree):
    out_shape = [jax.ShapeDtypeStruct(kept.shape[1:], F32)]
    out_shape += [jax.ShapeDtypeStruct(got.shape[1:], BF16)] * (kept.shape[0] - 1)
    own, *send = call(functools.partial(merge_kernel, degree), out_shape, [], 24, [kept, got])
    return own, send


def gathered_sum(own, received, k, rows):
    total = own[k, rows, :]
    for part in received:
        total = total + part[k, rows, :].astype(F32)
    return total


def first_kernel(rows_n, chips_n, vec_ref, row_own, col_own, *refs):
    row_refs, refs = refs[: chips_n - 1], refs[chips_n - 1 :]
    col_refs, refs = refs[: rows_n - 1], refs[rows_n - 1 :]
    first_ref, rounded_ref, degree_ref = refs
    group, vectors_n, width = rounded_ref.shape
    degree = jnp.zeros((group, width), F32)
    for own, received in ((row_own, row_refs), (col_own, col_refs)):
        degree += degree_of(own, 0, group, vectors_n)
        for part in received:
            degree += join_degree(part[group], group)
    degree = 0.5 * degree
    degree_ref[...] = degree
    every = slice(0, vectors_n)
    for k, vec in enumerate(tiles_first(vec_ref, width)):
        symmetric = 0.5 * (
            gathered_sum(row_own, row_refs, k, every) + gathered_sum(col_own, col_refs, k, every)
        )
        image = degree[k : k + 1, :] * vec - symmetric
        first = (image - CENTER * vec) / HALF_WIDTH
        first_ref[:, k * width : (k + 1) * width] = first
        rounded_ref[k] = first.astype(BF16)


def filter_kernel(rows_n, chips_n, start_ref, first_ref, degree_ref, row_own, col_own, *refs):
    row_refs, refs = refs[: chips_n - 1], refs[chips_n - 1 :]
    col_refs, refs = refs[: rows_n - 1], refs[rows_n - 1 :]
    filtered_ref, rounded_ref, gram_ref, both = refs
    group, vectors_n, width = rounded_ref.shape
    every = slice(0, vectors_n)
    for k, vec in enumerate(tiles_first(first_ref, width)):
        symmetric = 0.5 * (
            gathered_sum(row_own, row_refs, k, every) + gathered_sum(col_own, col_refs, k, every)
        )
        columns = slice(k * width, (k + 1) * width)
        image = degree_ref[k : k + 1, :] * vec - symmetric
        filtered = 2.0 * (image - CENTER * vec) / HALF_WIDTH - start_ref[:, columns]
        filtered_ref[:, columns] = filtered
        rounded_ref[k] = filtered.astype(BF16)
        both[:vectors_n, columns] = filtered
        both[vectors_n:, columns] = degree_ref[k : k + 1, :] * filtered
    gram_ref[...] = lax.dot_general(
        filtered_ref[...], both[...], NT, precision=HIGHEST, preferred_element_type=F32
    )


def form_kernel(offsets, meta, tile_rows, tile_cols, tiles_ref, gram_ref, *refs):
    row_end = 2 + len(offsets[1])
    col_parts, row_parts, refs = refs[:2], refs[2:row_end], refs[row_end:]
    out_ref, col_panel, row_panel, left, right = refs
    group, vectors_n, width = col_parts[0].shape[1:]
    fill(col_panel, col_parts, offsets[0])
    fill(row_panel, row_parts, offsets[1])
    for t in range(tiles_ref.shape[0]):
        columns = slice(t * width, (t + 1) * width)
        left[:, columns] = row_panel[place(tile_rows[t], group, meta[1], 0)]
        right[:, columns] = lax.dot_general(
            col_panel[place(tile_cols[t], group, meta[0], 0)],
            tiles_ref[t],
            NT,
            preferred_element_type=F32,
        ).astype(BF16)
    form = lax.dot_general(left[...], right[...], NT, preferred_element_type=F32)
    swapped = lax.dot_general(right[...], left[...], NT, preferred_element_type=F32)
    projected = gram_ref[:, vectors_n:] - 0.5 * (form + swapped)
    row, col = square_index(vectors_n)
    packed = jnp.where(col >= row, gram_ref[:, :vectors_n], projected)
    diagonal = jnp.sum(jnp.where(row == col, projected, 0.0), 0, keepdims=True)
    half = vectors_n // 2
    out_ref[:half] = jnp.concatenate([packed[:half], packed[half:]], 1)
    diagonal = jnp.broadcast_to(diagonal, (8, vectors_n))
    out_ref[half:] = jnp.concatenate([diagonal, jnp.zeros_like(diagonal)], 1)


def square_index(n):
    return tuple(lax.broadcasted_iota(jnp.int32, (n, n), axis) for axis in (0, 1))


def inverse_factor(gram):
    n = gram.shape[0]
    row, col = square_index(n)
    table = jnp.concatenate([gram, jnp.where(row == col, 1.0, 0.0)], 1)
    bands = [table[i : i + 8] for i in range(0, n, 8)]
    below = lax.broadcasted_iota(jnp.int32, (8, 2 * n), 0)
    for j in range(n):
        at, line = j // 8, j % 8
        pivot_row = bands[at][line : line + 1, :]
        pivot_row = jnp.broadcast_to(pivot_row / pivot_row[:, j : j + 1], (8, 2 * n))
        for i in range(at, n // 8):
            update = bands[i][:, j : j + 1] * pivot_row
            if i == at:
                update = jnp.where(below > line, update, 0.0)
            bands[i] = bands[i] - update
    table = jnp.concatenate(bands, 0)
    pivots = jnp.sum(jnp.where(row == col, table[:, :n], 0.0), 1, keepdims=True)
    return table[:, n:] / jnp.sqrt(pivots)


def last_kernel(total_nodes, filtered_ref, *refs):
    parts, (ritz_ref, rayleigh_ref) = refs[:-2], refs[-2:]
    n = filtered_ref.shape[0]
    half = n // 2
    sums = tree_sum([part[...] for part in parts]) * (1.0 / total_nodes)
    packed = jnp.concatenate([sums[:half, :n], sums[:half, n:]], 0)
    row, col = square_index(n)
    upper = jnp.where(col > row, packed, 0.0)
    gram = jnp.where(col >= row, packed, 0.0) + upper.T
    lower = jnp.where(col < row, packed, 0.0)
    diagonal = jnp.broadcast_to(sums[half : half + 1, :n], (n, n))
    projected = lower + lower.T + jnp.where(row == col, diagonal, 0.0)
    inverse = inverse_factor(gram)

    def dot(a, b, dims):
        return lax.dot_general(a, b, dims, precision=HIGHEST, preferred_element_type=F32)

    half_way = dot(inverse, projected, NN)
    rayleigh_ref[...] = dot(half_way, inverse, NT)
    turned = dot(inverse, half_way, NT)
    ritz_ref[...] = dot(dot(turned, inverse, NN), filtered_ref[...], NN)


def tree_sum(parts):
    while len(parts) > 1:
        parts = [a + b for a, b in zip(parts[::2], parts[1::2])]
    return parts[0]


def local(tiles, tile_rows, tile_cols, start):
    tiles, tile_rows, tile_cols = tiles[0, 0], tile_rows[0, 0], tile_cols[0, 0]
    width = tiles.shape[-1]
    vectors_n, own_nodes = start.shape
    rows_n, cols_n = lax.axis_size("row"), lax.axis_size("col")
    total_nodes = own_nodes * rows_n * cols_n
    group = own_nodes // width
    row_me, col_me = lax.axis_index("row"), lax.axis_index("col")
    meta = jnp.stack([row_me, col_me]).astype(jnp.int32)

    rounded_shape = jax.ShapeDtypeStruct((group, vectors_n, width), BF16)
    vector_shape = jax.ShapeDtypeStruct((vectors_n, own_nodes), F32)

    chips_n = cols_n // 2

    def gather(rounded):
        held, d = rounded[None], rows_n // 2
        while d:
            got = trade(held, "row", d)
            if d > 1:
                held = jnp.concatenate([held, got])
            d //= 2
        chips = [rounded, *exchange([rounded] * (chips_n - 1), "col", 2)]
        chips += [trade(chip, "col", 1) for chip in chips]
        return [held, got], [chip[None] for chip in chips]

    col_offsets, d = [0], rows_n // 2
    while d:
        col_offsets += [offset ^ d for offset in col_offsets]
        d //= 2
    row_offsets = [2 * d + core for core in range(2) for d in range(chips_n)]
    offsets = (col_offsets, row_offsets)

    def apply(rounded, degree):
        col_parts, row_parts = gather(rounded)
        kept, send, col_own, col_send = products(
            tiles, tile_rows, tile_cols, meta, col_parts, row_parts, offsets, degree
        )
        col_got = exchange(col_send, "row")
        row_own, row_send = merge(kept, trade(send, "col", 1), degree)
        row_got = exchange(row_send, "col", 2)
        return [row_own, col_own, *row_got, *col_got]

    rounded = call(round_kernel, rounded_shape, [], 16, [start])
    sums = apply(rounded, True)
    first, rounded, degree = call(
        functools.partial(first_kernel, rows_n, chips_n),
        [vector_shape, rounded_shape, jax.ShapeDtypeStruct((group, width), F32)],
        [],
        24,
        [start, *sums],
    )
    sums = apply(rounded, False)
    filtered, rounded, gram = call(
        functools.partial(filter_kernel, rows_n, chips_n),
        [vector_shape, rounded_shape, jax.ShapeDtypeStruct((vectors_n, 2 * vectors_n), F32)],
        [pltpu.VMEM((2 * vectors_n, own_nodes), F32)],
        24,
        [start, first, degree, *sums],
    )
    col_parts, row_parts = gather(rounded)
    spread = (vectors_n, tiles.shape[0] * width)
    sums = call(
        functools.partial(form_kernel, offsets),
        jax.ShapeDtypeStruct((vectors_n // 2 + 8, 2 * vectors_n), F32),
        [
            pltpu.VMEM((rows_n * group, vectors_n, width), BF16),
            pltpu.VMEM((cols_n * group, vectors_n, width), BF16),
            pltpu.VMEM(spread, BF16),
            pltpu.VMEM(spread, BF16),
        ],
        24,
        [meta, tile_rows, tile_cols, tiles, gram, *col_parts, *row_parts],
        4 * tiles.size * vectors_n,
        3,
    )
    sums = sums + trade(sums, "col", 1)
    sums = tree_sum([sums, *exchange([sums] * (chips_n - 1), "col", 2)])
    return call(
        functools.partial(last_kernel, total_nodes),
        [vector_shape, jax.ShapeDtypeStruct((vectors_n, vectors_n), F32)],
        [],
        24,
        [filtered, sums, *exchange([sums] * (rows_n - 1), "row")],
    )


def solution(mesh):
    placed = (
        P("row", "col", None, None, None),
        P("row", "col", None),
        P("row", "col", None),
        P(None, ("row", "col")),
    )
    return jax.shard_map(
        local, mesh=mesh, in_specs=placed, out_specs=(P(None, ("row", "col")), P()), check_vma=False
    )
```

```python
import functools

import jax
import jax.numpy as jnp
from jax import lax
from jax.experimental import pallas as pl
from jax.experimental.pallas import tpu as pltpu
from jax.sharding import PartitionSpec as P

CENTER = 1.0
HALF_WIDTH = 0.5
HIGHEST = lax.Precision.HIGHEST
NT = (((1,), (1,)), ((), ()))
NN = (((1,), (0,)), ((), ()))
BF16 = jnp.bfloat16
F32 = jnp.float32
VMEM = pl.BlockSpec(memory_space=pltpu.VMEM)
SMEM = pl.BlockSpec(memory_space=pltpu.SMEM)
DEGREE_ROWS = 16


def call(kernel, out_shape, scratch, limit, args, flops=0, smem=0):
    moved = sum(x.size * x.dtype.itemsize for x in args)
    return pl.pallas_call(
        kernel,
        out_shape=out_shape,
        in_specs=[SMEM] * smem + [VMEM] * (len(args) - smem),
        out_specs=jax.tree.map(lambda _: VMEM, out_shape),
        scratch_shapes=scratch,
        compiler_params=pltpu.CompilerParams(vmem_limit_bytes=limit * 2**20),
        cost_estimate=pl.CostEstimate(flops=flops, bytes_accessed=moved, transcendentals=0),
    )(*args)


def trade(part, axis, d):
    n = lax.axis_size(axis)
    return lax.ppermute(part, axis, [(i, i ^ d) for i in range(n)])


def exchange(parts, axis, step=1):
    far_first = [trade(part, axis, step * d) for d, part in reversed(list(enumerate(parts, 1)))]
    return far_first[::-1]


def tiles_first(ref, width):
    return [ref[:, k * width : (k + 1) * width] for k in range(ref.shape[1] // width)]


def round_kernel(vec_ref, out_ref):
    for k, piece in enumerate(tiles_first(vec_ref, out_ref.shape[2])):
        out_ref[k] = piece.astype(BF16)


def split_degree(sums):
    high = sums.astype(BF16).astype(F32)
    return jnp.concatenate([high, sums - high], 0).astype(BF16)


def join_degree(payload, group):
    parts = payload[payload.shape[0] - 2 * group :, :].astype(F32)
    return parts[:group] + parts[group:]


def fill(panel, parts, offsets):
    for part, offset in zip(parts, offsets):
        group = part.shape[0]
        panel[offset * group : (offset + 1) * group] = part[...]


def degree_kernel(table, tiles_ref, row_ref, col_ref):
    row_ref[...] = jnp.zeros_like(row_ref)
    col_ref[...] = jnp.zeros_like(col_ref)
    ones = jnp.ones((DEGREE_ROWS, tiles_ref.shape[2]), BF16)
    for t in range(tiles_ref.shape[0]):
        for ref, place, dims in ((row_ref, table[2, t], NT), (col_ref, table[0, t], NN)):
            sums = lax.dot_general(ones, tiles_ref[t], dims, preferred_element_type=F32)
            ref[pl.ds(place, 1), :] += sums[:1]


def product_kernel(offsets, degree, table, tiles_ref, *refs):
    col_offsets, row_offsets = offsets
    cols_n, rows_n = len(col_offsets), len(row_offsets)
    half = rows_n // 2
    col_parts, refs = refs[:cols_n], refs[cols_n:]
    row_parts, refs = refs[:rows_n], refs[rows_n:]
    if degree:
        row_degree, col_degree, *refs = refs
    kept_ref, swap_ref, own_ref, *send_refs = refs[:-4]
    col_panel, row_panel, row_total, col_total = refs[-4:]
    group, vectors_n, width = col_parts[0].shape
    fill(col_panel, col_parts, col_offsets)
    fill(row_panel, row_parts, row_offsets)
    row_total[...] = jnp.zeros_like(row_total)
    col_total[...] = jnp.zeros_like(col_total)
    for t in range(tiles_ref.shape[0]):
        tile, here = tiles_ref[t], table[0, t]
        row_total[table[2, t]] += lax.dot_general(
            col_panel[here], tile, NT, preferred_element_type=F32
        )
        col_total[here] += lax.dot_general(
            row_panel[table[1, t]], tile, NN, preferred_element_type=F32
        )
    for d in range(half):
        kept_ref[d] = row_total[d * group : (d + 1) * group]
    own_ref[...] = col_total[:group]
    sends = [(row_total, half + d, swap_ref.at[d]) for d in range(half)]
    sends += [(col_total, d, send) for d, send in enumerate(send_refs, 1)]
    for total, d, send in sends:
        for k in range(group):
            send[k * vectors_n : (k + 1) * vectors_n, :] = total[d * group + k].astype(BF16)
        if degree:
            sums = row_degree if total is row_total else col_degree
            send[group * vectors_n :, :] = split_degree(sums[d * group : (d + 1) * group, :])


def products(tiles, table, col_parts, row_parts, offsets, degree):
    group, vectors_n, width = col_parts[0].shape
    rows_n, half = len(offsets[0]), len(offsets[1]) // 2
    rows = group * vectors_n + (2 * group if degree else 0)
    out_shape = [
        jax.ShapeDtypeStruct((half, group, vectors_n, width), F32),
        jax.ShapeDtypeStruct((half, rows, width), BF16),
        jax.ShapeDtypeStruct((group, vectors_n, width), F32),
    ]
    out_shape += [jax.ShapeDtypeStruct((rows, width), BF16)] * (rows_n - 1)
    scratch = [
        pltpu.VMEM((rows_n * group, vectors_n, width), BF16),
        pltpu.VMEM((2 * half * group, vectors_n, width), BF16),
        pltpu.VMEM((2 * half * group, vectors_n, width), F32),
        pltpu.VMEM((rows_n * group, vectors_n, width), F32),
    ]
    kernel = functools.partial(product_kernel, offsets, bool(degree))
    args = [table, tiles, *col_parts, *row_parts, *degree]
    kept, swap, own, *send = call(
        kernel, out_shape, scratch, 32, args, 4 * tiles.size * vectors_n, 1
    )
    return kept, swap, own, send


def merge_kernel(degree, kept, got, *refs):
    if degree:
        row_degree, own_ref, own_degree, *send_refs = refs
    else:
        own_ref, *send_refs = refs
    _, group, vectors_n, _ = kept.shape
    for k in range(group):
        rows = slice(k * vectors_n, (k + 1) * vectors_n)
        own_ref[k] = kept[0, k] + got[0, rows, :].astype(F32)
        for d, send in enumerate(send_refs, 1):
            send[rows, :] = (kept[d, k] + got[d, rows, :].astype(F32)).astype(BF16)
    if degree:
        for d in range(kept.shape[0]):
            sums = row_degree[d * group : (d + 1) * group, :] + join_degree(got.at[d], group)
            if d:
                send_refs[d - 1][group * vectors_n :, :] = split_degree(sums)
            else:
                own_degree[...] = sums


def merge(kept, got, degree):
    _, group, _, width = kept.shape
    out_shape = [jax.ShapeDtypeStruct(kept.shape[1:], F32)]
    if degree:
        out_shape += [jax.ShapeDtypeStruct((group, width), F32)]
    out_shape += [jax.ShapeDtypeStruct(got.shape[1:], BF16)] * (kept.shape[0] - 1)
    kernel = functools.partial(merge_kernel, bool(degree))
    return call(kernel, out_shape, [], 24, [kept, got, *degree[:1]])


def gathered_sum(own, received, k):
    total = own[k]
    rows = slice(k * total.shape[0], (k + 1) * total.shape[0])
    for part in received:
        total = total + part[rows, :].astype(F32)
    return total


def symmetric_part(row_own, row_refs, col_own, col_refs, k):
    return 0.5 * (gathered_sum(row_own, row_refs, k) + gathered_sum(col_own, col_refs, k))


def first_kernel(chips_n, vec_ref, row_degree, col_degree, row_own, col_own, *refs):
    row_refs, refs = refs[: chips_n - 1], refs[chips_n - 1 :]
    col_refs, (first_ref, rounded_ref, degree_ref) = refs[:-3], refs[-3:]
    group, _, width = rounded_ref.shape
    degree = row_degree[...] + col_degree[:group, :]
    for part in (*row_refs, *col_refs):
        degree += join_degree(part, group)
    degree = 0.5 * degree
    degree_ref[...] = degree
    for k, vec in enumerate(tiles_first(vec_ref, width)):
        symmetric = symmetric_part(row_own, row_refs, col_own, col_refs, k)
        image = degree[k : k + 1, :] * vec - symmetric
        first = (image - CENTER * vec) / HALF_WIDTH
        first_ref[:, k * width : (k + 1) * width] = first
        rounded_ref[k] = first.astype(BF16)


def filter_kernel(chips_n, start_ref, first_ref, degree_ref, row_own, col_own, *refs):
    row_refs, refs = refs[: chips_n - 1], refs[chips_n - 1 :]
    col_refs, (filtered_ref, rounded_ref, gram_ref, both) = refs[:-4], refs[-4:]
    group, vectors_n, width = rounded_ref.shape
    for k, vec in enumerate(tiles_first(first_ref, width)):
        symmetric = symmetric_part(row_own, row_refs, col_own, col_refs, k)
        columns = slice(k * width, (k + 1) * width)
        image = degree_ref[k : k + 1, :] * vec - symmetric
        filtered = 2.0 * (image - CENTER * vec) / HALF_WIDTH - start_ref[:, columns]
        filtered_ref[:, columns] = filtered
        rounded_ref[k] = filtered.astype(BF16)
        both[:vectors_n, columns] = filtered
        both[vectors_n:, columns] = degree_ref[k : k + 1, :] * filtered
    gram_ref[...] = lax.dot_general(
        filtered_ref[...], both[...], NT, precision=HIGHEST, preferred_element_type=F32
    )


def form_kernel(offsets, table, tiles_ref, gram_ref, *refs):
    col_end = len(offsets[0])
    col_parts, row_parts = refs[:col_end], refs[col_end:-5]
    out_ref, col_panel, row_panel, left, right = refs[-5:]
    _, vectors_n, width = col_panel.shape
    fill(col_panel, col_parts, offsets[0])
    fill(row_panel, row_parts, offsets[1])
    for t in range(tiles_ref.shape[0]):
        columns = slice(t * width, (t + 1) * width)
        left[:, columns] = row_panel[table[1, t]]
        right[:, columns] = lax.dot_general(
            col_panel[table[0, t]], tiles_ref[t], NT, preferred_element_type=F32
        ).astype(BF16)
    form = lax.dot_general(left[...], right[...], NT, preferred_element_type=F32)
    projected = gram_ref[:, vectors_n:] - 0.5 * (form + form.T)
    row, col = square_index(vectors_n)
    packed = jnp.where(col >= row, gram_ref[:, :vectors_n], projected)
    diagonal = jnp.sum(jnp.where(row == col, projected, 0.0), 0, keepdims=True)
    half = vectors_n // 2
    out_ref[:half] = jnp.concatenate([packed[:half], packed[half:]], 1)
    diagonal = jnp.broadcast_to(diagonal, (8, vectors_n))
    out_ref[half:] = jnp.concatenate([diagonal, jnp.zeros_like(diagonal)], 1)


def square_index(n):
    return tuple(lax.broadcasted_iota(jnp.int32, (n, n), axis) for axis in (0, 1))


def inverse_factor(gram):
    n = gram.shape[0]
    row, col = square_index(n)
    table = jnp.concatenate([gram, jnp.where(row == col, 1.0, 0.0)], 1)
    bands = [table[i : i + 8] for i in range(0, n, 8)]
    line = lax.broadcasted_iota(jnp.int32, (8, 2 * n), 0)
    for j in range(0, n, 2):
        at, low = j // 8, j % 8
        one = bands[at][low : low + 1, :]
        two = bands[at][low + 1 : low + 2, :]
        a, b, c = one[:, j : j + 1], one[:, j + 1 : j + 2], two[:, j + 1 : j + 2]
        scale = 1.0 / (a * c - b * b)
        to_one = (c * scale) * one - (b * scale) * two
        to_two = (a * scale) * two - (b * scale) * one
        for i in range(at, n // 8):
            update = bands[i][:, j : j + 1] * to_one + bands[i][:, j + 1 : j + 2] * to_two
            if i == at:
                update = jnp.where(line > low + 1, update, 0.0)
            bands[i] = bands[i] - update
    table = jnp.concatenate(bands, 0)
    left, right = table[:, :n], table[:, n:]
    pivots = jnp.sum(jnp.where(row == col, left, 0.0), 1, keepdims=True)
    beside = jnp.sum(jnp.where(row + 1 == col, left, 0.0), 1, keepdims=True)
    odd = row % 2 == 1
    ratio = beside / pivots
    above = pltpu.roll(jnp.broadcast_to(ratio, (n, n)), 1, 0)
    right = jnp.where(odd, right - above * pltpu.roll(right, 1, 0), right)
    cut = pltpu.roll(jnp.broadcast_to(ratio * beside, (n, n)), 1, 0)
    return right / jnp.sqrt(jnp.where(odd, pivots - cut, pivots))


def last_kernel(total_nodes, filtered_ref, *refs):
    parts, (ritz_ref, rayleigh_ref) = refs[:-2], refs[-2:]
    n = filtered_ref.shape[0]
    half = n // 2
    sums = tree_sum([part[...] for part in parts]) * (1.0 / total_nodes)
    packed = jnp.concatenate([sums[:half, :n], sums[:half, n:]], 0)
    row, col = square_index(n)
    upper = jnp.where(col > row, packed, 0.0)
    gram = jnp.where(col >= row, packed, 0.0) + upper.T
    lower = jnp.where(col < row, packed, 0.0)
    diagonal = jnp.broadcast_to(sums[half : half + 1, :n], (n, n))
    projected = lower + lower.T + jnp.where(row == col, diagonal, 0.0)
    inverse = inverse_factor(gram)

    def dot(a, b, dims):
        return lax.dot_general(a, b, dims, precision=HIGHEST, preferred_element_type=F32)

    half_way = dot(inverse, projected, NN)
    rayleigh_ref[...] = dot(half_way, inverse, NT)
    turned = dot(inverse, half_way, NT)
    ritz_ref[...] = dot(dot(turned, inverse, NN), filtered_ref[...], NN)


def tree_sum(parts):
    while len(parts) > 1:
        parts = [a + b for a, b in zip(parts[::2], parts[1::2])]
    return parts[0]


def local(tiles, tile_rows, tile_cols, start):
    tiles, tile_rows, tile_cols = tiles[0, 0], tile_rows[0, 0], tile_cols[0, 0]
    width = tiles.shape[-1]
    vectors_n, own_nodes = start.shape
    rows_n, cols_n = lax.axis_size("row"), lax.axis_size("col")
    chips_n = cols_n // 2
    total_nodes = own_nodes * rows_n * cols_n
    group = own_nodes // width
    spread = (vectors_n, tiles.shape[0] * width)

    rounded_shape = jax.ShapeDtypeStruct((group, vectors_n, width), BF16)
    vector_shape = jax.ShapeDtypeStruct((vectors_n, own_nodes), F32)
    degree_shape = jax.ShapeDtypeStruct((group, width), F32)

    col_apart = (tile_cols // group) ^ lax.axis_index("row")
    row_apart = (tile_rows // group) ^ lax.axis_index("col")
    row_halves = row_apart % 2 * chips_n + row_apart // 2
    table = jnp.stack([col_apart, row_apart, row_halves]) * group
    table = (table + jnp.stack([tile_cols, tile_rows, tile_rows]) % group).astype(jnp.int32)

    col_offsets, d = [0], rows_n // 2
    while d:
        col_offsets += [offset ^ d for offset in col_offsets]
        d //= 2
    row_offsets = [2 * d + core for core in range(2) for d in range(chips_n)]
    offsets = (col_offsets, row_offsets)

    def gather(rounded):
        held, d = [rounded], rows_n // 2
        while d:
            near = trade(rounded, "row", d)
            if len(held) > 1:
                near, *rest = lax.optimization_barrier((near, *held[1:]))
                held = [rounded, *rest]
            held += [near, *(trade(part, "row", d) for part in held[1:])]
            d //= 2
        chips = [rounded, *exchange([rounded] * (chips_n - 1), "col", 2)]
        return held, chips + [trade(chip, "col", 1) for chip in chips]

    def apply(rounded, degree=()):
        kept, swap, col_own, col_send = products(tiles, table, *gather(rounded), offsets, degree)
        col_got = exchange(col_send, "row")
        row_own, *row_send = merge(kept, trade(swap, "col", 1), degree)
        if degree:
            own_degree, *row_send = row_send
        row_got = exchange(row_send, "col", 2)
        sums = [row_own, col_own, *row_got, *col_got]
        return [own_degree, degree[1], *sums] if degree else sums

    rounded = call(round_kernel, rounded_shape, [], 16, [start])
    degree = call(
        degree_kernel,
        [jax.ShapeDtypeStruct((n * group, width), F32) for n in (cols_n, rows_n)],
        [],
        16,
        [table, tiles],
        4 * tiles.size * DEGREE_ROWS,
        1,
    )
    first, rounded, degree = call(
        functools.partial(first_kernel, chips_n),
        [vector_shape, rounded_shape, degree_shape],
        [],
        24,
        [start, *apply(rounded, tuple(degree))],
    )
    filtered, rounded, gram = call(
        functools.partial(filter_kernel, chips_n),
        [vector_shape, rounded_shape, jax.ShapeDtypeStruct((vectors_n, 2 * vectors_n), F32)],
        [pltpu.VMEM((2 * vectors_n, own_nodes), F32)],
        24,
        [start, first, degree, *apply(rounded)],
    )
    col_parts, row_parts = gather(rounded)
    sums = call(
        functools.partial(form_kernel, offsets),
        jax.ShapeDtypeStruct((vectors_n // 2 + 8, 2 * vectors_n), F32),
        [
            pltpu.VMEM((rows_n * group, vectors_n, width), BF16),
            pltpu.VMEM((cols_n * group, vectors_n, width), BF16),
            pltpu.VMEM(spread, BF16),
            pltpu.VMEM(spread, BF16),
        ],
        24,
        [table, tiles, gram, *col_parts, *row_parts],
        4 * tiles.size * vectors_n,
        1,
    )
    sums = sums + trade(sums, "col", 1)
    sums = tree_sum([sums, *exchange([sums] * (chips_n - 1), "col", 2)])
    return call(
        functools.partial(last_kernel, total_nodes),
        [vector_shape, jax.ShapeDtypeStruct((vectors_n, vectors_n), F32)],
        [],
        24,
        [filtered, sums, *exchange([sums] * (rows_n - 1), "row")],
    )


def solution(mesh):
    placed = (
        P("row", "col", None, None, None),
        P("row", "col", None),
        P("row", "col", None),
        P(None, ("row", "col")),
    )
    return jax.shard_map(
        local, mesh=mesh, in_specs=placed, out_specs=(P(None, ("row", "col")), P()), check_vma=False
    )
```

```python
import functools

import jax
import jax.numpy as jnp
from jax import lax
from jax.experimental import pallas as pl
from jax.experimental.pallas import tpu as pltpu
from jax.sharding import PartitionSpec as P

CENTER = 1.0
HALF_WIDTH = 0.5
HIGHEST = lax.Precision.HIGHEST
NT = (((1,), (1,)), ((), ()))
NN = (((1,), (0,)), ((), ()))
BF16 = jnp.bfloat16
F32 = jnp.float32
VMEM = pl.BlockSpec(memory_space=pltpu.VMEM)
SMEM = pl.BlockSpec(memory_space=pltpu.SMEM)
DEGREE_ROWS = 16


def call(kernel, out_shape, scratch, limit, args, flops=0, smem=0):
    moved = sum(x.size * x.dtype.itemsize for x in args)
    return pl.pallas_call(
        kernel,
        out_shape=out_shape,
        in_specs=[SMEM] * smem + [VMEM] * (len(args) - smem),
        out_specs=jax.tree.map(lambda _: VMEM, out_shape),
        scratch_shapes=scratch,
        compiler_params=pltpu.CompilerParams(vmem_limit_bytes=limit * 2**20),
        cost_estimate=pl.CostEstimate(flops=flops, bytes_accessed=moved, transcendentals=0),
    )(*args)


def trade(part, axis, d):
    n = lax.axis_size(axis)
    return lax.ppermute(part, axis, [(i, i ^ d) for i in range(n)])


def exchange(parts, axis, step=1):
    far_first = [trade(part, axis, step * d) for d, part in reversed(list(enumerate(parts, 1)))]
    return far_first[::-1]


def tiles_first(ref, width):
    return [ref[:, k * width : (k + 1) * width] for k in range(ref.shape[1] // width)]


def round_kernel(vec_ref, out_ref):
    for k, piece in enumerate(tiles_first(vec_ref, out_ref.shape[2])):
        out_ref[k] = piece.astype(BF16)


def split_degree(sums):
    high = sums.astype(BF16).astype(F32)
    return jnp.concatenate([high, sums - high], 0).astype(BF16)


def join_degree(payload, group):
    parts = payload[payload.shape[0] - 2 * group :, :].astype(F32)
    return parts[:group] + parts[group:]


def fill(panel, parts, runs):
    for part, places in zip(parts, runs):
        at = 0
        for place, count in places:
            panel[place : place + count] = part[at : at + count]
            at += count


def degree_kernel(table, tiles_ref, row_ref, col_ref):
    row_ref[...] = jnp.zeros_like(row_ref)
    col_ref[...] = jnp.zeros_like(col_ref)
    ones = jnp.ones((DEGREE_ROWS, tiles_ref.shape[2]), BF16)
    for t in range(tiles_ref.shape[0]):
        for ref, place, dims in ((row_ref, table[2, t], NT), (col_ref, table[0, t], NN)):
            sums = lax.dot_general(ones, tiles_ref[t], dims, preferred_element_type=F32)
            ref[pl.ds(place, 1), :] += sums[:1]


def product_kernel(runs, order, degree, table, tiles_ref, *refs):
    col_runs, row_runs = runs
    half = len(row_runs) // 2
    col_parts, refs = refs[: len(col_runs)], refs[len(col_runs) :]
    row_parts, refs = refs[: len(row_runs)], refs[len(row_runs) :]
    if degree:
        row_degree, col_degree, *refs = refs
    kept_ref, swap_ref, own_ref, *send_refs = refs[:-4]
    col_panel, row_panel, row_total, col_total = refs[-4:]
    group, vectors_n, width = col_parts[0].shape
    fill(col_panel, col_parts, col_runs)
    fill(row_panel, row_parts, row_runs)
    row_total[...] = jnp.zeros_like(row_total)
    col_total[...] = jnp.zeros_like(col_total)
    for t in range(tiles_ref.shape[0]):
        tile, here = tiles_ref[t], table[0, t]
        row_total[table[2, t]] += lax.dot_general(
            col_panel[here], tile, NT, preferred_element_type=F32
        )
        col_total[here] += lax.dot_general(
            row_panel[table[1, t]], tile, NN, preferred_element_type=F32
        )
    for d in range(half):
        kept_ref[d] = row_total[d * group : (d + 1) * group]
    own_ref[...] = col_total[:group]
    sends = [(row_total, half + d, swap_ref.at[d]) for d in range(half)]
    sends += [(col_total, d, send) for d, send in zip(order, send_refs)]
    for total, d, send in sends:
        for k in range(group):
            send[k * vectors_n : (k + 1) * vectors_n, :] = total[d * group + k].astype(BF16)
        if degree:
            sums = row_degree if total is row_total else col_degree
            send[group * vectors_n :, :] = split_degree(sums[d * group : (d + 1) * group, :])


def products(tiles, table, col_parts, row_parts, runs, order, degree):
    group, vectors_n, width = col_parts[0].shape
    rows_n, half = len(order) + 1, len(row_parts) // 2
    rows = group * vectors_n + (2 * group if degree else 0)
    out_shape = [
        jax.ShapeDtypeStruct((half, group, vectors_n, width), F32),
        jax.ShapeDtypeStruct((half, rows, width), BF16),
        jax.ShapeDtypeStruct((group, vectors_n, width), F32),
    ]
    out_shape += [jax.ShapeDtypeStruct((rows, width), BF16)] * (rows_n - 1)
    scratch = [
        pltpu.VMEM((rows_n * group, vectors_n, width), BF16),
        pltpu.VMEM((2 * half * group, vectors_n, width), BF16),
        pltpu.VMEM((2 * half * group, vectors_n, width), F32),
        pltpu.VMEM((rows_n * group, vectors_n, width), F32),
    ]
    kernel = functools.partial(product_kernel, runs, order, bool(degree))
    args = [table, tiles, *col_parts, *row_parts, *degree]
    kept, swap, own, *send = call(
        kernel, out_shape, scratch, 32, args, 4 * tiles.size * vectors_n, 1
    )
    return kept, swap, own, send


def merge_kernel(degree, kept, got, *refs):
    if degree:
        row_degree, own_ref, own_degree, *send_refs = refs
    else:
        own_ref, *send_refs = refs
    _, group, vectors_n, _ = kept.shape
    for k in range(group):
        rows = slice(k * vectors_n, (k + 1) * vectors_n)
        own_ref[k] = kept[0, k] + got[0, rows, :].astype(F32)
        for d, send in enumerate(send_refs, 1):
            send[rows, :] = (kept[d, k] + got[d, rows, :].astype(F32)).astype(BF16)
    if degree:
        for d in range(kept.shape[0]):
            sums = row_degree[d * group : (d + 1) * group, :] + join_degree(got.at[d], group)
            if d:
                send_refs[d - 1][group * vectors_n :, :] = split_degree(sums)
            else:
                own_degree[...] = sums


def merge(kept, got, degree):
    _, group, _, width = kept.shape
    out_shape = [jax.ShapeDtypeStruct(kept.shape[1:], F32)]
    if degree:
        out_shape += [jax.ShapeDtypeStruct((group, width), F32)]
    out_shape += [jax.ShapeDtypeStruct(got.shape[1:], BF16)] * (kept.shape[0] - 1)
    kernel = functools.partial(merge_kernel, bool(degree))
    return call(kernel, out_shape, [], 24, [kept, got, *degree[:1]])


def gathered_sum(own, received, k):
    total = own[k]
    rows = slice(k * total.shape[0], (k + 1) * total.shape[0])
    for part in received:
        total = total + part[rows, :].astype(F32)
    return total


def symmetric_part(row_own, row_refs, col_own, col_refs, k):
    return 0.5 * (gathered_sum(row_own, row_refs, k) + gathered_sum(col_own, col_refs, k))


def first_kernel(chips_n, vec_ref, row_degree, col_degree, row_own, col_own, *refs):
    row_refs, refs = refs[: chips_n - 1], refs[chips_n - 1 :]
    col_refs, (first_ref, rounded_ref, degree_ref) = refs[:-3], refs[-3:]
    group, _, width = rounded_ref.shape
    degree = row_degree[...] + col_degree[:group, :]
    for part in (*row_refs, *col_refs):
        degree += join_degree(part, group)
    degree = 0.5 * degree
    degree_ref[...] = degree
    for k, vec in enumerate(tiles_first(vec_ref, width)):
        symmetric = symmetric_part(row_own, row_refs, col_own, col_refs, k)
        image = degree[k : k + 1, :] * vec - symmetric
        first = (image - CENTER * vec) / HALF_WIDTH
        first_ref[:, k * width : (k + 1) * width] = first
        rounded_ref[k] = first.astype(BF16)


def filter_kernel(chips_n, start_ref, first_ref, degree_ref, row_own, col_own, *refs):
    row_refs, refs = refs[: chips_n - 1], refs[chips_n - 1 :]
    col_refs, (filtered_ref, rounded_ref, gram_ref, both) = refs[:-4], refs[-4:]
    group, vectors_n, width = rounded_ref.shape
    for k, vec in enumerate(tiles_first(first_ref, width)):
        symmetric = symmetric_part(row_own, row_refs, col_own, col_refs, k)
        columns = slice(k * width, (k + 1) * width)
        image = degree_ref[k : k + 1, :] * vec - symmetric
        filtered = 2.0 * (image - CENTER * vec) / HALF_WIDTH - start_ref[:, columns]
        filtered_ref[:, columns] = filtered
        rounded_ref[k] = filtered.astype(BF16)
        both[:vectors_n, columns] = filtered
        both[vectors_n:, columns] = degree_ref[k : k + 1, :] * filtered
    gram_ref[...] = lax.dot_general(
        filtered_ref[...], both[...], NT, precision=HIGHEST, preferred_element_type=F32
    )


def form_kernel(runs, table, tiles_ref, gram_ref, *refs):
    col_end = len(runs[0])
    col_parts, row_parts = refs[:col_end], refs[col_end:-5]
    out_ref, col_panel, row_panel, left, right = refs[-5:]
    _, vectors_n, width = col_panel.shape
    fill(col_panel, col_parts, runs[0])
    fill(row_panel, row_parts, runs[1])
    for t in range(tiles_ref.shape[0]):
        columns = slice(t * width, (t + 1) * width)
        left[:, columns] = row_panel[table[1, t]]
        right[:, columns] = lax.dot_general(
            col_panel[table[0, t]], tiles_ref[t], NT, preferred_element_type=F32
        ).astype(BF16)
    form = lax.dot_general(left[...], right[...], NT, preferred_element_type=F32)
    projected = gram_ref[:, vectors_n:] - 0.5 * (form + form.T)
    row, col = square_index(vectors_n)
    packed = jnp.where(col >= row, gram_ref[:, :vectors_n], projected)
    diagonal = jnp.sum(jnp.where(row == col, projected, 0.0), 0, keepdims=True)
    half = vectors_n // 2
    out_ref[:half] = jnp.concatenate([packed[:half], packed[half:]], 1)
    diagonal = jnp.broadcast_to(diagonal, (8, vectors_n))
    out_ref[half:] = jnp.concatenate([diagonal, jnp.zeros_like(diagonal)], 1)


def square_index(n):
    return tuple(lax.broadcasted_iota(jnp.int32, (n, n), axis) for axis in (0, 1))


def inverse_factor(gram):
    n = gram.shape[0]
    row, col = square_index(n)
    table = jnp.concatenate([gram, jnp.where(row == col, 1.0, 0.0)], 1)
    bands = [table[i : i + 8] for i in range(0, n, 8)]
    below = lax.broadcasted_iota(jnp.int32, (8, 2 * n), 0)
    for j in range(n):
        at, line = j // 8, j % 8
        pivot_row = bands[at][line : line + 1, :]
        pivot_row = jnp.broadcast_to(pivot_row / pivot_row[:, j : j + 1], (8, 2 * n))
        for i in range(at, n // 8):
            update = bands[i][:, j : j + 1] * pivot_row
            if i == at:
                update = jnp.where(below > line, update, 0.0)
            bands[i] = bands[i] - update
    table = jnp.concatenate(bands, 0)
    pivots = jnp.sum(jnp.where(row == col, table[:, :n], 0.0), 1, keepdims=True)
    return table[:, n:] / jnp.sqrt(pivots)


def last_kernel(total_nodes, filtered_ref, *refs):
    parts, (ritz_ref, rayleigh_ref) = refs[:-2], refs[-2:]
    n = filtered_ref.shape[0]
    half = n // 2
    sums = tree_sum([part[...] for part in parts]) * (1.0 / total_nodes)
    packed = jnp.concatenate([sums[:half, :n], sums[:half, n:]], 0)
    row, col = square_index(n)
    upper = jnp.where(col > row, packed, 0.0)
    gram = jnp.where(col >= row, packed, 0.0) + upper.T
    lower = jnp.where(col < row, packed, 0.0)
    diagonal = jnp.broadcast_to(sums[half : half + 1, :n], (n, n))
    projected = lower + lower.T + jnp.where(row == col, diagonal, 0.0)
    inverse = inverse_factor(gram)

    def dot(a, b, dims):
        return lax.dot_general(a, b, dims, precision=HIGHEST, preferred_element_type=F32)

    half_way = dot(inverse, projected, NN)
    rayleigh_ref[...] = dot(half_way, inverse, NT)
    turned = dot(inverse, half_way, NT)
    ritz_ref[...] = dot(dot(turned, inverse, NN), filtered_ref[...], NN)


def tree_sum(parts):
    while len(parts) > 1:
        parts = [a + b for a, b in zip(parts[::2], parts[1::2])]
    return parts[0]


def local(tiles, tile_rows, tile_cols, start):
    tiles, tile_rows, tile_cols = tiles[0, 0], tile_rows[0, 0], tile_cols[0, 0]
    width = tiles.shape[-1]
    vectors_n, own_nodes = start.shape
    rows_n, cols_n = lax.axis_size("row"), lax.axis_size("col")
    chips_n = cols_n // 2
    total_nodes = own_nodes * rows_n * cols_n
    group = own_nodes // width
    spread = (vectors_n, tiles.shape[0] * width)

    rounded_shape = jax.ShapeDtypeStruct((group, vectors_n, width), BF16)
    vector_shape = jax.ShapeDtypeStruct((vectors_n, own_nodes), F32)
    degree_shape = jax.ShapeDtypeStruct((group, width), F32)

    col_apart = (tile_cols // group) ^ lax.axis_index("row")
    row_apart = (tile_rows // group) ^ lax.axis_index("col")
    row_halves = row_apart % 2 * chips_n + row_apart // 2
    table = jnp.stack([col_apart, row_apart, row_halves]) * group
    table = (table + jnp.stack([tile_cols, tile_rows, tile_rows]) % group).astype(jnp.int32)

    late = 1
    levels = [rows_n >> i for i in range(1, rows_n.bit_length())]
    col_runs = [[(0, group)]]
    for d in levels:
        if len(col_runs) == 1:
            col_runs += [[(d * group, group)]]
            continue
        cut = group - late
        passed = [((p // group ^ d) * group + p % group, n) for run in col_runs[1:] for p, n in run]
        col_runs += [[(d * group, cut)], [(d * group + cut, late), *passed]]
    row_runs = [[((2 * d + core) * group, group)] for core in range(2) for d in range(chips_n)]
    runs = (col_runs, row_runs)
    order = [*range(rows_n // 2, rows_n), *range(1, rows_n // 2)]

    def gather(rounded, first=()):
        held = [rounded]
        for d in levels:
            if len(held) == 1:
                held += [trade(rounded, "row", d)]
                continue
            near = trade(rounded[: group - late], "row", d)
            near, *passed = lax.optimization_barrier((near, *held[1:], *first))
            held[1:] = passed[: len(held) - 1]
            held += [near, trade(jnp.concatenate([rounded[group - late :], *held[1:]]), "row", d)]
        chips = [rounded, *exchange([rounded] * (chips_n - 1), "col", 2)]
        return held, chips + [trade(chip, "col", 1) for chip in chips]

    def apply(rounded, degree=()):
        kept, swap, col_own, col_send = products(
            tiles, table, *gather(rounded, degree), runs, order, degree
        )
        col_got = [trade(part, "row", d) for d, part in zip(order, col_send)]
        row_own, *row_send = merge(kept, trade(swap, "col", 1), degree)
        if degree:
            own_degree, *row_send = row_send
        row_got = exchange(row_send, "col", 2)
        sums = [row_own, col_own, *row_got, *col_got]
        return [own_degree, degree[1], *sums] if degree else sums

    rounded = call(round_kernel, rounded_shape, [], 16, [start])
    degree = call(
        degree_kernel,
        [jax.ShapeDtypeStruct((n * group, width), F32) for n in (cols_n, rows_n)],
        [],
        16,
        [table, tiles],
        4 * tiles.size * DEGREE_ROWS,
        1,
    )
    first, rounded, degree = call(
        functools.partial(first_kernel, chips_n),
        [vector_shape, rounded_shape, degree_shape],
        [],
        24,
        [start, *apply(rounded, tuple(degree))],
    )
    filtered, rounded, gram = call(
        functools.partial(filter_kernel, chips_n),
        [vector_shape, rounded_shape, jax.ShapeDtypeStruct((vectors_n, 2 * vectors_n), F32)],
        [pltpu.VMEM((2 * vectors_n, own_nodes), F32)],
        24,
        [start, first, degree, *apply(rounded)],
    )
    col_parts, row_parts = gather(rounded)
    sums = call(
        functools.partial(form_kernel, runs),
        jax.ShapeDtypeStruct((vectors_n // 2 + 8, 2 * vectors_n), F32),
        [
            pltpu.VMEM((rows_n * group, vectors_n, width), BF16),
            pltpu.VMEM((cols_n * group, vectors_n, width), BF16),
            pltpu.VMEM(spread, BF16),
            pltpu.VMEM(spread, BF16),
        ],
        24,
        [table, tiles, gram, *col_parts, *row_parts],
        4 * tiles.size * vectors_n,
        1,
    )
    sums = sums + trade(sums, "col", 1)
    sums = tree_sum([sums, *exchange([sums] * (chips_n - 1), "col", 2)])
    return call(
        functools.partial(last_kernel, total_nodes),
        [vector_shape, jax.ShapeDtypeStruct((vectors_n, vectors_n), F32)],
        [],
        24,
        [filtered, sums, *exchange([sums] * (rows_n - 1), "row")],
    )


def solution(mesh):
    placed = (
        P("row", "col", None, None, None),
        P("row", "col", None),
        P("row", "col", None),
        P(None, ("row", "col")),
    )
    return jax.shard_map(
        local, mesh=mesh, in_specs=placed, out_specs=(P(None, ("row", "col")), P()), check_vma=False
    )
```

```python
import functools

import jax
import jax.numpy as jnp
from jax import lax
from jax.experimental import pallas as pl
from jax.experimental.pallas import tpu as pltpu
from jax.sharding import PartitionSpec as P

CENTER = 1.0
HALF_WIDTH = 0.5
HIGHEST = lax.Precision.HIGHEST
NT = (((1,), (1,)), ((), ()))
NN = (((1,), (0,)), ((), ()))
BF16 = jnp.bfloat16
F32 = jnp.float32
VMEM = pl.BlockSpec(memory_space=pltpu.VMEM)
SMEM = pl.BlockSpec(memory_space=pltpu.SMEM)
DEGREE_ROWS = 16


def call(kernel, out_shape, scratch, limit, args, flops=0, smem=0):
    moved = sum(x.size * x.dtype.itemsize for x in args)
    return pl.pallas_call(
        kernel,
        out_shape=out_shape,
        in_specs=[SMEM] * smem + [VMEM] * (len(args) - smem),
        out_specs=jax.tree.map(lambda _: VMEM, out_shape),
        scratch_shapes=scratch,
        compiler_params=pltpu.CompilerParams(vmem_limit_bytes=limit * 2**20),
        cost_estimate=pl.CostEstimate(flops=flops, bytes_accessed=moved, transcendentals=0),
    )(*args)


def trade(part, axis, d):
    n = lax.axis_size(axis)
    return lax.ppermute(part, axis, [(i, i ^ d) for i in range(n)])


def exchange(parts, axis, step=1):
    far_first = [trade(part, axis, step * d) for d, part in reversed(list(enumerate(parts, 1)))]
    return far_first[::-1]


def tiles_first(ref, width):
    return [ref[:, k * width : (k + 1) * width] for k in range(ref.shape[1] // width)]


def round_kernel(vec_ref, out_ref):
    for k, piece in enumerate(tiles_first(vec_ref, out_ref.shape[2])):
        out_ref[k] = piece.astype(BF16)


def split_degree(sums):
    high = sums.astype(BF16).astype(F32)
    return jnp.concatenate([high, sums - high], 0).astype(BF16)


def join_degree(payload, group):
    parts = payload[payload.shape[0] - 2 * group :, :].astype(F32)
    return parts[:group] + parts[group:]


def fill(panel, parts, runs):
    for part, places in zip(parts, runs):
        at = 0
        for place, count in places:
            panel[place : place + count] = part[at : at + count]
            at += count


def degree_kernel(table, tiles_ref, row_ref, col_ref):
    row_ref[...] = jnp.zeros_like(row_ref)
    col_ref[...] = jnp.zeros_like(col_ref)
    ones = jnp.ones((DEGREE_ROWS, tiles_ref.shape[2]), BF16)
    for t in range(tiles_ref.shape[0]):
        for ref, place, dims in ((row_ref, table[2, t], NT), (col_ref, table[0, t], NN)):
            sums = lax.dot_general(ones, tiles_ref[t], dims, preferred_element_type=F32)
            ref[pl.ds(place, 1), :] += sums[:1]


def product_kernel(runs, order, degree, table, tiles_ref, *refs):
    col_runs, row_runs = runs
    half = len(row_runs) // 2
    col_parts, refs = refs[: len(col_runs)], refs[len(col_runs) :]
    row_parts, refs = refs[: len(row_runs)], refs[len(row_runs) :]
    if degree:
        row_degree, col_degree, *refs = refs
    kept_ref, swap_ref, own_ref, *send_refs = refs[:-4]
    col_panel, row_panel, row_total, col_total = refs[-4:]
    group, vectors_n, width = col_parts[0].shape
    fill(col_panel, col_parts, col_runs)
    fill(row_panel, row_parts, row_runs)
    row_total[...] = jnp.zeros_like(row_total)
    col_total[...] = jnp.zeros_like(col_total)
    for t in range(tiles_ref.shape[0]):
        tile, here = tiles_ref[t], table[0, t]
        row_total[table[2, t]] += lax.dot_general(
            col_panel[here], tile, NT, preferred_element_type=F32
        )
        col_total[here] += lax.dot_general(
            row_panel[table[1, t]], tile, NN, preferred_element_type=F32
        )
    for d in range(half):
        kept_ref[d] = row_total[d * group : (d + 1) * group]
    own_ref[...] = col_total[:group]
    sends = [(row_total, half + d, swap_ref.at[d]) for d in range(half)]
    sends += [(col_total, d, send) for d, send in zip(order, send_refs)]
    for total, d, send in sends:
        for k in range(group):
            send[k * vectors_n : (k + 1) * vectors_n, :] = total[d * group + k].astype(BF16)
        if degree:
            sums = row_degree if total is row_total else col_degree
            send[group * vectors_n :, :] = split_degree(sums[d * group : (d + 1) * group, :])


def products(tiles, table, col_parts, row_parts, runs, order, degree):
    group, vectors_n, width = col_parts[0].shape
    rows_n, half = len(order) + 1, len(row_parts) // 2
    rows = group * vectors_n + (2 * group if degree else 0)
    out_shape = [
        jax.ShapeDtypeStruct((half, group, vectors_n, width), F32),
        jax.ShapeDtypeStruct((half, rows, width), BF16),
        jax.ShapeDtypeStruct((group, vectors_n, width), F32),
    ]
    out_shape += [jax.ShapeDtypeStruct((rows, width), BF16)] * (rows_n - 1)
    scratch = [
        pltpu.VMEM((rows_n * group, vectors_n, width), BF16),
        pltpu.VMEM((2 * half * group, vectors_n, width), BF16),
        pltpu.VMEM((2 * half * group, vectors_n, width), F32),
        pltpu.VMEM((rows_n * group, vectors_n, width), F32),
    ]
    kernel = functools.partial(product_kernel, runs, order, bool(degree))
    args = [table, tiles, *col_parts, *row_parts, *degree]
    kept, swap, own, *send = call(
        kernel, out_shape, scratch, 32, args, 4 * tiles.size * vectors_n, 1
    )
    return kept, swap, own, send


def merge_kernel(degree, kept, got, *refs):
    if degree:
        row_degree, own_ref, own_degree, *send_refs = refs
    else:
        own_ref, *send_refs = refs
    _, group, vectors_n, _ = kept.shape
    for k in range(group):
        rows = slice(k * vectors_n, (k + 1) * vectors_n)
        own_ref[k] = kept[0, k] + got[0, rows, :].astype(F32)
        for d, send in enumerate(send_refs, 1):
            send[rows, :] = (kept[d, k] + got[d, rows, :].astype(F32)).astype(BF16)
    if degree:
        for d in range(kept.shape[0]):
            sums = row_degree[d * group : (d + 1) * group, :] + join_degree(got.at[d], group)
            if d:
                send_refs[d - 1][group * vectors_n :, :] = split_degree(sums)
            else:
                own_degree[...] = sums


def merge(kept, got, degree):
    _, group, _, width = kept.shape
    out_shape = [jax.ShapeDtypeStruct(kept.shape[1:], F32)]
    if degree:
        out_shape += [jax.ShapeDtypeStruct((group, width), F32)]
    out_shape += [jax.ShapeDtypeStruct(got.shape[1:], BF16)] * (kept.shape[0] - 1)
    kernel = functools.partial(merge_kernel, bool(degree))
    return call(kernel, out_shape, [], 24, [kept, got, *degree[:1]])


def gathered_sum(own, received, k):
    total = own[k]
    rows = slice(k * total.shape[0], (k + 1) * total.shape[0])
    for part in received:
        total = total + part[rows, :].astype(F32)
    return total


def symmetric_part(row_own, row_refs, col_own, col_refs, k):
    return 0.5 * (gathered_sum(row_own, row_refs, k) + gathered_sum(col_own, col_refs, k))


def first_kernel(chips_n, vec_ref, row_degree, col_degree, row_own, col_own, *refs):
    row_refs, refs = refs[: chips_n - 1], refs[chips_n - 1 :]
    col_refs, (first_ref, rounded_ref, degree_ref) = refs[:-3], refs[-3:]
    group, _, width = rounded_ref.shape
    degree = row_degree[...] + col_degree[:group, :]
    for part in (*row_refs, *col_refs):
        degree += join_degree(part, group)
    degree = 0.5 * degree
    degree_ref[...] = degree
    for k, vec in enumerate(tiles_first(vec_ref, width)):
        symmetric = symmetric_part(row_own, row_refs, col_own, col_refs, k)
        image = degree[k : k + 1, :] * vec - symmetric
        first = (image - CENTER * vec) / HALF_WIDTH
        first_ref[:, k * width : (k + 1) * width] = first
        rounded_ref[k] = first.astype(BF16)


def filter_kernel(chips_n, start_ref, first_ref, degree_ref, row_own, col_own, *refs):
    row_refs, refs = refs[: chips_n - 1], refs[chips_n - 1 :]
    col_refs, (filtered_ref, rounded_ref, gram_ref, both) = refs[:-4], refs[-4:]
    group, vectors_n, width = rounded_ref.shape
    for k, vec in enumerate(tiles_first(first_ref, width)):
        symmetric = symmetric_part(row_own, row_refs, col_own, col_refs, k)
        columns = slice(k * width, (k + 1) * width)
        image = degree_ref[k : k + 1, :] * vec - symmetric
        filtered = 2.0 * (image - CENTER * vec) / HALF_WIDTH - start_ref[:, columns]
        filtered_ref[:, columns] = filtered
        rounded_ref[k] = filtered.astype(BF16)
        both[:vectors_n, columns] = filtered
        both[vectors_n:, columns] = degree_ref[k : k + 1, :] * filtered
    gram_ref[...] = lax.dot_general(
        filtered_ref[...], both[...], NT, precision=HIGHEST, preferred_element_type=F32
    )


def form_kernel(runs, table, tiles_ref, gram_ref, *refs):
    col_end = len(runs[0])
    col_parts, row_parts = refs[:col_end], refs[col_end:-5]
    out_ref, col_panel, row_panel, left, right = refs[-5:]
    _, vectors_n, width = col_panel.shape
    fill(col_panel, col_parts, runs[0])
    fill(row_panel, row_parts, runs[1])
    for t in range(tiles_ref.shape[0]):
        columns = slice(t * width, (t + 1) * width)
        left[:, columns] = row_panel[table[1, t]]
        right[:, columns] = lax.dot_general(
            col_panel[table[0, t]], tiles_ref[t], NT, preferred_element_type=F32
        ).astype(BF16)
    form = lax.dot_general(left[...], right[...], NT, preferred_element_type=F32)
    projected = gram_ref[:, vectors_n:] - 0.5 * (form + form.T)
    row, col = square_index(vectors_n)
    packed = jnp.where(col >= row, gram_ref[:, :vectors_n], projected)
    diagonal = jnp.sum(jnp.where(row == col, projected, 0.0), 0, keepdims=True)
    half = vectors_n // 2
    out_ref[:half] = jnp.concatenate([packed[:half], packed[half:]], 1)
    diagonal = jnp.broadcast_to(diagonal, (8, vectors_n))
    out_ref[half:] = jnp.concatenate([diagonal, jnp.zeros_like(diagonal)], 1)


def square_index(n):
    return tuple(lax.broadcasted_iota(jnp.int32, (n, n), axis) for axis in (0, 1))


def inverse_factor(gram):
    n = gram.shape[0]
    row, col = square_index(n)
    table = jnp.concatenate([gram, jnp.where(row == col, 1.0, 0.0)], 1)
    bands = [table[i : i + 8] for i in range(0, n, 8)]
    below = lax.broadcasted_iota(jnp.int32, (8, 2 * n), 0)
    for j in range(n):
        at, line = j // 8, j % 8
        pivot_row = bands[at][line : line + 1, :]
        pivot_row = jnp.broadcast_to(pivot_row / pivot_row[:, j : j + 1], (8, 2 * n))
        for i in range(at, n // 8):
            update = bands[i][:, j : j + 1] * pivot_row
            if i == at:
                update = jnp.where(below > line, update, 0.0)
            bands[i] = bands[i] - update
    table = jnp.concatenate(bands, 0)
    pivots = jnp.sum(jnp.where(row == col, table[:, :n], 0.0), 1, keepdims=True)
    return table[:, n:] / jnp.sqrt(pivots)


def last_kernel(total_nodes, filtered_ref, *refs):
    parts, (ritz_ref, rayleigh_ref) = refs[:-2], refs[-2:]
    n = filtered_ref.shape[0]
    half = n // 2
    sums = tree_sum([part[...] for part in parts]) * (1.0 / total_nodes)
    packed = jnp.concatenate([sums[:half, :n], sums[:half, n:]], 0)
    row, col = square_index(n)
    upper = jnp.where(col > row, packed, 0.0)
    gram = jnp.where(col >= row, packed, 0.0) + upper.T
    lower = jnp.where(col < row, packed, 0.0)
    diagonal = jnp.broadcast_to(sums[half : half + 1, :n], (n, n))
    projected = lower + lower.T + jnp.where(row == col, diagonal, 0.0)
    inverse = inverse_factor(gram)

    def dot(a, b, dims):
        return lax.dot_general(a, b, dims, precision=HIGHEST, preferred_element_type=F32)

    half_way = dot(inverse, projected, NN)
    rayleigh_ref[...] = dot(half_way, inverse, NT)
    turned = dot(inverse, half_way, NT)
    ritz_ref[...] = dot(dot(turned, inverse, NN), filtered_ref[...], NN)


def tree_sum(parts):
    while len(parts) > 1:
        parts = [a + b for a, b in zip(parts[::2], parts[1::2])]
    return parts[0]


def local(tiles, tile_rows, tile_cols, start):
    tiles, tile_rows, tile_cols = tiles[0, 0], tile_rows[0, 0], tile_cols[0, 0]
    width = tiles.shape[-1]
    vectors_n, own_nodes = start.shape
    rows_n, cols_n = lax.axis_size("row"), lax.axis_size("col")
    chips_n = cols_n // 2
    total_nodes = own_nodes * rows_n * cols_n
    group = own_nodes // width
    spread = (vectors_n, tiles.shape[0] * width)

    rounded_shape = jax.ShapeDtypeStruct((group, vectors_n, width), BF16)
    vector_shape = jax.ShapeDtypeStruct((vectors_n, own_nodes), F32)
    degree_shape = jax.ShapeDtypeStruct((group, width), F32)

    col_apart = (tile_cols // group) ^ lax.axis_index("row")
    row_apart = (tile_rows // group) ^ lax.axis_index("col")
    row_halves = row_apart % 2 * chips_n + row_apart // 2
    table = jnp.stack([col_apart, row_apart, row_halves]) * group
    table = (table + jnp.stack([tile_cols, tile_rows, tile_rows]) % group).astype(jnp.int32)

    late = 1
    levels = [rows_n >> i for i in range(1, rows_n.bit_length())]
    col_runs = [[(0, group)]]
    for d in levels:
        if len(col_runs) == 1:
            col_runs += [[(d * group, group)]]
            continue
        cut = group - late
        passed = [((p // group ^ d) * group + p % group, n) for run in col_runs[1:] for p, n in run]
        col_runs += [[(d * group, cut)], [(d * group + cut, late), *passed]]
    row_runs = [[((2 * d + core) * group, group)] for core in range(2) for d in range(chips_n)]
    runs = (col_runs, row_runs)
    order = [*range(1, rows_n)]

    def gather(rounded, first=()):
        held = [rounded]
        for d in levels:
            if len(held) == 1:
                held += [trade(rounded, "row", d)]
                continue
            near = trade(rounded[: group - late], "row", d)
            near, *passed = lax.optimization_barrier((near, *held[1:], *first))
            held[1:] = passed[: len(held) - 1]
            held += [near, trade(jnp.concatenate([rounded[group - late :], *held[1:]]), "row", d)]
        chips = [rounded, *exchange([rounded] * (chips_n - 1), "col", 2)]
        return held, chips + [trade(chip, "col", 1) for chip in chips]

    def apply(rounded, degree=()):
        kept, swap, col_own, col_send = products(
            tiles, table, *gather(rounded), runs, order, degree
        )
        col_got = [trade(part, "row", d) for d, part in zip(order, col_send)]
        row_own, *row_send = merge(kept, trade(swap, "col", 1), degree)
        if degree:
            own_degree, *row_send = row_send
        row_got = exchange(row_send, "col", 2)
        sums = [row_own, col_own, *row_got, *col_got]
        return [own_degree, degree[1], *sums] if degree else sums

    rounded = call(round_kernel, rounded_shape, [], 16, [start])
    degree = call(
        degree_kernel,
        [jax.ShapeDtypeStruct((n * group, width), F32) for n in (cols_n, rows_n)],
        [],
        16,
        [table, tiles],
        4 * tiles.size * DEGREE_ROWS,
        1,
    )
    first, rounded, degree = call(
        functools.partial(first_kernel, chips_n),
        [vector_shape, rounded_shape, degree_shape],
        [],
        24,
        [start, *apply(rounded, tuple(degree))],
    )
    filtered, rounded, gram = call(
        functools.partial(filter_kernel, chips_n),
        [vector_shape, rounded_shape, jax.ShapeDtypeStruct((vectors_n, 2 * vectors_n), F32)],
        [pltpu.VMEM((2 * vectors_n, own_nodes), F32)],
        24,
        [start, first, degree, *apply(rounded)],
    )
    col_parts, row_parts = gather(rounded)
    sums = call(
        functools.partial(form_kernel, runs),
        jax.ShapeDtypeStruct((vectors_n // 2 + 8, 2 * vectors_n), F32),
        [
            pltpu.VMEM((rows_n * group, vectors_n, width), BF16),
            pltpu.VMEM((cols_n * group, vectors_n, width), BF16),
            pltpu.VMEM(spread, BF16),
            pltpu.VMEM(spread, BF16),
        ],
        24,
        [table, tiles, gram, *col_parts, *row_parts],
        4 * tiles.size * vectors_n,
        1,
    )
    sums = sums + trade(sums, "col", 1)
    sums = tree_sum([sums, *exchange([sums] * (chips_n - 1), "col", 2)])
    return call(
        functools.partial(last_kernel, total_nodes),
        [vector_shape, jax.ShapeDtypeStruct((vectors_n, vectors_n), F32)],
        [],
        24,
        [filtered, sums, *exchange([sums] * (rows_n - 1), "row")],
    )


def solution(mesh):
    placed = (
        P("row", "col", None, None, None),
        P("row", "col", None),
        P("row", "col", None),
        P(None, ("row", "col")),
    )
    return jax.shard_map(
        local, mesh=mesh, in_specs=placed, out_specs=(P(None, ("row", "col")), P()), check_vma=False
    )
```

```python
import functools

import jax
import jax.numpy as jnp
from jax import lax
from jax.experimental import pallas as pl
from jax.experimental.pallas import tpu as pltpu
from jax.sharding import PartitionSpec as P

CENTER = 1.0
HALF_WIDTH = 0.5
HIGHEST = lax.Precision.HIGHEST
NT = (((1,), (1,)), ((), ()))
NN = (((1,), (0,)), ((), ()))
BF16 = jnp.bfloat16
F32 = jnp.float32
VMEM = pl.BlockSpec(memory_space=pltpu.VMEM)
SMEM = pl.BlockSpec(memory_space=pltpu.SMEM)
ANY = pl.BlockSpec(memory_space=pl.ANY)
DEGREE_ROWS = 16


def call(kernel, out_shape, scratch, limit, args, flops=0, smem=0, after=()):
    moved = sum(x.size * x.dtype.itemsize for x in args)
    return pl.pallas_call(
        lambda *refs: kernel(*refs[len(after) :]),
        out_shape=out_shape,
        in_specs=[ANY] * len(after) + [SMEM] * smem + [VMEM] * (len(args) - smem),
        out_specs=jax.tree.map(lambda _: VMEM, out_shape),
        scratch_shapes=scratch,
        compiler_params=pltpu.CompilerParams(vmem_limit_bytes=limit * 2**20),
        cost_estimate=pl.CostEstimate(flops=flops, bytes_accessed=moved, transcendentals=0),
    )(*after, *args)


def trade(part, axis, d):
    n = lax.axis_size(axis)
    return lax.ppermute(part, axis, [(i, i ^ d) for i in range(n)])


def exchange(parts, axis, step=1):
    far_first = [trade(part, axis, step * d) for d, part in reversed(list(enumerate(parts, 1)))]
    return far_first[::-1]


def tiles_first(ref, width):
    return [ref[:, k * width : (k + 1) * width] for k in range(ref.shape[1] // width)]


def round_kernel(meta, rows_ref, cols_ref, vec_ref, out_ref, table_ref):
    group, _, width = out_ref.shape
    for k, piece in enumerate(tiles_first(vec_ref, width)):
        out_ref[k] = piece.astype(BF16)
    rows, cols = rows_ref[...], cols_ref[...]
    col_apart = lax.div(cols, group) ^ meta[0]
    row_apart = lax.div(rows, group) ^ meta[1]
    row_halves = lax.rem(row_apart, 2) * meta[2] + lax.div(row_apart, 2)
    inside = lax.rem(rows, group)
    table_ref[0:1, :] = col_apart * group + lax.rem(cols, group)
    table_ref[1:2, :] = row_apart * group + inside
    table_ref[2:3, :] = row_halves * group + inside


def split_degree(sums):
    high = sums.astype(BF16).astype(F32)
    return jnp.concatenate([high, sums - high], 0).astype(BF16)


def join_degree(payload, group):
    parts = payload[payload.shape[0] - 2 * group :, :].astype(F32)
    return parts[:group] + parts[group:]


def fill(panel, parts, runs):
    for part, places in zip(parts, runs):
        at = 0
        for place, count in places:
            panel[place : place + count] = part[at : at + count]
            at += count


def degree_kernel(table, tiles_ref, row_ref, col_ref):
    row_ref[...] = jnp.zeros_like(row_ref)
    col_ref[...] = jnp.zeros_like(col_ref)
    ones = jnp.ones((DEGREE_ROWS, tiles_ref.shape[2]), BF16)
    for t in range(tiles_ref.shape[0]):
        for ref, place, dims in ((row_ref, table[2, t], NT), (col_ref, table[0, t], NN)):
            sums = lax.dot_general(ones, tiles_ref[t], dims, preferred_element_type=F32)
            ref[pl.ds(place, 1), :] += sums[:1]


def column_kernel(runs, degree, table, tiles_ref, *refs):
    parts, refs = refs[: len(runs)], refs[len(runs) :]
    if degree:
        sums, *refs = refs
    own_ref, *send_refs, panel, total = refs
    group, vectors_n, _ = own_ref.shape
    fill(panel, parts, runs)
    total[...] = jnp.zeros_like(total)
    for t in range(tiles_ref.shape[0]):
        total[table[0, t]] += lax.dot_general(
            panel[table[1, t]], tiles_ref[t], NN, preferred_element_type=F32
        )
    own_ref[...] = total[:group]
    for d, send in enumerate(send_refs, 1):
        round_sums(send, total, d * group, group)
        if degree:
            send[group * vectors_n :, :] = split_degree(sums[d * group : (d + 1) * group, :])


def row_kernel(runs, degree, table, tiles_ref, *refs):
    parts, refs = refs[: len(runs)], refs[len(runs) :]
    if degree:
        sums, *refs = refs
    kept_ref, swap_ref, panel, total = refs
    half, group, vectors_n, _ = kept_ref.shape
    fill(panel, parts, runs)
    total[...] = jnp.zeros_like(total)
    for t in range(tiles_ref.shape[0]):
        total[table[2, t]] += lax.dot_general(
            panel[table[0, t]], tiles_ref[t], NT, preferred_element_type=F32
        )
    for d in range(half):
        kept_ref[d] = total[d * group : (d + 1) * group]
        round_sums(swap_ref.at[d], total, (half + d) * group, group)
        if degree:
            rows = slice((half + d) * group, (half + d + 1) * group)
            swap_ref[d, group * vectors_n :, :] = split_degree(sums[rows, :])


def round_sums(send, total, start, group):
    vectors_n = total.shape[1]
    for k in range(group):
        send[k * vectors_n : (k + 1) * vectors_n, :] = total[start + k].astype(BF16)


def products(tiles, table, col_parts, row_parts, runs, degree):
    group, vectors_n, width = col_parts[0].shape
    half = len(row_parts) // 2
    rows_n = max(place + count for run in runs[0] for place, count in run) // group
    rows = group * vectors_n + (2 * group if degree else 0)
    own_shape = jax.ShapeDtypeStruct((group, vectors_n, width), F32)
    send_shape = jax.ShapeDtypeStruct((rows, width), BF16)
    flops = 2 * tiles.size * vectors_n

    def panels(source, target):
        return [
            pltpu.VMEM((source * group, vectors_n, width), BF16),
            pltpu.VMEM((target * group, vectors_n, width), F32),
        ]

    col_own, *col_send = call(
        functools.partial(column_kernel, runs[1], bool(degree)),
        [own_shape] + [send_shape] * (rows_n - 1),
        panels(2 * half, rows_n),
        24,
        [table, tiles, *row_parts, *degree[1:]],
        flops,
        1,
    )
    kept, swap = call(
        functools.partial(row_kernel, runs[0], bool(degree)),
        [
            jax.ShapeDtypeStruct((half, group, vectors_n, width), F32),
            jax.ShapeDtypeStruct((half, rows, width), BF16),
        ],
        panels(rows_n, 2 * half),
        24,
        [table, tiles, *col_parts, *degree[:1]],
        flops,
        1,
        [col_own],
    )
    return kept, swap, col_own, col_send


def merge_kernel(degree, kept, got, *refs):
    if degree:
        row_degree, own_ref, own_degree, *send_refs = refs
    else:
        own_ref, *send_refs = refs
    _, group, vectors_n, _ = kept.shape
    for k in range(group):
        rows = slice(k * vectors_n, (k + 1) * vectors_n)
        own_ref[k] = kept[0, k] + got[0, rows, :].astype(F32)
        for d, send in enumerate(send_refs, 1):
            send[rows, :] = (kept[d, k] + got[d, rows, :].astype(F32)).astype(BF16)
    if degree:
        for d in range(kept.shape[0]):
            sums = row_degree[d * group : (d + 1) * group, :] + join_degree(got.at[d], group)
            if d:
                send_refs[d - 1][group * vectors_n :, :] = split_degree(sums)
            else:
                own_degree[...] = sums


def merge(kept, got, degree):
    _, group, _, width = kept.shape
    out_shape = [jax.ShapeDtypeStruct(kept.shape[1:], F32)]
    if degree:
        out_shape += [jax.ShapeDtypeStruct((group, width), F32)]
    out_shape += [jax.ShapeDtypeStruct(got.shape[1:], BF16)] * (kept.shape[0] - 1)
    kernel = functools.partial(merge_kernel, bool(degree))
    return call(kernel, out_shape, [], 24, [kept, got, *degree[:1]])


def gathered_sum(own, received, k):
    total = own[k]
    rows = slice(k * total.shape[0], (k + 1) * total.shape[0])
    for part in received:
        total = total + part[rows, :].astype(F32)
    return total


def symmetric_part(row_own, row_refs, col_own, col_refs, k):
    return 0.5 * (gathered_sum(row_own, row_refs, k) + gathered_sum(col_own, col_refs, k))


def first_kernel(chips_n, vec_ref, row_degree, col_degree, row_own, col_own, *refs):
    row_refs, refs = refs[: chips_n - 1], refs[chips_n - 1 :]
    col_refs, (first_ref, rounded_ref, degree_ref) = refs[:-3], refs[-3:]
    group, _, width = rounded_ref.shape
    degree = row_degree[...] + col_degree[:group, :]
    for part in (*row_refs, *col_refs):
        degree += join_degree(part, group)
    degree = 0.5 * degree
    degree_ref[...] = degree
    for k, vec in enumerate(tiles_first(vec_ref, width)):
        symmetric = symmetric_part(row_own, row_refs, col_own, col_refs, k)
        image = degree[k : k + 1, :] * vec - symmetric
        first = (image - CENTER * vec) / HALF_WIDTH
        first_ref[:, k * width : (k + 1) * width] = first
        rounded_ref[k] = first.astype(BF16)


def filter_kernel(chips_n, start_ref, first_ref, degree_ref, row_own, col_own, *refs):
    row_refs, refs = refs[: chips_n - 1], refs[chips_n - 1 :]
    col_refs, (filtered_ref, rounded_ref, gram_ref, both) = refs[:-4], refs[-4:]
    group, vectors_n, width = rounded_ref.shape
    for k, vec in enumerate(tiles_first(first_ref, width)):
        symmetric = symmetric_part(row_own, row_refs, col_own, col_refs, k)
        columns = slice(k * width, (k + 1) * width)
        image = degree_ref[k : k + 1, :] * vec - symmetric
        filtered = 2.0 * (image - CENTER * vec) / HALF_WIDTH - start_ref[:, columns]
        filtered_ref[:, columns] = filtered
        rounded_ref[k] = filtered.astype(BF16)
        both[:vectors_n, columns] = filtered
        both[vectors_n:, columns] = degree_ref[k : k + 1, :] * filtered
    gram_ref[...] = lax.dot_general(
        filtered_ref[...], both[...], NT, precision=HIGHEST, preferred_element_type=F32
    )


def half_form_kernel(runs, table, tiles_ref, *refs):
    parts, (out_ref, panel) = refs[:-2], refs[-2:]
    width = panel.shape[2]
    fill(panel, parts, runs)
    for t in range(tiles_ref.shape[0]):
        out_ref[:, t * width : (t + 1) * width] = lax.dot_general(
            panel[table[1, t]], tiles_ref[t], NN, preferred_element_type=F32
        ).astype(BF16)


def form_kernel(runs, table, left, gram_ref, *refs):
    parts, (out_ref, panel, right) = refs[:-3], refs[-3:]
    _, vectors_n, width = panel.shape
    fill(panel, parts, runs)
    for t in range(right.shape[1] // width):
        right[:, t * width : (t + 1) * width] = panel[table[0, t]]
    form = lax.dot_general(left[...], right[...], NT, preferred_element_type=F32)
    projected = gram_ref[:, vectors_n:] - 0.5 * (form + form.T)
    row, col = square_index(vectors_n)
    packed = jnp.where(col >= row, gram_ref[:, :vectors_n], projected)
    diagonal = jnp.sum(jnp.where(row == col, projected, 0.0), 0, keepdims=True)
    half = vectors_n // 2
    out_ref[:half] = jnp.concatenate([packed[:half], packed[half:]], 1)
    diagonal = jnp.broadcast_to(diagonal, (8, vectors_n))
    out_ref[half:] = jnp.concatenate([diagonal, jnp.zeros_like(diagonal)], 1)


def square_index(n):
    return tuple(lax.broadcasted_iota(jnp.int32, (n, n), axis) for axis in (0, 1))


def inverse_factor(gram):
    n = gram.shape[0]
    row, col = square_index(n)
    table = jnp.concatenate([gram, jnp.where(row == col, 1.0, 0.0)], 1)
    bands = [table[i : i + 8] for i in range(0, n, 8)]
    below = lax.broadcasted_iota(jnp.int32, (8, 2 * n), 0)
    for j in range(n):
        at, line = j // 8, j % 8
        lanes = {i: jnp.broadcast_to(bands[i][:, j : j + 1], below.shape) for i in range(at, n // 8)}
        pivot_row = bands[at][line : line + 1, :] * (1.0 / lanes[at][line : line + 1, :])
        pivot_row = jnp.broadcast_to(pivot_row, below.shape)
        for i in range(at, n // 8):
            update = lanes[i] * pivot_row
            if i == at:
                update = jnp.where(below > line, update, 0.0)
            bands[i] = bands[i] - update
    table = jnp.concatenate(bands, 0)
    pivots = jnp.sum(jnp.where(row == col, table[:, :n], 0.0), 1, keepdims=True)
    return table[:, n:] / jnp.sqrt(pivots)


def last_kernel(total_nodes, filtered_ref, *refs):
    parts, (ritz_ref, rayleigh_ref) = refs[:-2], refs[-2:]
    n = filtered_ref.shape[0]
    half = n // 2
    sums = tree_sum([part[...] for part in parts]) * (1.0 / total_nodes)
    packed = jnp.concatenate([sums[:half, :n], sums[:half, n:]], 0)
    row, col = square_index(n)
    upper = jnp.where(col > row, packed, 0.0)
    gram = jnp.where(col >= row, packed, 0.0) + upper.T
    lower = jnp.where(col < row, packed, 0.0)
    diagonal = jnp.broadcast_to(sums[half : half + 1, :n], (n, n))
    projected = lower + lower.T + jnp.where(row == col, diagonal, 0.0)
    inverse = inverse_factor(gram)

    def dot(a, b, dims):
        return lax.dot_general(a, b, dims, precision=HIGHEST, preferred_element_type=F32)

    half_way = dot(inverse, projected, NN)
    rayleigh_ref[...] = dot(half_way, inverse, NT)
    turned = dot(inverse, half_way, NT)
    ritz_ref[...] = dot(turned, dot(inverse, filtered_ref[...], NN), NN)


def tree_sum(parts):
    while len(parts) > 1:
        parts = [a + b for a, b in zip(parts[::2], parts[1::2])]
    return parts[0]


def local(tiles, tile_rows, tile_cols, start):
    tiles, tile_rows, tile_cols = tiles[0, 0], tile_rows[0, 0], tile_cols[0, 0]
    width = tiles.shape[-1]
    vectors_n, own_nodes = start.shape
    rows_n, cols_n = lax.axis_size("row"), lax.axis_size("col")
    chips_n = cols_n // 2
    total_nodes = own_nodes * rows_n * cols_n
    group = own_nodes // width
    spread = (vectors_n, tiles.shape[0] * width)

    rounded_shape = jax.ShapeDtypeStruct((group, vectors_n, width), BF16)
    vector_shape = jax.ShapeDtypeStruct((vectors_n, own_nodes), F32)
    degree_shape = jax.ShapeDtypeStruct((group, width), F32)

    late = 1
    levels = [rows_n >> i for i in range(1, rows_n.bit_length())]
    col_runs = [[(0, group)]]
    for d in levels:
        if len(col_runs) == 1:
            col_runs += [[(d * group, group)]]
            continue
        cut = group - late
        passed = [((p // group ^ d) * group + p % group, n) for run in col_runs[1:] for p, n in run]
        col_runs += [[(d * group, cut)], [(d * group + cut, late), *passed]]
    row_runs = [[((2 * d + core) * group, group)] for core in range(2) for d in range(chips_n)]
    runs = (col_runs, row_runs)
    def gather(rounded, first=()):
        held = [rounded]
        for d in levels:
            if len(held) == 1:
                held += [trade(rounded, "row", d)]
                continue
            near = trade(rounded[: group - late], "row", d)
            near, *passed = lax.optimization_barrier((near, *held[1:], *first))
            held[1:] = passed[: len(held) - 1]
            held += [near, trade(jnp.concatenate([rounded[group - late :], *held[1:]]), "row", d)]
        chips = [rounded, *exchange([rounded] * (chips_n - 1), "col", 2)]
        return held, chips + [trade(chip, "col", 1) for chip in chips]

    def apply(rounded, degree=()):
        kept, swap, col_own, col_send = products(tiles, table, *gather(rounded), runs, degree)
        col_got = exchange(col_send, "row")
        row_own, *row_send = merge(kept, trade(swap, "col", 1), degree)
        if degree:
            own_degree, *row_send = row_send
        row_got = exchange(row_send, "col", 2)
        sums = [row_own, col_own, *row_got, *col_got]
        return [own_degree, degree[1], *sums] if degree else sums

    meta = jnp.stack([lax.axis_index("row"), lax.axis_index("col"), chips_n]).astype(jnp.int32)
    rounded, table = call(
        round_kernel,
        [rounded_shape, jax.ShapeDtypeStruct((3, tiles.shape[0]), jnp.int32)],
        [],
        16,
        [meta, tile_rows[None], tile_cols[None], start],
        smem=1,
    )
    degree = call(
        degree_kernel,
        [jax.ShapeDtypeStruct((n * group, width), F32) for n in (cols_n, rows_n)],
        [],
        16,
        [table, tiles],
        4 * tiles.size * DEGREE_ROWS,
        1,
    )
    first, rounded, degree = call(
        functools.partial(first_kernel, chips_n),
        [vector_shape, rounded_shape, degree_shape],
        [],
        24,
        [start, *apply(rounded, tuple(degree))],
    )
    filtered, rounded, gram = call(
        functools.partial(filter_kernel, chips_n),
        [vector_shape, rounded_shape, jax.ShapeDtypeStruct((vectors_n, 2 * vectors_n), F32)],
        [pltpu.VMEM((2 * vectors_n, own_nodes), F32)],
        24,
        [start, first, degree, *apply(rounded)],
    )
    col_parts, row_parts = gather(rounded)
    left = call(
        functools.partial(half_form_kernel, runs[1]),
        jax.ShapeDtypeStruct(spread, BF16),
        [pltpu.VMEM((cols_n * group, vectors_n, width), BF16)],
        24,
        [table, tiles, *row_parts],
        2 * tiles.size * vectors_n,
        1,
    )
    sums = call(
        functools.partial(form_kernel, runs[0]),
        jax.ShapeDtypeStruct((vectors_n // 2 + 8, 2 * vectors_n), F32),
        [pltpu.VMEM((rows_n * group, vectors_n, width), BF16), pltpu.VMEM(spread, BF16)],
        24,
        [table, left, gram, *col_parts],
        2 * vectors_n * spread[0] * spread[1],
        1,
    )
    sums = sums + trade(sums, "col", 1)
    sums = tree_sum([sums, *exchange([sums] * (chips_n - 1), "col", 2)])
    return call(
        functools.partial(last_kernel, total_nodes),
        [vector_shape, jax.ShapeDtypeStruct((vectors_n, vectors_n), F32)],
        [],
        24,
        [filtered, sums, *exchange([sums] * (rows_n - 1), "row")],
    )


def solution(mesh):
    placed = (
        P("row", "col", None, None, None),
        P("row", "col", None),
        P("row", "col", None),
        P(None, ("row", "col")),
    )
    return jax.shard_map(
        local, mesh=mesh, in_specs=placed, out_specs=(P(None, ("row", "col")), P()), check_vma=False
    )
```

```python
import functools

import jax
import jax.numpy as jnp
from jax import lax
from jax.experimental import pallas as pl
from jax.experimental.pallas import tpu as pltpu
from jax.sharding import PartitionSpec as P

CENTER = 1.0
HALF_WIDTH = 0.5
HIGHEST = lax.Precision.HIGHEST
NT = (((1,), (1,)), ((), ()))
NN = (((1,), (0,)), ((), ()))
BF16 = jnp.bfloat16
F32 = jnp.float32
VMEM = pl.BlockSpec(memory_space=pltpu.VMEM)
SMEM = pl.BlockSpec(memory_space=pltpu.SMEM)
ANY = pl.BlockSpec(memory_space=pl.ANY)
DEGREE_ROWS = 16


def call(kernel, out_shape, scratch, limit, args, flops=0, smem=0, after=()):
    moved = sum(x.size * x.dtype.itemsize for x in args)
    return pl.pallas_call(
        lambda *refs: kernel(*refs[len(after) :]),
        out_shape=out_shape,
        in_specs=[ANY] * len(after) + [SMEM] * smem + [VMEM] * (len(args) - smem),
        out_specs=jax.tree.map(lambda _: VMEM, out_shape),
        scratch_shapes=scratch,
        compiler_params=pltpu.CompilerParams(vmem_limit_bytes=limit * 2**20),
        cost_estimate=pl.CostEstimate(flops=flops, bytes_accessed=moved, transcendentals=0),
    )(*after, *args)


def trade(part, axis, d):
    n = lax.axis_size(axis)
    return lax.ppermute(part, axis, [(i, i ^ d) for i in range(n)])


def exchange(parts, axis, step=1):
    far_first = [trade(part, axis, step * d) for d, part in reversed(list(enumerate(parts, 1)))]
    return far_first[::-1]


def tiles_first(ref, width):
    return [ref[:, k * width : (k + 1) * width] for k in range(ref.shape[1] // width)]


def round_kernel(meta, rows_ref, cols_ref, vec_ref, out_ref, table_ref):
    group, _, width = out_ref.shape
    for k, piece in enumerate(tiles_first(vec_ref, width)):
        out_ref[k] = piece.astype(BF16)
    rows, cols = rows_ref[...], cols_ref[...]
    col_apart = lax.div(cols, group) ^ meta[0]
    row_apart = lax.div(rows, group) ^ meta[1]
    row_halves = lax.rem(row_apart, 2) * meta[2] + lax.div(row_apart, 2)
    inside = lax.rem(rows, group)
    table_ref[0:1, :] = col_apart * group + lax.rem(cols, group)
    table_ref[1:2, :] = row_apart * group + inside
    table_ref[2:3, :] = row_halves * group + inside


def split_degree(sums):
    high = sums.astype(BF16).astype(F32)
    return jnp.concatenate([high, sums - high], 0).astype(BF16)


def join_degree(payload, group):
    parts = payload[payload.shape[0] - 2 * group :, :].astype(F32)
    return parts[:group] + parts[group:]


def fill(panel, parts, runs):
    for part, places in zip(parts, runs):
        at = 0
        for place, count in places:
            panel[place : place + count] = part[at : at + count]
            at += count


def degree_kernel(table, tiles_ref, row_ref, col_ref):
    row_ref[...] = jnp.zeros_like(row_ref)
    col_ref[...] = jnp.zeros_like(col_ref)
    ones = jnp.ones((DEGREE_ROWS, tiles_ref.shape[2]), BF16)
    for t in range(tiles_ref.shape[0]):
        for ref, place, dims in ((row_ref, table[2, t], NT), (col_ref, table[0, t], NN)):
            sums = lax.dot_general(ones, tiles_ref[t], dims, preferred_element_type=F32)
            ref[pl.ds(place, 1), :] += sums[:1]


def column_kernel(runs, degree, table, tiles_ref, *refs):
    parts, refs = refs[: len(runs)], refs[len(runs) :]
    if degree:
        sums, *refs = refs
    own_ref, *send_refs, panel, total = refs
    group, vectors_n, _ = own_ref.shape
    fill(panel, parts, runs)
    total[...] = jnp.zeros_like(total)
    for t in range(tiles_ref.shape[0]):
        total[table[0, t]] += lax.dot_general(
            panel[table[1, t]], tiles_ref[t], NN, preferred_element_type=F32
        )
    own_ref[...] = total[:group]
    for d, send in enumerate(send_refs, 1):
        round_sums(send, total, d * group, group)
        if degree:
            send[group * vectors_n :, :] = split_degree(sums[d * group : (d + 1) * group, :])


def row_kernel(runs, degree, table, tiles_ref, *refs):
    parts, refs = refs[: len(runs)], refs[len(runs) :]
    if degree:
        sums, *refs = refs
    kept_ref, swap_ref, panel, total = refs
    half, group, vectors_n, _ = kept_ref.shape
    fill(panel, parts, runs)
    total[...] = jnp.zeros_like(total)
    for t in range(tiles_ref.shape[0]):
        total[table[2, t]] += lax.dot_general(
            panel[table[0, t]], tiles_ref[t], NT, preferred_element_type=F32
        )
    for d in range(half):
        kept_ref[d] = total[d * group : (d + 1) * group]
        round_sums(swap_ref.at[d], total, (half + d) * group, group)
        if degree:
            rows = slice((half + d) * group, (half + d + 1) * group)
            swap_ref[d, group * vectors_n :, :] = split_degree(sums[rows, :])


def round_sums(send, total, start, group):
    vectors_n = total.shape[1]
    for k in range(group):
        send[k * vectors_n : (k + 1) * vectors_n, :] = total[start + k].astype(BF16)


def products(tiles, table, col_parts, row_parts, runs, degree):
    group, vectors_n, width = col_parts[0].shape
    half = len(row_parts) // 2
    rows_n = max(place + count for run in runs[0] for place, count in run) // group
    rows = group * vectors_n + (2 * group if degree else 0)
    own_shape = jax.ShapeDtypeStruct((group, vectors_n, width), F32)
    send_shape = jax.ShapeDtypeStruct((rows, width), BF16)
    flops = 2 * tiles.size * vectors_n

    def panels(source, target):
        return [
            pltpu.VMEM((source * group, vectors_n, width), BF16),
            pltpu.VMEM((target * group, vectors_n, width), F32),
        ]

    col_own, *col_send = call(
        functools.partial(column_kernel, runs[1], bool(degree)),
        [own_shape] + [send_shape] * (rows_n - 1),
        panels(2 * half, rows_n),
        24,
        [table, tiles, *row_parts, *degree[1:]],
        flops,
        1,
    )
    kept, swap = call(
        functools.partial(row_kernel, runs[0], bool(degree)),
        [
            jax.ShapeDtypeStruct((half, group, vectors_n, width), F32),
            jax.ShapeDtypeStruct((half, rows, width), BF16),
        ],
        panels(rows_n, 2 * half),
        24,
        [table, tiles, *col_parts, *degree[:1]],
        flops,
        1,
        [col_own],
    )
    return kept, swap, col_own, col_send


def merge_kernel(degree, kept, got, *refs):
    if degree:
        row_degree, own_ref, own_degree, *send_refs = refs
    else:
        own_ref, *send_refs = refs
    _, group, vectors_n, _ = kept.shape
    for k in range(group):
        rows = slice(k * vectors_n, (k + 1) * vectors_n)
        own_ref[k] = kept[0, k] + got[0, rows, :].astype(F32)
        for d, send in enumerate(send_refs, 1):
            send[rows, :] = (kept[d, k] + got[d, rows, :].astype(F32)).astype(BF16)
    if degree:
        for d in range(kept.shape[0]):
            sums = row_degree[d * group : (d + 1) * group, :] + join_degree(got.at[d], group)
            if d:
                send_refs[d - 1][group * vectors_n :, :] = split_degree(sums)
            else:
                own_degree[...] = sums


def merge(kept, got, degree):
    _, group, _, width = kept.shape
    out_shape = [jax.ShapeDtypeStruct(kept.shape[1:], F32)]
    if degree:
        out_shape += [jax.ShapeDtypeStruct((group, width), F32)]
    out_shape += [jax.ShapeDtypeStruct(got.shape[1:], BF16)] * (kept.shape[0] - 1)
    kernel = functools.partial(merge_kernel, bool(degree))
    return call(kernel, out_shape, [], 24, [kept, got, *degree[:1]])


def gathered_sum(own, received, k):
    total = own[k]
    rows = slice(k * total.shape[0], (k + 1) * total.shape[0])
    for part in received:
        total = total + part[rows, :].astype(F32)
    return total


def symmetric_part(row_own, row_refs, col_own, col_refs, k):
    return 0.5 * (gathered_sum(row_own, row_refs, k) + gathered_sum(col_own, col_refs, k))


def first_kernel(chips_n, vec_ref, row_degree, col_degree, row_own, col_own, *refs):
    row_refs, refs = refs[: chips_n - 1], refs[chips_n - 1 :]
    col_refs, (first_ref, rounded_ref, degree_ref) = refs[:-3], refs[-3:]
    group, _, width = rounded_ref.shape
    degree = row_degree[...] + col_degree[:group, :]
    for part in (*row_refs, *col_refs):
        degree += join_degree(part, group)
    degree = 0.5 * degree
    degree_ref[...] = degree
    for k, vec in enumerate(tiles_first(vec_ref, width)):
        symmetric = symmetric_part(row_own, row_refs, col_own, col_refs, k)
        image = degree[k : k + 1, :] * vec - symmetric
        first = (image - CENTER * vec) / HALF_WIDTH
        first_ref[:, k * width : (k + 1) * width] = first
        rounded_ref[k] = first.astype(BF16)


def filter_kernel(chips_n, start_ref, first_ref, degree_ref, row_own, col_own, *refs):
    row_refs, refs = refs[: chips_n - 1], refs[chips_n - 1 :]
    col_refs, (filtered_ref, rounded_ref, gram_ref, both) = refs[:-4], refs[-4:]
    group, vectors_n, width = rounded_ref.shape
    for k, vec in enumerate(tiles_first(first_ref, width)):
        symmetric = symmetric_part(row_own, row_refs, col_own, col_refs, k)
        columns = slice(k * width, (k + 1) * width)
        image = degree_ref[k : k + 1, :] * vec - symmetric
        filtered = 2.0 * (image - CENTER * vec) / HALF_WIDTH - start_ref[:, columns]
        filtered_ref[:, columns] = filtered
        rounded_ref[k] = filtered.astype(BF16)
        both[:vectors_n, columns] = filtered
        both[vectors_n:, columns] = degree_ref[k : k + 1, :] * filtered
    gram_ref[...] = lax.dot_general(
        filtered_ref[...], both[...], NT, precision=HIGHEST, preferred_element_type=F32
    )


def half_form_kernel(runs, table, tiles_ref, *refs):
    parts, (out_ref, panel) = refs[:-2], refs[-2:]
    width = panel.shape[2]
    fill(panel, parts, runs)
    for t in range(tiles_ref.shape[0]):
        out_ref[:, t * width : (t + 1) * width] = lax.dot_general(
            panel[table[1, t]], tiles_ref[t], NN, preferred_element_type=F32
        ).astype(BF16)


def form_kernel(runs, table, left, gram_ref, *refs):
    parts, (out_ref, panel, right) = refs[:-3], refs[-3:]
    _, vectors_n, width = panel.shape
    fill(panel, parts, runs)
    for t in range(right.shape[1] // width):
        right[:, t * width : (t + 1) * width] = panel[table[0, t]]
    form = lax.dot_general(left[...], right[...], NT, preferred_element_type=F32)
    projected = gram_ref[:, vectors_n:] - 0.5 * (form + form.T)
    row, col = square_index(vectors_n)
    packed = jnp.where(col >= row, gram_ref[:, :vectors_n], projected)
    diagonal = jnp.sum(jnp.where(row == col, projected, 0.0), 0, keepdims=True)
    half = vectors_n // 2
    diagonal = jnp.broadcast_to(diagonal, (8, vectors_n))
    for d in range(out_ref.shape[0]):
        out_ref[d, :half] = jnp.concatenate([packed[:half], packed[half:]], 1)
        out_ref[d, half:] = jnp.concatenate([diagonal, jnp.zeros_like(diagonal)], 1)


def square_index(n):
    return tuple(lax.broadcasted_iota(jnp.int32, (n, n), axis) for axis in (0, 1))


def inverse_factor(gram):
    n = gram.shape[0]
    row, col = square_index(n)
    table = jnp.concatenate([gram, jnp.where(row == col, 1.0, 0.0)], 1)
    bands = [table[i : i + 8] for i in range(0, n, 8)]
    shape = (8, 2 * n)
    line = lax.broadcasted_iota(jnp.int32, shape, 0)

    def spread(values, j):
        return jnp.broadcast_to(values[:, j : j + 1], shape)

    def pick(values, i):
        return jnp.broadcast_to(values[i : i + 1, :], shape)

    for at in range(n // 8):
        block = [spread(bands[at], 8 * at + c) for c in range(8)]
        forward, solved = bands[at], bands[at]
        solved_block = list(block)
        for s in range(8):
            scale = 1.0 / pick(block[s], s)
            below = jnp.where(line > s, block[s], 0.0) * scale
            above = jnp.where(line < s, solved_block[s] * scale, 0.0)
            both = below + above
            pivot_row = pick(forward, s)
            forward = forward - below * pivot_row
            solved = solved - both * pivot_row
            for c in range(s + 1, 8):
                pivot = pick(block[c], s)
                block[c] = block[c] - below * pivot
                solved_block[c] = solved_block[c] - both * pivot
        pivots = block[0]
        for s in range(1, 8):
            pivots = jnp.where(line == s, block[s], pivots)
        solved = solved / pivots
        bands[at] = forward / jnp.sqrt(pivots)
        for i in range(at + 1, n // 8):
            update = spread(bands[i], 8 * at) * pick(solved, 0)
            for c in range(1, 8):
                update = update + spread(bands[i], 8 * at + c) * pick(solved, c)
            bands[i] = bands[i] - update
    return jnp.concatenate(bands, 0)[:, n:]


def last_kernel(total_nodes, filtered_ref, sums_ref, ritz_ref, rayleigh_ref):
    n = filtered_ref.shape[0]
    half = n // 2
    sums = jnp.sum(sums_ref[...], 0) * (1.0 / total_nodes)
    packed = jnp.concatenate([sums[:half, :n], sums[:half, n:]], 0)
    row, col = square_index(n)
    upper = jnp.where(col > row, packed, 0.0)
    gram = jnp.where(col >= row, packed, 0.0) + upper.T
    lower = jnp.where(col < row, packed, 0.0)
    diagonal = jnp.broadcast_to(sums[half : half + 1, :n], (n, n))
    projected = lower + lower.T + jnp.where(row == col, diagonal, 0.0)
    inverse = inverse_factor(gram)

    def dot(a, b, dims):
        return lax.dot_general(a, b, dims, precision=HIGHEST, preferred_element_type=F32)

    half_way = dot(inverse, projected, NN)
    rayleigh_ref[...] = dot(half_way, inverse, NT)
    turned = dot(inverse, half_way, NT)
    ritz_ref[...] = dot(turned, dot(inverse, filtered_ref[...], NN), NN)


def local(tiles, tile_rows, tile_cols, start):
    tiles, tile_rows, tile_cols = tiles[0, 0], tile_rows[0, 0], tile_cols[0, 0]
    width = tiles.shape[-1]
    vectors_n, own_nodes = start.shape
    rows_n, cols_n = lax.axis_size("row"), lax.axis_size("col")
    chips_n = cols_n // 2
    total_nodes = own_nodes * rows_n * cols_n
    group = own_nodes // width
    spread = (vectors_n, tiles.shape[0] * width)

    rounded_shape = jax.ShapeDtypeStruct((group, vectors_n, width), BF16)
    vector_shape = jax.ShapeDtypeStruct((vectors_n, own_nodes), F32)
    degree_shape = jax.ShapeDtypeStruct((group, width), F32)

    late = 1
    levels = [rows_n >> i for i in range(1, rows_n.bit_length())]
    col_runs = [[(0, group)]]
    for d in levels:
        if len(col_runs) == 1:
            col_runs += [[(d * group, group)]]
            continue
        cut = group - late
        passed = [((p // group ^ d) * group + p % group, n) for run in col_runs[1:] for p, n in run]
        col_runs += [[(d * group, cut)], [(d * group + cut, late), *passed]]
    row_runs = [[((2 * d + core) * group, group)] for core in range(2) for d in range(chips_n)]
    runs = (col_runs, row_runs)
    def gather(rounded, first=()):
        held = [rounded]
        for d in levels:
            if len(held) == 1:
                held += [trade(rounded, "row", d)]
                continue
            near = trade(rounded[: group - late], "row", d)
            near, *passed = lax.optimization_barrier((near, *held[1:], *first))
            held[1:] = passed[: len(held) - 1]
            held += [near, trade(jnp.concatenate([rounded[group - late :], *held[1:]]), "row", d)]
        chips = [rounded, *exchange([rounded] * (chips_n - 1), "col", 2)]
        return held, chips + [trade(chip, "col", 1) for chip in chips]

    def apply(rounded, degree=()):
        kept, swap, col_own, col_send = products(tiles, table, *gather(rounded), runs, degree)
        col_got = exchange(col_send, "row")
        row_own, *row_send = merge(kept, trade(swap, "col", 1), degree)
        if degree:
            own_degree, *row_send = row_send
        row_got = exchange(row_send, "col", 2)
        sums = [row_own, col_own, *row_got, *col_got]
        return [own_degree, degree[1], *sums] if degree else sums

    meta = jnp.stack([lax.axis_index("row"), lax.axis_index("col"), chips_n]).astype(jnp.int32)
    rounded, table = call(
        round_kernel,
        [rounded_shape, jax.ShapeDtypeStruct((3, tiles.shape[0]), jnp.int32)],
        [],
        16,
        [meta, tile_rows[None], tile_cols[None], start],
        smem=1,
    )
    degree = call(
        degree_kernel,
        [jax.ShapeDtypeStruct((n * group, width), F32) for n in (cols_n, rows_n)],
        [],
        16,
        [table, tiles],
        4 * tiles.size * DEGREE_ROWS,
        1,
    )
    first, rounded, degree = call(
        functools.partial(first_kernel, chips_n),
        [vector_shape, rounded_shape, degree_shape],
        [],
        24,
        [start, *apply(rounded, tuple(degree))],
    )
    filtered, rounded, gram = call(
        functools.partial(filter_kernel, chips_n),
        [vector_shape, rounded_shape, jax.ShapeDtypeStruct((vectors_n, 2 * vectors_n), F32)],
        [pltpu.VMEM((2 * vectors_n, own_nodes), F32)],
        24,
        [start, first, degree, *apply(rounded)],
    )
    col_parts, row_parts = gather(rounded)
    left = call(
        functools.partial(half_form_kernel, runs[1]),
        jax.ShapeDtypeStruct(spread, BF16),
        [pltpu.VMEM((cols_n * group, vectors_n, width), BF16)],
        24,
        [table, tiles, *row_parts],
        2 * tiles.size * vectors_n,
        1,
    )
    sums = call(
        functools.partial(form_kernel, runs[0]),
        jax.ShapeDtypeStruct((cols_n, vectors_n // 2 + 8, 2 * vectors_n), F32),
        [pltpu.VMEM((rows_n * group, vectors_n, width), BF16), pltpu.VMEM(spread, BF16)],
        24,
        [table, left, gram, *col_parts],
        2 * vectors_n * spread[0] * spread[1],
        1,
    )
    sums = jnp.sum(lax.all_to_all(sums, "col", 0, 0, tiled=True), 0)
    sums = jnp.broadcast_to(sums, (rows_n, *sums.shape))
    sums = lax.all_to_all(sums, "row", 0, 0, tiled=True)
    return call(
        functools.partial(last_kernel, total_nodes),
        [vector_shape, jax.ShapeDtypeStruct((vectors_n, vectors_n), F32)],
        [],
        24,
        [filtered, sums],
    )


def solution(mesh):
    placed = (
        P("row", "col", None, None, None),
        P("row", "col", None),
        P("row", "col", None),
        P(None, ("row", "col")),
    )
    return jax.shard_map(
        local, mesh=mesh, in_specs=placed, out_specs=(P(None, ("row", "col")), P()), check_vma=False
    )
```

```python
import functools

import jax
import jax.numpy as jnp
from jax import lax
from jax.experimental import pallas as pl
from jax.experimental.pallas import tpu as pltpu
from jax.sharding import PartitionSpec as P

CENTER = 1.0
HALF_WIDTH = 0.5
HIGHEST = lax.Precision.HIGHEST
NT = (((1,), (1,)), ((), ()))
NN = (((1,), (0,)), ((), ()))
BF16 = jnp.bfloat16
F32 = jnp.float32
VMEM = pl.BlockSpec(memory_space=pltpu.VMEM)
SMEM = pl.BlockSpec(memory_space=pltpu.SMEM)
ANY = pl.BlockSpec(memory_space=pl.ANY)
DEGREE_ROWS = 16


def call(kernel, out_shape, scratch, limit, args, flops=0, smem=0, after=(), outs=None):
    moved = sum(x.size * x.dtype.itemsize for x in args)
    return pl.pallas_call(
        lambda *refs: kernel(*refs[len(after) :]),
        out_shape=out_shape,
        in_specs=[ANY] * len(after) + [SMEM] * smem + [VMEM] * (len(args) - smem),
        out_specs=outs or jax.tree.map(lambda _: VMEM, out_shape),
        scratch_shapes=scratch,
        compiler_params=pltpu.CompilerParams(vmem_limit_bytes=limit * 2**20),
        cost_estimate=pl.CostEstimate(flops=flops, bytes_accessed=moved, transcendentals=0),
    )(*after, *args)


def trade(part, axis, d):
    n = lax.axis_size(axis)
    return lax.ppermute(part, axis, [(i, i ^ d) for i in range(n)])


def exchange(parts, axis, step=1):
    far_first = [trade(part, axis, step * d) for d, part in reversed(list(enumerate(parts, 1)))]
    return far_first[::-1]


def tiles_first(ref, width):
    return [ref[:, k * width : (k + 1) * width] for k in range(ref.shape[1] // width)]


def round_kernel(vec_ref, out_ref):
    for k, piece in enumerate(tiles_first(vec_ref, out_ref.shape[2])):
        out_ref[k] = piece.astype(BF16)


def split_degree(sums):
    high = sums.astype(BF16).astype(F32)
    return jnp.concatenate([high, sums - high], 0).astype(BF16)


def join_degree(payload, group):
    parts = payload[payload.shape[0] - 2 * group :, :].astype(F32)
    return parts[:group] + parts[group:]


def fill(panel, parts, runs):
    for part, places in zip(parts, runs):
        at = 0
        for place, count in places:
            panel[place : place + count] = part[at : at + count]
            at += count


def degree_kernel(group, meta, tile_rows, tile_cols, tiles_ref, row_ref, col_ref, table):
    row_ref[...] = jnp.zeros_like(row_ref)
    col_ref[...] = jnp.zeros_like(col_ref)
    ones = jnp.ones((DEGREE_ROWS, tiles_ref.shape[2]), BF16)
    for t in range(tiles_ref.shape[0]):
        row, col = tile_rows[t], tile_cols[t]
        apart = lax.div(row, group) ^ meta[1]
        halves = lax.rem(apart, 2) * meta[2] + lax.div(apart, 2)
        inside = lax.rem(row, group)
        table[0, t] = (lax.div(col, group) ^ meta[0]) * group + lax.rem(col, group)
        table[1, t] = apart * group + inside
        table[2, t] = halves * group + inside
        for ref, place, dims in ((row_ref, table[2, t], NT), (col_ref, table[0, t], NN)):
            sums = lax.dot_general(ones, tiles_ref[t], dims, preferred_element_type=F32)
            ref[pl.ds(place, 1), :] += sums[:1]


def column_kernel(runs, degree, table, tiles_ref, *refs):
    parts, refs = refs[: len(runs)], refs[len(runs) :]
    if degree:
        sums, *refs = refs
    own_ref, *send_refs, panel, total = refs
    group, vectors_n, _ = own_ref.shape
    fill(panel, parts, runs)
    total[...] = jnp.zeros_like(total)
    for t in range(tiles_ref.shape[0]):
        total[table[0, t]] += lax.dot_general(
            panel[table[1, t]], tiles_ref[t], NN, preferred_element_type=F32
        )
    own_ref[...] = total[:group]
    for d, send in enumerate(send_refs, 1):
        round_sums(send, total, d * group, group)
        if degree:
            send[group * vectors_n :, :] = split_degree(sums[d * group : (d + 1) * group, :])


def row_kernel(runs, degree, table, tiles_ref, *refs):
    parts, refs = refs[: len(runs)], refs[len(runs) :]
    if degree:
        sums, *refs = refs
    kept_ref, swap_ref, panel, total = refs
    half, group, vectors_n, _ = kept_ref.shape
    fill(panel, parts, runs)
    total[...] = jnp.zeros_like(total)
    for t in range(tiles_ref.shape[0]):
        total[table[2, t]] += lax.dot_general(
            panel[table[0, t]], tiles_ref[t], NT, preferred_element_type=F32
        )
    for d in range(half):
        kept_ref[d] = total[d * group : (d + 1) * group]
        round_sums(swap_ref.at[d], total, (half + d) * group, group)
        if degree:
            rows = slice((half + d) * group, (half + d + 1) * group)
            swap_ref[d, group * vectors_n :, :] = split_degree(sums[rows, :])


def round_sums(send, total, start, group):
    vectors_n = total.shape[1]
    for k in range(group):
        send[k * vectors_n : (k + 1) * vectors_n, :] = total[start + k].astype(BF16)


def products(tiles, table, col_parts, row_parts, runs, degree):
    group, vectors_n, width = col_parts[0].shape
    half = len(row_parts) // 2
    rows_n = max(place + count for run in runs[0] for place, count in run) // group
    rows = group * vectors_n + (2 * group if degree else 0)
    own_shape = jax.ShapeDtypeStruct((group, vectors_n, width), F32)
    send_shape = jax.ShapeDtypeStruct((rows, width), BF16)
    flops = 2 * tiles.size * vectors_n

    def panels(source, target):
        return [
            pltpu.VMEM((source * group, vectors_n, width), BF16),
            pltpu.VMEM((target * group, vectors_n, width), F32),
        ]

    col_own, *col_send = call(
        functools.partial(column_kernel, runs[1], bool(degree)),
        [own_shape] + [send_shape] * (rows_n - 1),
        panels(2 * half, rows_n),
        24,
        [table, tiles, *row_parts, *degree[1:]],
        flops,
        1,
    )
    kept, swap = call(
        functools.partial(row_kernel, runs[0], bool(degree)),
        [
            jax.ShapeDtypeStruct((half, group, vectors_n, width), F32),
            jax.ShapeDtypeStruct((half, rows, width), BF16),
        ],
        panels(rows_n, 2 * half),
        24,
        [table, tiles, *col_parts, *degree[:1]],
        flops,
        1,
        [col_own],
    )
    return kept, swap, col_own, col_send


def merge_kernel(degree, kept, got, *refs):
    if degree:
        row_degree, own_ref, own_degree, *send_refs = refs
    else:
        own_ref, *send_refs = refs
    _, group, vectors_n, _ = kept.shape
    for k in range(group):
        rows = slice(k * vectors_n, (k + 1) * vectors_n)
        own_ref[k] = kept[0, k] + got[0, rows, :].astype(F32)
        for d, send in enumerate(send_refs, 1):
            send[rows, :] = (kept[d, k] + got[d, rows, :].astype(F32)).astype(BF16)
    if degree:
        for d in range(kept.shape[0]):
            sums = row_degree[d * group : (d + 1) * group, :] + join_degree(got.at[d], group)
            if d:
                send_refs[d - 1][group * vectors_n :, :] = split_degree(sums)
            else:
                own_degree[...] = sums


def merge(kept, got, degree):
    _, group, _, width = kept.shape
    out_shape = [jax.ShapeDtypeStruct(kept.shape[1:], F32)]
    if degree:
        out_shape += [jax.ShapeDtypeStruct((group, width), F32)]
    out_shape += [jax.ShapeDtypeStruct(got.shape[1:], BF16)] * (kept.shape[0] - 1)
    kernel = functools.partial(merge_kernel, bool(degree))
    return call(kernel, out_shape, [], 24, [kept, got, *degree[:1]])


def gathered_sum(own, received, k):
    total = own[k]
    rows = slice(k * total.shape[0], (k + 1) * total.shape[0])
    for part in received:
        total = total + part[rows, :].astype(F32)
    return total


def symmetric_part(row_own, row_refs, col_own, col_refs, k):
    return 0.5 * (gathered_sum(row_own, row_refs, k) + gathered_sum(col_own, col_refs, k))


def first_kernel(chips_n, vec_ref, row_degree, col_degree, row_own, col_own, *refs):
    row_refs, refs = refs[: chips_n - 1], refs[chips_n - 1 :]
    col_refs, (first_ref, rounded_ref, degree_ref) = refs[:-3], refs[-3:]
    group, _, width = rounded_ref.shape
    degree = row_degree[...] + col_degree[:group, :]
    for part in (*row_refs, *col_refs):
        degree += join_degree(part, group)
    degree = 0.5 * degree
    degree_ref[...] = degree
    for k, vec in enumerate(tiles_first(vec_ref, width)):
        symmetric = symmetric_part(row_own, row_refs, col_own, col_refs, k)
        image = degree[k : k + 1, :] * vec - symmetric
        first = (image - CENTER * vec) / HALF_WIDTH
        first_ref[:, k * width : (k + 1) * width] = first
        rounded_ref[k] = first.astype(BF16)


def filter_kernel(chips_n, start_ref, first_ref, degree_ref, row_own, col_own, *refs):
    row_refs, refs = refs[: chips_n - 1], refs[chips_n - 1 :]
    col_refs, (filtered_ref, rounded_ref, gram_ref, both) = refs[:-4], refs[-4:]
    group, vectors_n, width = rounded_ref.shape
    for k, vec in enumerate(tiles_first(first_ref, width)):
        symmetric = symmetric_part(row_own, row_refs, col_own, col_refs, k)
        columns = slice(k * width, (k + 1) * width)
        image = degree_ref[k : k + 1, :] * vec - symmetric
        filtered = 2.0 * (image - CENTER * vec) / HALF_WIDTH - start_ref[:, columns]
        filtered_ref[:, columns] = filtered
        rounded_ref[k] = filtered.astype(BF16)
        both[:vectors_n, columns] = filtered
        both[vectors_n:, columns] = degree_ref[k : k + 1, :] * filtered
    gram_ref[...] = lax.dot_general(
        filtered_ref[...], both[...], NT, precision=HIGHEST, preferred_element_type=F32
    )


def half_form_kernel(runs, table, tiles_ref, *refs):
    parts, (out_ref, panel) = refs[:-2], refs[-2:]
    width = panel.shape[2]
    fill(panel, parts, runs)
    for t in range(tiles_ref.shape[0]):
        out_ref[:, t * width : (t + 1) * width] = lax.dot_general(
            panel[table[1, t]], tiles_ref[t], NN, preferred_element_type=F32
        ).astype(BF16)


def form_kernel(runs, table, left, gram_ref, *refs):
    parts, (out_ref, panel, right) = refs[:-3], refs[-3:]
    _, vectors_n, width = panel.shape
    fill(panel, parts, runs)
    for t in range(right.shape[1] // width):
        right[:, t * width : (t + 1) * width] = panel[table[0, t]]
    form = lax.dot_general(left[...], right[...], NT, preferred_element_type=F32)
    projected = gram_ref[:, vectors_n:] - 0.5 * (form + form.T)
    row, col = square_index(vectors_n)
    packed = jnp.where(col >= row, gram_ref[:, :vectors_n], projected)
    diagonal = jnp.sum(jnp.where(row == col, projected, 0.0), 0, keepdims=True)
    half = vectors_n // 2
    out_ref[:half] = jnp.concatenate([packed[:half], packed[half:]], 1)
    diagonal = jnp.broadcast_to(diagonal, (8, vectors_n))
    out_ref[half:] = jnp.concatenate([diagonal, jnp.zeros_like(diagonal)], 1)


def square_index(n):
    return tuple(lax.broadcasted_iota(jnp.int32, (n, n), axis) for axis in (0, 1))


def inverse_factor(gram):
    n = gram.shape[0]
    row, col = square_index(n)
    table = jnp.concatenate([gram, jnp.where(row == col, 1.0, 0.0)], 1)
    bands = [table[i : i + 8] for i in range(0, n, 8)]
    shape = (8, 2 * n)
    line = lax.broadcasted_iota(jnp.int32, shape, 0)

    def spread(values, j):
        return jnp.broadcast_to(values[:, j : j + 1], shape)

    def pick(values, i):
        return jnp.broadcast_to(values[i : i + 1, :], shape)

    for at in range(n // 8):
        block = [spread(bands[at], 8 * at + c) for c in range(8)]
        forward, solved = bands[at], bands[at]
        solved_block = list(block)
        for s in range(8):
            scale = 1.0 / pick(block[s], s)
            below = jnp.where(line > s, block[s], 0.0) * scale
            above = jnp.where(line < s, solved_block[s] * scale, 0.0)
            both = below + above
            pivot_row = pick(forward, s)
            forward = forward - below * pivot_row
            solved = solved - both * pivot_row
            for c in range(s + 1, 8):
                pivot = pick(block[c], s)
                block[c] = block[c] - below * pivot
                solved_block[c] = solved_block[c] - both * pivot
        pivots = block[0]
        for s in range(1, 8):
            pivots = jnp.where(line == s, block[s], pivots)
        solved = solved / pivots
        bands[at] = forward / jnp.sqrt(pivots)
        for i in range(at + 1, n // 8):
            update = spread(bands[i], 8 * at) * pick(solved, 0)
            for c in range(1, 8):
                update = update + spread(bands[i], 8 * at + c) * pick(solved, c)
            bands[i] = bands[i] - update
    return jnp.concatenate(bands, 0)[:, n:]


def last_kernel(total_nodes, filtered_ref, *refs):
    parts, (ritz_ref, rayleigh_ref) = refs[:-2], refs[-2:]
    n = filtered_ref.shape[0]
    half = n // 2
    sums = tree_sum([part[...] for part in parts]) * (1.0 / total_nodes)
    packed = jnp.concatenate([sums[:half, :n], sums[:half, n:]], 0)
    row, col = square_index(n)
    upper = jnp.where(col > row, packed, 0.0)
    gram = jnp.where(col >= row, packed, 0.0) + upper.T
    lower = jnp.where(col < row, packed, 0.0)
    diagonal = jnp.broadcast_to(sums[half : half + 1, :n], (n, n))
    projected = lower + lower.T + jnp.where(row == col, diagonal, 0.0)
    inverse = inverse_factor(gram)

    def dot(a, b, dims):
        return lax.dot_general(a, b, dims, precision=HIGHEST, preferred_element_type=F32)

    half_way = dot(inverse, projected, NN)
    rayleigh_ref[...] = dot(half_way, inverse, NT)
    turned = dot(inverse, half_way, NT)
    ritz_ref[...] = dot(turned, dot(inverse, filtered_ref[...], NN), NN)


def tree_sum(parts):
    while len(parts) > 1:
        parts = [a + b for a, b in zip(parts[::2], parts[1::2])]
    return parts[0]


def local(tiles, tile_rows, tile_cols, start):
    tiles, tile_rows, tile_cols = tiles[0, 0], tile_rows[0, 0], tile_cols[0, 0]
    width = tiles.shape[-1]
    vectors_n, own_nodes = start.shape
    rows_n, cols_n = lax.axis_size("row"), lax.axis_size("col")
    chips_n = cols_n // 2
    total_nodes = own_nodes * rows_n * cols_n
    group = own_nodes // width
    spread = (vectors_n, tiles.shape[0] * width)

    rounded_shape = jax.ShapeDtypeStruct((group, vectors_n, width), BF16)
    vector_shape = jax.ShapeDtypeStruct((vectors_n, own_nodes), F32)
    degree_shape = jax.ShapeDtypeStruct((group, width), F32)

    late = 1
    levels = [rows_n >> i for i in range(1, rows_n.bit_length())]
    col_runs = [[(0, group)]]
    for d in levels:
        if len(col_runs) == 1:
            col_runs += [[(d * group, group)]]
            continue
        cut = group - late
        passed = [((p // group ^ d) * group + p % group, n) for run in col_runs[1:] for p, n in run]
        col_runs += [[(d * group, cut)], [(d * group + cut, late), *passed]]
    row_runs = [[((2 * d + core) * group, group)] for core in range(2) for d in range(chips_n)]
    runs = (col_runs, row_runs)
    def gather(rounded, first=()):
        held = [rounded]
        for d in levels:
            if len(held) == 1:
                held += [trade(rounded, "row", d)]
                continue
            near = trade(rounded[: group - late], "row", d)
            near, *passed = lax.optimization_barrier((near, *held[1:], *first))
            held[1:] = passed[: len(held) - 1]
            held += [near, trade(jnp.concatenate([rounded[group - late :], *held[1:]]), "row", d)]
        chips = [rounded, *exchange([rounded] * (chips_n - 1), "col", 2)]
        return held, chips + [trade(chip, "col", 1) for chip in chips]

    def apply(rounded, degree=()):
        kept, swap, col_own, col_send = products(tiles, table, *gather(rounded, degree), runs, degree)
        col_got = exchange(col_send, "row")
        row_own, *row_send = merge(kept, trade(swap, "col", 1), degree)
        if degree:
            own_degree, *row_send = row_send
        row_got = exchange(row_send, "col", 2)
        sums = [row_own, col_own, *row_got, *col_got]
        return [own_degree, degree[1], *sums] if degree else sums

    rounded = call(round_kernel, rounded_shape, [], 16, [start])
    meta = jnp.stack([lax.axis_index("row"), lax.axis_index("col"), chips_n]).astype(jnp.int32)
    *degree, table = call(
        functools.partial(degree_kernel, group),
        [jax.ShapeDtypeStruct((n * group, width), F32) for n in (cols_n, rows_n)]
        + [jax.ShapeDtypeStruct((3, tiles.shape[0]), jnp.int32)],
        [],
        16,
        [meta, tile_rows, tile_cols, tiles],
        4 * tiles.size * DEGREE_ROWS,
        3,
        outs=[VMEM, VMEM, SMEM],
    )
    first, rounded, degree = call(
        functools.partial(first_kernel, chips_n),
        [vector_shape, rounded_shape, degree_shape],
        [],
        24,
        [start, *apply(rounded, tuple(degree))],
    )
    filtered, rounded, gram = call(
        functools.partial(filter_kernel, chips_n),
        [vector_shape, rounded_shape, jax.ShapeDtypeStruct((vectors_n, 2 * vectors_n), F32)],
        [pltpu.VMEM((2 * vectors_n, own_nodes), F32)],
        24,
        [start, first, degree, *apply(rounded)],
    )
    col_parts, row_parts = gather(rounded)
    left = call(
        functools.partial(half_form_kernel, runs[1]),
        jax.ShapeDtypeStruct(spread, BF16),
        [pltpu.VMEM((cols_n * group, vectors_n, width), BF16)],
        24,
        [table, tiles, *row_parts],
        2 * tiles.size * vectors_n,
        1,
    )
    sums = call(
        functools.partial(form_kernel, runs[0]),
        jax.ShapeDtypeStruct((vectors_n // 2 + 8, 2 * vectors_n), F32),
        [pltpu.VMEM((rows_n * group, vectors_n, width), BF16), pltpu.VMEM(spread, BF16)],
        24,
        [table, left, gram, *col_parts],
        2 * vectors_n * spread[0] * spread[1],
        1,
    )
    sums = sums + trade(sums, "col", 1)
    sums = tree_sum([sums, *exchange([sums] * (chips_n - 1), "col", 2)])
    return call(
        functools.partial(last_kernel, total_nodes),
        [vector_shape, jax.ShapeDtypeStruct((vectors_n, vectors_n), F32)],
        [],
        24,
        [filtered, sums, *exchange([sums] * (rows_n - 1), "row")],
    )


def solution(mesh):
    placed = (
        P("row", "col", None, None, None),
        P("row", "col", None),
        P("row", "col", None),
        P(None, ("row", "col")),
    )
    return jax.shard_map(
        local, mesh=mesh, in_specs=placed, out_specs=(P(None, ("row", "col")), P()), check_vma=False
    )
```

```python
import functools

import jax
import jax.numpy as jnp
from jax import lax
from jax.experimental import pallas as pl
from jax.experimental.pallas import tpu as pltpu
from jax.sharding import PartitionSpec as P

CENTER = 1.0
HALF_WIDTH = 0.5
HIGHEST = lax.Precision.HIGHEST
NT = (((1,), (1,)), ((), ()))
NN = (((1,), (0,)), ((), ()))
BF16 = jnp.bfloat16
F32 = jnp.float32
VMEM = pl.BlockSpec(memory_space=pltpu.VMEM)
SMEM = pl.BlockSpec(memory_space=pltpu.SMEM)
ANY = pl.BlockSpec(memory_space=pl.ANY)
DEGREE_ROWS = 16


def call(kernel, out_shape, scratch, limit, args, flops=0, smem=0, after=(), outs=None):
    moved = sum(x.size * x.dtype.itemsize for x in args)
    return pl.pallas_call(
        lambda *refs: kernel(*refs[len(after) :]),
        out_shape=out_shape,
        in_specs=[ANY] * len(after) + [SMEM] * smem + [VMEM] * (len(args) - smem),
        out_specs=outs or jax.tree.map(lambda _: VMEM, out_shape),
        scratch_shapes=scratch,
        compiler_params=pltpu.CompilerParams(vmem_limit_bytes=limit * 2**20),
        cost_estimate=pl.CostEstimate(flops=flops, bytes_accessed=moved, transcendentals=0),
    )(*after, *args)


def trade(part, axis, d):
    n = lax.axis_size(axis)
    return lax.ppermute(part, axis, [(i, i ^ d) for i in range(n)])


def exchange(parts, axis, step=1):
    far_first = [trade(part, axis, step * d) for d, part in reversed(list(enumerate(parts, 1)))]
    return far_first[::-1]


def tiles_first(ref, width):
    return [ref[:, k * width : (k + 1) * width] for k in range(ref.shape[1] // width)]


def round_kernel(vec_ref, out_ref):
    for k, piece in enumerate(tiles_first(vec_ref, out_ref.shape[2])):
        out_ref[k] = piece.astype(BF16)


def split_degree(sums):
    high = sums.astype(BF16).astype(F32)
    return jnp.concatenate([high, sums - high], 0).astype(BF16)


def join_degree(payload, group):
    parts = payload[payload.shape[0] - 2 * group :, :].astype(F32)
    return parts[:group] + parts[group:]


def fill(panel, parts, runs):
    for part, places in zip(parts, runs):
        at = 0
        for place, count in places:
            panel[place : place + count] = part[at : at + count]
            at += count


def degree_kernel(group, meta, tile_rows, tile_cols, tiles_ref, row_ref, col_ref, table):
    row_ref[...] = jnp.zeros_like(row_ref)
    col_ref[...] = jnp.zeros_like(col_ref)
    ones = jnp.ones((DEGREE_ROWS, tiles_ref.shape[2]), BF16)
    for t in range(tiles_ref.shape[0]):
        row, col = tile_rows[t], tile_cols[t]
        apart = lax.div(row, group) ^ meta[1]
        halves = lax.rem(apart, 2) * meta[2] + lax.div(apart, 2)
        inside = lax.rem(row, group)
        table[0, t] = (lax.div(col, group) ^ meta[0]) * group + lax.rem(col, group)
        table[1, t] = apart * group + inside
        table[2, t] = halves * group + inside
        sums = lax.dot_general(ones, tiles_ref[t], NT, preferred_element_type=F32)
        row_ref[pl.ds(table[2, t], 1), :] += sums[:1]
        col_ref[pl.ds(table[0, t], 1), :] += jnp.sum(tiles_ref[t].astype(F32), 0, keepdims=True)


def column_kernel(runs, degree, table, tiles_ref, *refs):
    parts, refs = refs[: len(runs)], refs[len(runs) :]
    if degree:
        sums, *refs = refs
    own_ref, *send_refs, panel, total = refs
    group, vectors_n, _ = own_ref.shape
    fill(panel, parts, runs)
    total[...] = jnp.zeros_like(total)
    for t in range(tiles_ref.shape[0]):
        total[table[0, t]] += lax.dot_general(
            panel[table[1, t]], tiles_ref[t], NN, preferred_element_type=F32
        )
    own_ref[...] = total[:group]
    for d, send in enumerate(send_refs, 1):
        round_sums(send, total, d * group, group)
        if degree:
            send[group * vectors_n :, :] = split_degree(sums[d * group : (d + 1) * group, :])


def row_kernel(runs, degree, table, tiles_ref, *refs):
    parts, refs = refs[: len(runs)], refs[len(runs) :]
    if degree:
        sums, *refs = refs
    total, swap_ref, panel = refs
    half, vectors_n = swap_ref.shape[0], total.shape[1]
    group = total.shape[0] // (2 * half)
    fill(panel, parts, runs)
    total[...] = jnp.zeros_like(total)
    for t in range(tiles_ref.shape[0]):
        total[table[2, t]] += lax.dot_general(
            panel[table[0, t]], tiles_ref[t], NT, preferred_element_type=F32
        )
    for d in range(half):
        round_sums(swap_ref.at[d], total, (half + d) * group, group)
        if degree:
            rows = slice((half + d) * group, (half + d + 1) * group)
            swap_ref[d, group * vectors_n :, :] = split_degree(sums[rows, :])


def round_sums(send, total, start, group):
    vectors_n = total.shape[1]
    for k in range(group):
        send[k * vectors_n : (k + 1) * vectors_n, :] = total[start + k].astype(BF16)


def products(tiles, table, col_parts, row_parts, runs, degree):
    group, vectors_n, width = col_parts[0].shape
    half = len(row_parts) // 2
    rows_n = max(place + count for run in runs[0] for place, count in run) // group
    rows = group * vectors_n + (2 * group if degree else 0)
    own_shape = jax.ShapeDtypeStruct((group, vectors_n, width), F32)
    send_shape = jax.ShapeDtypeStruct((rows, width), BF16)
    flops = 2 * tiles.size * vectors_n

    def panels(source, target):
        return [
            pltpu.VMEM((source * group, vectors_n, width), BF16),
            pltpu.VMEM((target * group, vectors_n, width), F32),
        ]

    col_own, *col_send = call(
        functools.partial(column_kernel, runs[1], bool(degree)),
        [own_shape] + [send_shape] * (rows_n - 1),
        panels(2 * half, rows_n),
        24,
        [table, tiles, *row_parts, *degree[1:]],
        flops,
        1,
    )
    kept, swap = call(
        functools.partial(row_kernel, runs[0], bool(degree)),
        [
            jax.ShapeDtypeStruct((2 * half * group, vectors_n, width), F32),
            jax.ShapeDtypeStruct((half, rows, width), BF16),
        ],
        panels(rows_n, 2 * half)[:1],
        24,
        [table, tiles, *col_parts, *degree[:1]],
        flops,
        1,
        [col_own],
    )
    return kept, swap, col_own, col_send


def merge_kernel(degree, kept, got, *refs):
    if degree:
        row_degree, own_ref, own_degree, *send_refs = refs
    else:
        own_ref, *send_refs = refs
    group, vectors_n, _ = own_ref.shape
    for k in range(group):
        rows = slice(k * vectors_n, (k + 1) * vectors_n)
        own_ref[k] = kept[k] + got[0, rows, :].astype(F32)
        for d, send in enumerate(send_refs, 1):
            send[rows, :] = (kept[d * group + k] + got[d, rows, :].astype(F32)).astype(BF16)
    if degree:
        for d in range(got.shape[0]):
            sums = row_degree[d * group : (d + 1) * group, :] + join_degree(got.at[d], group)
            if d:
                send_refs[d - 1][group * vectors_n :, :] = split_degree(sums)
            else:
                own_degree[...] = sums


def merge(kept, got, degree):
    half, (_, vectors_n, width) = got.shape[0], kept.shape
    group = kept.shape[0] // (2 * half)
    out_shape = [jax.ShapeDtypeStruct((group, vectors_n, width), F32)]
    if degree:
        out_shape += [jax.ShapeDtypeStruct((group, width), F32)]
    out_shape += [jax.ShapeDtypeStruct(got.shape[1:], BF16)] * (half - 1)
    kernel = functools.partial(merge_kernel, bool(degree))
    return call(kernel, out_shape, [], 24, [kept, got, *degree[:1]])


def gathered_sum(own, received, k):
    total = own[k]
    rows = slice(k * total.shape[0], (k + 1) * total.shape[0])
    for part in received:
        total = total + part[rows, :].astype(F32)
    return total


def symmetric_part(row_own, row_refs, col_own, col_refs, k):
    return 0.5 * (gathered_sum(row_own, row_refs, k) + gathered_sum(col_own, col_refs, k))


def first_kernel(chips_n, vec_ref, row_degree, col_degree, row_own, col_own, *refs):
    row_refs, refs = refs[: chips_n - 1], refs[chips_n - 1 :]
    col_refs, (first_ref, rounded_ref, degree_ref) = refs[:-3], refs[-3:]
    group, _, width = rounded_ref.shape
    degree = row_degree[...] + col_degree[:group, :]
    for part in (*row_refs, *col_refs):
        degree += join_degree(part, group)
    degree = 0.5 * degree
    degree_ref[...] = degree
    for k, vec in enumerate(tiles_first(vec_ref, width)):
        symmetric = symmetric_part(row_own, row_refs, col_own, col_refs, k)
        image = degree[k : k + 1, :] * vec - symmetric
        first = (image - CENTER * vec) / HALF_WIDTH
        first_ref[:, k * width : (k + 1) * width] = first
        rounded_ref[k] = first.astype(BF16)


def filter_kernel(chips_n, start_ref, first_ref, degree_ref, row_own, col_own, *refs):
    row_refs, refs = refs[: chips_n - 1], refs[chips_n - 1 :]
    col_refs, (filtered_ref, rounded_ref) = refs[:-2], refs[-2:]
    width = rounded_ref.shape[2]
    for k, vec in enumerate(tiles_first(first_ref, width)):
        symmetric = symmetric_part(row_own, row_refs, col_own, col_refs, k)
        columns = slice(k * width, (k + 1) * width)
        image = degree_ref[k : k + 1, :] * vec - symmetric
        filtered = 2.0 * (image - CENTER * vec) / HALF_WIDTH - start_ref[:, columns]
        filtered_ref[:, columns] = filtered
        rounded_ref[k] = filtered.astype(BF16)


def gram_kernel(filtered_ref, degree_ref, gram_ref, both):
    vectors_n, width = filtered_ref.shape[0], degree_ref.shape[1]
    for k, vec in enumerate(tiles_first(filtered_ref, width)):
        columns = slice(k * width, (k + 1) * width)
        both[:vectors_n, columns] = vec
        both[vectors_n:, columns] = degree_ref[k : k + 1, :] * vec
    gram_ref[...] = lax.dot_general(
        filtered_ref[...], both[...], NT, precision=HIGHEST, preferred_element_type=F32
    )


def half_form_kernel(runs, table, tiles_ref, *refs):
    parts, (out_ref, panel) = refs[:-2], refs[-2:]
    width = panel.shape[2]
    fill(panel, parts, runs)
    for t in range(tiles_ref.shape[0]):
        out_ref[:, t * width : (t + 1) * width] = lax.dot_general(
            panel[table[1, t]], tiles_ref[t], NN, preferred_element_type=F32
        ).astype(BF16)


def form_kernel(runs, table, left, gram_ref, *refs):
    parts, (out_ref, panel, right) = refs[:-3], refs[-3:]
    _, vectors_n, width = panel.shape
    fill(panel, parts, runs)
    for t in range(right.shape[1] // width):
        right[:, t * width : (t + 1) * width] = panel[table[0, t]]
    form = lax.dot_general(left[...], right[...], NT, preferred_element_type=F32)
    projected = gram_ref[:, vectors_n:] - 0.5 * (form + form.T)
    row, col = square_index(vectors_n)
    packed = jnp.where(col >= row, gram_ref[:, :vectors_n], projected)
    diagonal = jnp.sum(jnp.where(row == col, projected, 0.0), 0, keepdims=True)
    half = vectors_n // 2
    out_ref[:half] = jnp.concatenate([packed[:half], packed[half:]], 1)
    diagonal = jnp.broadcast_to(diagonal, (8, vectors_n))
    out_ref[half:] = jnp.concatenate([diagonal, jnp.zeros_like(diagonal)], 1)


def square_index(n):
    return tuple(lax.broadcasted_iota(jnp.int32, (n, n), axis) for axis in (0, 1))


def inverse_factor(gram):
    n = gram.shape[0]
    row, col = square_index(n)
    table = jnp.concatenate([gram, jnp.where(row == col, 1.0, 0.0)], 1)
    bands = [table[i : i + 8] for i in range(0, n, 8)]
    shape = (8, 2 * n)
    line = lax.broadcasted_iota(jnp.int32, shape, 0)

    def spread(values, j):
        return jnp.broadcast_to(values[:, j : j + 1], shape)

    def pick(values, i):
        return jnp.broadcast_to(values[i : i + 1, :], shape)

    for at in range(n // 8):
        block = [spread(bands[at], 8 * at + c) for c in range(8)]
        forward, solved = bands[at], bands[at]
        solved_block = list(block)
        for s in range(8):
            scale = 1.0 / pick(block[s], s)
            below = jnp.where(line > s, block[s], 0.0) * scale
            above = jnp.where(line < s, solved_block[s] * scale, 0.0)
            both = below + above
            pivot_row = pick(forward, s)
            forward = forward - below * pivot_row
            solved = solved - both * pivot_row
            for c in range(s + 1, 8):
                pivot = pick(block[c], s)
                block[c] = block[c] - below * pivot
                solved_block[c] = solved_block[c] - both * pivot
        pivots = block[0]
        for s in range(1, 8):
            pivots = jnp.where(line == s, block[s], pivots)
        solved = solved / pivots
        bands[at] = forward / jnp.sqrt(pivots)
        for i in range(at + 1, n // 8):
            update = spread(bands[i], 8 * at) * pick(solved, 0)
            for c in range(1, 8):
                update = update + spread(bands[i], 8 * at + c) * pick(solved, c)
            bands[i] = bands[i] - update
    return jnp.concatenate(bands, 0)[:, n:]


def last_kernel(total_nodes, filtered_ref, *refs):
    parts, (ritz_ref, rayleigh_ref) = refs[:-2], refs[-2:]
    n = filtered_ref.shape[0]
    half = n // 2
    sums = tree_sum([part[...] for part in parts]) * (1.0 / total_nodes)
    packed = jnp.concatenate([sums[:half, :n], sums[:half, n:]], 0)
    row, col = square_index(n)
    upper = jnp.where(col > row, packed, 0.0)
    gram = jnp.where(col >= row, packed, 0.0) + upper.T
    lower = jnp.where(col < row, packed, 0.0)
    diagonal = jnp.broadcast_to(sums[half : half + 1, :n], (n, n))
    projected = lower + lower.T + jnp.where(row == col, diagonal, 0.0)
    inverse = inverse_factor(gram)

    def dot(a, b, dims):
        return lax.dot_general(a, b, dims, precision=HIGHEST, preferred_element_type=F32)

    half_way = dot(inverse, projected, NN)
    rayleigh_ref[...] = dot(half_way, inverse, NT)
    turned = dot(inverse, half_way, NT)
    ritz_ref[...] = dot(turned, dot(inverse, filtered_ref[...], NN), NN)


def tree_sum(parts):
    while len(parts) > 1:
        parts = [a + b for a, b in zip(parts[::2], parts[1::2])]
    return parts[0]


def local(tiles, tile_rows, tile_cols, start):
    tiles, tile_rows, tile_cols = tiles[0, 0], tile_rows[0, 0], tile_cols[0, 0]
    width = tiles.shape[-1]
    vectors_n, own_nodes = start.shape
    rows_n, cols_n = lax.axis_size("row"), lax.axis_size("col")
    chips_n = cols_n // 2
    total_nodes = own_nodes * rows_n * cols_n
    group = own_nodes // width
    spread = (vectors_n, tiles.shape[0] * width)

    rounded_shape = jax.ShapeDtypeStruct((group, vectors_n, width), BF16)
    vector_shape = jax.ShapeDtypeStruct((vectors_n, own_nodes), F32)
    degree_shape = jax.ShapeDtypeStruct((group, width), F32)

    late = 1
    levels = [rows_n >> i for i in range(1, rows_n.bit_length())]
    col_runs = [[(0, group)]]
    for d in levels:
        if len(col_runs) == 1:
            col_runs += [[(d * group, group)]]
            continue
        cut = group - late
        passed = [((p // group ^ d) * group + p % group, n) for run in col_runs[1:] for p, n in run]
        col_runs += [[(d * group, cut)], [(d * group + cut, late), *passed]]
    row_runs = [[((2 * d + core) * group, group)] for core in range(2) for d in range(chips_n)]
    runs = (col_runs, row_runs)
    def gather(rounded, first=()):
        held = [rounded]
        for d in levels:
            if len(held) == 1:
                held += [trade(rounded, "row", d)]
                continue
            near = trade(rounded[: group - late], "row", d)
            near, *passed = lax.optimization_barrier((near, *held[1:], *first))
            held[1:] = passed[: len(held) - 1]
            held += [near, trade(jnp.concatenate([rounded[group - late :], *held[1:]]), "row", d)]
        chips = [rounded, *exchange([rounded] * (chips_n - 1), "col", 2)]
        return held, chips + [trade(chip, "col", 1) for chip in chips]

    def apply(rounded, degree=()):
        kept, swap, col_own, col_send = products(tiles, table, *gather(rounded, degree), runs, degree)
        col_got = exchange(col_send, "row")
        row_own, *row_send = merge(kept, trade(swap, "col", 1), degree)
        if degree:
            own_degree, *row_send = row_send
        row_got = exchange(row_send, "col", 2)
        sums = [row_own, col_own, *row_got, *col_got]
        return [own_degree, degree[1], *sums] if degree else sums

    rounded = call(round_kernel, rounded_shape, [], 16, [start])
    meta = jnp.stack([lax.axis_index("row"), lax.axis_index("col"), chips_n]).astype(jnp.int32)
    *degree, table = call(
        functools.partial(degree_kernel, group),
        [jax.ShapeDtypeStruct((n * group, width), F32) for n in (cols_n, rows_n)]
        + [jax.ShapeDtypeStruct((3, tiles.shape[0]), jnp.int32)],
        [],
        16,
        [meta, tile_rows, tile_cols, tiles],
        4 * tiles.size * DEGREE_ROWS,
        3,
        outs=[VMEM, VMEM, SMEM],
    )
    first, rounded, degree = call(
        functools.partial(first_kernel, chips_n),
        [vector_shape, rounded_shape, degree_shape],
        [],
        24,
        [start, *apply(rounded, tuple(degree))],
    )
    filtered, rounded = call(
        functools.partial(filter_kernel, chips_n),
        [vector_shape, rounded_shape],
        [],
        24,
        [start, first, degree, *apply(rounded)],
    )
    gram = call(
        gram_kernel,
        jax.ShapeDtypeStruct((vectors_n, 2 * vectors_n), F32),
        [pltpu.VMEM((2 * vectors_n, own_nodes), F32)],
        16,
        [filtered, degree],
        24 * vectors_n * vectors_n * own_nodes,
    )
    col_parts, row_parts = gather(rounded, (gram,))
    left = call(
        functools.partial(half_form_kernel, runs[1]),
        jax.ShapeDtypeStruct(spread, BF16),
        [pltpu.VMEM((cols_n * group, vectors_n, width), BF16)],
        24,
        [table, tiles, *row_parts],
        2 * tiles.size * vectors_n,
        1,
    )
    sums = call(
        functools.partial(form_kernel, runs[0]),
        jax.ShapeDtypeStruct((vectors_n // 2 + 8, 2 * vectors_n), F32),
        [pltpu.VMEM((rows_n * group, vectors_n, width), BF16), pltpu.VMEM(spread, BF16)],
        24,
        [table, left, gram, *col_parts],
        2 * vectors_n * spread[0] * spread[1],
        1,
    )
    sums = sums + trade(sums, "col", 1)
    sums = tree_sum([sums, *exchange([sums] * (chips_n - 1), "col", 2)])
    return call(
        functools.partial(last_kernel, total_nodes),
        [vector_shape, jax.ShapeDtypeStruct((vectors_n, vectors_n), F32)],
        [],
        24,
        [filtered, sums, *exchange([sums] * (rows_n - 1), "row")],
    )


def solution(mesh):
    placed = (
        P("row", "col", None, None, None),
        P("row", "col", None),
        P("row", "col", None),
        P(None, ("row", "col")),
    )
    return jax.shard_map(
        local, mesh=mesh, in_specs=placed, out_specs=(P(None, ("row", "col")), P()), check_vma=False
    )
```

```python
import functools

import jax
import jax.numpy as jnp
from jax import lax
from jax.experimental import pallas as pl
from jax.experimental.pallas import tpu as pltpu
from jax.sharding import PartitionSpec as P

CENTER = 1.0
HALF_WIDTH = 0.5
HIGHEST = lax.Precision.HIGHEST
NT = (((1,), (1,)), ((), ()))
NN = (((1,), (0,)), ((), ()))
BF16 = jnp.bfloat16
F32 = jnp.float32
VMEM = pl.BlockSpec(memory_space=pltpu.VMEM)
SMEM = pl.BlockSpec(memory_space=pltpu.SMEM)
ANY = pl.BlockSpec(memory_space=pl.ANY)
DEGREE_ROWS = 16


def call(kernel, out_shape, scratch, limit, args, flops=0, smem=0, after=(), outs=None):
    moved = sum(x.size * x.dtype.itemsize for x in args)
    return pl.pallas_call(
        lambda *refs: kernel(*refs[len(after) :]),
        out_shape=out_shape,
        in_specs=[ANY] * len(after) + [SMEM] * smem + [VMEM] * (len(args) - smem),
        out_specs=outs or jax.tree.map(lambda _: VMEM, out_shape),
        scratch_shapes=scratch,
        compiler_params=pltpu.CompilerParams(vmem_limit_bytes=limit * 2**20),
        cost_estimate=pl.CostEstimate(flops=flops, bytes_accessed=moved, transcendentals=0),
    )(*after, *args)


def trade(part, axis, d):
    n = lax.axis_size(axis)
    return lax.ppermute(part, axis, [(i, i ^ d) for i in range(n)])


def exchange(parts, axis, step=1):
    far_first = [trade(part, axis, step * d) for d, part in reversed(list(enumerate(parts, 1)))]
    return far_first[::-1]


def tiles_first(ref, width):
    return [ref[:, k * width : (k + 1) * width] for k in range(ref.shape[1] // width)]


def round_kernel(vec_ref, out_ref):
    for k, piece in enumerate(tiles_first(vec_ref, out_ref.shape[2])):
        out_ref[k] = piece.astype(BF16)


def split_degree(sums):
    high = sums.astype(BF16).astype(F32)
    return jnp.concatenate([high, sums - high], 0).astype(BF16)


def join_degree(payload, group):
    parts = payload[payload.shape[0] - 2 * group :, :].astype(F32)
    return parts[:group] + parts[group:]


def fill(panel, parts, runs):
    for part, places in zip(parts, runs):
        at = 0
        for place, count in places:
            panel[place : place + count] = part[at : at + count]
            at += count


def degree_kernel(group, meta, tile_rows, tile_cols, tiles_ref, row_ref, col_ref, table, held_ref):
    row_ref[...] = jnp.zeros_like(row_ref)
    col_ref[...] = jnp.zeros_like(col_ref)
    ones = jnp.ones((DEGREE_ROWS, tiles_ref.shape[2]), BF16)
    for t in range(tiles_ref.shape[0]):
        row, col = tile_rows[t], tile_cols[t]
        apart = lax.div(row, group) ^ meta[1]
        halves = lax.rem(apart, 2) * meta[2] + lax.div(apart, 2)
        inside = lax.rem(row, group)
        table[0, t] = (lax.div(col, group) ^ meta[0]) * group + lax.rem(col, group)
        table[1, t] = apart * group + inside
        table[2, t] = halves * group + inside
        tile = tiles_ref[t]
        held_ref[t] = tile
        sums = lax.dot_general(ones, tile, NT, preferred_element_type=F32)
        row_ref[pl.ds(table[2, t], 1), :] += sums[:1]
        col_ref[pl.ds(table[0, t], 1), :] += jnp.sum(tile.astype(F32), 0, keepdims=True)


def column_kernel(runs, degree, table, tiles_ref, *refs):
    parts, refs = refs[: len(runs)], refs[len(runs) :]
    if degree:
        sums, *refs = refs
    own_ref, *send_refs, panel, total = refs
    group, vectors_n, _ = own_ref.shape
    fill(panel, parts, runs)
    total[...] = jnp.zeros_like(total)
    for t in range(tiles_ref.shape[0]):
        total[table[0, t]] += lax.dot_general(
            panel[table[1, t]], tiles_ref[t], NN, preferred_element_type=F32
        )
    own_ref[...] = total[:group]
    for d, send in enumerate(send_refs, 1):
        round_sums(send, total, d * group, group)
        if degree:
            send[group * vectors_n :, :] = split_degree(sums[d * group : (d + 1) * group, :])


def row_kernel(runs, degree, table, tiles_ref, *refs):
    parts, refs = refs[: len(runs)], refs[len(runs) :]
    if degree:
        sums, *refs = refs
    total, swap_ref, panel = refs
    half, vectors_n = swap_ref.shape[0], total.shape[1]
    group = total.shape[0] // (2 * half)
    fill(panel, parts, runs)
    total[...] = jnp.zeros_like(total)
    for t in range(tiles_ref.shape[0]):
        total[table[2, t]] += lax.dot_general(
            panel[table[0, t]], tiles_ref[t], NT, preferred_element_type=F32
        )
    for d in range(half):
        round_sums(swap_ref.at[d], total, (half + d) * group, group)
        if degree:
            rows = slice((half + d) * group, (half + d + 1) * group)
            swap_ref[d, group * vectors_n :, :] = split_degree(sums[rows, :])


def round_sums(send, total, start, group):
    vectors_n = total.shape[1]
    for k in range(group):
        send[k * vectors_n : (k + 1) * vectors_n, :] = total[start + k].astype(BF16)


def products(tiles, table, col_parts, row_parts, runs, degree):
    group, vectors_n, width = col_parts[0].shape
    half = len(row_parts) // 2
    rows_n = max(place + count for run in runs[0] for place, count in run) // group
    rows = group * vectors_n + (2 * group if degree else 0)
    own_shape = jax.ShapeDtypeStruct((group, vectors_n, width), F32)
    send_shape = jax.ShapeDtypeStruct((rows, width), BF16)
    flops = 2 * tiles.size * vectors_n

    def panels(source, target):
        return [
            pltpu.VMEM((source * group, vectors_n, width), BF16),
            pltpu.VMEM((target * group, vectors_n, width), F32),
        ]

    col_own, *col_send = call(
        functools.partial(column_kernel, runs[1], bool(degree)),
        [own_shape] + [send_shape] * (rows_n - 1),
        panels(2 * half, rows_n),
        24,
        [table, tiles, *row_parts, *degree[1:]],
        flops,
        1,
    )
    kept, swap = call(
        functools.partial(row_kernel, runs[0], bool(degree)),
        [
            jax.ShapeDtypeStruct((2 * half * group, vectors_n, width), F32),
            jax.ShapeDtypeStruct((half, rows, width), BF16),
        ],
        panels(rows_n, 2 * half)[:1],
        24,
        [table, tiles, *col_parts, *degree[:1]],
        flops,
        1,
        [col_own],
    )
    return kept, swap, col_own, col_send


def merge_kernel(degree, kept, got, *refs):
    if degree:
        row_degree, own_ref, own_degree, *send_refs = refs
    else:
        own_ref, *send_refs = refs
    group, vectors_n, _ = own_ref.shape
    for k in range(group):
        rows = slice(k * vectors_n, (k + 1) * vectors_n)
        own_ref[k] = kept[k] + got[0, rows, :].astype(F32)
        for d, send in enumerate(send_refs, 1):
            send[rows, :] = (kept[d * group + k] + got[d, rows, :].astype(F32)).astype(BF16)
    if degree:
        for d in range(got.shape[0]):
            sums = row_degree[d * group : (d + 1) * group, :] + join_degree(got.at[d], group)
            if d:
                send_refs[d - 1][group * vectors_n :, :] = split_degree(sums)
            else:
                own_degree[...] = sums


def merge(kept, got, degree):
    half, (_, vectors_n, width) = got.shape[0], kept.shape
    group = kept.shape[0] // (2 * half)
    out_shape = [jax.ShapeDtypeStruct((group, vectors_n, width), F32)]
    if degree:
        out_shape += [jax.ShapeDtypeStruct((group, width), F32)]
    out_shape += [jax.ShapeDtypeStruct(got.shape[1:], BF16)] * (half - 1)
    kernel = functools.partial(merge_kernel, bool(degree))
    return call(kernel, out_shape, [], 24, [kept, got, *degree[:1]])


def gathered_sum(own, received, k):
    total = own[k]
    rows = slice(k * total.shape[0], (k + 1) * total.shape[0])
    for part in received:
        total = total + part[rows, :].astype(F32)
    return total


def symmetric_part(row_own, row_refs, col_own, col_refs, k):
    return 0.5 * (gathered_sum(row_own, row_refs, k) + gathered_sum(col_own, col_refs, k))


def first_kernel(chips_n, vec_ref, row_degree, col_degree, row_own, col_own, *refs):
    row_refs, refs = refs[: chips_n - 1], refs[chips_n - 1 :]
    col_refs, (first_ref, rounded_ref, degree_ref) = refs[:-3], refs[-3:]
    group, _, width = rounded_ref.shape
    degree = row_degree[...] + col_degree[:group, :]
    for part in (*row_refs, *col_refs):
        degree += join_degree(part, group)
    degree = 0.5 * degree
    degree_ref[...] = degree
    for k, vec in enumerate(tiles_first(vec_ref, width)):
        symmetric = symmetric_part(row_own, row_refs, col_own, col_refs, k)
        image = degree[k : k + 1, :] * vec - symmetric
        first = (image - CENTER * vec) / HALF_WIDTH
        first_ref[:, k * width : (k + 1) * width] = first
        rounded_ref[k] = first.astype(BF16)


def filter_kernel(chips_n, start_ref, first_ref, degree_ref, row_own, col_own, *refs):
    row_refs, refs = refs[: chips_n - 1], refs[chips_n - 1 :]
    col_refs, (filtered_ref, rounded_ref) = refs[:-2], refs[-2:]
    width = rounded_ref.shape[2]
    for k, vec in enumerate(tiles_first(first_ref, width)):
        symmetric = symmetric_part(row_own, row_refs, col_own, col_refs, k)
        columns = slice(k * width, (k + 1) * width)
        image = degree_ref[k : k + 1, :] * vec - symmetric
        filtered = 2.0 * (image - CENTER * vec) / HALF_WIDTH - start_ref[:, columns]
        filtered_ref[:, columns] = filtered
        rounded_ref[k] = filtered.astype(BF16)


def gram_kernel(filtered_ref, degree_ref, gram_ref, both):
    vectors_n, width = filtered_ref.shape[0], degree_ref.shape[1]
    for k, vec in enumerate(tiles_first(filtered_ref, width)):
        columns = slice(k * width, (k + 1) * width)
        both[:vectors_n, columns] = vec
        both[vectors_n:, columns] = degree_ref[k : k + 1, :] * vec
    gram_ref[...] = lax.dot_general(
        filtered_ref[...], both[...], NT, precision=HIGHEST, preferred_element_type=F32
    )


def half_form_kernel(runs, table, tiles_ref, *refs):
    parts, (out_ref, panel) = refs[:-2], refs[-2:]
    width = panel.shape[2]
    fill(panel, parts, runs)
    for t in range(tiles_ref.shape[0]):
        out_ref[:, t * width : (t + 1) * width] = lax.dot_general(
            panel[table[1, t]], tiles_ref[t], NN, preferred_element_type=F32
        ).astype(BF16)


def form_kernel(runs, table, left, gram_ref, *refs):
    parts, (out_ref, panel, right) = refs[:-3], refs[-3:]
    _, vectors_n, width = panel.shape
    fill(panel, parts, runs)
    for t in range(right.shape[1] // width):
        right[:, t * width : (t + 1) * width] = panel[table[0, t]]
    form = lax.dot_general(left[...], right[...], NT, preferred_element_type=F32)
    projected = gram_ref[:, vectors_n:] - 0.5 * (form + form.T)
    row, col = square_index(vectors_n)
    packed = jnp.where(col >= row, gram_ref[:, :vectors_n], projected)
    diagonal = jnp.sum(jnp.where(row == col, projected, 0.0), 0, keepdims=True)
    half = vectors_n // 2
    out_ref[:half] = jnp.concatenate([packed[:half], packed[half:]], 1)
    diagonal = jnp.broadcast_to(diagonal, (8, vectors_n))
    out_ref[half:] = jnp.concatenate([diagonal, jnp.zeros_like(diagonal)], 1)


def square_index(n):
    return tuple(lax.broadcasted_iota(jnp.int32, (n, n), axis) for axis in (0, 1))


def inverse_factor(gram):
    n = gram.shape[0]
    row, col = square_index(n)
    table = jnp.concatenate([gram, jnp.where(row == col, 1.0, 0.0)], 1)
    bands = [table[i : i + 8] for i in range(0, n, 8)]
    shape = (8, 2 * n)
    line = lax.broadcasted_iota(jnp.int32, shape, 0)

    def spread(values, j):
        return jnp.broadcast_to(values[:, j : j + 1], shape)

    def pick(values, i):
        return jnp.broadcast_to(values[i : i + 1, :], shape)

    for at in range(n // 8):
        block = [spread(bands[at], 8 * at + c) for c in range(8)]
        forward, solved = bands[at], bands[at]
        solved_block = list(block)
        for s in range(8):
            scale = 1.0 / pick(block[s], s)
            below = jnp.where(line > s, block[s], 0.0) * scale
            above = jnp.where(line < s, solved_block[s] * scale, 0.0)
            both = below + above
            pivot_row = pick(forward, s)
            forward = forward - below * pivot_row
            solved = solved - both * pivot_row
            for c in range(s + 1, 8):
                pivot = pick(block[c], s)
                block[c] = block[c] - below * pivot
                solved_block[c] = solved_block[c] - both * pivot
        pivots = block[0]
        for s in range(1, 8):
            pivots = jnp.where(line == s, block[s], pivots)
        solved = solved / pivots
        bands[at] = forward / jnp.sqrt(pivots)
        for i in range(at + 1, n // 8):
            update = spread(bands[i], 8 * at) * pick(solved, 0)
            for c in range(1, 8):
                update = update + spread(bands[i], 8 * at + c) * pick(solved, c)
            bands[i] = bands[i] - update
    return jnp.concatenate(bands, 0)[:, n:]


def last_kernel(total_nodes, filtered_ref, *refs):
    parts, (ritz_ref, rayleigh_ref) = refs[:-2], refs[-2:]
    n = filtered_ref.shape[0]
    half = n // 2
    sums = tree_sum([part[...] for part in parts]) * (1.0 / total_nodes)
    packed = jnp.concatenate([sums[:half, :n], sums[:half, n:]], 0)
    row, col = square_index(n)
    upper = jnp.where(col > row, packed, 0.0)
    gram = jnp.where(col >= row, packed, 0.0) + upper.T
    lower = jnp.where(col < row, packed, 0.0)
    diagonal = jnp.broadcast_to(sums[half : half + 1, :n], (n, n))
    projected = lower + lower.T + jnp.where(row == col, diagonal, 0.0)
    inverse = inverse_factor(gram)

    def dot(a, b, dims):
        return lax.dot_general(a, b, dims, precision=HIGHEST, preferred_element_type=F32)

    half_way = dot(inverse, projected, NN)
    rayleigh_ref[...] = dot(half_way, inverse, NT)
    turned = dot(inverse, half_way, NT)
    ritz_ref[...] = dot(turned, dot(inverse, filtered_ref[...], NN), NN)


def tree_sum(parts):
    while len(parts) > 1:
        parts = [a + b for a, b in zip(parts[::2], parts[1::2])]
    return parts[0]


def local(tiles, tile_rows, tile_cols, start):
    tiles, tile_rows, tile_cols = tiles[0, 0], tile_rows[0, 0], tile_cols[0, 0]
    width = tiles.shape[-1]
    vectors_n, own_nodes = start.shape
    rows_n, cols_n = lax.axis_size("row"), lax.axis_size("col")
    chips_n = cols_n // 2
    total_nodes = own_nodes * rows_n * cols_n
    group = own_nodes // width
    spread = (vectors_n, tiles.shape[0] * width)

    rounded_shape = jax.ShapeDtypeStruct((group, vectors_n, width), BF16)
    vector_shape = jax.ShapeDtypeStruct((vectors_n, own_nodes), F32)
    degree_shape = jax.ShapeDtypeStruct((group, width), F32)

    late = 1
    levels = [rows_n >> i for i in range(1, rows_n.bit_length())]
    col_runs = [[(0, group)]]
    for d in levels:
        if len(col_runs) == 1:
            col_runs += [[(d * group, group)]]
            continue
        cut = group - late
        passed = [((p // group ^ d) * group + p % group, n) for run in col_runs[1:] for p, n in run]
        col_runs += [[(d * group, cut)], [(d * group + cut, late), *passed]]
    row_runs = [[((2 * d + core) * group, group)] for core in range(2) for d in range(chips_n)]
    runs = (col_runs, row_runs)
    def gather(rounded, first=()):
        held = [rounded]
        for d in levels:
            if len(held) == 1:
                held += [trade(rounded, "row", d)]
                continue
            near = trade(rounded[: group - late], "row", d)
            near, *passed = lax.optimization_barrier((near, *held[1:], *first))
            held[1:] = passed[: len(held) - 1]
            held += [near, trade(jnp.concatenate([rounded[group - late :], *held[1:]]), "row", d)]
        chips = [rounded, *exchange([rounded] * (chips_n - 1), "col", 2)]
        return held, chips + [trade(chip, "col", 1) for chip in chips]

    def apply(rounded, degree=()):
        kept, swap, col_own, col_send = products(tiles, table, *gather(rounded, degree), runs, degree)
        col_got = exchange(col_send, "row")
        row_own, *row_send = merge(kept, trade(swap, "col", 1), degree)
        if degree:
            own_degree, *row_send = row_send
        row_got = exchange(row_send, "col", 2)
        sums = [row_own, col_own, *row_got, *col_got]
        return [own_degree, degree[1], *sums] if degree else sums

    rounded = call(round_kernel, rounded_shape, [], 16, [start])
    meta = jnp.stack([lax.axis_index("row"), lax.axis_index("col"), chips_n]).astype(jnp.int32)
    *degree, table, tiles = call(
        functools.partial(degree_kernel, group),
        [jax.ShapeDtypeStruct((n * group, width), F32) for n in (cols_n, rows_n)]
        + [jax.ShapeDtypeStruct((3, tiles.shape[0]), jnp.int32)]
        + [jax.ShapeDtypeStruct(tiles.shape, BF16)],
        [],
        16,
        [meta, tile_rows, tile_cols, tiles],
        4 * tiles.size * DEGREE_ROWS,
        3,
        outs=[VMEM, VMEM, SMEM, VMEM],
    )
    first, rounded, degree = call(
        functools.partial(first_kernel, chips_n),
        [vector_shape, rounded_shape, degree_shape],
        [],
        24,
        [start, *apply(rounded, tuple(degree))],
    )
    filtered, rounded = call(
        functools.partial(filter_kernel, chips_n),
        [vector_shape, rounded_shape],
        [],
        24,
        [start, first, degree, *apply(rounded)],
    )
    gram = call(
        gram_kernel,
        jax.ShapeDtypeStruct((vectors_n, 2 * vectors_n), F32),
        [pltpu.VMEM((2 * vectors_n, own_nodes), F32)],
        16,
        [filtered, degree],
        24 * vectors_n * vectors_n * own_nodes,
    )
    col_parts, row_parts = gather(rounded, (gram,))
    left = call(
        functools.partial(half_form_kernel, runs[1]),
        jax.ShapeDtypeStruct(spread, BF16),
        [pltpu.VMEM((cols_n * group, vectors_n, width), BF16)],
        24,
        [table, tiles, *row_parts],
        2 * tiles.size * vectors_n,
        1,
    )
    sums = call(
        functools.partial(form_kernel, runs[0]),
        jax.ShapeDtypeStruct((vectors_n // 2 + 8, 2 * vectors_n), F32),
        [pltpu.VMEM((rows_n * group, vectors_n, width), BF16), pltpu.VMEM(spread, BF16)],
        24,
        [table, left, gram, *col_parts],
        2 * vectors_n * spread[0] * spread[1],
        1,
    )
    sums = sums + trade(sums, "col", 1)
    sums = tree_sum([sums, *exchange([sums] * (chips_n - 1), "col", 2)])
    return call(
        functools.partial(last_kernel, total_nodes),
        [vector_shape, jax.ShapeDtypeStruct((vectors_n, vectors_n), F32)],
        [],
        24,
        [filtered, sums, *exchange([sums] * (rows_n - 1), "row")],
    )


def solution(mesh):
    placed = (
        P("row", "col", None, None, None),
        P("row", "col", None),
        P("row", "col", None),
        P(None, ("row", "col")),
    )
    return jax.shard_map(
        local, mesh=mesh, in_specs=placed, out_specs=(P(None, ("row", "col")), P()), check_vma=False
    )
```

```python
import functools

import jax
import jax.numpy as jnp
from jax import lax
from jax.experimental import pallas as pl
from jax.experimental.pallas import tpu as pltpu
from jax.sharding import PartitionSpec as P

CENTER = 1.0
HALF_WIDTH = 0.5
HIGHEST = lax.Precision.HIGHEST
NT = (((1,), (1,)), ((), ()))
NN = (((1,), (0,)), ((), ()))
BF16 = jnp.bfloat16
F32 = jnp.float32
VMEM = pl.BlockSpec(memory_space=pltpu.VMEM)
SMEM = pl.BlockSpec(memory_space=pltpu.SMEM)
ANY = pl.BlockSpec(memory_space=pl.ANY)
DEGREE_ROWS = 16


def call(kernel, out_shape, scratch, limit, args, flops=0, smem=0, after=()):
    moved = sum(x.size * x.dtype.itemsize for x in args)
    return pl.pallas_call(
        lambda *refs: kernel(*refs[len(after) :]),
        out_shape=out_shape,
        in_specs=[ANY] * len(after) + [SMEM] * smem + [VMEM] * (len(args) - smem),
        out_specs=jax.tree.map(lambda _: VMEM, out_shape),
        scratch_shapes=scratch,
        compiler_params=pltpu.CompilerParams(vmem_limit_bytes=limit * 2**20),
        cost_estimate=pl.CostEstimate(flops=flops, bytes_accessed=moved, transcendentals=0),
    )(*after, *args)


def trade(part, axis, d):
    n = lax.axis_size(axis)
    return lax.ppermute(part, axis, [(i, i ^ d) for i in range(n)])


def exchange(parts, axis, step=1):
    far_first = [trade(part, axis, step * d) for d, part in reversed(list(enumerate(parts, 1)))]
    return far_first[::-1]


def tiles_first(ref, width):
    return [ref[:, k * width : (k + 1) * width] for k in range(ref.shape[1] // width)]


def round_kernel(vec_ref, out_ref):
    for k, piece in enumerate(tiles_first(vec_ref, out_ref.shape[2])):
        out_ref[k] = piece.astype(BF16)


def split_degree(sums):
    high = sums.astype(BF16).astype(F32)
    return jnp.concatenate([high, sums - high], 0).astype(BF16)


def join_degree(payload, group):
    parts = payload[payload.shape[0] - 2 * group :, :].astype(F32)
    return parts[:group] + parts[group:]


def fill(panel, parts, runs):
    for part, places in zip(parts, runs):
        at = 0
        for place, count in places:
            panel[place : place + count, : part.shape[1], :] = part[at : at + count]
            at += count


def table_kernel(group, meta, tile_rows, tile_cols, table):
    for t in range(table.shape[1]):
        row, col = tile_rows[t], tile_cols[t]
        apart = lax.div(row, group) ^ meta[1]
        halves = lax.rem(apart, 2) * meta[2] + lax.div(apart, 2)
        inside = lax.rem(row, group)
        table[0, t] = (lax.div(col, group) ^ meta[0]) * group + lax.rem(col, group)
        table[1, t] = apart * group + inside
        table[2, t] = halves * group + inside


def fill_ones(panel, vectors_n):
    rows = panel.shape[1] - vectors_n
    if rows:
        panel[:, vectors_n:, :] = jnp.ones((panel.shape[0], rows, panel.shape[2]), BF16)


def degree_of(total, start, group, vectors_n):
    return jnp.concatenate(
        [total[start + k, vectors_n : vectors_n + 1, :] for k in range(group)], 0
    )


def column_kernel(runs, table, tiles_ref, *refs):
    parts, (own_ref, *send_refs, panel, total) = refs[: len(runs)], refs[len(runs) :]
    group, vectors_n, _ = parts[0].shape
    fill(panel, parts, runs)
    fill_ones(panel, vectors_n)
    total[...] = jnp.zeros_like(total)
    for t in range(tiles_ref.shape[0]):
        total[table[0, t]] += lax.dot_general(
            panel[table[1, t]], tiles_ref[t], NN, preferred_element_type=F32
        )
    own_ref[...] = total[:group]
    for d, send in enumerate(send_refs, 1):
        round_sums(send, total, d * group, group, vectors_n)


def row_kernel(runs, table, tiles_ref, *refs):
    parts, (total, swap_ref, panel) = refs[: len(runs)], refs[len(runs) :]
    group, vectors_n, _ = parts[0].shape
    half = swap_ref.shape[0]
    fill(panel, parts, runs)
    fill_ones(panel, vectors_n)
    total[...] = jnp.zeros_like(total)
    for t in range(tiles_ref.shape[0]):
        total[table[2, t]] += lax.dot_general(
            panel[table[0, t]], tiles_ref[t], NT, preferred_element_type=F32
        )
    for d in range(half):
        round_sums(swap_ref.at[d], total, (half + d) * group, group, vectors_n)


def round_sums(send, total, start, group, vectors_n):
    for k in range(group):
        send[k * vectors_n : (k + 1) * vectors_n, :] = total[start + k, :vectors_n, :].astype(BF16)
    if total.shape[1] > vectors_n:
        send[group * vectors_n :, :] = split_degree(degree_of(total, start, group, vectors_n))


def products(tiles, table, col_parts, row_parts, runs, degree):
    group, vectors_n, width = col_parts[0].shape
    half = len(row_parts) // 2
    rows_n = max(place + count for run in runs[0] for place, count in run) // group
    rows = group * vectors_n + (2 * group if degree else 0)
    height = vectors_n + (DEGREE_ROWS if degree else 0)
    send_shape = jax.ShapeDtypeStruct((rows, width), BF16)
    flops = 2 * tiles.size * vectors_n

    def panel(count):
        return pltpu.VMEM((count * group, height, width), BF16)

    col_own, *col_send = call(
        functools.partial(column_kernel, runs[1]),
        [jax.ShapeDtypeStruct((group, height, width), F32)] + [send_shape] * (rows_n - 1),
        [panel(2 * half), pltpu.VMEM((rows_n * group, height, width), F32)],
        24,
        [table, tiles, *row_parts],
        flops,
        1,
    )
    kept, swap = call(
        functools.partial(row_kernel, runs[0]),
        [
            jax.ShapeDtypeStruct((2 * half * group, height, width), F32),
            jax.ShapeDtypeStruct((half, rows, width), BF16),
        ],
        [panel(rows_n)],
        24,
        [table, tiles, *col_parts],
        flops,
        1,
        [col_own],
    )
    return kept, swap, col_own, col_send


def merge_kernel(degree, vectors_n, kept, got, own_ref, *send_refs):
    if degree:
        own_degree, *send_refs = send_refs
    group = own_ref.shape[0]
    for k in range(group):
        rows = slice(k * vectors_n, (k + 1) * vectors_n)
        own_ref[k] = kept[k, :vectors_n, :] + got[0, rows, :].astype(F32)
        for d, send in enumerate(send_refs, 1):
            both = kept[d * group + k, :vectors_n, :] + got[d, rows, :].astype(F32)
            send[rows, :] = both.astype(BF16)
    if degree:
        for d in range(got.shape[0]):
            sums = degree_of(kept, d * group, group, vectors_n) + join_degree(got.at[d], group)
            if d:
                send_refs[d - 1][group * vectors_n :, :] = split_degree(sums)
            else:
                own_degree[...] = sums


def merge(kept, got, vectors_n, degree):
    half, width = got.shape[0], got.shape[2]
    group = kept.shape[0] // (2 * half)
    out_shape = [jax.ShapeDtypeStruct((group, vectors_n, width), F32)]
    if degree:
        out_shape += [jax.ShapeDtypeStruct((group, width), F32)]
    out_shape += [jax.ShapeDtypeStruct(got.shape[1:], BF16)] * (half - 1)
    kernel = functools.partial(merge_kernel, degree, vectors_n)
    return call(kernel, out_shape, [], 24, [kept, got])


def gathered_sum(own, received, k, vectors_n):
    total = own[k, :vectors_n, :]
    rows = slice(k * vectors_n, (k + 1) * vectors_n)
    for part in received:
        total = total + part[rows, :].astype(F32)
    return total


def symmetric_part(row_own, row_refs, col_own, col_refs, k, vectors_n):
    return 0.5 * (
        gathered_sum(row_own, row_refs, k, vectors_n)
        + gathered_sum(col_own, col_refs, k, vectors_n)
    )


def first_kernel(chips_n, vec_ref, row_degree, row_own, col_own, *refs):
    row_refs, refs = refs[: chips_n - 1], refs[chips_n - 1 :]
    col_refs, (first_ref, rounded_ref, degree_ref) = refs[:-3], refs[-3:]
    group, vectors_n, width = rounded_ref.shape
    degree = row_degree[...] + degree_of(col_own, 0, group, vectors_n)
    for part in (*row_refs, *col_refs):
        degree += join_degree(part, group)
    degree = 0.5 * degree
    degree_ref[...] = degree
    for k, vec in enumerate(tiles_first(vec_ref, width)):
        symmetric = symmetric_part(row_own, row_refs, col_own, col_refs, k, vectors_n)
        image = degree[k : k + 1, :] * vec - symmetric
        first = (image - CENTER * vec) / HALF_WIDTH
        first_ref[:, k * width : (k + 1) * width] = first
        rounded_ref[k] = first.astype(BF16)


def filter_kernel(chips_n, start_ref, first_ref, degree_ref, row_own, col_own, *refs):
    row_refs, refs = refs[: chips_n - 1], refs[chips_n - 1 :]
    col_refs, (filtered_ref, rounded_ref) = refs[:-2], refs[-2:]
    _, vectors_n, width = rounded_ref.shape
    for k, vec in enumerate(tiles_first(first_ref, width)):
        symmetric = symmetric_part(row_own, row_refs, col_own, col_refs, k, vectors_n)
        columns = slice(k * width, (k + 1) * width)
        image = degree_ref[k : k + 1, :] * vec - symmetric
        filtered = 2.0 * (image - CENTER * vec) / HALF_WIDTH - start_ref[:, columns]
        filtered_ref[:, columns] = filtered
        rounded_ref[k] = filtered.astype(BF16)


def gram_kernel(filtered_ref, degree_ref, gram_ref, both):
    vectors_n, width = filtered_ref.shape[0], degree_ref.shape[1]
    for k, vec in enumerate(tiles_first(filtered_ref, width)):
        columns = slice(k * width, (k + 1) * width)
        both[:vectors_n, columns] = vec
        both[vectors_n:, columns] = degree_ref[k : k + 1, :] * vec
    gram_ref[...] = lax.dot_general(
        filtered_ref[...], both[...], NT, precision=HIGHEST, preferred_element_type=F32
    )


def half_form_kernel(runs, table, tiles_ref, *refs):
    parts, (out_ref, panel) = refs[:-2], refs[-2:]
    width = panel.shape[2]
    fill(panel, parts, runs)
    for t in range(tiles_ref.shape[0]):
        out_ref[:, t * width : (t + 1) * width] = lax.dot_general(
            panel[table[1, t]], tiles_ref[t], NN, preferred_element_type=F32
        ).astype(BF16)


def form_kernel(runs, table, left, gram_ref, *refs):
    parts, (out_ref, panel, right) = refs[:-3], refs[-3:]
    _, vectors_n, width = panel.shape
    fill(panel, parts, runs)
    for t in range(right.shape[1] // width):
        right[:, t * width : (t + 1) * width] = panel[table[0, t]]
    form = lax.dot_general(left[...], right[...], NT, preferred_element_type=F32)
    projected = gram_ref[:, vectors_n:] - 0.5 * (form + form.T)
    row, col = square_index(vectors_n)
    packed = jnp.where(col >= row, gram_ref[:, :vectors_n], projected)
    diagonal = jnp.sum(jnp.where(row == col, projected, 0.0), 0, keepdims=True)
    half = vectors_n // 2
    out_ref[:half] = jnp.concatenate([packed[:half], packed[half:]], 1)
    diagonal = jnp.broadcast_to(diagonal, (8, vectors_n))
    out_ref[half:] = jnp.concatenate([diagonal, jnp.zeros_like(diagonal)], 1)


def square_index(n):
    return tuple(lax.broadcasted_iota(jnp.int32, (n, n), axis) for axis in (0, 1))


def inverse_factor(gram):
    n = gram.shape[0]
    row, col = square_index(n)
    table = jnp.concatenate([gram, jnp.where(row == col, 1.0, 0.0)], 1)
    bands = [table[i : i + 8] for i in range(0, n, 8)]
    shape = (8, 2 * n)
    line = lax.broadcasted_iota(jnp.int32, shape, 0)

    def spread(values, j):
        return jnp.broadcast_to(values[:, j : j + 1], shape)

    def pick(values, i):
        return jnp.broadcast_to(values[i : i + 1, :], shape)

    for at in range(n // 8):
        block = [spread(bands[at], 8 * at + c) for c in range(8)]
        forward, solved = bands[at], bands[at]
        solved_block = list(block)
        for s in range(8):
            scale = 1.0 / pick(block[s], s)
            below = jnp.where(line > s, block[s], 0.0) * scale
            above = jnp.where(line < s, solved_block[s] * scale, 0.0)
            both = below + above
            pivot_row = pick(forward, s)
            forward = forward - below * pivot_row
            solved = solved - both * pivot_row
            for c in range(s + 1, 8):
                pivot = pick(block[c], s)
                block[c] = block[c] - below * pivot
                solved_block[c] = solved_block[c] - both * pivot
        pivots = block[0]
        for s in range(1, 8):
            pivots = jnp.where(line == s, block[s], pivots)
        solved = solved / pivots
        bands[at] = forward / jnp.sqrt(pivots)
        for i in range(at + 1, n // 8):
            update = spread(bands[i], 8 * at) * pick(solved, 0)
            for c in range(1, 8):
                update = update + spread(bands[i], 8 * at + c) * pick(solved, c)
            bands[i] = bands[i] - update
    return jnp.concatenate(bands, 0)[:, n:]


def last_kernel(total_nodes, filtered_ref, *refs):
    parts, (ritz_ref, rayleigh_ref) = refs[:-2], refs[-2:]
    n = filtered_ref.shape[0]
    half = n // 2
    sums = tree_sum([part[...] for part in parts]) * (1.0 / total_nodes)
    packed = jnp.concatenate([sums[:half, :n], sums[:half, n:]], 0)
    row, col = square_index(n)
    upper = jnp.where(col > row, packed, 0.0)
    gram = jnp.where(col >= row, packed, 0.0) + upper.T
    lower = jnp.where(col < row, packed, 0.0)
    diagonal = jnp.broadcast_to(sums[half : half + 1, :n], (n, n))
    projected = lower + lower.T + jnp.where(row == col, diagonal, 0.0)
    inverse = inverse_factor(gram)

    def dot(a, b, dims):
        return lax.dot_general(a, b, dims, precision=HIGHEST, preferred_element_type=F32)

    half_way = dot(inverse, projected, NN)
    rayleigh_ref[...] = dot(half_way, inverse, NT)
    turned = dot(inverse, half_way, NT)
    ritz_ref[...] = dot(turned, dot(inverse, filtered_ref[...], NN), NN)


def tree_sum(parts):
    while len(parts) > 1:
        parts = [a + b for a, b in zip(parts[::2], parts[1::2])]
    return parts[0]


def local(tiles, tile_rows, tile_cols, start):
    tiles, tile_rows, tile_cols = tiles[0, 0], tile_rows[0, 0], tile_cols[0, 0]
    width = tiles.shape[-1]
    vectors_n, own_nodes = start.shape
    rows_n, cols_n = lax.axis_size("row"), lax.axis_size("col")
    chips_n = cols_n // 2
    total_nodes = own_nodes * rows_n * cols_n
    group = own_nodes // width
    spread = (vectors_n, tiles.shape[0] * width)

    rounded_shape = jax.ShapeDtypeStruct((group, vectors_n, width), BF16)
    vector_shape = jax.ShapeDtypeStruct((vectors_n, own_nodes), F32)
    degree_shape = jax.ShapeDtypeStruct((group, width), F32)

    late = 1
    levels = [rows_n >> i for i in range(1, rows_n.bit_length())]
    col_runs = [[(0, group)]]
    for d in levels:
        if len(col_runs) == 1:
            col_runs += [[(d * group, group)]]
            continue
        cut = group - late
        passed = [((p // group ^ d) * group + p % group, n) for run in col_runs[1:] for p, n in run]
        col_runs += [[(d * group, cut)], [(d * group + cut, late), *passed]]
    row_runs = [[((2 * d + core) * group, group)] for core in range(2) for d in range(chips_n)]
    runs = (col_runs, row_runs)
    def gather(rounded, first=()):
        held = [rounded]
        for d in levels:
            if len(held) == 1:
                held += [trade(rounded, "row", d)]
                continue
            near = trade(rounded[: group - late], "row", d)
            near, *passed = lax.optimization_barrier((near, *held[1:], *first))
            held[1:] = passed[: len(held) - 1]
            held += [near, trade(jnp.concatenate([rounded[group - late :], *held[1:]]), "row", d)]
        chips = [rounded, *exchange([rounded] * (chips_n - 1), "col", 2)]
        return held, chips + [trade(chip, "col", 1) for chip in chips]

    def apply(rounded, table, degree, first=()):
        kept, swap, col_own, col_send = products(
            tiles, table, *gather(rounded, first), runs, degree
        )
        col_got = exchange(col_send, "row")
        row_own, *row_send = merge(kept, trade(swap, "col", 1), vectors_n, degree)
        row_degree = row_send[:1] if degree else []
        row_got = exchange(row_send[len(row_degree) :], "col", 2)
        return [*row_degree, row_own, col_own, *row_got, *col_got]

    rounded = call(round_kernel, rounded_shape, [], 16, [start])
    meta = jnp.stack([lax.axis_index("row"), lax.axis_index("col"), chips_n]).astype(jnp.int32)
    table = pl.pallas_call(
        functools.partial(table_kernel, group),
        out_shape=jax.ShapeDtypeStruct((3, tiles.shape[0]), jnp.int32),
        in_specs=[SMEM] * 3,
        out_specs=SMEM,
    )(meta, tile_rows, tile_cols)
    first, rounded, degree = call(
        functools.partial(first_kernel, chips_n),
        [vector_shape, rounded_shape, degree_shape],
        [],
        24,
        [start, *apply(rounded, table, True, (table,))],
    )
    filtered, rounded = call(
        functools.partial(filter_kernel, chips_n),
        [vector_shape, rounded_shape],
        [],
        24,
        [start, first, degree, *apply(rounded, table, False)],
    )
    gram = call(
        gram_kernel,
        jax.ShapeDtypeStruct((vectors_n, 2 * vectors_n), F32),
        [pltpu.VMEM((2 * vectors_n, own_nodes), F32)],
        16,
        [filtered, degree],
        24 * vectors_n * vectors_n * own_nodes,
    )
    col_parts, row_parts = gather(rounded, (gram,))
    left = call(
        functools.partial(half_form_kernel, runs[1]),
        jax.ShapeDtypeStruct(spread, BF16),
        [pltpu.VMEM((cols_n * group, vectors_n, width), BF16)],
        24,
        [table, tiles, *row_parts],
        2 * tiles.size * vectors_n,
        1,
    )
    sums = call(
        functools.partial(form_kernel, runs[0]),
        jax.ShapeDtypeStruct((vectors_n // 2 + 8, 2 * vectors_n), F32),
        [pltpu.VMEM((rows_n * group, vectors_n, width), BF16), pltpu.VMEM(spread, BF16)],
        24,
        [table, left, gram, *col_parts],
        2 * vectors_n * spread[0] * spread[1],
        1,
    )
    sums = sums + trade(sums, "col", 1)
    sums = tree_sum([sums, *exchange([sums] * (chips_n - 1), "col", 2)])
    return call(
        functools.partial(last_kernel, total_nodes),
        [vector_shape, jax.ShapeDtypeStruct((vectors_n, vectors_n), F32)],
        [],
        24,
        [filtered, sums, *exchange([sums] * (rows_n - 1), "row")],
    )


def solution(mesh):
    placed = (
        P("row", "col", None, None, None),
        P("row", "col", None),
        P("row", "col", None),
        P(None, ("row", "col")),
    )
    return jax.shard_map(
        local, mesh=mesh, in_specs=placed, out_specs=(P(None, ("row", "col")), P()), check_vma=False
    )
```

```python
import functools

import jax
import jax.numpy as jnp
from jax import lax
from jax.experimental import pallas as pl
from jax.experimental.pallas import tpu as pltpu
from jax.sharding import PartitionSpec as P

CENTER = 1.0
HALF_WIDTH = 0.5
HIGHEST = lax.Precision.HIGHEST
NT = (((1,), (1,)), ((), ()))
NN = (((1,), (0,)), ((), ()))
BF16 = jnp.bfloat16
F32 = jnp.float32
VMEM = pl.BlockSpec(memory_space=pltpu.VMEM)
SMEM = pl.BlockSpec(memory_space=pltpu.SMEM)
ANY = pl.BlockSpec(memory_space=pl.ANY)
DEGREE_ROWS = 16


def call(kernel, out_shape, scratch, limit, args, flops=0, smem=0, after=(), aliases={}):
    moved = sum(x.size * x.dtype.itemsize for x in args)
    return pl.pallas_call(
        lambda *refs: kernel(*refs[len(after) :]),
        out_shape=jax.tree.map(lambda x: jax.ShapeDtypeStruct(x.shape, x.dtype), out_shape),
        in_specs=[ANY] * len(after) + [SMEM] * smem + [VMEM] * (len(args) - smem),
        out_specs=jax.tree.map(lambda _: VMEM, out_shape),
        scratch_shapes=scratch,
        input_output_aliases=aliases,
        compiler_params=pltpu.CompilerParams(vmem_limit_bytes=limit * 2**20),
        cost_estimate=pl.CostEstimate(flops=flops, bytes_accessed=moved, transcendentals=0),
    )(*after, *args)


def trade(part, axis, d):
    n = lax.axis_size(axis)
    return lax.ppermute(part, axis, [(i, i ^ d) for i in range(n)])


def exchange(parts, axis, step=1):
    far_first = [trade(part, axis, step * d) for d, part in reversed(list(enumerate(parts, 1)))]
    return far_first[::-1]


def tiles_first(ref, width):
    return [ref[:, k * width : (k + 1) * width] for k in range(ref.shape[1] // width)]


def round_kernel(vec_ref, out_ref):
    for k, piece in enumerate(tiles_first(vec_ref, out_ref.shape[2])):
        out_ref[k] = piece.astype(BF16)


def split_degree(sums):
    high = sums.astype(BF16).astype(F32)
    return jnp.concatenate([high, sums - high], 0).astype(BF16)


def join_degree(payload, group):
    parts = payload[payload.shape[0] - 2 * group :, :].astype(F32)
    return parts[:group] + parts[group:]


def fill(panel, parts, runs):
    for part, places in zip(parts, runs):
        at = 0
        for place, count in places:
            panel[place : place + count, : part.shape[1], :] = part[at : at + count]
            at += count


def table_kernel(group, meta, rows_ref, cols_ref, table):
    rows, cols = rows_ref[...], cols_ref[...]
    apart = lax.div(rows, group) ^ meta[1]
    halves = lax.rem(apart, 2) * meta[2] + lax.div(apart, 2)
    inside = lax.rem(rows, group)
    table[0:1, :] = (lax.div(cols, group) ^ meta[0]) * group + lax.rem(cols, group)
    table[1:2, :] = apart * group + inside
    table[2:3, :] = halves * group + inside


def fill_ones(panel, vectors_n):
    rows = panel.shape[1] - vectors_n
    if rows:
        panel[:, vectors_n:, :] = jnp.ones((panel.shape[0], rows, panel.shape[2]), BF16)


def degree_of(total, start, group, vectors_n):
    return jnp.concatenate(
        [total[start + k, vectors_n : vectors_n + 1, :] for k in range(group)], 0
    )


def zero_kernel(*refs):
    for ref in refs:
        ref[...] = jnp.zeros_like(ref)


def column_kernel(runs, table, tiles_ref, *refs):
    parts, (_, own_ref, total, *send_refs, panel) = refs[: len(runs)], refs[len(runs) :]
    group, vectors_n, _ = parts[0].shape
    fill(panel, parts, runs)
    fill_ones(panel, vectors_n)
    for t in range(tiles_ref.shape[0]):
        total[table[0, t]] += lax.dot_general(
            panel[table[1, t]], tiles_ref[t], NN, preferred_element_type=F32
        )
    own_ref[...] = total[:group]
    for d, send in enumerate(send_refs, 1):
        round_sums(send, total, d * group, group, vectors_n)


def row_kernel(runs, table, tiles_ref, *refs):
    parts, (_, total, swap_ref, panel) = refs[: len(runs)], refs[len(runs) :]
    group, vectors_n, _ = parts[0].shape
    half = swap_ref.shape[0]
    fill(panel, parts, runs)
    fill_ones(panel, vectors_n)
    for t in range(tiles_ref.shape[0]):
        total[table[2, t]] += lax.dot_general(
            panel[table[0, t]], tiles_ref[t], NT, preferred_element_type=F32
        )
    for d in range(half):
        round_sums(swap_ref.at[d], total, (half + d) * group, group, vectors_n)


def round_sums(send, total, start, group, vectors_n):
    for k in range(group):
        send[k * vectors_n : (k + 1) * vectors_n, :] = total[start + k, :vectors_n, :].astype(BF16)
    if total.shape[1] > vectors_n:
        send[group * vectors_n :, :] = split_degree(degree_of(total, start, group, vectors_n))


def products(tiles, table, col_parts, row_parts, zeros, runs, degree):
    group, vectors_n, width = col_parts[0].shape
    half = len(row_parts) // 2
    rows_n = max(place + count for run in runs[0] for place, count in run) // group
    rows = group * vectors_n + (2 * group if degree else 0)
    height = vectors_n + (DEGREE_ROWS if degree else 0)
    send_shape = jax.ShapeDtypeStruct((rows, width), BF16)
    flops = 2 * tiles.size * vectors_n

    def panel(count):
        return pltpu.VMEM((count * group, height, width), BF16)

    col_own, _, *col_send = call(
        functools.partial(column_kernel, runs[1]),
        [jax.ShapeDtypeStruct((group, height, width), F32), zeros[1]] + [send_shape] * (rows_n - 1),
        [panel(2 * half)],
        24,
        [table, tiles, *row_parts, zeros[1]],
        flops,
        1,
        (),
        {2 + len(row_parts): 1},
    )
    kept, swap = call(
        functools.partial(row_kernel, runs[0]),
        [zeros[0], jax.ShapeDtypeStruct((half, rows, width), BF16)],
        [panel(rows_n)],
        24,
        [table, tiles, *col_parts, zeros[0]],
        flops,
        1,
        [col_own],
        {3 + len(col_parts): 0},
    )
    return kept, swap, col_own, col_send


def merge_kernel(degree, vectors_n, kept, got, own_ref, *send_refs):
    if degree:
        own_degree, *send_refs = send_refs
    group = own_ref.shape[0]
    for k in range(group):
        rows = slice(k * vectors_n, (k + 1) * vectors_n)
        own_ref[k] = kept[k, :vectors_n, :] + got[0, rows, :].astype(F32)
        for d, send in enumerate(send_refs, 1):
            both = kept[d * group + k, :vectors_n, :] + got[d, rows, :].astype(F32)
            send[rows, :] = both.astype(BF16)
    if degree:
        for d in range(got.shape[0]):
            sums = degree_of(kept, d * group, group, vectors_n) + join_degree(got.at[d], group)
            if d:
                send_refs[d - 1][group * vectors_n :, :] = split_degree(sums)
            else:
                own_degree[...] = sums


def merge(kept, got, vectors_n, degree):
    half, width = got.shape[0], got.shape[2]
    group = kept.shape[0] // (2 * half)
    out_shape = [jax.ShapeDtypeStruct((group, vectors_n, width), F32)]
    if degree:
        out_shape += [jax.ShapeDtypeStruct((group, width), F32)]
    out_shape += [jax.ShapeDtypeStruct(got.shape[1:], BF16)] * (half - 1)
    kernel = functools.partial(merge_kernel, degree, vectors_n)
    return call(kernel, out_shape, [], 24, [kept, got])


def gathered_sum(own, received, k, vectors_n):
    total = own[k, :vectors_n, :]
    rows = slice(k * vectors_n, (k + 1) * vectors_n)
    for part in received:
        total = total + part[rows, :].astype(F32)
    return total


def symmetric_part(row_own, row_refs, col_own, col_refs, k, vectors_n):
    return 0.5 * (
        gathered_sum(row_own, row_refs, k, vectors_n)
        + gathered_sum(col_own, col_refs, k, vectors_n)
    )


def first_kernel(chips_n, vec_ref, row_degree, row_own, col_own, *refs):
    row_refs, refs = refs[: chips_n - 1], refs[chips_n - 1 :]
    col_refs, (first_ref, rounded_ref, degree_ref) = refs[:-3], refs[-3:]
    group, vectors_n, width = rounded_ref.shape
    degree = row_degree[...] + degree_of(col_own, 0, group, vectors_n)
    for part in (*row_refs, *col_refs):
        degree += join_degree(part, group)
    degree = 0.5 * degree
    degree_ref[...] = degree
    for k, vec in enumerate(tiles_first(vec_ref, width)):
        symmetric = symmetric_part(row_own, row_refs, col_own, col_refs, k, vectors_n)
        image = degree[k : k + 1, :] * vec - symmetric
        first = (image - CENTER * vec) / HALF_WIDTH
        first_ref[:, k * width : (k + 1) * width] = first
        rounded_ref[k] = first.astype(BF16)


def filter_kernel(chips_n, start_ref, first_ref, degree_ref, row_own, col_own, *refs):
    row_refs, refs = refs[: chips_n - 1], refs[chips_n - 1 :]
    col_refs, (filtered_ref, rounded_ref) = refs[:-2], refs[-2:]
    _, vectors_n, width = rounded_ref.shape
    for k, vec in enumerate(tiles_first(first_ref, width)):
        symmetric = symmetric_part(row_own, row_refs, col_own, col_refs, k, vectors_n)
        columns = slice(k * width, (k + 1) * width)
        image = degree_ref[k : k + 1, :] * vec - symmetric
        filtered = 2.0 * (image - CENTER * vec) / HALF_WIDTH - start_ref[:, columns]
        filtered_ref[:, columns] = filtered
        rounded_ref[k] = filtered.astype(BF16)


def gram_kernel(filtered_ref, degree_ref, gram_ref, both):
    vectors_n, width = filtered_ref.shape[0], degree_ref.shape[1]
    for k, vec in enumerate(tiles_first(filtered_ref, width)):
        columns = slice(k * width, (k + 1) * width)
        both[:vectors_n, columns] = vec
        both[vectors_n:, columns] = degree_ref[k : k + 1, :] * vec
    gram_ref[...] = lax.dot_general(
        filtered_ref[...], both[...], NT, precision=HIGHEST, preferred_element_type=F32
    )


def half_form_kernel(runs, table, tiles_ref, *refs):
    parts, (out_ref, panel) = refs[:-2], refs[-2:]
    width = panel.shape[2]
    fill(panel, parts, runs)
    for t in range(tiles_ref.shape[0]):
        out_ref[:, t * width : (t + 1) * width] = lax.dot_general(
            panel[table[1, t]], tiles_ref[t], NN, preferred_element_type=F32
        ).astype(BF16)


def form_kernel(runs, table, left, gram_ref, *refs):
    parts, (out_ref, panel, right) = refs[:-3], refs[-3:]
    _, vectors_n, width = panel.shape
    fill(panel, parts, runs)
    for t in range(right.shape[1] // width):
        right[:, t * width : (t + 1) * width] = panel[table[0, t]]
    form = lax.dot_general(left[...], right[...], NT, preferred_element_type=F32)
    projected = gram_ref[:, vectors_n:] - 0.5 * (form + form.T)
    row, col = square_index(vectors_n)
    packed = jnp.where(col >= row, gram_ref[:, :vectors_n], projected)
    diagonal = jnp.sum(jnp.where(row == col, projected, 0.0), 0, keepdims=True)
    half = vectors_n // 2
    out_ref[:half] = jnp.concatenate([packed[:half], packed[half:]], 1)
    diagonal = jnp.broadcast_to(diagonal, (8, vectors_n))
    out_ref[half:] = jnp.concatenate([diagonal, jnp.zeros_like(diagonal)], 1)


def square_index(n):
    return tuple(lax.broadcasted_iota(jnp.int32, (n, n), axis) for axis in (0, 1))


def inverse_factor(gram):
    n = gram.shape[0]
    row, col = square_index(n)
    table = jnp.concatenate([gram, jnp.where(row == col, 1.0, 0.0)], 1)
    bands = [table[i : i + 8] for i in range(0, n, 8)]
    shape = (8, 2 * n)
    line = lax.broadcasted_iota(jnp.int32, shape, 0)

    def spread(values, j):
        return jnp.broadcast_to(values[:, j : j + 1], shape)

    def pick(values, i):
        return jnp.broadcast_to(values[i : i + 1, :], shape)

    for at in range(n // 8):
        block = [spread(bands[at], 8 * at + c) for c in range(8)]
        forward, solved = bands[at], bands[at]
        solved_block = list(block)
        for s in range(8):
            scale = 1.0 / pick(block[s], s)
            below = jnp.where(line > s, block[s], 0.0) * scale
            above = jnp.where(line < s, solved_block[s] * scale, 0.0)
            both = below + above
            pivot_row = pick(forward, s)
            forward = forward - below * pivot_row
            solved = solved - both * pivot_row
            for c in range(s + 1, 8):
                pivot = pick(block[c], s)
                block[c] = block[c] - below * pivot
                solved_block[c] = solved_block[c] - both * pivot
        pivots = block[0]
        for s in range(1, 8):
            pivots = jnp.where(line == s, block[s], pivots)
        solved = solved / pivots
        bands[at] = forward / jnp.sqrt(pivots)
        for i in range(at + 1, n // 8):
            update = spread(bands[i], 8 * at) * pick(solved, 0)
            for c in range(1, 8):
                update = update + spread(bands[i], 8 * at + c) * pick(solved, c)
            bands[i] = bands[i] - update
    return jnp.concatenate(bands, 0)[:, n:]


def last_kernel(total_nodes, filtered_ref, *refs):
    parts, (ritz_ref, rayleigh_ref) = refs[:-2], refs[-2:]
    n = filtered_ref.shape[0]
    half = n // 2
    sums = tree_sum([part[...] for part in parts]) * (1.0 / total_nodes)
    packed = jnp.concatenate([sums[:half, :n], sums[:half, n:]], 0)
    row, col = square_index(n)
    upper = jnp.where(col > row, packed, 0.0)
    gram = jnp.where(col >= row, packed, 0.0) + upper.T
    lower = jnp.where(col < row, packed, 0.0)
    diagonal = jnp.broadcast_to(sums[half : half + 1, :n], (n, n))
    projected = lower + lower.T + jnp.where(row == col, diagonal, 0.0)
    inverse = inverse_factor(gram)

    def dot(a, b, dims, precision=HIGHEST):
        return lax.dot_general(a, b, dims, precision=precision, preferred_element_type=F32)

    half_way = dot(inverse, projected, NN)
    rayleigh_ref[...] = dot(half_way, inverse, NT)
    turned = dot(inverse, half_way, NT)
    block = dot(inverse, filtered_ref[...], NN, lax.Precision.HIGH)
    ritz_ref[...] = dot(turned, block, NN, lax.Precision.HIGH)


def tree_sum(parts):
    while len(parts) > 1:
        parts = [a + b for a, b in zip(parts[::2], parts[1::2])]
    return parts[0]


def local(tiles, tile_rows, tile_cols, start):
    tiles, tile_rows, tile_cols = tiles[0, 0], tile_rows[0, 0], tile_cols[0, 0]
    width = tiles.shape[-1]
    vectors_n, own_nodes = start.shape
    rows_n, cols_n = lax.axis_size("row"), lax.axis_size("col")
    chips_n = cols_n // 2
    total_nodes = own_nodes * rows_n * cols_n
    group = own_nodes // width
    spread = (vectors_n, tiles.shape[0] * width)

    rounded_shape = jax.ShapeDtypeStruct((group, vectors_n, width), BF16)
    vector_shape = jax.ShapeDtypeStruct((vectors_n, own_nodes), F32)
    degree_shape = jax.ShapeDtypeStruct((group, width), F32)

    late = 1
    levels = [rows_n >> i for i in range(1, rows_n.bit_length())]
    col_runs = [[(0, group)]]
    for d in levels:
        if len(col_runs) == 1:
            col_runs += [[(d * group, group)]]
            continue
        cut = group - late
        passed = [((p // group ^ d) * group + p % group, n) for run in col_runs[1:] for p, n in run]
        col_runs += [[(d * group, cut)], [(d * group + cut, late), *passed]]
    chip_order = [0, *range(chips_n - 1, 0, -1)]
    row_runs = [[((2 * d + core) * group, group)] for core in range(2) for d in chip_order]
    runs = (col_runs, row_runs)
    def gather(rounded, first=()):
        held = [rounded]
        for d in levels:
            if len(held) == 1:
                held += [trade(rounded, "row", d)]
                continue
            near = trade(rounded[: group - late], "row", d)
            near, *passed = lax.optimization_barrier((near, *held[1:], *first))
            held[1:] = passed[: len(held) - 1]
            held += [near, trade(jnp.concatenate([rounded[group - late :], *held[1:]]), "row", d)]
        chips = [rounded, *exchange([rounded] * (chips_n - 1), "col", 2)[::-1]]
        return held, chips + [trade(chip, "col", 1) for chip in chips]

    def apply(rounded, table, degree, first=()):
        height = vectors_n + (DEGREE_ROWS if degree else 0)
        zeros = call(
            zero_kernel,
            [jax.ShapeDtypeStruct((n * group, height, width), F32) for n in (cols_n, rows_n)],
            [],
            16,
            [],
            4 * total_nodes * vectors_n,
        )
        parts = gather(rounded, (*first, *zeros))
        kept, swap, col_own, col_send = products(tiles, table, *parts, zeros, runs, degree)
        col_got = exchange(col_send, "row")
        row_own, *row_send = merge(kept, trade(swap, "col", 1), vectors_n, degree)
        row_degree = row_send[:1] if degree else []
        row_got = exchange(row_send[len(row_degree) :], "col", 2)[::-1]
        return [*row_degree, row_own, col_own, *row_got, *col_got]

    rounded = call(round_kernel, rounded_shape, [], 16, [start])
    meta = jnp.stack([lax.axis_index("row"), lax.axis_index("col"), chips_n]).astype(jnp.int32)
    table = call(
        functools.partial(table_kernel, group),
        jax.ShapeDtypeStruct((3, tiles.shape[0]), jnp.int32),
        [],
        16,
        [meta, tile_rows[None], tile_cols[None]],
        smem=1,
    )
    first, rounded, degree = call(
        functools.partial(first_kernel, chips_n),
        [vector_shape, rounded_shape, degree_shape],
        [],
        24,
        [start, *apply(rounded, table, True, (table,))],
    )
    filtered, rounded = call(
        functools.partial(filter_kernel, chips_n),
        [vector_shape, rounded_shape],
        [],
        24,
        [start, first, degree, *apply(rounded, table, False)],
    )
    gram = call(
        gram_kernel,
        jax.ShapeDtypeStruct((vectors_n, 2 * vectors_n), F32),
        [pltpu.VMEM((2 * vectors_n, own_nodes), F32)],
        16,
        [filtered, degree],
        24 * vectors_n * vectors_n * own_nodes,
    )
    col_parts, row_parts = gather(rounded, (gram,))
    left = call(
        functools.partial(half_form_kernel, runs[1]),
        jax.ShapeDtypeStruct(spread, BF16),
        [pltpu.VMEM((cols_n * group, vectors_n, width), BF16)],
        24,
        [table, tiles, *row_parts],
        2 * tiles.size * vectors_n,
        1,
    )
    sums = call(
        functools.partial(form_kernel, runs[0]),
        jax.ShapeDtypeStruct((vectors_n // 2 + 8, 2 * vectors_n), F32),
        [pltpu.VMEM((rows_n * group, vectors_n, width), BF16), pltpu.VMEM(spread, BF16)],
        24,
        [table, left, gram, *col_parts],
        2 * vectors_n * spread[0] * spread[1],
        1,
    )
    sums = sums + trade(sums, "col", 1)
    sums = tree_sum([sums, *exchange([sums] * (chips_n - 1), "col", 2)])
    return call(
        functools.partial(last_kernel, total_nodes),
        [vector_shape, jax.ShapeDtypeStruct((vectors_n, vectors_n), F32)],
        [],
        24,
        [filtered, sums, *exchange([sums] * (rows_n - 1), "row")],
    )


def solution(mesh):
    placed = (
        P("row", "col", None, None, None),
        P("row", "col", None),
        P("row", "col", None),
        P(None, ("row", "col")),
    )
    return jax.shard_map(
        local, mesh=mesh, in_specs=placed, out_specs=(P(None, ("row", "col")), P()), check_vma=False
    )
```

```python
import functools

import jax
import jax.numpy as jnp
from jax import lax
from jax.experimental import pallas as pl
from jax.experimental.pallas import tpu as pltpu
from jax.sharding import PartitionSpec as P

CENTER = 1.0
HALF_WIDTH = 0.5
HIGHEST = lax.Precision.HIGHEST
NT = (((1,), (1,)), ((), ()))
NN = (((1,), (0,)), ((), ()))
BF16 = jnp.bfloat16
F32 = jnp.float32
VMEM = pl.BlockSpec(memory_space=pltpu.VMEM)
SMEM = pl.BlockSpec(memory_space=pltpu.SMEM)
ANY = pl.BlockSpec(memory_space=pl.ANY)
DEGREE_ROWS = 16


def call(kernel, out_shape, scratch, limit, args, flops=0, smem=0, after=(), aliases={}):
    moved = sum(x.size * x.dtype.itemsize for x in args)
    return pl.pallas_call(
        lambda *refs: kernel(*refs[len(after) :]),
        out_shape=jax.tree.map(lambda x: jax.ShapeDtypeStruct(x.shape, x.dtype), out_shape),
        in_specs=[ANY] * len(after) + [SMEM] * smem + [VMEM] * (len(args) - smem),
        out_specs=jax.tree.map(lambda _: VMEM, out_shape),
        scratch_shapes=scratch,
        input_output_aliases=aliases,
        compiler_params=pltpu.CompilerParams(vmem_limit_bytes=limit * 2**20),
        cost_estimate=pl.CostEstimate(flops=flops, bytes_accessed=moved, transcendentals=0),
    )(*after, *args)


def trade(part, axis, d):
    n = lax.axis_size(axis)
    return lax.ppermute(part, axis, [(i, i ^ d) for i in range(n)])


def exchange(parts, axis, step=1):
    far_first = [trade(part, axis, step * d) for d, part in reversed(list(enumerate(parts, 1)))]
    return far_first[::-1]


def tiles_first(ref, width):
    return [ref[:, k * width : (k + 1) * width] for k in range(ref.shape[1] // width)]


def round_kernel(vec_ref, out_ref):
    for k, piece in enumerate(tiles_first(vec_ref, out_ref.shape[2])):
        out_ref[k] = piece.astype(BF16)


def split_degree(sums):
    high = sums.astype(BF16).astype(F32)
    return jnp.concatenate([high, sums - high], 0).astype(BF16)


def join_degree(payload, group):
    parts = payload[payload.shape[0] - 2 * group :, :].astype(F32)
    return parts[:group] + parts[group:]


def fill(panel, parts, runs):
    for part, places in zip(parts, runs):
        at = 0
        for place, count in places:
            panel[place : place + count, : part.shape[1], :] = part[at : at + count]
            at += count


def table_kernel(group, meta, rows_ref, cols_ref, table):
    rows, cols = rows_ref[...], cols_ref[...]
    apart = lax.div(rows, group) ^ meta[1]
    halves = lax.rem(apart, 2) * meta[2] + lax.div(apart, 2)
    inside = lax.rem(rows, group)
    table[0:1, :] = (lax.div(cols, group) ^ meta[0]) * group + lax.rem(cols, group)
    table[1:2, :] = apart * group + inside
    table[2:3, :] = halves * group + inside


def fill_ones(panel, vectors_n):
    rows = panel.shape[1] - vectors_n
    if rows:
        panel[:, vectors_n:, :] = jnp.ones((panel.shape[0], rows, panel.shape[2]), BF16)


def degree_of(total, start, group, vectors_n):
    return jnp.concatenate(
        [total[start + k, vectors_n : vectors_n + 1, :] for k in range(group)], 0
    )


def zero_kernel(*refs):
    for ref in refs:
        ref[...] = jnp.zeros_like(ref)


def column_kernel(runs, table, tiles_ref, *refs):
    parts, (_, own_ref, total, *send_refs, panel) = refs[: len(runs)], refs[len(runs) :]
    group, vectors_n, _ = parts[0].shape
    fill(panel, parts, runs)
    fill_ones(panel, vectors_n)
    for t in range(tiles_ref.shape[0]):
        total[table[0, t]] += lax.dot_general(
            panel[table[1, t]], tiles_ref[t], NN, preferred_element_type=F32
        )
    own_ref[...] = total[:group]
    for d, send in enumerate(send_refs, 1):
        round_sums(send, total, d * group, group, vectors_n)


def row_kernel(runs, table, tiles_ref, *refs):
    parts, (_, total, swap_ref, panel) = refs[: len(runs)], refs[len(runs) :]
    group, vectors_n, _ = parts[0].shape
    half = swap_ref.shape[0]
    fill(panel, parts, runs)
    fill_ones(panel, vectors_n)
    for t in range(tiles_ref.shape[0]):
        total[table[2, t]] += lax.dot_general(
            panel[table[0, t]], tiles_ref[t], NT, preferred_element_type=F32
        )
    for d in range(half):
        round_sums(swap_ref.at[d], total, (half + d) * group, group, vectors_n)


def round_sums(send, total, start, group, vectors_n):
    for k in range(group):
        send[k * vectors_n : (k + 1) * vectors_n, :] = total[start + k, :vectors_n, :].astype(BF16)
    if total.shape[1] > vectors_n:
        send[group * vectors_n :, :] = split_degree(degree_of(total, start, group, vectors_n))


def products(tiles, table, col_parts, row_parts, zeros, runs, degree):
    group, vectors_n, width = col_parts[0].shape
    half = len(row_parts) // 2
    rows_n = max(place + count for run in runs[0] for place, count in run) // group
    rows = group * vectors_n + (2 * group if degree else 0)
    height = vectors_n + (DEGREE_ROWS if degree else 0)
    send_shape = jax.ShapeDtypeStruct((rows, width), BF16)
    flops = 2 * tiles.size * vectors_n

    def panel(count):
        return pltpu.VMEM((count * group, height, width), BF16)

    col_own, _, *col_send = call(
        functools.partial(column_kernel, runs[1]),
        [jax.ShapeDtypeStruct((group, height, width), F32), zeros[1]] + [send_shape] * (rows_n - 1),
        [panel(2 * half)],
        24,
        [table, tiles, *row_parts, zeros[1]],
        flops,
        1,
        (),
        {2 + len(row_parts): 1},
    )
    kept, swap = call(
        functools.partial(row_kernel, runs[0]),
        [zeros[0], jax.ShapeDtypeStruct((half, rows, width), BF16)],
        [panel(rows_n)],
        24,
        [table, tiles, *col_parts, zeros[0]],
        flops,
        1,
        [col_own],
        {3 + len(col_parts): 0},
    )
    return kept, swap, col_own, col_send


def merge_kernel(degree, vectors_n, kept, got, own_ref, *send_refs):
    if degree:
        own_degree, *send_refs = send_refs
    group = own_ref.shape[0]
    for k in range(group):
        rows = slice(k * vectors_n, (k + 1) * vectors_n)
        own_ref[k] = kept[k, :vectors_n, :] + got[0, rows, :].astype(F32)
        for d, send in enumerate(send_refs, 1):
            both = kept[d * group + k, :vectors_n, :] + got[d, rows, :].astype(F32)
            send[rows, :] = both.astype(BF16)
    if degree:
        for d in range(got.shape[0]):
            sums = degree_of(kept, d * group, group, vectors_n) + join_degree(got.at[d], group)
            if d:
                send_refs[d - 1][group * vectors_n :, :] = split_degree(sums)
            else:
                own_degree[...] = sums


def merge(kept, got, vectors_n, degree):
    half, width = got.shape[0], got.shape[2]
    group = kept.shape[0] // (2 * half)
    out_shape = [jax.ShapeDtypeStruct((group, vectors_n, width), F32)]
    if degree:
        out_shape += [jax.ShapeDtypeStruct((group, width), F32)]
    out_shape += [jax.ShapeDtypeStruct(got.shape[1:], BF16)] * (half - 1)
    kernel = functools.partial(merge_kernel, degree, vectors_n)
    return call(kernel, out_shape, [], 24, [kept, got])


def gathered_sum(own, received, k, vectors_n):
    total = own[k, :vectors_n, :]
    rows = slice(k * vectors_n, (k + 1) * vectors_n)
    for part in received:
        total = total + part[rows, :].astype(F32)
    return total


def symmetric_part(row_own, row_refs, col_own, col_refs, k, vectors_n):
    return 0.5 * (
        gathered_sum(row_own, row_refs, k, vectors_n)
        + gathered_sum(col_own, col_refs, k, vectors_n)
    )


def first_kernel(chips_n, vec_ref, row_degree, row_own, col_own, *refs):
    row_refs, refs = refs[: chips_n - 1], refs[chips_n - 1 :]
    col_refs, (first_ref, rounded_ref, degree_ref) = refs[:-3], refs[-3:]
    group, vectors_n, width = rounded_ref.shape
    degree = row_degree[...] + degree_of(col_own, 0, group, vectors_n)
    for part in (*row_refs, *col_refs):
        degree += join_degree(part, group)
    degree = 0.5 * degree
    degree_ref[...] = degree
    for k, vec in enumerate(tiles_first(vec_ref, width)):
        symmetric = symmetric_part(row_own, row_refs, col_own, col_refs, k, vectors_n)
        image = degree[k : k + 1, :] * vec - symmetric
        first = (image - CENTER * vec) / HALF_WIDTH
        first_ref[:, k * width : (k + 1) * width] = first
        rounded_ref[k] = first.astype(BF16)


def filter_kernel(chips_n, start_ref, first_ref, degree_ref, row_own, col_own, *refs):
    row_refs, refs = refs[: chips_n - 1], refs[chips_n - 1 :]
    col_refs, (filtered_ref, rounded_ref) = refs[:-2], refs[-2:]
    _, vectors_n, width = rounded_ref.shape
    for k, vec in enumerate(tiles_first(first_ref, width)):
        symmetric = symmetric_part(row_own, row_refs, col_own, col_refs, k, vectors_n)
        columns = slice(k * width, (k + 1) * width)
        image = degree_ref[k : k + 1, :] * vec - symmetric
        filtered = 2.0 * (image - CENTER * vec) / HALF_WIDTH - start_ref[:, columns]
        filtered_ref[:, columns] = filtered
        rounded_ref[k] = filtered.astype(BF16)


def gram_kernel(filtered_ref, degree_ref, gram_ref, both):
    vectors_n, width = filtered_ref.shape[0], degree_ref.shape[1]
    for k, vec in enumerate(tiles_first(filtered_ref, width)):
        columns = slice(k * width, (k + 1) * width)
        both[:vectors_n, columns] = vec
        both[vectors_n:, columns] = degree_ref[k : k + 1, :] * vec
    gram_ref[...] = lax.dot_general(
        filtered_ref[...], both[...], NT, precision=HIGHEST, preferred_element_type=F32
    )


def half_form_kernel(runs, table, tiles_ref, *refs):
    parts, (out_ref, panel) = refs[:-2], refs[-2:]
    width = panel.shape[2]
    fill(panel, parts, runs)
    for t in range(tiles_ref.shape[0]):
        out_ref[:, t * width : (t + 1) * width] = lax.dot_general(
            panel[table[1, t]], tiles_ref[t], NN, preferred_element_type=F32
        ).astype(BF16)


def form_kernel(runs, table, left, gram_ref, *refs):
    parts, (out_ref, panel, right) = refs[:-3], refs[-3:]
    _, vectors_n, width = panel.shape
    fill(panel, parts, runs)
    for t in range(right.shape[1] // width):
        right[:, t * width : (t + 1) * width] = panel[table[0, t]]
    form = lax.dot_general(left[...], right[...], NT, preferred_element_type=F32)
    projected = gram_ref[:, vectors_n:] - 0.5 * (form + form.T)
    row, col = square_index(vectors_n)
    packed = jnp.where(col >= row, gram_ref[:, :vectors_n], projected)
    diagonal = jnp.sum(jnp.where(row == col, projected, 0.0), 0, keepdims=True)
    half = vectors_n // 2
    out_ref[:half] = jnp.concatenate([packed[:half], packed[half:]], 1)
    diagonal = jnp.broadcast_to(diagonal, (8, vectors_n))
    out_ref[half:] = jnp.concatenate([diagonal, jnp.zeros_like(diagonal)], 1)


def square_index(n):
    return tuple(lax.broadcasted_iota(jnp.int32, (n, n), axis) for axis in (0, 1))


def inverse_factor(gram):
    n = gram.shape[0]
    row, col = square_index(n)
    table = jnp.concatenate([gram, jnp.where(row == col, 1.0, 0.0)], 1)
    bands = [table[i : i + 8] for i in range(0, n, 8)]
    shape = (8, 2 * n)
    line = lax.broadcasted_iota(jnp.int32, shape, 0)

    def spread(values, j):
        return jnp.broadcast_to(values[:, j : j + 1], shape)

    def pick(values, i):
        return jnp.broadcast_to(values[i : i + 1, :], shape)

    for at in range(n // 8):
        block = [spread(bands[at], 8 * at + c) for c in range(8)]
        forward, solved = bands[at], bands[at]
        solved_block = list(block)
        for s in range(8):
            scale = 1.0 / pick(block[s], s)
            below = jnp.where(line > s, block[s], 0.0) * scale
            above = jnp.where(line < s, solved_block[s] * scale, 0.0)
            both = below + above
            pivot_row = pick(forward, s)
            forward = forward - below * pivot_row
            solved = solved - both * pivot_row
            for c in range(s + 1, 8):
                pivot = pick(block[c], s)
                block[c] = block[c] - below * pivot
                solved_block[c] = solved_block[c] - both * pivot
        pivots = block[0]
        for s in range(1, 8):
            pivots = jnp.where(line == s, block[s], pivots)
        solved = solved / pivots
        bands[at] = forward / jnp.sqrt(pivots)
        for i in range(at + 1, n // 8):
            update = spread(bands[i], 8 * at) * pick(solved, 0)
            for c in range(1, 8):
                update = update + spread(bands[i], 8 * at + c) * pick(solved, c)
            bands[i] = bands[i] - update
    return jnp.concatenate(bands, 0)[:, n:]


def last_kernel(total_nodes, filtered_ref, *refs):
    (own, *parts), (ritz_ref, rayleigh_ref) = refs[:-2], refs[-2:]
    parts = [own, *parts[::-1]]
    n = filtered_ref.shape[0]
    half = n // 2
    sums = tree_sum([part[...] for part in parts]) * (1.0 / total_nodes)
    packed = jnp.concatenate([sums[:half, :n], sums[:half, n:]], 0)
    row, col = square_index(n)
    upper = jnp.where(col > row, packed, 0.0)
    gram = jnp.where(col >= row, packed, 0.0) + upper.T
    lower = jnp.where(col < row, packed, 0.0)
    diagonal = jnp.broadcast_to(sums[half : half + 1, :n], (n, n))
    projected = lower + lower.T + jnp.where(row == col, diagonal, 0.0)
    inverse = inverse_factor(gram)

    def dot(a, b, dims):
        return lax.dot_general(a, b, dims, precision=HIGHEST, preferred_element_type=F32)

    half_way = dot(inverse, projected, NN)
    rayleigh_ref[...] = dot(half_way, inverse, NT)
    turned = dot(inverse, half_way, NT)
    ritz_ref[...] = dot(turned, dot(inverse, filtered_ref[...], NN), NN)


def tree_sum(parts):
    while len(parts) > 1:
        parts = [a + b for a, b in zip(parts[::2], parts[1::2])]
    return parts[0]


def local(tiles, tile_rows, tile_cols, start):
    tiles, tile_rows, tile_cols = tiles[0, 0], tile_rows[0, 0], tile_cols[0, 0]
    width = tiles.shape[-1]
    vectors_n, own_nodes = start.shape
    rows_n, cols_n = lax.axis_size("row"), lax.axis_size("col")
    chips_n = cols_n // 2
    total_nodes = own_nodes * rows_n * cols_n
    group = own_nodes // width
    spread = (vectors_n, tiles.shape[0] * width)

    rounded_shape = jax.ShapeDtypeStruct((group, vectors_n, width), BF16)
    vector_shape = jax.ShapeDtypeStruct((vectors_n, own_nodes), F32)
    degree_shape = jax.ShapeDtypeStruct((group, width), F32)

    late = 1
    levels = [rows_n >> i for i in range(1, rows_n.bit_length())]
    col_runs = [[(0, group)]]
    for d in levels:
        if len(col_runs) == 1:
            col_runs += [[(d * group, group)]]
            continue
        cut = group - late
        passed = [((p // group ^ d) * group + p % group, n) for run in col_runs[1:] for p, n in run]
        col_runs += [[(d * group, cut)], [(d * group + cut, late), *passed]]
    chip_order = [0, *range(chips_n - 1, 0, -1)]
    row_runs = [[((2 * d + core) * group, group)] for core in range(2) for d in chip_order]
    runs = (col_runs, row_runs)
    def gather(rounded, first=()):
        held = [rounded]
        for d in levels:
            if len(held) == 1:
                held += [trade(rounded, "row", d)]
                continue
            near = trade(rounded[: group - late], "row", d)
            near, *passed = lax.optimization_barrier((near, *held[1:], *first))
            held[1:] = passed[: len(held) - 1]
            held += [near, trade(jnp.concatenate([rounded[group - late :], *held[1:]]), "row", d)]
        chips = [rounded, *exchange([rounded] * (chips_n - 1), "col", 2)[::-1]]
        return held, chips + [trade(chip, "col", 1) for chip in chips]

    def apply(rounded, table, degree, first=()):
        height = vectors_n + (DEGREE_ROWS if degree else 0)
        zeros = call(
            zero_kernel,
            [jax.ShapeDtypeStruct((n * group, height, width), F32) for n in (cols_n, rows_n)],
            [],
            16,
            [],
            4 * total_nodes * vectors_n,
        )
        parts = gather(rounded, (*first, *zeros))
        kept, swap, col_own, col_send = products(tiles, table, *parts, zeros, runs, degree)
        col_got = exchange(col_send, "row")
        row_own, *row_send = merge(kept, trade(swap, "col", 1), vectors_n, degree)
        row_degree = row_send[:1] if degree else []
        row_got = exchange(row_send[len(row_degree) :], "col", 2)[::-1]
        return [*row_degree, row_own, col_own, *row_got, *col_got]

    rounded = call(round_kernel, rounded_shape, [], 16, [start])
    meta = jnp.stack([lax.axis_index("row"), lax.axis_index("col"), chips_n]).astype(jnp.int32)
    table = call(
        functools.partial(table_kernel, group),
        jax.ShapeDtypeStruct((3, tiles.shape[0]), jnp.int32),
        [],
        16,
        [meta, tile_rows[None], tile_cols[None]],
        smem=1,
    )
    first, rounded, degree = call(
        functools.partial(first_kernel, chips_n),
        [vector_shape, rounded_shape, degree_shape],
        [],
        24,
        [start, *apply(rounded, table, True, (table,))],
    )
    filtered, rounded = call(
        functools.partial(filter_kernel, chips_n),
        [vector_shape, rounded_shape],
        [],
        24,
        [start, first, degree, *apply(rounded, table, False)],
    )
    gram = call(
        gram_kernel,
        jax.ShapeDtypeStruct((vectors_n, 2 * vectors_n), F32),
        [pltpu.VMEM((2 * vectors_n, own_nodes), F32)],
        16,
        [filtered, degree],
        24 * vectors_n * vectors_n * own_nodes,
    )
    col_parts, row_parts = gather(rounded, (gram,))
    left = call(
        functools.partial(half_form_kernel, runs[1]),
        jax.ShapeDtypeStruct(spread, BF16),
        [pltpu.VMEM((cols_n * group, vectors_n, width), BF16)],
        24,
        [table, tiles, *row_parts],
        2 * tiles.size * vectors_n,
        1,
    )
    sums = call(
        functools.partial(form_kernel, runs[0]),
        jax.ShapeDtypeStruct((vectors_n // 2 + 8, 2 * vectors_n), F32),
        [pltpu.VMEM((rows_n * group, vectors_n, width), BF16), pltpu.VMEM(spread, BF16)],
        24,
        [table, left, gram, *col_parts],
        2 * vectors_n * spread[0] * spread[1],
        1,
    )
    sums = sums + trade(sums, "col", 1)
    sums = tree_sum([*exchange([sums] * (chips_n - 1), "col", 2)[::-1], sums])
    return call(
        functools.partial(last_kernel, total_nodes),
        [vector_shape, jax.ShapeDtypeStruct((vectors_n, vectors_n), F32)],
        [],
        24,
        [filtered, sums, *exchange([sums] * (rows_n - 1), "row")[::-1]],
    )


def solution(mesh):
    placed = (
        P("row", "col", None, None, None),
        P("row", "col", None),
        P("row", "col", None),
        P(None, ("row", "col")),
    )
    return jax.shard_map(
        local, mesh=mesh, in_specs=placed, out_specs=(P(None, ("row", "col")), P()), check_vma=False
    )
```

```python
import functools

import jax
import jax.numpy as jnp
from jax import lax
from jax.experimental import pallas as pl
from jax.experimental.pallas import tpu as pltpu
from jax.sharding import PartitionSpec as P

CENTER = 1.0
HALF_WIDTH = 0.5
HIGHEST = lax.Precision.HIGHEST
NT = (((1,), (1,)), ((), ()))
NN = (((1,), (0,)), ((), ()))
BF16 = jnp.bfloat16
F32 = jnp.float32
VMEM = pl.BlockSpec(memory_space=pltpu.VMEM)
SMEM = pl.BlockSpec(memory_space=pltpu.SMEM)
ANY = pl.BlockSpec(memory_space=pl.ANY)
HBM = pl.BlockSpec(memory_space=pltpu.HBM)
DEGREE_ROWS = 16


def call(kernel, out_shape, scratch, limit, args, flops=0, smem=0, after=(), aliases={}):
    moved = sum(x.size * x.dtype.itemsize for x in args)
    return pl.pallas_call(
        lambda *refs: kernel(*refs[len(after) :]),
        out_shape=jax.tree.map(lambda x: jax.ShapeDtypeStruct(x.shape, x.dtype), out_shape),
        in_specs=[ANY] * len(after) + [SMEM] * smem + [VMEM] * (len(args) - smem),
        out_specs=jax.tree.map(lambda _: VMEM, out_shape),
        scratch_shapes=scratch,
        input_output_aliases=aliases,
        compiler_params=pltpu.CompilerParams(vmem_limit_bytes=limit * 2**20),
        cost_estimate=pl.CostEstimate(flops=flops, bytes_accessed=moved, transcendentals=0),
    )(*after, *args)


def trade(part, axis, d):
    n = lax.axis_size(axis)
    return lax.ppermute(part, axis, [(i, i ^ d) for i in range(n)])


def exchange(parts, axis, step=1):
    far_first = [trade(part, axis, step * d) for d, part in reversed(list(enumerate(parts, 1)))]
    return far_first[::-1]


def tiles_first(ref, width):
    return [ref[:, k * width : (k + 1) * width] for k in range(ref.shape[1] // width)]


def bring(sources, targets, arrived):
    copies = [
        pltpu.make_async_copy(source, target, arrived.at[i])
        for i, (source, target) in enumerate(zip(sources, targets))
    ]
    for copy in copies:
        copy.start()
    for copy in copies:
        copy.wait()


def round_kernel(source, out_ref, vec_ref, arrived):
    bring([source], [vec_ref], arrived)
    for k, piece in enumerate(tiles_first(vec_ref, out_ref.shape[2])):
        out_ref[k] = piece.astype(BF16)


def split_degree(sums):
    high = sums.astype(BF16).astype(F32)
    return jnp.concatenate([high, sums - high], 0).astype(BF16)


def join_degree(payload, group):
    parts = payload[payload.shape[0] - 2 * group :, :].astype(F32)
    return parts[:group] + parts[group:]


def fill(panel, parts, runs):
    for part, places in zip(parts, runs):
        at = 0
        for place, count in places:
            panel[place : place + count, : part.shape[1], :] = part[at : at + count]
            at += count


def table_kernel(group, rows_source, cols_source, meta, table, rows_ref, cols_ref, arrived):
    bring([rows_source, cols_source], [rows_ref, cols_ref], arrived)
    rows, cols = rows_ref[...], cols_ref[...]
    apart = lax.div(rows, group) ^ meta[1]
    halves = lax.rem(apart, 2) * meta[2] + lax.div(apart, 2)
    inside = lax.rem(rows, group)
    table[0:1, :] = (lax.div(cols, group) ^ meta[0]) * group + lax.rem(cols, group)
    table[1:2, :] = apart * group + inside
    table[2:3, :] = halves * group + inside


def fill_ones(panel, vectors_n):
    rows = panel.shape[1] - vectors_n
    if rows:
        panel[:, vectors_n:, :] = jnp.ones((panel.shape[0], rows, panel.shape[2]), BF16)


def degree_of(total, start, group, vectors_n):
    return jnp.concatenate(
        [total[start + k, vectors_n : vectors_n + 1, :] for k in range(group)], 0
    )


def zero_kernel(*refs):
    for ref in refs:
        ref[...] = jnp.zeros_like(ref)


def column_kernel(runs, table, tiles_ref, *refs):
    parts, (_, own_ref, total, *send_refs, panel) = refs[: len(runs)], refs[len(runs) :]
    group, vectors_n, _ = parts[0].shape
    fill(panel, parts, runs)
    fill_ones(panel, vectors_n)
    for t in range(tiles_ref.shape[0]):
        total[table[0, t]] += lax.dot_general(
            panel[table[1, t]], tiles_ref[t], NN, preferred_element_type=F32
        )
    own_ref[...] = total[:group]
    for d, send in enumerate(send_refs, 1):
        round_sums(send, total, d * group, group, vectors_n)


def row_kernel(runs, table, tiles_ref, *refs):
    parts, (_, total, swap_ref, panel) = refs[: len(runs)], refs[len(runs) :]
    group, vectors_n, _ = parts[0].shape
    half = swap_ref.shape[0]
    fill(panel, parts, runs)
    fill_ones(panel, vectors_n)
    for t in range(tiles_ref.shape[0]):
        total[table[2, t]] += lax.dot_general(
            panel[table[0, t]], tiles_ref[t], NT, preferred_element_type=F32
        )
    for d in range(half):
        round_sums(swap_ref.at[d], total, (half + d) * group, group, vectors_n)


def round_sums(send, total, start, group, vectors_n):
    for k in range(group):
        send[k * vectors_n : (k + 1) * vectors_n, :] = total[start + k, :vectors_n, :].astype(BF16)
    if total.shape[1] > vectors_n:
        send[group * vectors_n :, :] = split_degree(degree_of(total, start, group, vectors_n))


def products(tiles, table, col_parts, row_parts, zeros, runs, degree):
    group, vectors_n, width = col_parts[0].shape
    half = len(row_parts) // 2
    rows_n = max(place + count for run in runs[0] for place, count in run) // group
    rows = group * vectors_n + (2 * group if degree else 0)
    height = vectors_n + (DEGREE_ROWS if degree else 0)
    send_shape = jax.ShapeDtypeStruct((rows, width), BF16)
    flops = 2 * tiles.size * vectors_n

    def panel(count):
        return pltpu.VMEM((count * group, height, width), BF16)

    col_own, _, *col_send = call(
        functools.partial(column_kernel, runs[1]),
        [jax.ShapeDtypeStruct((group, height, width), F32), zeros[1]] + [send_shape] * (rows_n - 1),
        [panel(2 * half)],
        24,
        [table, tiles, *row_parts, zeros[1]],
        flops,
        1,
        (),
        {2 + len(row_parts): 1},
    )
    kept, swap = call(
        functools.partial(row_kernel, runs[0]),
        [zeros[0], jax.ShapeDtypeStruct((half, rows, width), BF16)],
        [panel(rows_n)],
        24,
        [table, tiles, *col_parts, zeros[0]],
        flops,
        1,
        [col_own],
        {3 + len(col_parts): 0},
    )
    return kept, swap, col_own, col_send


def merge_kernel(degree, vectors_n, kept, got, own_ref, *send_refs):
    if degree:
        own_degree, *send_refs = send_refs
    group = own_ref.shape[0]
    for k in range(group):
        rows = slice(k * vectors_n, (k + 1) * vectors_n)
        own_ref[k] = kept[k, :vectors_n, :] + got[0, rows, :].astype(F32)
        for d, send in enumerate(send_refs, 1):
            both = kept[d * group + k, :vectors_n, :] + got[d, rows, :].astype(F32)
            send[rows, :] = both.astype(BF16)
    if degree:
        for d in range(got.shape[0]):
            sums = degree_of(kept, d * group, group, vectors_n) + join_degree(got.at[d], group)
            if d:
                send_refs[d - 1][group * vectors_n :, :] = split_degree(sums)
            else:
                own_degree[...] = sums


def merge(kept, got, vectors_n, degree):
    half, width = got.shape[0], got.shape[2]
    group = kept.shape[0] // (2 * half)
    out_shape = [jax.ShapeDtypeStruct((group, vectors_n, width), F32)]
    if degree:
        out_shape += [jax.ShapeDtypeStruct((group, width), F32)]
    out_shape += [jax.ShapeDtypeStruct(got.shape[1:], BF16)] * (half - 1)
    kernel = functools.partial(merge_kernel, degree, vectors_n)
    return call(kernel, out_shape, [], 24, [kept, got])


def gathered_sum(own, received, k, vectors_n):
    total = own[k, :vectors_n, :]
    rows = slice(k * vectors_n, (k + 1) * vectors_n)
    for part in received:
        total = total + part[rows, :].astype(F32)
    return total


def symmetric_part(row_own, row_refs, col_own, col_refs, k, vectors_n):
    return 0.5 * (
        gathered_sum(row_own, row_refs, k, vectors_n)
        + gathered_sum(col_own, col_refs, k, vectors_n)
    )


def first_kernel(chips_n, vec_ref, row_degree, row_own, col_own, *refs):
    row_refs, refs = refs[: chips_n - 1], refs[chips_n - 1 :]
    col_refs, (first_ref, rounded_ref, degree_ref) = refs[:-3], refs[-3:]
    group, vectors_n, width = rounded_ref.shape
    degree = row_degree[...] + degree_of(col_own, 0, group, vectors_n)
    for part in (*row_refs, *col_refs):
        degree += join_degree(part, group)
    degree = 0.5 * degree
    degree_ref[...] = degree
    for k, vec in enumerate(tiles_first(vec_ref, width)):
        symmetric = symmetric_part(row_own, row_refs, col_own, col_refs, k, vectors_n)
        image = degree[k : k + 1, :] * vec - symmetric
        first = (image - CENTER * vec) / HALF_WIDTH
        first_ref[:, k * width : (k + 1) * width] = first
        rounded_ref[k] = first.astype(BF16)


def filter_kernel(chips_n, start_ref, first_ref, degree_ref, row_own, col_own, *refs):
    row_refs, refs = refs[: chips_n - 1], refs[chips_n - 1 :]
    col_refs, (filtered_ref, rounded_ref) = refs[:-2], refs[-2:]
    _, vectors_n, width = rounded_ref.shape
    for k, vec in enumerate(tiles_first(first_ref, width)):
        symmetric = symmetric_part(row_own, row_refs, col_own, col_refs, k, vectors_n)
        columns = slice(k * width, (k + 1) * width)
        image = degree_ref[k : k + 1, :] * vec - symmetric
        filtered = 2.0 * (image - CENTER * vec) / HALF_WIDTH - start_ref[:, columns]
        filtered_ref[:, columns] = filtered
        rounded_ref[k] = filtered.astype(BF16)


def gram_kernel(filtered_ref, degree_ref, gram_ref, both):
    vectors_n, width = filtered_ref.shape[0], degree_ref.shape[1]
    for k, vec in enumerate(tiles_first(filtered_ref, width)):
        columns = slice(k * width, (k + 1) * width)
        both[:vectors_n, columns] = vec
        both[vectors_n:, columns] = degree_ref[k : k + 1, :] * vec
    gram_ref[...] = lax.dot_general(
        filtered_ref[...], both[...], NT, precision=HIGHEST, preferred_element_type=F32
    )


def half_form_kernel(runs, table, tiles_ref, *refs):
    parts, (out_ref, panel) = refs[:-2], refs[-2:]
    width = panel.shape[2]
    fill(panel, parts, runs)
    for t in range(tiles_ref.shape[0]):
        out_ref[:, t * width : (t + 1) * width] = lax.dot_general(
            panel[table[1, t]], tiles_ref[t], NN, preferred_element_type=F32
        ).astype(BF16)


def form_kernel(runs, table, left, gram_ref, *refs):
    parts, (out_ref, panel, right) = refs[:-3], refs[-3:]
    _, vectors_n, width = panel.shape
    fill(panel, parts, runs)
    for t in range(right.shape[1] // width):
        right[:, t * width : (t + 1) * width] = panel[table[0, t]]
    form = lax.dot_general(left[...], right[...], NT, preferred_element_type=F32)
    projected = gram_ref[:, vectors_n:] - 0.5 * (form + form.T)
    row, col = square_index(vectors_n)
    packed = jnp.where(col >= row, gram_ref[:, :vectors_n], projected)
    diagonal = jnp.sum(jnp.where(row == col, projected, 0.0), 0, keepdims=True)
    half = vectors_n // 2
    out_ref[:half] = jnp.concatenate([packed[:half], packed[half:]], 1)
    diagonal = jnp.broadcast_to(diagonal, (8, vectors_n))
    out_ref[half:] = jnp.concatenate([diagonal, jnp.zeros_like(diagonal)], 1)


def square_index(n):
    return tuple(lax.broadcasted_iota(jnp.int32, (n, n), axis) for axis in (0, 1))


def inverse_factor(gram):
    n = gram.shape[0]
    row, col = square_index(n)
    table = jnp.concatenate([gram, jnp.where(row == col, 1.0, 0.0)], 1)
    bands = [table[i : i + 8] for i in range(0, n, 8)]
    shape = (8, 2 * n)
    line = lax.broadcasted_iota(jnp.int32, shape, 0)

    def spread(values, j):
        return jnp.broadcast_to(values[:, j : j + 1], shape)

    def pick(values, i):
        return jnp.broadcast_to(values[i : i + 1, :], shape)

    for at in range(n // 8):
        block = [spread(bands[at], 8 * at + c) for c in range(8)]
        forward, solved = bands[at], bands[at]
        solved_block = list(block)
        for s in range(8):
            scale = 1.0 / pick(block[s], s)
            below = jnp.where(line > s, block[s], 0.0) * scale
            above = jnp.where(line < s, solved_block[s] * scale, 0.0)
            both = below + above
            pivot_row = pick(forward, s)
            forward = forward - below * pivot_row
            solved = solved - both * pivot_row
            for c in range(s + 1, 8):
                pivot = pick(block[c], s)
                block[c] = block[c] - below * pivot
                solved_block[c] = solved_block[c] - both * pivot
        pivots = block[0]
        for s in range(1, 8):
            pivots = jnp.where(line == s, block[s], pivots)
        solved = solved / pivots
        bands[at] = forward / jnp.sqrt(pivots)
        for i in range(at + 1, n // 8):
            update = spread(bands[i], 8 * at) * pick(solved, 0)
            for c in range(1, 8):
                update = update + spread(bands[i], 8 * at + c) * pick(solved, c)
            bands[i] = bands[i] - update
    return jnp.concatenate(bands, 0)[:, n:]


def last_kernel(total_nodes, filtered_ref, *refs):
    (own, *parts), (ritz_ref, rayleigh_ref) = refs[:-2], refs[-2:]
    parts = [own, *parts[::-1]]
    n = filtered_ref.shape[0]
    half = n // 2
    sums = tree_sum([part[...] for part in parts]) * (1.0 / total_nodes)
    packed = jnp.concatenate([sums[:half, :n], sums[:half, n:]], 0)
    row, col = square_index(n)
    upper = jnp.where(col > row, packed, 0.0)
    gram = jnp.where(col >= row, packed, 0.0) + upper.T
    lower = jnp.where(col < row, packed, 0.0)
    diagonal = jnp.broadcast_to(sums[half : half + 1, :n], (n, n))
    projected = lower + lower.T + jnp.where(row == col, diagonal, 0.0)
    inverse = inverse_factor(gram)

    def dot(a, b, dims):
        return lax.dot_general(a, b, dims, precision=HIGHEST, preferred_element_type=F32)

    half_way = dot(inverse, projected, NN)
    rayleigh_ref[...] = dot(half_way, inverse, NT)
    turned = dot(inverse, half_way, NT)
    ritz_ref[...] = dot(turned, dot(inverse, filtered_ref[...], NN), NN)


def tree_sum(parts):
    while len(parts) > 1:
        parts = [a + b for a, b in zip(parts[::2], parts[1::2])]
    return parts[0]


def local(tiles, tile_rows, tile_cols, start):
    tiles, tile_rows, tile_cols = tiles[0, 0], tile_rows[0, 0], tile_cols[0, 0]
    width = tiles.shape[-1]
    vectors_n, own_nodes = start.shape
    rows_n, cols_n = lax.axis_size("row"), lax.axis_size("col")
    chips_n = cols_n // 2
    total_nodes = own_nodes * rows_n * cols_n
    group = own_nodes // width
    spread = (vectors_n, tiles.shape[0] * width)

    rounded_shape = jax.ShapeDtypeStruct((group, vectors_n, width), BF16)
    vector_shape = jax.ShapeDtypeStruct((vectors_n, own_nodes), F32)
    degree_shape = jax.ShapeDtypeStruct((group, width), F32)

    late = 1
    levels = [rows_n >> i for i in range(1, rows_n.bit_length())]
    col_runs = [[(0, group)]]
    for d in levels:
        if len(col_runs) == 1:
            col_runs += [[(d * group, group)]]
            continue
        cut = group - late
        passed = [((p // group ^ d) * group + p % group, n) for run in col_runs[1:] for p, n in run]
        col_runs += [[(d * group, cut)], [(d * group + cut, late), *passed]]
    chip_order = [0, *range(chips_n - 1, 0, -1)]
    row_runs = [[((2 * d + core) * group, group)] for core in range(2) for d in chip_order]
    runs = (col_runs, row_runs)
    def gather(rounded, first=()):
        held, other = [rounded], trade(rounded, "col", 1)
        for d in levels:
            if len(held) == 1:
                held += [trade(rounded, "row", d)]
                continue
            near = trade(rounded[: group - late], "row", d)
            near, other, *passed = lax.optimization_barrier((near, other, *held[1:], *first))
            held[1:] = passed[: len(held) - 1]
            held += [near, trade(jnp.concatenate([rounded[group - late :], *held[1:]]), "row", d)]
        chips = [rounded, *exchange([rounded] * (chips_n - 1), "col", 2)[::-1]]
        return held, [*chips, other, *(trade(chip, "col", 1) for chip in chips[1:])]

    def apply(rounded, table, degree, first=()):
        height = vectors_n + (DEGREE_ROWS if degree else 0)
        zeros = call(
            zero_kernel,
            [jax.ShapeDtypeStruct((n * group, height, width), F32) for n in (cols_n, rows_n)],
            [],
            16,
            [],
            4 * total_nodes * vectors_n,
        )
        parts = gather(rounded, (*first, *zeros))
        kept, swap, col_own, col_send = products(tiles, table, *parts, zeros, runs, degree)
        col_got = exchange(col_send, "row")
        row_own, *row_send = merge(kept, trade(swap, "col", 1), vectors_n, degree)
        row_degree = row_send[:1] if degree else []
        row_got = exchange(row_send[len(row_degree) :], "col", 2)[::-1]
        return [*row_degree, row_own, col_own, *row_got, *col_got]

    rounded = pl.pallas_call(
        round_kernel,
        out_shape=rounded_shape,
        in_specs=[HBM],
        out_specs=VMEM,
        scratch_shapes=[pltpu.VMEM(start.shape, F32), pltpu.SemaphoreType.DMA((1,))],
    )(start)
    meta = jnp.stack([lax.axis_index("row"), lax.axis_index("col"), chips_n]).astype(jnp.int32)
    indices = (1, tiles.shape[0])
    table = pl.pallas_call(
        functools.partial(table_kernel, group),
        out_shape=jax.ShapeDtypeStruct((3, tiles.shape[0]), jnp.int32),
        in_specs=[HBM, HBM, SMEM],
        out_specs=VMEM,
        scratch_shapes=[pltpu.VMEM(indices, jnp.int32)] * 2 + [pltpu.SemaphoreType.DMA((2,))],
    )(tile_rows[None], tile_cols[None], meta)
    first, rounded, degree = call(
        functools.partial(first_kernel, chips_n),
        [vector_shape, rounded_shape, degree_shape],
        [],
        24,
        [start, *apply(rounded, table, True, (table,))],
    )
    filtered, rounded = call(
        functools.partial(filter_kernel, chips_n),
        [vector_shape, rounded_shape],
        [],
        24,
        [start, first, degree, *apply(rounded, table, False)],
    )
    gram = call(
        gram_kernel,
        jax.ShapeDtypeStruct((vectors_n, 2 * vectors_n), F32),
        [pltpu.VMEM((2 * vectors_n, own_nodes), F32)],
        16,
        [filtered, degree],
        24 * vectors_n * vectors_n * own_nodes,
    )
    col_parts, row_parts = gather(rounded, (gram,))
    left = call(
        functools.partial(half_form_kernel, runs[1]),
        jax.ShapeDtypeStruct(spread, BF16),
        [pltpu.VMEM((cols_n * group, vectors_n, width), BF16)],
        24,
        [table, tiles, *row_parts],
        2 * tiles.size * vectors_n,
        1,
    )
    sums = call(
        functools.partial(form_kernel, runs[0]),
        jax.ShapeDtypeStruct((vectors_n // 2 + 8, 2 * vectors_n), F32),
        [pltpu.VMEM((rows_n * group, vectors_n, width), BF16), pltpu.VMEM(spread, BF16)],
        24,
        [table, left, gram, *col_parts],
        2 * vectors_n * spread[0] * spread[1],
        1,
    )
    sums = sums + trade(sums, "col", 1)
    sums = tree_sum([*exchange([sums] * (chips_n - 1), "col", 2)[::-1], sums])
    return call(
        functools.partial(last_kernel, total_nodes),
        [vector_shape, jax.ShapeDtypeStruct((vectors_n, vectors_n), F32)],
        [],
        24,
        [filtered, sums, *exchange([sums] * (rows_n - 1), "row")[::-1]],
    )


def solution(mesh):
    placed = (
        P("row", "col", None, None, None),
        P("row", "col", None),
        P("row", "col", None),
        P(None, ("row", "col")),
    )
    return jax.shard_map(
        local, mesh=mesh, in_specs=placed, out_specs=(P(None, ("row", "col")), P()), check_vma=False
    )
```

```python
import functools

import jax
import jax.numpy as jnp
from jax import lax
from jax.experimental import pallas as pl
from jax.experimental.pallas import tpu as pltpu
from jax.sharding import PartitionSpec as P

CENTER = 1.0
HALF_WIDTH = 0.5
HIGHEST = lax.Precision.HIGHEST
NT = (((1,), (1,)), ((), ()))
NN = (((1,), (0,)), ((), ()))
BF16 = jnp.bfloat16
F32 = jnp.float32
VMEM = pl.BlockSpec(memory_space=pltpu.VMEM)
SMEM = pl.BlockSpec(memory_space=pltpu.SMEM)
ANY = pl.BlockSpec(memory_space=pl.ANY)
DEGREE_ROWS = 16


def call(kernel, out_shape, scratch, limit, args, flops=0, smem=0, after=(), aliases={}):
    moved = sum(x.size * x.dtype.itemsize for x in args)
    return pl.pallas_call(
        lambda *refs: kernel(*refs[len(after) :]),
        out_shape=jax.tree.map(lambda x: jax.ShapeDtypeStruct(x.shape, x.dtype), out_shape),
        in_specs=[ANY] * len(after) + [SMEM] * smem + [VMEM] * (len(args) - smem),
        out_specs=jax.tree.map(lambda _: VMEM, out_shape),
        scratch_shapes=scratch,
        input_output_aliases=aliases,
        compiler_params=pltpu.CompilerParams(vmem_limit_bytes=limit * 2**20),
        cost_estimate=pl.CostEstimate(flops=flops, bytes_accessed=moved, transcendentals=0),
    )(*after, *args)


def trade(part, axis, d):
    n = lax.axis_size(axis)
    return lax.ppermute(part, axis, [(i, i ^ d) for i in range(n)])


def exchange(parts, axis, step=1):
    far_first = [trade(part, axis, step * d) for d, part in reversed(list(enumerate(parts, 1)))]
    return far_first[::-1]


def tiles_first(ref, width):
    return [ref[:, k * width : (k + 1) * width] for k in range(ref.shape[1] // width)]


def round_kernel(vec_ref, out_ref):
    for k, piece in enumerate(tiles_first(vec_ref, out_ref.shape[2])):
        out_ref[k] = piece.astype(BF16)


def split_degree(sums):
    high = sums.astype(BF16).astype(F32)
    return jnp.concatenate([high, sums - high], 0).astype(BF16)


def join_degree(payload, group):
    parts = payload[payload.shape[0] - 2 * group :, :].astype(F32)
    return parts[:group] + parts[group:]


def fill(panel, parts, runs):
    for part, places in zip(parts, runs):
        at = 0
        for place, count in places:
            panel[place : place + count, : part.shape[1], :] = part[at : at + count]
            at += count


def table_kernel(group, meta, rows_ref, cols_ref, table):
    rows, cols = rows_ref[...], cols_ref[...]
    apart = lax.div(rows, group) ^ meta[1:2, :]
    halves = lax.rem(apart, 2) * meta[2:3, :] + lax.div(apart, 2)
    inside = lax.rem(rows, group)
    table[0:1, :] = (lax.div(cols, group) ^ meta[0:1, :]) * group + lax.rem(cols, group)
    table[1:2, :] = apart * group + inside
    table[2:3, :] = halves * group + inside


def fetch(source, table, arrived):
    copy = pltpu.make_async_copy(source, table, arrived)
    copy.start()
    return copy


def fill_ones(panel, vectors_n):
    rows = panel.shape[1] - vectors_n
    if rows:
        panel[:, vectors_n:, :] = jnp.ones((panel.shape[0], rows, panel.shape[2]), BF16)


def degree_of(total, start, group, vectors_n):
    return jnp.concatenate(
        [total[start + k, vectors_n : vectors_n + 1, :] for k in range(group)], 0
    )


def zero_kernel(*refs):
    for ref in refs:
        ref[...] = jnp.zeros_like(ref)


def column_kernel(runs, source, tiles_ref, *refs):
    parts, refs = refs[: len(runs)], refs[len(runs) :]
    _, own_ref, total, *send_refs, panel, table, arrived = refs
    copy = fetch(source, table, arrived)
    group, vectors_n, _ = parts[0].shape
    fill(panel, parts, runs)
    fill_ones(panel, vectors_n)
    copy.wait()
    for t in range(tiles_ref.shape[0]):
        total[table[0, t]] += lax.dot_general(
            panel[table[1, t]], tiles_ref[t], NN, preferred_element_type=F32
        )
    own_ref[...] = total[:group]
    for d, send in enumerate(send_refs, 1):
        round_sums(send, total, d * group, group, vectors_n)


def row_kernel(runs, source, tiles_ref, *refs):
    parts, refs = refs[: len(runs)], refs[len(runs) :]
    _, total, swap_ref, panel, table, arrived = refs
    copy = fetch(source, table, arrived)
    group, vectors_n, _ = parts[0].shape
    half = swap_ref.shape[0]
    fill(panel, parts, runs)
    fill_ones(panel, vectors_n)
    copy.wait()
    for t in range(tiles_ref.shape[0]):
        total[table[2, t]] += lax.dot_general(
            panel[table[0, t]], tiles_ref[t], NT, preferred_element_type=F32
        )
    for d in range(half):
        round_sums(swap_ref.at[d], total, (half + d) * group, group, vectors_n)


def round_sums(send, total, start, group, vectors_n):
    for k in range(group):
        send[k * vectors_n : (k + 1) * vectors_n, :] = total[start + k, :vectors_n, :].astype(BF16)
    if total.shape[1] > vectors_n:
        send[group * vectors_n :, :] = split_degree(degree_of(total, start, group, vectors_n))


def products(tiles, table, col_parts, row_parts, zeros, runs, degree):
    group, vectors_n, width = col_parts[0].shape
    half = len(row_parts) // 2
    rows_n = max(place + count for run in runs[0] for place, count in run) // group
    rows = group * vectors_n + (2 * group if degree else 0)
    height = vectors_n + (DEGREE_ROWS if degree else 0)
    send_shape = jax.ShapeDtypeStruct((rows, width), BF16)
    flops = 2 * tiles.size * vectors_n

    def panel(count):
        return pltpu.VMEM((count * group, height, width), BF16)

    fetched = [pltpu.SMEM(table.shape, table.dtype), pltpu.SemaphoreType.DMA(())]
    col_own, _, *col_send = call(
        functools.partial(column_kernel, runs[1]),
        [jax.ShapeDtypeStruct((group, height, width), F32), zeros[1]] + [send_shape] * (rows_n - 1),
        [panel(2 * half), *fetched],
        24,
        [table, tiles, *row_parts, zeros[1]],
        flops,
        0,
        (),
        {2 + len(row_parts): 1},
    )
    kept, swap = call(
        functools.partial(row_kernel, runs[0]),
        [zeros[0], jax.ShapeDtypeStruct((half, rows, width), BF16)],
        [panel(rows_n), *fetched],
        24,
        [table, tiles, *col_parts, zeros[0]],
        flops,
        0,
        [col_own],
        {3 + len(col_parts): 0},
    )
    return kept, swap, col_own, col_send


def merge_kernel(degree, vectors_n, kept, got, own_ref, *send_refs):
    if degree:
        own_degree, *send_refs = send_refs
    group = own_ref.shape[0]
    for k in range(group):
        rows = slice(k * vectors_n, (k + 1) * vectors_n)
        own_ref[k] = kept[k, :vectors_n, :] + got[0, rows, :].astype(F32)
        for d, send in enumerate(send_refs, 1):
            both = kept[d * group + k, :vectors_n, :] + got[d, rows, :].astype(F32)
            send[rows, :] = both.astype(BF16)
    if degree:
        for d in range(got.shape[0]):
            sums = degree_of(kept, d * group, group, vectors_n) + join_degree(got.at[d], group)
            if d:
                send_refs[d - 1][group * vectors_n :, :] = split_degree(sums)
            else:
                own_degree[...] = sums


def merge(kept, got, vectors_n, degree):
    half, width = got.shape[0], got.shape[2]
    group = kept.shape[0] // (2 * half)
    out_shape = [jax.ShapeDtypeStruct((group, vectors_n, width), F32)]
    if degree:
        out_shape += [jax.ShapeDtypeStruct((group, width), F32)]
    out_shape += [jax.ShapeDtypeStruct(got.shape[1:], BF16)] * (half - 1)
    kernel = functools.partial(merge_kernel, degree, vectors_n)
    return call(kernel, out_shape, [], 24, [kept, got])


def gathered_sum(own, received, k, vectors_n):
    total = own[k, :vectors_n, :]
    rows = slice(k * vectors_n, (k + 1) * vectors_n)
    for part in received:
        total = total + part[rows, :].astype(F32)
    return total


def symmetric_part(row_own, row_refs, col_own, col_refs, k, vectors_n):
    return 0.5 * (
        gathered_sum(row_own, row_refs, k, vectors_n)
        + gathered_sum(col_own, col_refs, k, vectors_n)
    )


def first_kernel(chips_n, vec_ref, row_degree, row_own, col_own, *refs):
    row_refs, refs = refs[: chips_n - 1], refs[chips_n - 1 :]
    col_refs, (first_ref, rounded_ref, degree_ref) = refs[:-3], refs[-3:]
    group, vectors_n, width = rounded_ref.shape
    degree = row_degree[...] + degree_of(col_own, 0, group, vectors_n)
    for part in (*row_refs, *col_refs):
        degree += join_degree(part, group)
    degree = 0.5 * degree
    degree_ref[...] = degree
    for k, vec in enumerate(tiles_first(vec_ref, width)):
        symmetric = symmetric_part(row_own, row_refs, col_own, col_refs, k, vectors_n)
        image = degree[k : k + 1, :] * vec - symmetric
        first = (image - CENTER * vec) / HALF_WIDTH
        first_ref[:, k * width : (k + 1) * width] = first
        rounded_ref[k] = first.astype(BF16)


def filter_kernel(chips_n, start_ref, first_ref, degree_ref, row_own, col_own, *refs):
    row_refs, refs = refs[: chips_n - 1], refs[chips_n - 1 :]
    col_refs, (filtered_ref, rounded_ref) = refs[:-2], refs[-2:]
    _, vectors_n, width = rounded_ref.shape
    for k, vec in enumerate(tiles_first(first_ref, width)):
        symmetric = symmetric_part(row_own, row_refs, col_own, col_refs, k, vectors_n)
        columns = slice(k * width, (k + 1) * width)
        image = degree_ref[k : k + 1, :] * vec - symmetric
        filtered = 2.0 * (image - CENTER * vec) / HALF_WIDTH - start_ref[:, columns]
        filtered_ref[:, columns] = filtered
        rounded_ref[k] = filtered.astype(BF16)


def gram_kernel(filtered_ref, degree_ref, gram_ref, both):
    vectors_n, width = filtered_ref.shape[0], degree_ref.shape[1]
    for k, vec in enumerate(tiles_first(filtered_ref, width)):
        columns = slice(k * width, (k + 1) * width)
        both[:vectors_n, columns] = vec
        both[vectors_n:, columns] = degree_ref[k : k + 1, :] * vec
    gram_ref[...] = lax.dot_general(
        filtered_ref[...], both[...], NT, precision=HIGHEST, preferred_element_type=F32
    )


def half_form_kernel(runs, source, tiles_ref, *refs):
    parts, (out_ref, panel, table, arrived) = refs[:-4], refs[-4:]
    copy = fetch(source, table, arrived)
    width = panel.shape[2]
    fill(panel, parts, runs)
    copy.wait()
    for t in range(tiles_ref.shape[0]):
        out_ref[:, t * width : (t + 1) * width] = lax.dot_general(
            panel[table[1, t]], tiles_ref[t], NN, preferred_element_type=F32
        ).astype(BF16)


def form_kernel(runs, source, left, gram_ref, *refs):
    parts, (out_ref, panel, right, table, arrived) = refs[:-5], refs[-5:]
    copy = fetch(source, table, arrived)
    _, vectors_n, width = panel.shape
    fill(panel, parts, runs)
    copy.wait()
    for t in range(right.shape[1] // width):
        right[:, t * width : (t + 1) * width] = panel[table[0, t]]
    form = lax.dot_general(left[...], right[...], NT, preferred_element_type=F32)
    projected = gram_ref[:, vectors_n:] - 0.5 * (form + form.T)
    row, col = square_index(vectors_n)
    packed = jnp.where(col >= row, gram_ref[:, :vectors_n], projected)
    diagonal = jnp.sum(jnp.where(row == col, projected, 0.0), 0, keepdims=True)
    half = vectors_n // 2
    out_ref[:half] = jnp.concatenate([packed[:half], packed[half:]], 1)
    diagonal = jnp.broadcast_to(diagonal, (8, vectors_n))
    out_ref[half:] = jnp.concatenate([diagonal, jnp.zeros_like(diagonal)], 1)


def square_index(n):
    return tuple(lax.broadcasted_iota(jnp.int32, (n, n), axis) for axis in (0, 1))


def inverse_factor(gram):
    n = gram.shape[0]
    row, col = square_index(n)
    table = jnp.concatenate([gram, jnp.where(row == col, 1.0, 0.0)], 1)
    bands = [table[i : i + 8] for i in range(0, n, 8)]
    shape = (8, 2 * n)
    line = lax.broadcasted_iota(jnp.int32, shape, 0)

    def spread(values, j):
        return jnp.broadcast_to(values[:, j : j + 1], shape)

    def pick(values, i):
        return jnp.broadcast_to(values[i : i + 1, :], shape)

    for at in range(n // 8):
        block = [spread(bands[at], 8 * at + c) for c in range(8)]
        forward, solved = bands[at], bands[at]
        solved_block = list(block)
        for s in range(8):
            scale = 1.0 / pick(block[s], s)
            below = jnp.where(line > s, block[s], 0.0) * scale
            above = jnp.where(line < s, solved_block[s] * scale, 0.0)
            both = below + above
            pivot_row = pick(forward, s)
            forward = forward - below * pivot_row
            solved = solved - both * pivot_row
            for c in range(s + 1, 8):
                pivot = pick(block[c], s)
                block[c] = block[c] - below * pivot
                solved_block[c] = solved_block[c] - both * pivot
        pivots = block[0]
        for s in range(1, 8):
            pivots = jnp.where(line == s, block[s], pivots)
        solved = solved / pivots
        bands[at] = forward / jnp.sqrt(pivots)
        for i in range(at + 1, n // 8):
            update = spread(bands[i], 8 * at) * pick(solved, 0)
            for c in range(1, 8):
                update = update + spread(bands[i], 8 * at + c) * pick(solved, c)
            bands[i] = bands[i] - update
    return jnp.concatenate(bands, 0)[:, n:]


def last_kernel(total_nodes, filtered_ref, *refs):
    (own, *parts), (ritz_ref, rayleigh_ref) = refs[:-2], refs[-2:]
    parts = [own, *parts[::-1]]
    n = filtered_ref.shape[0]
    half = n // 2
    sums = tree_sum([part[...] for part in parts]) * (1.0 / total_nodes)
    packed = jnp.concatenate([sums[:half, :n], sums[:half, n:]], 0)
    row, col = square_index(n)
    upper = jnp.where(col > row, packed, 0.0)
    gram = jnp.where(col >= row, packed, 0.0) + upper.T
    lower = jnp.where(col < row, packed, 0.0)
    diagonal = jnp.broadcast_to(sums[half : half + 1, :n], (n, n))
    projected = lower + lower.T + jnp.where(row == col, diagonal, 0.0)
    inverse = inverse_factor(gram)

    def dot(a, b, dims):
        return lax.dot_general(a, b, dims, precision=HIGHEST, preferred_element_type=F32)

    half_way = dot(inverse, projected, NN)
    rayleigh_ref[...] = dot(half_way, inverse, NT)
    turned = dot(inverse, half_way, NT)
    ritz_ref[...] = dot(turned, dot(inverse, filtered_ref[...], NN), NN)


def tree_sum(parts):
    while len(parts) > 1:
        parts = [a + b for a, b in zip(parts[::2], parts[1::2])]
    return parts[0]


def local(tiles, tile_rows, tile_cols, start):
    tiles, tile_rows, tile_cols = tiles[0, 0], tile_rows[0, 0], tile_cols[0, 0]
    width = tiles.shape[-1]
    vectors_n, own_nodes = start.shape
    rows_n, cols_n = lax.axis_size("row"), lax.axis_size("col")
    chips_n = cols_n // 2
    total_nodes = own_nodes * rows_n * cols_n
    group = own_nodes // width
    spread = (vectors_n, tiles.shape[0] * width)

    rounded_shape = jax.ShapeDtypeStruct((group, vectors_n, width), BF16)
    vector_shape = jax.ShapeDtypeStruct((vectors_n, own_nodes), F32)
    degree_shape = jax.ShapeDtypeStruct((group, width), F32)

    late = 1
    levels = [rows_n >> i for i in range(1, rows_n.bit_length())]
    col_runs = [[(0, group)]]
    for d in levels:
        if len(col_runs) == 1:
            col_runs += [[(d * group, group)]]
            continue
        cut = group - late
        passed = [((p // group ^ d) * group + p % group, n) for run in col_runs[1:] for p, n in run]
        col_runs += [[(d * group, cut)], [(d * group + cut, late), *passed]]
    chip_order = [0, *range(chips_n - 1, 0, -1)]
    row_runs = [[((2 * d + core) * group, group)] for core in range(2) for d in chip_order]
    runs = (col_runs, row_runs)
    def gather(rounded, first=()):
        held = [rounded]
        for d in levels:
            if len(held) == 1:
                held += [trade(rounded, "row", d)]
                continue
            near = trade(rounded[: group - late], "row", d)
            near, *passed = lax.optimization_barrier((near, *held[1:], *first))
            held[1:] = passed[: len(held) - 1]
            held += [near, trade(jnp.concatenate([rounded[group - late :], *held[1:]]), "row", d)]
        chips = [rounded, *exchange([rounded] * (chips_n - 1), "col", 2)[::-1]]
        return held, chips + [trade(chip, "col", 1) for chip in chips]

    def apply(rounded, table, degree, first=()):
        height = vectors_n + (DEGREE_ROWS if degree else 0)
        zeros = call(
            zero_kernel,
            [jax.ShapeDtypeStruct((n * group, height, width), F32) for n in (cols_n, rows_n)],
            [],
            16,
            [],
            4 * total_nodes * vectors_n,
        )
        parts = gather(rounded, (*first, *zeros))
        kept, swap, col_own, col_send = products(tiles, table, *parts, zeros, runs, degree)
        col_got = exchange(col_send, "row")
        row_own, *row_send = merge(kept, trade(swap, "col", 1), vectors_n, degree)
        row_degree = row_send[:1] if degree else []
        row_got = exchange(row_send[len(row_degree) :], "col", 2)[::-1]
        return [*row_degree, row_own, col_own, *row_got, *col_got]

    rounded = call(round_kernel, rounded_shape, [], 16, [start])
    meta = jnp.stack([lax.axis_index("row"), lax.axis_index("col"), chips_n]).astype(jnp.int32)
    meta = jnp.broadcast_to(meta[:, None], (3, tiles.shape[0]))
    table = call(
        functools.partial(table_kernel, group),
        jax.ShapeDtypeStruct((3, tiles.shape[0]), jnp.int32),
        [],
        16,
        [meta, tile_rows[None], tile_cols[None]],
    )
    first, rounded, degree = call(
        functools.partial(first_kernel, chips_n),
        [vector_shape, rounded_shape, degree_shape],
        [],
        24,
        [start, *apply(rounded, table, True, (table,))],
    )
    filtered, rounded = call(
        functools.partial(filter_kernel, chips_n),
        [vector_shape, rounded_shape],
        [],
        24,
        [start, first, degree, *apply(rounded, table, False)],
    )
    gram = call(
        gram_kernel,
        jax.ShapeDtypeStruct((vectors_n, 2 * vectors_n), F32),
        [pltpu.VMEM((2 * vectors_n, own_nodes), F32)],
        16,
        [filtered, degree],
        24 * vectors_n * vectors_n * own_nodes,
    )
    col_parts, row_parts = gather(rounded, (gram,))
    fetched = [pltpu.SMEM(table.shape, table.dtype), pltpu.SemaphoreType.DMA(())]
    left = call(
        functools.partial(half_form_kernel, runs[1]),
        jax.ShapeDtypeStruct(spread, BF16),
        [pltpu.VMEM((cols_n * group, vectors_n, width), BF16), *fetched],
        24,
        [table, tiles, *row_parts],
        2 * tiles.size * vectors_n,
    )
    sums = call(
        functools.partial(form_kernel, runs[0]),
        jax.ShapeDtypeStruct((vectors_n // 2 + 8, 2 * vectors_n), F32),
        [pltpu.VMEM((rows_n * group, vectors_n, width), BF16), pltpu.VMEM(spread, BF16), *fetched],
        24,
        [table, left, gram, *col_parts],
        2 * vectors_n * spread[0] * spread[1],
    )
    sums = sums + trade(sums, "col", 1)
    sums = tree_sum([*exchange([sums] * (chips_n - 1), "col", 2)[::-1], sums])
    return call(
        functools.partial(last_kernel, total_nodes),
        [vector_shape, jax.ShapeDtypeStruct((vectors_n, vectors_n), F32)],
        [],
        24,
        [filtered, sums, *exchange([sums] * (rows_n - 1), "row")[::-1]],
    )


def solution(mesh):
    placed = (
        P("row", "col", None, None, None),
        P("row", "col", None),
        P("row", "col", None),
        P(None, ("row", "col")),
    )
    return jax.shard_map(
        local, mesh=mesh, in_specs=placed, out_specs=(P(None, ("row", "col")), P()), check_vma=False
    )
```

```python
import functools

import jax
import jax.numpy as jnp
from jax import lax
from jax.experimental import pallas as pl
from jax.experimental.pallas import tpu as pltpu
from jax.sharding import PartitionSpec as P

CENTER = 1.0
HALF_WIDTH = 0.5
HIGHEST = lax.Precision.HIGHEST
NT = (((1,), (1,)), ((), ()))
NN = (((1,), (0,)), ((), ()))
BF16 = jnp.bfloat16
F32 = jnp.float32
VMEM = pl.BlockSpec(memory_space=pltpu.VMEM)
SMEM = pl.BlockSpec(memory_space=pltpu.SMEM)
ANY = pl.BlockSpec(memory_space=pl.ANY)
DEGREE_ROWS = 16


def call(kernel, out_shape, scratch, limit, args, flops=0, smem=0, after=(), aliases={}):
    moved = sum(x.size * x.dtype.itemsize for x in args)
    return pl.pallas_call(
        lambda *refs: kernel(*refs[len(after) :]),
        out_shape=jax.tree.map(lambda x: jax.ShapeDtypeStruct(x.shape, x.dtype), out_shape),
        in_specs=[ANY] * len(after) + [SMEM] * smem + [VMEM] * (len(args) - smem),
        out_specs=jax.tree.map(lambda _: VMEM, out_shape),
        scratch_shapes=scratch,
        input_output_aliases=aliases,
        compiler_params=pltpu.CompilerParams(vmem_limit_bytes=limit * 2**20),
        cost_estimate=pl.CostEstimate(flops=flops, bytes_accessed=moved, transcendentals=0),
    )(*after, *args)


def trade(part, axis, d):
    n = lax.axis_size(axis)
    return lax.ppermute(part, axis, [(i, i ^ d) for i in range(n)])


def exchange(parts, axis, step=1):
    far_first = [trade(part, axis, step * d) for d, part in reversed(list(enumerate(parts, 1)))]
    return far_first[::-1]


def tiles_first(ref, width):
    return [ref[:, k * width : (k + 1) * width] for k in range(ref.shape[1] // width)]


def round_kernel(vec_ref, out_ref):
    for k, piece in enumerate(tiles_first(vec_ref, out_ref.shape[2])):
        out_ref[k] = piece.astype(BF16)


def split_degree(sums):
    high = sums.astype(BF16).astype(F32)
    return jnp.concatenate([high, sums - high], 0).astype(BF16)


def join_degree(payload, group):
    parts = payload[payload.shape[0] - 2 * group :, :].astype(F32)
    return parts[:group] + parts[group:]


def fill(panel, parts, runs):
    for part, places in zip(parts, runs):
        at = 0
        for place, count in places:
            panel[place : place + count, : part.shape[1], :] = part[at : at + count]
            at += count


def table_kernel(group, meta, rows_ref, cols_ref, table):
    rows, cols = rows_ref[...], cols_ref[...]
    apart = lax.div(rows, group) ^ meta[1:2, :]
    halves = lax.rem(apart, 2) * meta[2:3, :] + lax.div(apart, 2)
    inside = lax.rem(rows, group)
    table[0:1, :] = (lax.div(cols, group) ^ meta[0:1, :]) * group + lax.rem(cols, group)
    table[1:2, :] = apart * group + inside
    table[2:3, :] = halves * group + inside


def fetch(source, table, arrived):
    copy = pltpu.make_async_copy(source, table, arrived)
    copy.start()
    return copy


def fill_ones(panel, vectors_n):
    rows = panel.shape[1] - vectors_n
    if rows:
        panel[:, vectors_n:, :] = jnp.ones((panel.shape[0], rows, panel.shape[2]), BF16)


def degree_of(total, start, group, vectors_n):
    return jnp.concatenate(
        [total[start + k, vectors_n : vectors_n + 1, :] for k in range(group)], 0
    )


def zero_kernel(*refs):
    for ref in refs:
        ref[...] = jnp.zeros_like(ref)


def column_kernel(runs, source, tiles_ref, *refs):
    parts, refs = refs[: len(runs)], refs[len(runs) :]
    _, own_ref, total, *send_refs, panel, table, arrived = refs
    copy = fetch(source, table, arrived)
    group, vectors_n, _ = parts[0].shape
    fill(panel, parts, runs)
    fill_ones(panel, vectors_n)
    copy.wait()
    for t in range(tiles_ref.shape[0]):
        total[table[0, t]] += lax.dot_general(
            panel[table[1, t]], tiles_ref[t], NN, preferred_element_type=F32
        )
    own_ref[...] = total[:group]
    for d, send in enumerate(send_refs, 1):
        round_sums(send, total, d * group, group, vectors_n)


def row_kernel(runs, source, tiles_ref, *refs):
    parts, refs = refs[: len(runs)], refs[len(runs) :]
    _, total, swap_ref, panel, table, arrived = refs
    copy = fetch(source, table, arrived)
    group, vectors_n, _ = parts[0].shape
    half = swap_ref.shape[0]
    fill(panel, parts, runs)
    fill_ones(panel, vectors_n)
    copy.wait()
    for t in range(tiles_ref.shape[0]):
        total[table[2, t]] += lax.dot_general(
            panel[table[0, t]], tiles_ref[t], NT, preferred_element_type=F32
        )
    for d in range(half):
        round_sums(swap_ref.at[d], total, (half + d) * group, group, vectors_n)


def round_sums(send, total, start, group, vectors_n):
    for k in range(group):
        send[k * vectors_n : (k + 1) * vectors_n, :] = total[start + k, :vectors_n, :].astype(BF16)
    if total.shape[1] > vectors_n:
        send[group * vectors_n :, :] = split_degree(degree_of(total, start, group, vectors_n))


def products(tiles, table, col_parts, row_parts, zeros, runs, degree):
    group, vectors_n, width = col_parts[0].shape
    half = len(row_parts) // 2
    rows_n = max(place + count for run in runs[0] for place, count in run) // group
    rows = group * vectors_n + (2 * group if degree else 0)
    height = vectors_n + (DEGREE_ROWS if degree else 0)
    send_shape = jax.ShapeDtypeStruct((rows, width), BF16)
    flops = 2 * tiles.size * vectors_n

    def panel(count):
        return pltpu.VMEM((count * group, height, width), BF16)

    fetched = [pltpu.SMEM(table.shape, table.dtype), pltpu.SemaphoreType.DMA(())]
    col_own, _, *col_send = call(
        functools.partial(column_kernel, runs[1]),
        [jax.ShapeDtypeStruct((group, height, width), F32), zeros[1]] + [send_shape] * (rows_n - 1),
        [panel(2 * half), *fetched],
        24,
        [table, tiles, *row_parts, zeros[1]],
        flops,
        0,
        (),
        {2 + len(row_parts): 1},
    )
    kept, swap = call(
        functools.partial(row_kernel, runs[0]),
        [zeros[0], jax.ShapeDtypeStruct((half, rows, width), BF16)],
        [panel(rows_n), *fetched],
        24,
        [table, tiles, *col_parts, zeros[0]],
        flops,
        0,
        [col_own],
        {3 + len(col_parts): 0},
    )
    return kept, swap, col_own, col_send


def merge_kernel(degree, vectors_n, kept, got, own_ref, *send_refs):
    if degree:
        own_degree, *send_refs = send_refs
    group = own_ref.shape[0]
    for k in range(group):
        rows = slice(k * vectors_n, (k + 1) * vectors_n)
        own_ref[k] = kept[k, :vectors_n, :] + got[0, rows, :].astype(F32)
        for d, send in enumerate(send_refs, 1):
            both = kept[d * group + k, :vectors_n, :] + got[d, rows, :].astype(F32)
            send[rows, :] = both.astype(BF16)
    if degree:
        for d in range(got.shape[0]):
            sums = degree_of(kept, d * group, group, vectors_n) + join_degree(got.at[d], group)
            if d:
                send_refs[d - 1][group * vectors_n :, :] = split_degree(sums)
            else:
                own_degree[...] = sums


def merge(kept, got, vectors_n, degree):
    half, width = got.shape[0], got.shape[2]
    group = kept.shape[0] // (2 * half)
    out_shape = [jax.ShapeDtypeStruct((group, vectors_n, width), F32)]
    if degree:
        out_shape += [jax.ShapeDtypeStruct((group, width), F32)]
    out_shape += [jax.ShapeDtypeStruct(got.shape[1:], BF16)] * (half - 1)
    kernel = functools.partial(merge_kernel, degree, vectors_n)
    return call(kernel, out_shape, [], 24, [kept, got])


def gathered_sum(own, received, k, vectors_n):
    total = own[k, :vectors_n, :]
    rows = slice(k * vectors_n, (k + 1) * vectors_n)
    for part in received:
        total = total + part[rows, :].astype(F32)
    return total


def symmetric_part(row_own, row_refs, col_own, col_refs, k, vectors_n):
    return 0.5 * (
        gathered_sum(row_own, row_refs, k, vectors_n)
        + gathered_sum(col_own, col_refs, k, vectors_n)
    )


def first_kernel(chips_n, vec_ref, row_degree, row_own, col_own, *refs):
    row_refs, refs = refs[: chips_n - 1], refs[chips_n - 1 :]
    col_refs, (first_ref, rounded_ref, degree_ref) = refs[:-3], refs[-3:]
    group, vectors_n, width = rounded_ref.shape
    degree = row_degree[...] + degree_of(col_own, 0, group, vectors_n)
    for part in (*row_refs, *col_refs):
        degree += join_degree(part, group)
    degree = 0.5 * degree
    degree_ref[...] = degree
    for k, vec in enumerate(tiles_first(vec_ref, width)):
        symmetric = symmetric_part(row_own, row_refs, col_own, col_refs, k, vectors_n)
        image = degree[k : k + 1, :] * vec - symmetric
        first = (image - CENTER * vec) / HALF_WIDTH
        first_ref[:, k * width : (k + 1) * width] = first
        rounded_ref[k] = first.astype(BF16)


def filter_kernel(chips_n, start_ref, first_ref, degree_ref, row_own, col_own, *refs):
    row_refs, refs = refs[: chips_n - 1], refs[chips_n - 1 :]
    col_refs, (filtered_ref, rounded_ref) = refs[:-2], refs[-2:]
    _, vectors_n, width = rounded_ref.shape
    for k, vec in enumerate(tiles_first(first_ref, width)):
        symmetric = symmetric_part(row_own, row_refs, col_own, col_refs, k, vectors_n)
        columns = slice(k * width, (k + 1) * width)
        image = degree_ref[k : k + 1, :] * vec - symmetric
        filtered = 2.0 * (image - CENTER * vec) / HALF_WIDTH - start_ref[:, columns]
        filtered_ref[:, columns] = filtered
        rounded_ref[k] = filtered.astype(BF16)


def gram_kernel(filtered_ref, degree_ref, gram_ref, both):
    vectors_n, width = filtered_ref.shape[0], degree_ref.shape[1]
    for k, vec in enumerate(tiles_first(filtered_ref, width)):
        columns = slice(k * width, (k + 1) * width)
        both[:vectors_n, columns] = vec
        both[vectors_n:, columns] = degree_ref[k : k + 1, :] * vec
    gram_ref[...] = lax.dot_general(
        filtered_ref[...], both[...], NT, precision=HIGHEST, preferred_element_type=F32
    )


def half_form_kernel(runs, source, tiles_ref, *refs):
    parts, (out_ref, panel, table, arrived) = refs[:-4], refs[-4:]
    copy = fetch(source, table, arrived)
    width = panel.shape[2]
    fill(panel, parts, runs)
    copy.wait()
    for t in range(tiles_ref.shape[0]):
        out_ref[:, t * width : (t + 1) * width] = lax.dot_general(
            panel[table[1, t]], tiles_ref[t], NN, preferred_element_type=F32
        ).astype(BF16)


def form_kernel(runs, source, left, gram_ref, *refs):
    parts, (out_ref, panel, right, table, arrived) = refs[:-5], refs[-5:]
    copy = fetch(source, table, arrived)
    _, vectors_n, width = panel.shape
    fill(panel, parts, runs)
    copy.wait()
    for t in range(right.shape[1] // width):
        right[:, t * width : (t + 1) * width] = panel[table[0, t]]
    form = lax.dot_general(left[...], right[...], NT, preferred_element_type=F32)
    projected = gram_ref[:, vectors_n:] - 0.5 * (form + form.T)
    row, col = square_index(vectors_n)
    packed = jnp.where(col >= row, gram_ref[:, :vectors_n], projected)
    diagonal = jnp.sum(jnp.where(row == col, projected, 0.0), 0, keepdims=True)
    half = vectors_n // 2
    out_ref[:half] = jnp.concatenate([packed[:half], packed[half:]], 1)
    diagonal = jnp.broadcast_to(diagonal, (8, vectors_n))
    out_ref[half:] = jnp.concatenate([diagonal, jnp.zeros_like(diagonal)], 1)


def square_index(n):
    return tuple(lax.broadcasted_iota(jnp.int32, (n, n), axis) for axis in (0, 1))


def refined_reciprocal(x):
    y = pl.reciprocal(x, approx=True)
    for _ in range(2):
        y = y * (2.0 - x * y)
    return y


def inverse_factor(gram):
    n = gram.shape[0]
    row, col = square_index(n)
    table = jnp.concatenate([gram, jnp.where(row == col, 1.0, 0.0)], 1)
    bands = [table[i : i + 8] for i in range(0, n, 8)]
    shape = (8, 2 * n)
    line = lax.broadcasted_iota(jnp.int32, shape, 0)

    def spread(values, j):
        return jnp.broadcast_to(values[:, j : j + 1], shape)

    def pick(values, i):
        return jnp.broadcast_to(values[i : i + 1, :], shape)

    for at in range(n // 8):
        block = [spread(bands[at], 8 * at + c) for c in range(8)]
        forward, solved = bands[at], bands[at]
        solved_block = list(block)
        for s in range(8):
            scale = refined_reciprocal(pick(block[s], s))
            below = jnp.where(line > s, block[s], 0.0) * scale
            above = jnp.where(line < s, solved_block[s] * scale, 0.0)
            both = below + above
            pivot_row = pick(forward, s)
            forward = forward - below * pivot_row
            solved = solved - both * pivot_row
            for c in range(s + 1, 8):
                pivot = pick(block[c], s)
                block[c] = block[c] - below * pivot
                solved_block[c] = solved_block[c] - both * pivot
        pivots = block[0]
        for s in range(1, 8):
            pivots = jnp.where(line == s, block[s], pivots)
        solved = solved / pivots
        bands[at] = forward / jnp.sqrt(pivots)
        for i in range(at + 1, n // 8):
            update = spread(bands[i], 8 * at) * pick(solved, 0)
            for c in range(1, 8):
                update = update + spread(bands[i], 8 * at + c) * pick(solved, c)
            bands[i] = bands[i] - update
    return jnp.concatenate(bands, 0)[:, n:]


def last_kernel(total_nodes, filtered_ref, *refs):
    (own, *parts), (ritz_ref, rayleigh_ref) = refs[:-2], refs[-2:]
    parts = [own, *parts[::-1]]
    n = filtered_ref.shape[0]
    half = n // 2
    sums = tree_sum([part[...] for part in parts]) * (1.0 / total_nodes)
    packed = jnp.concatenate([sums[:half, :n], sums[:half, n:]], 0)
    row, col = square_index(n)
    upper = jnp.where(col > row, packed, 0.0)
    gram = jnp.where(col >= row, packed, 0.0) + upper.T
    lower = jnp.where(col < row, packed, 0.0)
    diagonal = jnp.broadcast_to(sums[half : half + 1, :n], (n, n))
    projected = lower + lower.T + jnp.where(row == col, diagonal, 0.0)
    inverse = inverse_factor(gram)

    def dot(a, b, dims):
        return lax.dot_general(a, b, dims, precision=HIGHEST, preferred_element_type=F32)

    half_way = dot(inverse, projected, NN)
    rayleigh_ref[...] = dot(half_way, inverse, NT)
    turned = dot(inverse, half_way, NT)
    ritz_ref[...] = dot(turned, dot(inverse, filtered_ref[...], NN), NN)


def tree_sum(parts):
    while len(parts) > 1:
        parts = [a + b for a, b in zip(parts[::2], parts[1::2])]
    return parts[0]


def local(tiles, tile_rows, tile_cols, start):
    tiles, tile_rows, tile_cols = tiles[0, 0], tile_rows[0, 0], tile_cols[0, 0]
    width = tiles.shape[-1]
    vectors_n, own_nodes = start.shape
    rows_n, cols_n = lax.axis_size("row"), lax.axis_size("col")
    chips_n = cols_n // 2
    total_nodes = own_nodes * rows_n * cols_n
    group = own_nodes // width
    spread = (vectors_n, tiles.shape[0] * width)

    rounded_shape = jax.ShapeDtypeStruct((group, vectors_n, width), BF16)
    vector_shape = jax.ShapeDtypeStruct((vectors_n, own_nodes), F32)
    degree_shape = jax.ShapeDtypeStruct((group, width), F32)

    late = 1
    levels = [rows_n >> i for i in range(1, rows_n.bit_length())]
    col_runs = [[(0, group)]]
    for d in levels:
        if len(col_runs) == 1:
            col_runs += [[(d * group, group)]]
            continue
        cut = group - late
        passed = [((p // group ^ d) * group + p % group, n) for run in col_runs[1:] for p, n in run]
        col_runs += [[(d * group, cut)], [(d * group + cut, late), *passed]]
    chip_order = [0, *range(chips_n - 1, 0, -1)]
    row_runs = [[((2 * d + core) * group, group)] for core in range(2) for d in chip_order]
    runs = (col_runs, row_runs)
    def gather(rounded, first=()):
        held = [rounded]
        for d in levels:
            if len(held) == 1:
                held += [trade(rounded, "row", d)]
                continue
            near = trade(rounded[: group - late], "row", d)
            near, *passed = lax.optimization_barrier((near, *held[1:], *first))
            held[1:] = passed[: len(held) - 1]
            held += [near, trade(jnp.concatenate([rounded[group - late :], *held[1:]]), "row", d)]
        chips = [rounded, *exchange([rounded] * (chips_n - 1), "col", 2)[::-1]]
        return held, chips + [trade(chip, "col", 1) for chip in chips]

    def apply(rounded, table, degree, first=()):
        height = vectors_n + (DEGREE_ROWS if degree else 0)
        zeros = call(
            zero_kernel,
            [jax.ShapeDtypeStruct((n * group, height, width), F32) for n in (cols_n, rows_n)],
            [],
            16,
            [],
            4 * total_nodes * vectors_n,
        )
        parts = gather(rounded, (*first, *zeros))
        kept, swap, col_own, col_send = products(tiles, table, *parts, zeros, runs, degree)
        col_got = exchange(col_send, "row")
        row_own, *row_send = merge(kept, trade(swap, "col", 1), vectors_n, degree)
        row_degree = row_send[:1] if degree else []
        row_got = exchange(row_send[len(row_degree) :], "col", 2)[::-1]
        return [*row_degree, row_own, col_own, *row_got, *col_got]

    rounded = call(round_kernel, rounded_shape, [], 16, [start])
    meta = jnp.stack([lax.axis_index("row"), lax.axis_index("col"), chips_n]).astype(jnp.int32)
    meta = jnp.broadcast_to(meta[:, None], (3, tiles.shape[0]))
    table = call(
        functools.partial(table_kernel, group),
        jax.ShapeDtypeStruct((3, tiles.shape[0]), jnp.int32),
        [],
        16,
        [meta, tile_rows[None], tile_cols[None]],
    )
    first, rounded, degree = call(
        functools.partial(first_kernel, chips_n),
        [vector_shape, rounded_shape, degree_shape],
        [],
        24,
        [start, *apply(rounded, table, True, (table,))],
    )
    filtered, rounded = call(
        functools.partial(filter_kernel, chips_n),
        [vector_shape, rounded_shape],
        [],
        24,
        [start, first, degree, *apply(rounded, table, False)],
    )
    gram = call(
        gram_kernel,
        jax.ShapeDtypeStruct((vectors_n, 2 * vectors_n), F32),
        [pltpu.VMEM((2 * vectors_n, own_nodes), F32)],
        16,
        [filtered, degree],
        24 * vectors_n * vectors_n * own_nodes,
    )
    col_parts, row_parts = gather(rounded, (gram,))
    fetched = [pltpu.SMEM(table.shape, table.dtype), pltpu.SemaphoreType.DMA(())]
    left = call(
        functools.partial(half_form_kernel, runs[1]),
        jax.ShapeDtypeStruct(spread, BF16),
        [pltpu.VMEM((cols_n * group, vectors_n, width), BF16), *fetched],
        24,
        [table, tiles, *row_parts],
        2 * tiles.size * vectors_n,
    )
    sums = call(
        functools.partial(form_kernel, runs[0]),
        jax.ShapeDtypeStruct((vectors_n // 2 + 8, 2 * vectors_n), F32),
        [pltpu.VMEM((rows_n * group, vectors_n, width), BF16), pltpu.VMEM(spread, BF16), *fetched],
        24,
        [table, left, gram, *col_parts],
        2 * vectors_n * spread[0] * spread[1],
    )
    sums = sums + trade(sums, "col", 1)
    sums = tree_sum([*exchange([sums] * (chips_n - 1), "col", 2)[::-1], sums])
    return call(
        functools.partial(last_kernel, total_nodes),
        [vector_shape, jax.ShapeDtypeStruct((vectors_n, vectors_n), F32)],
        [],
        24,
        [filtered, sums, *exchange([sums] * (rows_n - 1), "row")[::-1]],
    )


def solution(mesh):
    placed = (
        P("row", "col", None, None, None),
        P("row", "col", None),
        P("row", "col", None),
        P(None, ("row", "col")),
    )
    return jax.shard_map(
        local, mesh=mesh, in_specs=placed, out_specs=(P(None, ("row", "col")), P()), check_vma=False
    )
```

```python
import functools

import jax
import jax.numpy as jnp
from jax import lax
from jax.experimental import pallas as pl
from jax.experimental.pallas import tpu as pltpu
from jax.sharding import PartitionSpec as P

CENTER = 1.0
HALF_WIDTH = 0.5
HIGHEST = lax.Precision.HIGHEST
NT = (((1,), (1,)), ((), ()))
NN = (((1,), (0,)), ((), ()))
BF16 = jnp.bfloat16
F32 = jnp.float32
VMEM = pl.BlockSpec(memory_space=pltpu.VMEM)
SMEM = pl.BlockSpec(memory_space=pltpu.SMEM)
ANY = pl.BlockSpec(memory_space=pl.ANY)
DEGREE_ROWS = 16


def call(kernel, out_shape, scratch, limit, args, flops=0, smem=0, after=(), aliases={}):
    moved = sum(x.size * x.dtype.itemsize for x in args)
    return pl.pallas_call(
        lambda *refs: kernel(*refs[len(after) :]),
        out_shape=jax.tree.map(lambda x: jax.ShapeDtypeStruct(x.shape, x.dtype), out_shape),
        in_specs=[ANY] * len(after) + [SMEM] * smem + [VMEM] * (len(args) - smem),
        out_specs=jax.tree.map(lambda _: VMEM, out_shape),
        scratch_shapes=scratch,
        input_output_aliases=aliases,
        compiler_params=pltpu.CompilerParams(vmem_limit_bytes=limit * 2**20),
        cost_estimate=pl.CostEstimate(flops=flops, bytes_accessed=moved, transcendentals=0),
    )(*after, *args)


def trade(part, axis, d):
    n = lax.axis_size(axis)
    return lax.ppermute(part, axis, [(i, i ^ d) for i in range(n)])


def exchange(parts, axis, step=1):
    far_first = [trade(part, axis, step * d) for d, part in reversed(list(enumerate(parts, 1)))]
    return far_first[::-1]


def tiles_first(ref, width):
    return [ref[:, k * width : (k + 1) * width] for k in range(ref.shape[1] // width)]


def round_kernel(vec_ref, out_ref):
    for k, piece in enumerate(tiles_first(vec_ref, out_ref.shape[2])):
        out_ref[k] = piece.astype(BF16)


def split_degree(sums):
    high = sums.astype(BF16).astype(F32)
    return jnp.concatenate([high, sums - high], 0).astype(BF16)


def join_degree(payload, group):
    parts = payload[payload.shape[0] - 2 * group :, :].astype(F32)
    return parts[:group] + parts[group:]


def fill(panel, parts, runs):
    for part, places in zip(parts, runs):
        at = 0
        for place, count in places:
            panel[place : place + count, : part.shape[1], :] = part[at : at + count]
            at += count


def table_kernel(group, meta, rows_ref, cols_ref, table):
    rows, cols = rows_ref[...], cols_ref[...]
    apart = lax.div(rows, group) ^ meta[1:2, :]
    halves = lax.rem(apart, 2) * meta[2:3, :] + lax.div(apart, 2)
    inside = lax.rem(rows, group)
    table[0:1, :] = (lax.div(cols, group) ^ meta[0:1, :]) * group + lax.rem(cols, group)
    table[1:2, :] = apart * group + inside
    table[2:3, :] = halves * group + inside


def fetch(source, table, arrived):
    copy = pltpu.make_async_copy(source, table, arrived)
    copy.start()
    return copy


def fill_ones(panel, vectors_n):
    rows = panel.shape[1] - vectors_n
    if rows:
        panel[:, vectors_n:, :] = jnp.ones((panel.shape[0], rows, panel.shape[2]), BF16)


def degree_of(total, start, group, vectors_n):
    return jnp.concatenate(
        [total[start + k, vectors_n : vectors_n + 1, :] for k in range(group)], 0
    )


def hold_kernel(tiles_ref, held_ref):
    held_ref[...] = tiles_ref[...]


def zero_kernel(*refs):
    for ref in refs:
        ref[...] = jnp.zeros_like(ref)


def column_kernel(runs, source, tiles_ref, *refs):
    parts, refs = refs[: len(runs)], refs[len(runs) :]
    _, own_ref, total, *send_refs, panel, table, arrived = refs
    copy = fetch(source, table, arrived)
    group, vectors_n, _ = parts[0].shape
    fill(panel, parts, runs)
    fill_ones(panel, vectors_n)
    copy.wait()
    for t in range(tiles_ref.shape[0]):
        total[table[0, t]] += lax.dot_general(
            panel[table[1, t]], tiles_ref[t], NN, preferred_element_type=F32
        )
    own_ref[...] = total[:group]
    for d, send in enumerate(send_refs, 1):
        round_sums(send, total, d * group, group, vectors_n)


def row_kernel(runs, source, tiles_ref, *refs):
    parts, refs = refs[: len(runs)], refs[len(runs) :]
    _, total, swap_ref, panel, table, arrived = refs
    copy = fetch(source, table, arrived)
    group, vectors_n, _ = parts[0].shape
    half = swap_ref.shape[0]
    fill(panel, parts, runs)
    fill_ones(panel, vectors_n)
    copy.wait()
    for t in range(tiles_ref.shape[0]):
        total[table[2, t]] += lax.dot_general(
            panel[table[0, t]], tiles_ref[t], NT, preferred_element_type=F32
        )
    for d in range(half):
        round_sums(swap_ref.at[d], total, (half + d) * group, group, vectors_n)


def round_sums(send, total, start, group, vectors_n):
    for k in range(group):
        send[k * vectors_n : (k + 1) * vectors_n, :] = total[start + k, :vectors_n, :].astype(BF16)
    if total.shape[1] > vectors_n:
        send[group * vectors_n :, :] = split_degree(degree_of(total, start, group, vectors_n))


def products(tiles, table, col_parts, row_parts, zeros, runs, degree):
    group, vectors_n, width = col_parts[0].shape
    half = len(row_parts) // 2
    rows_n = max(place + count for run in runs[0] for place, count in run) // group
    rows = group * vectors_n + (2 * group if degree else 0)
    height = vectors_n + (DEGREE_ROWS if degree else 0)
    send_shape = jax.ShapeDtypeStruct((rows, width), BF16)
    flops = 2 * tiles.size * vectors_n

    def panel(count):
        return pltpu.VMEM((count * group, height, width), BF16)

    fetched = [pltpu.SMEM(table.shape, table.dtype), pltpu.SemaphoreType.DMA(())]
    col_own, _, *col_send = call(
        functools.partial(column_kernel, runs[1]),
        [jax.ShapeDtypeStruct((group, height, width), F32), zeros[1]] + [send_shape] * (rows_n - 1),
        [panel(2 * half), *fetched],
        24,
        [table, tiles, *row_parts, zeros[1]],
        flops,
        0,
        (),
        {2 + len(row_parts): 1},
    )
    kept, swap = call(
        functools.partial(row_kernel, runs[0]),
        [zeros[0], jax.ShapeDtypeStruct((half, rows, width), BF16)],
        [panel(rows_n), *fetched],
        24,
        [table, tiles, *col_parts, zeros[0]],
        flops,
        0,
        [col_own],
        {3 + len(col_parts): 0},
    )
    return kept, swap, col_own, col_send


def merge_kernel(degree, vectors_n, kept, got, own_ref, *send_refs):
    if degree:
        own_degree, *send_refs = send_refs
    group = own_ref.shape[0]
    for k in range(group):
        rows = slice(k * vectors_n, (k + 1) * vectors_n)
        own_ref[k] = kept[k, :vectors_n, :] + got[0, rows, :].astype(F32)
        for d, send in enumerate(send_refs, 1):
            both = kept[d * group + k, :vectors_n, :] + got[d, rows, :].astype(F32)
            send[rows, :] = both.astype(BF16)
    if degree:
        for d in range(got.shape[0]):
            sums = degree_of(kept, d * group, group, vectors_n) + join_degree(got.at[d], group)
            if d:
                send_refs[d - 1][group * vectors_n :, :] = split_degree(sums)
            else:
                own_degree[...] = sums


def merge(kept, got, vectors_n, degree):
    half, width = got.shape[0], got.shape[2]
    group = kept.shape[0] // (2 * half)
    out_shape = [jax.ShapeDtypeStruct((group, vectors_n, width), F32)]
    if degree:
        out_shape += [jax.ShapeDtypeStruct((group, width), F32)]
    out_shape += [jax.ShapeDtypeStruct(got.shape[1:], BF16)] * (half - 1)
    kernel = functools.partial(merge_kernel, degree, vectors_n)
    return call(kernel, out_shape, [], 24, [kept, got])


def gathered_sum(own, received, k, vectors_n):
    total = own[k, :vectors_n, :]
    rows = slice(k * vectors_n, (k + 1) * vectors_n)
    for part in received:
        total = total + part[rows, :].astype(F32)
    return total


def symmetric_part(row_own, row_refs, col_own, col_refs, k, vectors_n):
    return 0.5 * (
        gathered_sum(row_own, row_refs, k, vectors_n)
        + gathered_sum(col_own, col_refs, k, vectors_n)
    )


def first_kernel(chips_n, vec_ref, row_degree, row_own, col_own, *refs):
    row_refs, refs = refs[: chips_n - 1], refs[chips_n - 1 :]
    col_refs, (first_ref, rounded_ref, degree_ref) = refs[:-3], refs[-3:]
    group, vectors_n, width = rounded_ref.shape
    degree = row_degree[...] + degree_of(col_own, 0, group, vectors_n)
    for part in (*row_refs, *col_refs):
        degree += join_degree(part, group)
    degree = 0.5 * degree
    degree_ref[...] = degree
    for k, vec in enumerate(tiles_first(vec_ref, width)):
        symmetric = symmetric_part(row_own, row_refs, col_own, col_refs, k, vectors_n)
        image = degree[k : k + 1, :] * vec - symmetric
        first = (image - CENTER * vec) / HALF_WIDTH
        first_ref[:, k * width : (k + 1) * width] = first
        rounded_ref[k] = first.astype(BF16)


def filter_kernel(chips_n, start_ref, first_ref, degree_ref, row_own, col_own, *refs):
    row_refs, refs = refs[: chips_n - 1], refs[chips_n - 1 :]
    col_refs, (filtered_ref, rounded_ref) = refs[:-2], refs[-2:]
    _, vectors_n, width = rounded_ref.shape
    for k, vec in enumerate(tiles_first(first_ref, width)):
        symmetric = symmetric_part(row_own, row_refs, col_own, col_refs, k, vectors_n)
        columns = slice(k * width, (k + 1) * width)
        image = degree_ref[k : k + 1, :] * vec - symmetric
        filtered = 2.0 * (image - CENTER * vec) / HALF_WIDTH - start_ref[:, columns]
        filtered_ref[:, columns] = filtered
        rounded_ref[k] = filtered.astype(BF16)


def gram_kernel(filtered_ref, degree_ref, gram_ref, both):
    vectors_n, width = filtered_ref.shape[0], degree_ref.shape[1]
    for k, vec in enumerate(tiles_first(filtered_ref, width)):
        columns = slice(k * width, (k + 1) * width)
        both[:vectors_n, columns] = vec
        both[vectors_n:, columns] = degree_ref[k : k + 1, :] * vec
    gram_ref[...] = lax.dot_general(
        filtered_ref[...], both[...], NT, precision=HIGHEST, preferred_element_type=F32
    )


def half_form_kernel(runs, source, tiles_ref, *refs):
    parts, (out_ref, panel, table, arrived) = refs[:-4], refs[-4:]
    copy = fetch(source, table, arrived)
    width = panel.shape[2]
    fill(panel, parts, runs)
    copy.wait()
    for t in range(tiles_ref.shape[0]):
        out_ref[:, t * width : (t + 1) * width] = lax.dot_general(
            panel[table[1, t]], tiles_ref[t], NN, preferred_element_type=F32
        ).astype(BF16)


def form_kernel(runs, source, left, gram_ref, *refs):
    parts, (out_ref, panel, right, table, arrived) = refs[:-5], refs[-5:]
    copy = fetch(source, table, arrived)
    _, vectors_n, width = panel.shape
    fill(panel, parts, runs)
    copy.wait()
    for t in range(right.shape[1] // width):
        right[:, t * width : (t + 1) * width] = panel[table[0, t]]
    form = lax.dot_general(left[...], right[...], NT, preferred_element_type=F32)
    projected = gram_ref[:, vectors_n:] - 0.5 * (form + form.T)
    row, col = square_index(vectors_n)
    packed = jnp.where(col >= row, gram_ref[:, :vectors_n], projected)
    diagonal = jnp.sum(jnp.where(row == col, projected, 0.0), 0, keepdims=True)
    half = vectors_n // 2
    out_ref[:half] = jnp.concatenate([packed[:half], packed[half:]], 1)
    diagonal = jnp.broadcast_to(diagonal, (8, vectors_n))
    out_ref[half:] = jnp.concatenate([diagonal, jnp.zeros_like(diagonal)], 1)


def square_index(n):
    return tuple(lax.broadcasted_iota(jnp.int32, (n, n), axis) for axis in (0, 1))


def inverse_factor(gram):
    n = gram.shape[0]
    row, col = square_index(n)
    table = jnp.concatenate([gram, jnp.where(row == col, 1.0, 0.0)], 1)
    bands = [table[i : i + 8] for i in range(0, n, 8)]
    shape = (8, 2 * n)
    line = lax.broadcasted_iota(jnp.int32, shape, 0)

    def spread(values, j):
        return jnp.broadcast_to(values[:, j : j + 1], shape)

    def pick(values, i):
        return jnp.broadcast_to(values[i : i + 1, :], shape)

    for at in range(n // 8):
        block = [spread(bands[at], 8 * at + c) for c in range(8)]
        forward, solved = bands[at], bands[at]
        solved_block = list(block)
        for s in range(8):
            scale = 1.0 / pick(block[s], s)
            below = jnp.where(line > s, block[s], 0.0) * scale
            above = jnp.where(line < s, solved_block[s] * scale, 0.0)
            both = below + above
            pivot_row = pick(forward, s)
            forward = forward - below * pivot_row
            solved = solved - both * pivot_row
            for c in range(s + 1, 8):
                pivot = pick(block[c], s)
                block[c] = block[c] - below * pivot
                solved_block[c] = solved_block[c] - both * pivot
        pivots = block[0]
        for s in range(1, 8):
            pivots = jnp.where(line == s, block[s], pivots)
        solved = solved / pivots
        bands[at] = forward / jnp.sqrt(pivots)
        for i in range(at + 1, n // 8):
            update = spread(bands[i], 8 * at) * pick(solved, 0)
            for c in range(1, 8):
                update = update + spread(bands[i], 8 * at + c) * pick(solved, c)
            bands[i] = bands[i] - update
    return jnp.concatenate(bands, 0)[:, n:]


def last_kernel(total_nodes, filtered_ref, *refs):
    (own, *parts), (ritz_ref, rayleigh_ref) = refs[:-2], refs[-2:]
    parts = [own, *parts[::-1]]
    n = filtered_ref.shape[0]
    half = n // 2
    sums = tree_sum([part[...] for part in parts]) * (1.0 / total_nodes)
    packed = jnp.concatenate([sums[:half, :n], sums[:half, n:]], 0)
    row, col = square_index(n)
    upper = jnp.where(col > row, packed, 0.0)
    gram = jnp.where(col >= row, packed, 0.0) + upper.T
    lower = jnp.where(col < row, packed, 0.0)
    diagonal = jnp.broadcast_to(sums[half : half + 1, :n], (n, n))
    projected = lower + lower.T + jnp.where(row == col, diagonal, 0.0)
    inverse = inverse_factor(gram)

    def dot(a, b, dims):
        return lax.dot_general(a, b, dims, precision=HIGHEST, preferred_element_type=F32)

    half_way = dot(inverse, projected, NN)
    rayleigh_ref[...] = dot(half_way, inverse, NT)
    turned = dot(inverse, half_way, NT)
    ritz_ref[...] = dot(turned, dot(inverse, filtered_ref[...], NN), NN)


def tree_sum(parts):
    while len(parts) > 1:
        parts = [a + b for a, b in zip(parts[::2], parts[1::2])]
    return parts[0]


def local(tiles, tile_rows, tile_cols, start):
    tiles, tile_rows, tile_cols = tiles[0, 0], tile_rows[0, 0], tile_cols[0, 0]
    width = tiles.shape[-1]
    vectors_n, own_nodes = start.shape
    rows_n, cols_n = lax.axis_size("row"), lax.axis_size("col")
    chips_n = cols_n // 2
    total_nodes = own_nodes * rows_n * cols_n
    group = own_nodes // width
    spread = (vectors_n, tiles.shape[0] * width)

    rounded_shape = jax.ShapeDtypeStruct((group, vectors_n, width), BF16)
    vector_shape = jax.ShapeDtypeStruct((vectors_n, own_nodes), F32)
    degree_shape = jax.ShapeDtypeStruct((group, width), F32)

    late = 1
    levels = [rows_n >> i for i in range(1, rows_n.bit_length())]
    col_runs = [[(0, group)]]
    for d in levels:
        if len(col_runs) == 1:
            col_runs += [[(d * group, group)]]
            continue
        cut = group - late
        passed = [((p // group ^ d) * group + p % group, n) for run in col_runs[1:] for p, n in run]
        col_runs += [[(d * group, cut)], [(d * group + cut, late), *passed]]
    chip_order = [0, *range(chips_n - 1, 0, -1)]
    row_runs = [[((2 * d + core) * group, group)] for core in range(2) for d in chip_order]
    runs = (col_runs, row_runs)
    def gather(rounded, first=()):
        held = [rounded]
        for d in levels:
            if len(held) == 1:
                held += [trade(rounded, "row", d)]
                continue
            near = trade(rounded[: group - late], "row", d)
            near, *passed = lax.optimization_barrier((near, *held[1:], *first))
            held[1:] = passed[: len(held) - 1]
            held += [near, trade(jnp.concatenate([rounded[group - late :], *held[1:]]), "row", d)]
        chips = [rounded, *exchange([rounded] * (chips_n - 1), "col", 2)[::-1]]
        return held, chips + [trade(chip, "col", 1) for chip in chips]

    def apply(rounded, table, degree, first=()):
        height = vectors_n + (DEGREE_ROWS if degree else 0)
        zeros = call(
            zero_kernel,
            [jax.ShapeDtypeStruct((n * group, height, width), F32) for n in (cols_n, rows_n)],
            [],
            16,
            [],
            4 * total_nodes * vectors_n,
        )
        parts = gather(rounded, (*first, *zeros))
        kept, swap, col_own, col_send = products(tiles, table, *parts, zeros, runs, degree)
        col_got = exchange(col_send, "row")
        row_own, *row_send = merge(kept, trade(swap, "col", 1), vectors_n, degree)
        row_degree = row_send[:1] if degree else []
        row_got = exchange(row_send[len(row_degree) :], "col", 2)[::-1]
        return [*row_degree, row_own, col_own, *row_got, *col_got]

    rounded = call(round_kernel, rounded_shape, [], 16, [start])
    meta = jnp.stack([lax.axis_index("row"), lax.axis_index("col"), chips_n]).astype(jnp.int32)
    meta = jnp.broadcast_to(meta[:, None], (3, tiles.shape[0]))
    table = call(
        functools.partial(table_kernel, group),
        jax.ShapeDtypeStruct((3, tiles.shape[0]), jnp.int32),
        [],
        16,
        [meta, tile_rows[None], tile_cols[None]],
    )
    tiles = call(
        hold_kernel,
        jax.ShapeDtypeStruct(tiles.shape, BF16),
        [],
        16,
        [tiles],
        4 * tiles.size * DEGREE_ROWS,
    )
    first, rounded, degree = call(
        functools.partial(first_kernel, chips_n),
        [vector_shape, rounded_shape, degree_shape],
        [],
        24,
        [start, *apply(rounded, table, True, (table,))],
    )
    filtered, rounded = call(
        functools.partial(filter_kernel, chips_n),
        [vector_shape, rounded_shape],
        [],
        24,
        [start, first, degree, *apply(rounded, table, False)],
    )
    gram = call(
        gram_kernel,
        jax.ShapeDtypeStruct((vectors_n, 2 * vectors_n), F32),
        [pltpu.VMEM((2 * vectors_n, own_nodes), F32)],
        16,
        [filtered, degree],
        24 * vectors_n * vectors_n * own_nodes,
    )
    col_parts, row_parts = gather(rounded, (gram,))
    fetched = [pltpu.SMEM(table.shape, table.dtype), pltpu.SemaphoreType.DMA(())]
    left = call(
        functools.partial(half_form_kernel, runs[1]),
        jax.ShapeDtypeStruct(spread, BF16),
        [pltpu.VMEM((cols_n * group, vectors_n, width), BF16), *fetched],
        24,
        [table, tiles, *row_parts],
        2 * tiles.size * vectors_n,
    )
    sums = call(
        functools.partial(form_kernel, runs[0]),
        jax.ShapeDtypeStruct((vectors_n // 2 + 8, 2 * vectors_n), F32),
        [pltpu.VMEM((rows_n * group, vectors_n, width), BF16), pltpu.VMEM(spread, BF16), *fetched],
        24,
        [table, left, gram, *col_parts],
        2 * vectors_n * spread[0] * spread[1],
    )
    sums = sums + trade(sums, "col", 1)
    sums = tree_sum([*exchange([sums] * (chips_n - 1), "col", 2)[::-1], sums])
    return call(
        functools.partial(last_kernel, total_nodes),
        [vector_shape, jax.ShapeDtypeStruct((vectors_n, vectors_n), F32)],
        [],
        24,
        [filtered, sums, *exchange([sums] * (rows_n - 1), "row")[::-1]],
    )


def solution(mesh):
    placed = (
        P("row", "col", None, None, None),
        P("row", "col", None),
        P("row", "col", None),
        P(None, ("row", "col")),
    )
    return jax.shard_map(
        local, mesh=mesh, in_specs=placed, out_specs=(P(None, ("row", "col")), P()), check_vma=False
    )
```

```python
import functools

import jax
import jax.numpy as jnp
from jax import lax
from jax.experimental import pallas as pl
from jax.experimental.pallas import tpu as pltpu
from jax.sharding import PartitionSpec as P

CENTER = 1.0
HALF_WIDTH = 0.5
HIGHEST = lax.Precision.HIGHEST
NT = (((1,), (1,)), ((), ()))
NN = (((1,), (0,)), ((), ()))
BF16 = jnp.bfloat16
F32 = jnp.float32
VMEM = pl.BlockSpec(memory_space=pltpu.VMEM)
SMEM = pl.BlockSpec(memory_space=pltpu.SMEM)
ANY = pl.BlockSpec(memory_space=pl.ANY)
DEGREE_ROWS = 16


def call(kernel, out_shape, scratch, limit, args, flops=0, smem=0, after=(), aliases={}):
    moved = sum(x.size * x.dtype.itemsize for x in args)
    return pl.pallas_call(
        lambda *refs: kernel(*refs[len(after) :]),
        out_shape=jax.tree.map(lambda x: jax.ShapeDtypeStruct(x.shape, x.dtype), out_shape),
        in_specs=[ANY] * len(after) + [SMEM] * smem + [VMEM] * (len(args) - smem),
        out_specs=jax.tree.map(lambda _: VMEM, out_shape),
        scratch_shapes=scratch,
        input_output_aliases=aliases,
        compiler_params=pltpu.CompilerParams(vmem_limit_bytes=limit * 2**20),
        cost_estimate=pl.CostEstimate(flops=flops, bytes_accessed=moved, transcendentals=0),
    )(*after, *args)


def trade(part, axis, d):
    n = lax.axis_size(axis)
    return lax.ppermute(part, axis, [(i, i ^ d) for i in range(n)])


def exchange(parts, axis, step=1):
    far_first = [trade(part, axis, step * d) for d, part in reversed(list(enumerate(parts, 1)))]
    return far_first[::-1]


def tiles_first(ref, width):
    return [ref[:, k * width : (k + 1) * width] for k in range(ref.shape[1] // width)]


def round_kernel(vec_ref, meta, rows_ref, cols_ref, out_ref, table):
    group = out_ref.shape[0]
    for k, piece in enumerate(tiles_first(vec_ref, out_ref.shape[2])):
        out_ref[k] = piece.astype(BF16)
    rows, cols = rows_ref[...], cols_ref[...]
    apart = lax.div(rows, group) ^ meta[1:2, :]
    halves = lax.rem(apart, 2) * meta[2:3, :] + lax.div(apart, 2)
    inside = lax.rem(rows, group)
    table[0:1, :] = (lax.div(cols, group) ^ meta[0:1, :]) * group + lax.rem(cols, group)
    table[1:2, :] = apart * group + inside
    table[2:3, :] = halves * group + inside


def split_degree(sums):
    high = sums.astype(BF16).astype(F32)
    return jnp.concatenate([high, sums - high], 0).astype(BF16)


def join_degree(payload, group):
    parts = payload[payload.shape[0] - 2 * group :, :].astype(F32)
    return parts[:group] + parts[group:]


def fill(panel, parts, runs):
    for part, places in zip(parts, runs):
        at = 0
        for place, count in places:
            panel[place : place + count, : part.shape[1], :] = part[at : at + count]
            at += count


def fetch(source, table, arrived):
    copy = pltpu.make_async_copy(source, table, arrived)
    copy.start()
    return copy


def fill_ones(panel, vectors_n):
    rows = panel.shape[1] - vectors_n
    if rows:
        panel[:, vectors_n:, :] = jnp.ones((panel.shape[0], rows, panel.shape[2]), BF16)


def degree_of(total, start, group, vectors_n):
    return jnp.concatenate(
        [total[start + k, vectors_n : vectors_n + 1, :] for k in range(group)], 0
    )


def hold_kernel(tiles_ref, held_ref):
    held_ref[...] = tiles_ref[...]


def zero_kernel(*refs):
    for ref in refs:
        ref[...] = jnp.zeros_like(ref)


def column_kernel(runs, source, tiles_ref, *refs):
    parts, refs = refs[: len(runs)], refs[len(runs) :]
    _, own_ref, total, *send_refs, panel, table, arrived = refs
    copy = fetch(source, table, arrived)
    group, vectors_n, _ = parts[0].shape
    fill(panel, parts, runs)
    fill_ones(panel, vectors_n)
    copy.wait()
    for t in range(tiles_ref.shape[0]):
        total[table[0, t]] += lax.dot_general(
            panel[table[1, t]], tiles_ref[t], NN, preferred_element_type=F32
        )
    own_ref[...] = total[:group]
    for d, send in enumerate(send_refs, 1):
        round_sums(send, total, d * group, group, vectors_n)


def row_kernel(runs, source, tiles_ref, *refs):
    parts, refs = refs[: len(runs)], refs[len(runs) :]
    _, total, swap_ref, panel, table, arrived = refs
    copy = fetch(source, table, arrived)
    group, vectors_n, _ = parts[0].shape
    half = swap_ref.shape[0]
    fill(panel, parts, runs)
    fill_ones(panel, vectors_n)
    copy.wait()
    for t in range(tiles_ref.shape[0]):
        total[table[2, t]] += lax.dot_general(
            panel[table[0, t]], tiles_ref[t], NT, preferred_element_type=F32
        )
    for d in range(half):
        round_sums(swap_ref.at[d], total, (half + d) * group, group, vectors_n)


def round_sums(send, total, start, group, vectors_n):
    for k in range(group):
        send[k * vectors_n : (k + 1) * vectors_n, :] = total[start + k, :vectors_n, :].astype(BF16)
    if total.shape[1] > vectors_n:
        send[group * vectors_n :, :] = split_degree(degree_of(total, start, group, vectors_n))


def products(tiles, table, col_parts, row_parts, zeros, runs, degree):
    group, vectors_n, width = col_parts[0].shape
    half = len(row_parts) // 2
    rows_n = max(place + count for run in runs[0] for place, count in run) // group
    rows = group * vectors_n + (2 * group if degree else 0)
    height = vectors_n + (DEGREE_ROWS if degree else 0)
    send_shape = jax.ShapeDtypeStruct((rows, width), BF16)
    flops = 2 * tiles.size * vectors_n

    def panel(count):
        return pltpu.VMEM((count * group, height, width), BF16)

    fetched = [pltpu.SMEM(table.shape, table.dtype), pltpu.SemaphoreType.DMA(())]
    col_own, _, *col_send = call(
        functools.partial(column_kernel, runs[1]),
        [jax.ShapeDtypeStruct((group, height, width), F32), zeros[1]] + [send_shape] * (rows_n - 1),
        [panel(2 * half), *fetched],
        24,
        [table, tiles, *row_parts, zeros[1]],
        flops,
        0,
        (),
        {2 + len(row_parts): 1},
    )
    kept, swap = call(
        functools.partial(row_kernel, runs[0]),
        [zeros[0], jax.ShapeDtypeStruct((half, rows, width), BF16)],
        [panel(rows_n), *fetched],
        24,
        [table, tiles, *col_parts, zeros[0]],
        flops,
        0,
        [col_own],
        {3 + len(col_parts): 0},
    )
    return kept, swap, col_own, col_send


def merge_kernel(degree, vectors_n, kept, got, own_ref, *send_refs):
    if degree:
        own_degree, *send_refs = send_refs
    group = own_ref.shape[0]
    for k in range(group):
        rows = slice(k * vectors_n, (k + 1) * vectors_n)
        own_ref[k] = kept[k, :vectors_n, :] + got[0, rows, :].astype(F32)
        for d, send in enumerate(send_refs, 1):
            both = kept[d * group + k, :vectors_n, :] + got[d, rows, :].astype(F32)
            send[rows, :] = both.astype(BF16)
    if degree:
        for d in range(got.shape[0]):
            sums = degree_of(kept, d * group, group, vectors_n) + join_degree(got.at[d], group)
            if d:
                send_refs[d - 1][group * vectors_n :, :] = split_degree(sums)
            else:
                own_degree[...] = sums


def merge(kept, got, vectors_n, degree):
    half, width = got.shape[0], got.shape[2]
    group = kept.shape[0] // (2 * half)
    out_shape = [jax.ShapeDtypeStruct((group, vectors_n, width), F32)]
    if degree:
        out_shape += [jax.ShapeDtypeStruct((group, width), F32)]
    out_shape += [jax.ShapeDtypeStruct(got.shape[1:], BF16)] * (half - 1)
    kernel = functools.partial(merge_kernel, degree, vectors_n)
    return call(kernel, out_shape, [], 24, [kept, got])


def gathered_sum(own, received, k, vectors_n):
    total = own[k, :vectors_n, :]
    rows = slice(k * vectors_n, (k + 1) * vectors_n)
    for part in received:
        total = total + part[rows, :].astype(F32)
    return total


def symmetric_part(row_own, row_refs, col_own, col_refs, k, vectors_n):
    return 0.5 * (
        gathered_sum(row_own, row_refs, k, vectors_n)
        + gathered_sum(col_own, col_refs, k, vectors_n)
    )


def first_kernel(chips_n, vec_ref, row_degree, row_own, col_own, *refs):
    row_refs, refs = refs[: chips_n - 1], refs[chips_n - 1 :]
    col_refs, (first_ref, rounded_ref, degree_ref) = refs[:-3], refs[-3:]
    group, vectors_n, width = rounded_ref.shape
    degree = row_degree[...] + degree_of(col_own, 0, group, vectors_n)
    for part in (*row_refs, *col_refs):
        degree += join_degree(part, group)
    degree = 0.5 * degree
    degree_ref[...] = degree
    for k, vec in enumerate(tiles_first(vec_ref, width)):
        symmetric = symmetric_part(row_own, row_refs, col_own, col_refs, k, vectors_n)
        image = degree[k : k + 1, :] * vec - symmetric
        first = (image - CENTER * vec) / HALF_WIDTH
        first_ref[:, k * width : (k + 1) * width] = first
        rounded_ref[k] = first.astype(BF16)


def filter_kernel(chips_n, start_ref, first_ref, degree_ref, row_own, col_own, *refs):
    row_refs, refs = refs[: chips_n - 1], refs[chips_n - 1 :]
    col_refs, (filtered_ref, rounded_ref) = refs[:-2], refs[-2:]
    _, vectors_n, width = rounded_ref.shape
    for k, vec in enumerate(tiles_first(first_ref, width)):
        symmetric = symmetric_part(row_own, row_refs, col_own, col_refs, k, vectors_n)
        columns = slice(k * width, (k + 1) * width)
        image = degree_ref[k : k + 1, :] * vec - symmetric
        filtered = 2.0 * (image - CENTER * vec) / HALF_WIDTH - start_ref[:, columns]
        filtered_ref[:, columns] = filtered
        rounded_ref[k] = filtered.astype(BF16)


def gram_kernel(filtered_ref, degree_ref, gram_ref, both):
    vectors_n, width = filtered_ref.shape[0], degree_ref.shape[1]
    for k, vec in enumerate(tiles_first(filtered_ref, width)):
        columns = slice(k * width, (k + 1) * width)
        both[:vectors_n, columns] = vec
        both[vectors_n:, columns] = degree_ref[k : k + 1, :] * vec
    gram_ref[...] = lax.dot_general(
        filtered_ref[...], both[...], NT, precision=HIGHEST, preferred_element_type=F32
    )


def half_form_kernel(runs, source, tiles_ref, *refs):
    parts, (out_ref, panel, table, arrived) = refs[:-4], refs[-4:]
    copy = fetch(source, table, arrived)
    width = panel.shape[2]
    fill(panel, parts, runs)
    copy.wait()
    for t in range(tiles_ref.shape[0]):
        out_ref[:, t * width : (t + 1) * width] = lax.dot_general(
            panel[table[1, t]], tiles_ref[t], NN, preferred_element_type=F32
        ).astype(BF16)


def form_kernel(runs, source, left, gram_ref, *refs):
    parts, (out_ref, panel, right, table, arrived) = refs[:-5], refs[-5:]
    copy = fetch(source, table, arrived)
    _, vectors_n, width = panel.shape
    fill(panel, parts, runs)
    copy.wait()
    for t in range(right.shape[1] // width):
        right[:, t * width : (t + 1) * width] = panel[table[0, t]]
    form = lax.dot_general(left[...], right[...], NT, preferred_element_type=F32)
    projected = gram_ref[:, vectors_n:] - 0.5 * (form + form.T)
    row, col = square_index(vectors_n)
    packed = jnp.where(col >= row, gram_ref[:, :vectors_n], projected)
    diagonal = jnp.sum(jnp.where(row == col, projected, 0.0), 0, keepdims=True)
    half = vectors_n // 2
    out_ref[:half] = jnp.concatenate([packed[:half], packed[half:]], 1)
    diagonal = jnp.broadcast_to(diagonal, (8, vectors_n))
    out_ref[half:] = jnp.concatenate([diagonal, jnp.zeros_like(diagonal)], 1)


def square_index(n):
    return tuple(lax.broadcasted_iota(jnp.int32, (n, n), axis) for axis in (0, 1))


def inverse_factor(gram):
    n = gram.shape[0]
    row, col = square_index(n)
    table = jnp.concatenate([gram, jnp.where(row == col, 1.0, 0.0)], 1)
    bands = [table[i : i + 8] for i in range(0, n, 8)]
    shape = (8, 2 * n)
    line = lax.broadcasted_iota(jnp.int32, shape, 0)

    def spread(values, j):
        return jnp.broadcast_to(values[:, j : j + 1], shape)

    def pick(values, i):
        return jnp.broadcast_to(values[i : i + 1, :], shape)

    for at in range(n // 8):
        block = [spread(bands[at], 8 * at + c) for c in range(8)]
        forward, solved = bands[at], bands[at]
        solved_block = list(block)
        for s in range(8):
            scale = 1.0 / pick(block[s], s)
            below = jnp.where(line > s, block[s], 0.0) * scale
            above = jnp.where(line < s, solved_block[s] * scale, 0.0)
            both = below + above
            pivot_row = pick(forward, s)
            forward = forward - below * pivot_row
            solved = solved - both * pivot_row
            for c in range(s + 1, 8):
                pivot = pick(block[c], s)
                block[c] = block[c] - below * pivot
                solved_block[c] = solved_block[c] - both * pivot
        pivots = block[0]
        for s in range(1, 8):
            pivots = jnp.where(line == s, block[s], pivots)
        solved = solved / pivots
        bands[at] = forward / jnp.sqrt(pivots)
        for i in range(at + 1, n // 8):
            update = spread(bands[i], 8 * at) * pick(solved, 0)
            for c in range(1, 8):
                update = update + spread(bands[i], 8 * at + c) * pick(solved, c)
            bands[i] = bands[i] - update
    return jnp.concatenate(bands, 0)[:, n:]


def last_kernel(total_nodes, filtered_ref, *refs):
    (own, *parts), (ritz_ref, rayleigh_ref) = refs[:-2], refs[-2:]
    parts = [own, *parts[::-1]]
    n = filtered_ref.shape[0]
    half = n // 2
    sums = tree_sum([part[...] for part in parts]) * (1.0 / total_nodes)
    packed = jnp.concatenate([sums[:half, :n], sums[:half, n:]], 0)
    row, col = square_index(n)
    upper = jnp.where(col > row, packed, 0.0)
    gram = jnp.where(col >= row, packed, 0.0) + upper.T
    lower = jnp.where(col < row, packed, 0.0)
    diagonal = jnp.broadcast_to(sums[half : half + 1, :n], (n, n))
    projected = lower + lower.T + jnp.where(row == col, diagonal, 0.0)
    inverse = inverse_factor(gram)

    def dot(a, b, dims):
        return lax.dot_general(a, b, dims, precision=HIGHEST, preferred_element_type=F32)

    half_way = dot(inverse, projected, NN)
    rayleigh_ref[...] = dot(half_way, inverse, NT)
    turned = dot(inverse, half_way, NT)
    ritz_ref[...] = dot(turned, dot(inverse, filtered_ref[...], NN), NN)


def tree_sum(parts):
    while len(parts) > 1:
        parts = [a + b for a, b in zip(parts[::2], parts[1::2])]
    return parts[0]


def local(tiles, tile_rows, tile_cols, start):
    tiles, tile_rows, tile_cols = tiles[0, 0], tile_rows[0, 0], tile_cols[0, 0]
    width = tiles.shape[-1]
    vectors_n, own_nodes = start.shape
    rows_n, cols_n = lax.axis_size("row"), lax.axis_size("col")
    chips_n = cols_n // 2
    total_nodes = own_nodes * rows_n * cols_n
    group = own_nodes // width
    spread = (vectors_n, tiles.shape[0] * width)

    rounded_shape = jax.ShapeDtypeStruct((group, vectors_n, width), BF16)
    vector_shape = jax.ShapeDtypeStruct((vectors_n, own_nodes), F32)
    degree_shape = jax.ShapeDtypeStruct((group, width), F32)

    late = 1
    levels = [rows_n >> i for i in range(1, rows_n.bit_length())]
    col_runs = [[(0, group)]]
    for d in levels:
        if len(col_runs) == 1:
            col_runs += [[(d * group, group)]]
            continue
        cut = group - late
        passed = [((p // group ^ d) * group + p % group, n) for run in col_runs[1:] for p, n in run]
        col_runs += [[(d * group, cut)], [(d * group + cut, late), *passed]]
    chip_order = [0, *range(chips_n - 1, 0, -1)]
    row_runs = [[((2 * d + core) * group, group)] for core in range(2) for d in chip_order]
    runs = (col_runs, row_runs)
    def gather(rounded, first=()):
        held = [rounded]
        for d in levels:
            if len(held) == 1:
                held += [trade(rounded, "row", d)]
                continue
            near = trade(rounded[: group - late], "row", d)
            near, *passed = lax.optimization_barrier((near, *held[1:], *first))
            held[1:] = passed[: len(held) - 1]
            held += [near, trade(jnp.concatenate([rounded[group - late :], *held[1:]]), "row", d)]
        chips = [rounded, *exchange([rounded] * (chips_n - 1), "col", 2)[::-1]]
        return held, chips + [trade(chip, "col", 1) for chip in chips]

    def apply(rounded, table, degree, first=()):
        height = vectors_n + (DEGREE_ROWS if degree else 0)
        zeros = call(
            zero_kernel,
            [jax.ShapeDtypeStruct((n * group, height, width), F32) for n in (cols_n, rows_n)],
            [],
            16,
            [],
            4 * total_nodes * vectors_n,
        )
        parts = gather(rounded, (*first, *zeros))
        kept, swap, col_own, col_send = products(tiles, table, *parts, zeros, runs, degree)
        col_got = exchange(col_send, "row")
        row_own, *row_send = merge(kept, trade(swap, "col", 1), vectors_n, degree)
        row_degree = row_send[:1] if degree else []
        row_got = exchange(row_send[len(row_degree) :], "col", 2)[::-1]
        return [*row_degree, row_own, col_own, *row_got, *col_got]

    meta = jnp.stack([lax.axis_index("row"), lax.axis_index("col"), chips_n]).astype(jnp.int32)
    meta = jnp.broadcast_to(meta[:, None], (3, tiles.shape[0]))
    rounded, table = call(
        round_kernel,
        [rounded_shape, jax.ShapeDtypeStruct((3, tiles.shape[0]), jnp.int32)],
        [],
        16,
        [start, meta, tile_rows[None], tile_cols[None]],
    )
    tiles = call(
        hold_kernel,
        jax.ShapeDtypeStruct(tiles.shape, BF16),
        [],
        16,
        [tiles],
        4 * tiles.size * DEGREE_ROWS,
    )
    first, rounded, degree = call(
        functools.partial(first_kernel, chips_n),
        [vector_shape, rounded_shape, degree_shape],
        [],
        24,
        [start, *apply(rounded, table, True)],
    )
    filtered, rounded = call(
        functools.partial(filter_kernel, chips_n),
        [vector_shape, rounded_shape],
        [],
        24,
        [start, first, degree, *apply(rounded, table, False)],
    )
    gram = call(
        gram_kernel,
        jax.ShapeDtypeStruct((vectors_n, 2 * vectors_n), F32),
        [pltpu.VMEM((2 * vectors_n, own_nodes), F32)],
        16,
        [filtered, degree],
        24 * vectors_n * vectors_n * own_nodes,
    )
    col_parts, row_parts = gather(rounded, (gram,))
    fetched = [pltpu.SMEM(table.shape, table.dtype), pltpu.SemaphoreType.DMA(())]
    left = call(
        functools.partial(half_form_kernel, runs[1]),
        jax.ShapeDtypeStruct(spread, BF16),
        [pltpu.VMEM((cols_n * group, vectors_n, width), BF16), *fetched],
        24,
        [table, tiles, *row_parts],
        2 * tiles.size * vectors_n,
    )
    sums = call(
        functools.partial(form_kernel, runs[0]),
        jax.ShapeDtypeStruct((vectors_n // 2 + 8, 2 * vectors_n), F32),
        [pltpu.VMEM((rows_n * group, vectors_n, width), BF16), pltpu.VMEM(spread, BF16), *fetched],
        24,
        [table, left, gram, *col_parts],
        2 * vectors_n * spread[0] * spread[1],
    )
    sums = sums + trade(sums, "col", 1)
    sums = tree_sum([*exchange([sums] * (chips_n - 1), "col", 2)[::-1], sums])
    return call(
        functools.partial(last_kernel, total_nodes),
        [vector_shape, jax.ShapeDtypeStruct((vectors_n, vectors_n), F32)],
        [],
        24,
        [filtered, sums, *exchange([sums] * (rows_n - 1), "row")[::-1]],
    )


def solution(mesh):
    placed = (
        P("row", "col", None, None, None),
        P("row", "col", None),
        P("row", "col", None),
        P(None, ("row", "col")),
    )
    return jax.shard_map(
        local, mesh=mesh, in_specs=placed, out_specs=(P(None, ("row", "col")), P()), check_vma=False
    )
```

```python
import functools

import jax
import jax.numpy as jnp
from jax import lax
from jax.experimental import pallas as pl
from jax.experimental.pallas import tpu as pltpu
from jax.sharding import PartitionSpec as P

CENTER = 1.0
HALF_WIDTH = 0.5
HIGHEST = lax.Precision.HIGHEST
NT = (((1,), (1,)), ((), ()))
NN = (((1,), (0,)), ((), ()))
BF16 = jnp.bfloat16
F32 = jnp.float32
VMEM = pl.BlockSpec(memory_space=pltpu.VMEM)
SMEM = pl.BlockSpec(memory_space=pltpu.SMEM)
ANY = pl.BlockSpec(memory_space=pl.ANY)
DEGREE_ROWS = 16


def call(kernel, out_shape, scratch, limit, args, flops=0, smem=0, after=(), aliases={}):
    moved = sum(x.size * x.dtype.itemsize for x in args)
    return pl.pallas_call(
        lambda *refs: kernel(*refs[len(after) :]),
        out_shape=jax.tree.map(lambda x: jax.ShapeDtypeStruct(x.shape, x.dtype), out_shape),
        in_specs=[ANY] * len(after) + [SMEM] * smem + [VMEM] * (len(args) - smem),
        out_specs=jax.tree.map(lambda _: VMEM, out_shape),
        scratch_shapes=scratch,
        input_output_aliases=aliases,
        compiler_params=pltpu.CompilerParams(vmem_limit_bytes=limit * 2**20),
        cost_estimate=pl.CostEstimate(flops=flops, bytes_accessed=moved, transcendentals=0),
    )(*after, *args)


def trade(part, axis, d):
    n = lax.axis_size(axis)
    return lax.ppermute(part, axis, [(i, i ^ d) for i in range(n)])


def exchange(parts, axis, step=1):
    far_first = [trade(part, axis, step * d) for d, part in reversed(list(enumerate(parts, 1)))]
    return far_first[::-1]


def tiles_first(ref, width):
    return [ref[:, k * width : (k + 1) * width] for k in range(ref.shape[1] // width)]


def round_kernel(vec_ref, out_ref):
    for k, piece in enumerate(tiles_first(vec_ref, out_ref.shape[2])):
        out_ref[k] = piece.astype(BF16)


def split_degree(sums):
    high = sums.astype(BF16).astype(F32)
    return jnp.concatenate([high, sums - high], 0).astype(BF16)


def join_degree(payload, group):
    parts = payload[payload.shape[0] - 2 * group :, :].astype(F32)
    return parts[:group] + parts[group:]


def fill(panel, parts, runs):
    for part, places in zip(parts, runs):
        at = 0
        for place, count in places:
            panel[place : place + count, : part.shape[1], :] = part[at : at + count]
            at += count


def table_kernel(group, meta, rows_ref, cols_ref, table):
    rows, cols = rows_ref[...], cols_ref[...]
    apart = lax.div(rows, group) ^ meta[1:2, :]
    halves = lax.rem(apart, 2) * meta[2:3, :] + lax.div(apart, 2)
    inside = lax.rem(rows, group)
    table[0:1, :] = (lax.div(cols, group) ^ meta[0:1, :]) * group + lax.rem(cols, group)
    table[1:2, :] = apart * group + inside
    table[2:3, :] = halves * group + inside


def fetch(source, table, arrived):
    copy = pltpu.make_async_copy(source, table, arrived)
    copy.start()
    return copy


def fill_ones(panel, vectors_n):
    rows = panel.shape[1] - vectors_n
    if rows:
        panel[:, vectors_n:, :] = jnp.ones((panel.shape[0], rows, panel.shape[2]), BF16)


def degree_of(total, start, group, vectors_n):
    return jnp.concatenate(
        [total[start + k, vectors_n : vectors_n + 1, :] for k in range(group)], 0
    )


def hold_kernel(tiles_ref, held_ref):
    held_ref[...] = tiles_ref[...]


def zero_kernel(*refs):
    for ref in refs:
        ref[...] = jnp.zeros_like(ref)


def column_kernel(runs, source, tiles_ref, *refs):
    parts, refs = refs[: len(runs)], refs[len(runs) :]
    _, own_ref, total, *send_refs, panel, table, arrived = refs
    copy = fetch(source, table, arrived)
    group, vectors_n, _ = parts[0].shape
    fill(panel, parts, runs)
    fill_ones(panel, vectors_n)
    copy.wait()
    for t in range(tiles_ref.shape[0]):
        total[table[0, t]] += lax.dot_general(
            panel[table[1, t]], tiles_ref[t], NN, preferred_element_type=F32
        )
    own_ref[...] = total[:group]
    for d, send in enumerate(send_refs, 1):
        round_sums(send, total, d * group, group, vectors_n)


def row_kernel(runs, source, tiles_ref, *refs):
    parts, refs = refs[: len(runs)], refs[len(runs) :]
    _, total, swap_ref, panel, table, arrived = refs
    copy = fetch(source, table, arrived)
    group, vectors_n, _ = parts[0].shape
    half = swap_ref.shape[0]
    fill(panel, parts, runs)
    fill_ones(panel, vectors_n)
    copy.wait()
    for t in range(tiles_ref.shape[0]):
        total[table[2, t]] += lax.dot_general(
            panel[table[0, t]], tiles_ref[t], NT, preferred_element_type=F32
        )
    for d in range(half):
        round_sums(swap_ref.at[d], total, (half + d) * group, group, vectors_n)


def round_sums(send, total, start, group, vectors_n):
    for k in range(group):
        send[k * vectors_n : (k + 1) * vectors_n, :] = total[start + k, :vectors_n, :].astype(BF16)
    if total.shape[1] > vectors_n:
        send[group * vectors_n :, :] = split_degree(degree_of(total, start, group, vectors_n))


def products(tiles, table, col_parts, row_parts, zeros, runs, degree):
    group, vectors_n, width = col_parts[0].shape
    half = len(row_parts) // 2
    rows_n = max(place + count for run in runs[0] for place, count in run) // group
    rows = group * vectors_n + (2 * group if degree else 0)
    height = vectors_n + (DEGREE_ROWS if degree else 0)
    send_shape = jax.ShapeDtypeStruct((rows, width), BF16)
    flops = 2 * tiles.size * vectors_n

    def panel(count):
        return pltpu.VMEM((count * group, height, width), BF16)

    fetched = [pltpu.SMEM(table.shape, table.dtype), pltpu.SemaphoreType.DMA(())]
    col_own, _, *col_send = call(
        functools.partial(column_kernel, runs[1]),
        [jax.ShapeDtypeStruct((group, height, width), F32), zeros[1]] + [send_shape] * (rows_n - 1),
        [panel(2 * half), *fetched],
        24,
        [table, tiles, *row_parts, zeros[1]],
        flops,
        0,
        (),
        {2 + len(row_parts): 1},
    )
    kept, swap = call(
        functools.partial(row_kernel, runs[0]),
        [zeros[0], jax.ShapeDtypeStruct((half, rows, width), BF16)],
        [panel(rows_n), *fetched],
        24,
        [table, tiles, *col_parts, zeros[0]],
        flops,
        0,
        [col_own],
        {3 + len(col_parts): 0},
    )
    return kept, swap, col_own, col_send


def merge_kernel(degree, vectors_n, kept, got, own_ref, *send_refs):
    if degree:
        own_degree, *send_refs = send_refs
    group = own_ref.shape[0]
    for k in range(group):
        rows = slice(k * vectors_n, (k + 1) * vectors_n)
        own_ref[k] = kept[k, :vectors_n, :] + got[0, rows, :].astype(F32)
        for d, send in enumerate(send_refs, 1):
            both = kept[d * group + k, :vectors_n, :] + got[d, rows, :].astype(F32)
            send[rows, :] = both.astype(BF16)
    if degree:
        for d in range(got.shape[0]):
            sums = degree_of(kept, d * group, group, vectors_n) + join_degree(got.at[d], group)
            if d:
                send_refs[d - 1][group * vectors_n :, :] = split_degree(sums)
            else:
                own_degree[...] = sums


def merge(kept, got, vectors_n, degree):
    half, width = got.shape[0], got.shape[2]
    group = kept.shape[0] // (2 * half)
    out_shape = [jax.ShapeDtypeStruct((group, vectors_n, width), F32)]
    if degree:
        out_shape += [jax.ShapeDtypeStruct((group, width), F32)]
    out_shape += [jax.ShapeDtypeStruct(got.shape[1:], BF16)] * (half - 1)
    kernel = functools.partial(merge_kernel, degree, vectors_n)
    return call(kernel, out_shape, [], 24, [kept, got])


def gathered_sum(own, received, k, vectors_n):
    total = own[k, :vectors_n, :]
    rows = slice(k * vectors_n, (k + 1) * vectors_n)
    for part in received:
        total = total + part[rows, :].astype(F32)
    return total


def symmetric_part(row_own, row_refs, col_own, col_refs, k, vectors_n):
    return 0.5 * (
        gathered_sum(row_own, row_refs, k, vectors_n)
        + gathered_sum(col_own, col_refs, k, vectors_n)
    )


def first_kernel(chips_n, vec_ref, row_degree, row_own, col_own, *refs):
    row_refs, refs = refs[: chips_n - 1], refs[chips_n - 1 :]
    col_refs, (first_ref, rounded_ref, degree_ref) = refs[:-3], refs[-3:]
    group, vectors_n, width = rounded_ref.shape
    degree = row_degree[...] + degree_of(col_own, 0, group, vectors_n)
    for part in (*row_refs, *col_refs):
        degree += join_degree(part, group)
    degree = 0.5 * degree
    degree_ref[...] = degree
    for k, vec in enumerate(tiles_first(vec_ref, width)):
        symmetric = symmetric_part(row_own, row_refs, col_own, col_refs, k, vectors_n)
        image = degree[k : k + 1, :] * vec - symmetric
        first = (image - CENTER * vec) / HALF_WIDTH
        first_ref[:, k * width : (k + 1) * width] = first
        rounded_ref[k] = first.astype(BF16)


def filter_kernel(chips_n, start_ref, first_ref, degree_ref, row_own, col_own, *refs):
    row_refs, refs = refs[: chips_n - 1], refs[chips_n - 1 :]
    col_refs, (filtered_ref, rounded_ref) = refs[:-2], refs[-2:]
    _, vectors_n, width = rounded_ref.shape
    for k, vec in enumerate(tiles_first(first_ref, width)):
        symmetric = symmetric_part(row_own, row_refs, col_own, col_refs, k, vectors_n)
        columns = slice(k * width, (k + 1) * width)
        image = degree_ref[k : k + 1, :] * vec - symmetric
        filtered = 2.0 * (image - CENTER * vec) / HALF_WIDTH - start_ref[:, columns]
        filtered_ref[:, columns] = filtered
        rounded_ref[k] = filtered.astype(BF16)


def gram_kernel(filtered_ref, degree_ref, gram_ref, both):
    vectors_n, width = filtered_ref.shape[0], degree_ref.shape[1]
    for k, vec in enumerate(tiles_first(filtered_ref, width)):
        columns = slice(k * width, (k + 1) * width)
        both[:vectors_n, columns] = vec
        both[vectors_n:, columns] = degree_ref[k : k + 1, :] * vec
    gram_ref[...] = lax.dot_general(
        filtered_ref[...], both[...], NT, precision=HIGHEST, preferred_element_type=F32
    )


def half_form_kernel(runs, source, tiles_ref, *refs):
    parts, (out_ref, panel, table, arrived) = refs[:-4], refs[-4:]
    copy = fetch(source, table, arrived)
    width = panel.shape[2]
    fill(panel, parts, runs)
    copy.wait()
    for t in range(tiles_ref.shape[0]):
        out_ref[:, t * width : (t + 1) * width] = lax.dot_general(
            panel[table[1, t]], tiles_ref[t], NN, preferred_element_type=F32
        ).astype(BF16)


def form_kernel(runs, source, left, gram_ref, *refs):
    parts, (out_ref, panel, right, table, arrived) = refs[:-5], refs[-5:]
    copy = fetch(source, table, arrived)
    _, vectors_n, width = panel.shape
    fill(panel, parts, runs)
    copy.wait()
    for t in range(right.shape[1] // width):
        right[:, t * width : (t + 1) * width] = panel[table[0, t]]
    form = lax.dot_general(left[...], right[...], NT, preferred_element_type=F32)
    projected = gram_ref[:, vectors_n:] - 0.5 * (form + form.T)
    row, col = square_index(vectors_n)
    packed = jnp.where(col >= row, gram_ref[:, :vectors_n], projected)
    diagonal = jnp.sum(jnp.where(row == col, projected, 0.0), 0, keepdims=True)
    half = vectors_n // 2
    out_ref[:half] = jnp.concatenate([packed[:half], packed[half:]], 1)
    diagonal = jnp.broadcast_to(diagonal, (8, vectors_n))
    out_ref[half:] = jnp.concatenate([diagonal, jnp.zeros_like(diagonal)], 1)


def square_index(n):
    return tuple(lax.broadcasted_iota(jnp.int32, (n, n), axis) for axis in (0, 1))


def inverse_factor(gram):
    n = gram.shape[0]
    row, col = square_index(n)
    table = jnp.concatenate([gram, jnp.where(row == col, 1.0, 0.0)], 1)
    bands = [table[i : i + 8] for i in range(0, n, 8)]
    shape = (8, 2 * n)
    line = lax.broadcasted_iota(jnp.int32, shape, 0)

    def spread(values, j):
        return jnp.broadcast_to(values[:, j : j + 1], shape)

    def pick(values, i):
        return jnp.broadcast_to(values[i : i + 1, :], shape)

    for at in range(n // 8):
        block = [spread(bands[at], 8 * at + c) for c in range(8)]
        forward, solved = bands[at], bands[at]
        solved_block = list(block)
        for s in range(8):
            scale = 1.0 / pick(block[s], s)
            below = jnp.where(line > s, block[s], 0.0) * scale
            above = jnp.where(line < s, solved_block[s] * scale, 0.0)
            both = below + above
            pivot_row = pick(forward, s)
            forward = forward - below * pivot_row
            solved = solved - both * pivot_row
            for c in range(s + 1, 8):
                pivot = pick(block[c], s)
                block[c] = block[c] - below * pivot
                solved_block[c] = solved_block[c] - both * pivot
        pivots = block[0]
        for s in range(1, 8):
            pivots = jnp.where(line == s, block[s], pivots)
        solved = solved / pivots
        bands[at] = forward / jnp.sqrt(pivots)
        for i in range(at + 1, n // 8):
            update = spread(bands[i], 8 * at) * pick(solved, 0)
            for c in range(1, 8):
                update = update + spread(bands[i], 8 * at + c) * pick(solved, c)
            bands[i] = bands[i] - update
    return jnp.concatenate(bands, 0)[:, n:]


def last_kernel(total_nodes, filtered_ref, *refs):
    (own, *parts), (ritz_ref, rayleigh_ref) = refs[:-2], refs[-2:]
    parts = [own, *parts[::-1]]
    n = filtered_ref.shape[0]
    half = n // 2
    sums = tree_sum([part[...] for part in parts]) * (1.0 / total_nodes)
    packed = jnp.concatenate([sums[:half, :n], sums[:half, n:]], 0)
    row, col = square_index(n)
    upper = jnp.where(col > row, packed, 0.0)
    gram = jnp.where(col >= row, packed, 0.0) + upper.T
    lower = jnp.where(col < row, packed, 0.0)
    diagonal = jnp.broadcast_to(sums[half : half + 1, :n], (n, n))
    projected = lower + lower.T + jnp.where(row == col, diagonal, 0.0)
    inverse = inverse_factor(gram)

    def dot(a, b, dims):
        return lax.dot_general(a, b, dims, precision=HIGHEST, preferred_element_type=F32)

    half_way = dot(inverse, projected, NN)
    rayleigh_ref[...] = dot(half_way, inverse, NT)
    turned = dot(inverse, half_way, NT)
    ritz_ref[...] = dot(turned, dot(inverse, filtered_ref[...], NN), NN)


def tree_sum(parts):
    while len(parts) > 1:
        parts = [a + b for a, b in zip(parts[::2], parts[1::2])]
    return parts[0]


def local(tiles, tile_rows, tile_cols, start):
    tiles, tile_rows, tile_cols = tiles[0, 0], tile_rows[0, 0], tile_cols[0, 0]
    width = tiles.shape[-1]
    vectors_n, own_nodes = start.shape
    rows_n, cols_n = lax.axis_size("row"), lax.axis_size("col")
    chips_n = cols_n // 2
    total_nodes = own_nodes * rows_n * cols_n
    group = own_nodes // width
    spread = (vectors_n, tiles.shape[0] * width)

    rounded_shape = jax.ShapeDtypeStruct((group, vectors_n, width), BF16)
    vector_shape = jax.ShapeDtypeStruct((vectors_n, own_nodes), F32)
    degree_shape = jax.ShapeDtypeStruct((group, width), F32)

    late = 1
    levels = [rows_n >> i for i in range(1, rows_n.bit_length())]
    col_runs = [[(0, group)]]
    for d in levels:
        if len(col_runs) == 1:
            col_runs += [[(d * group, group)]]
            continue
        cut = group - late
        passed = [((p // group ^ d) * group + p % group, n) for run in col_runs[1:] for p, n in run]
        col_runs += [[(d * group, cut)], [(d * group + cut, late), *passed]]
    chip_order = [0, *range(chips_n - 1, 0, -1)]
    row_runs = [[((2 * d + core) * group, group)] for core in range(2) for d in chip_order]
    runs = (col_runs, row_runs)
    def gather(rounded, first=()):
        held = [rounded]
        for d in levels:
            if len(held) == 1:
                held += [trade(rounded, "row", d)]
                continue
            near = trade(rounded[: group - late], "row", d)
            near, *passed = lax.optimization_barrier((near, *held[1:], *first))
            held[1:] = passed[: len(held) - 1]
            held += [near, trade(jnp.concatenate([rounded[group - late :], *held[1:]]), "row", d)]
        sent, other = lax.optimization_barrier((rounded, trade(rounded, "col", 1)))
        chips = [rounded, *exchange([sent] * (chips_n - 1), "col", 2)[::-1]]
        return held, [*chips, other, *(trade(chip, "col", 1) for chip in chips[1:])]

    def apply(rounded, table, degree, first=()):
        height = vectors_n + (DEGREE_ROWS if degree else 0)
        zeros = call(
            zero_kernel,
            [jax.ShapeDtypeStruct((n * group, height, width), F32) for n in (cols_n, rows_n)],
            [],
            16,
            [],
            4 * total_nodes * vectors_n,
        )
        parts = gather(rounded, (*first, *zeros))
        kept, swap, col_own, col_send = products(tiles, table, *parts, zeros, runs, degree)
        col_got = exchange(col_send, "row")
        row_own, *row_send = merge(kept, trade(swap, "col", 1), vectors_n, degree)
        row_degree = row_send[:1] if degree else []
        row_got = exchange(row_send[len(row_degree) :], "col", 2)[::-1]
        return [*row_degree, row_own, col_own, *row_got, *col_got]

    rounded = call(round_kernel, rounded_shape, [], 16, [start])
    meta = jnp.stack([lax.axis_index("row"), lax.axis_index("col"), chips_n]).astype(jnp.int32)
    meta = jnp.broadcast_to(meta[:, None], (3, tiles.shape[0]))
    table = call(
        functools.partial(table_kernel, group),
        jax.ShapeDtypeStruct((3, tiles.shape[0]), jnp.int32),
        [],
        16,
        [meta, tile_rows[None], tile_cols[None]],
    )
    tiles = call(
        hold_kernel,
        jax.ShapeDtypeStruct(tiles.shape, BF16),
        [],
        16,
        [tiles],
        4 * tiles.size * DEGREE_ROWS,
    )
    first, rounded, degree = call(
        functools.partial(first_kernel, chips_n),
        [vector_shape, rounded_shape, degree_shape],
        [],
        24,
        [start, *apply(rounded, table, True, (table,))],
    )
    filtered, rounded = call(
        functools.partial(filter_kernel, chips_n),
        [vector_shape, rounded_shape],
        [],
        24,
        [start, first, degree, *apply(rounded, table, False)],
    )
    gram = call(
        gram_kernel,
        jax.ShapeDtypeStruct((vectors_n, 2 * vectors_n), F32),
        [pltpu.VMEM((2 * vectors_n, own_nodes), F32)],
        16,
        [filtered, degree],
        24 * vectors_n * vectors_n * own_nodes,
    )
    col_parts, row_parts = gather(rounded, (gram,))
    fetched = [pltpu.SMEM(table.shape, table.dtype), pltpu.SemaphoreType.DMA(())]
    left = call(
        functools.partial(half_form_kernel, runs[1]),
        jax.ShapeDtypeStruct(spread, BF16),
        [pltpu.VMEM((cols_n * group, vectors_n, width), BF16), *fetched],
        24,
        [table, tiles, *row_parts],
        2 * tiles.size * vectors_n,
    )
    sums = call(
        functools.partial(form_kernel, runs[0]),
        jax.ShapeDtypeStruct((vectors_n // 2 + 8, 2 * vectors_n), F32),
        [pltpu.VMEM((rows_n * group, vectors_n, width), BF16), pltpu.VMEM(spread, BF16), *fetched],
        24,
        [table, left, gram, *col_parts],
        2 * vectors_n * spread[0] * spread[1],
    )
    sums = sums + trade(sums, "col", 1)
    sums = tree_sum([*exchange([sums] * (chips_n - 1), "col", 2)[::-1], sums])
    return call(
        functools.partial(last_kernel, total_nodes),
        [vector_shape, jax.ShapeDtypeStruct((vectors_n, vectors_n), F32)],
        [],
        24,
        [filtered, sums, *exchange([sums] * (rows_n - 1), "row")[::-1]],
    )


def solution(mesh):
    placed = (
        P("row", "col", None, None, None),
        P("row", "col", None),
        P("row", "col", None),
        P(None, ("row", "col")),
    )
    return jax.shard_map(
        local, mesh=mesh, in_specs=placed, out_specs=(P(None, ("row", "col")), P()), check_vma=False
    )
```

```python
import functools

import jax
import jax.numpy as jnp
from jax import lax
from jax.experimental import pallas as pl
from jax.experimental.pallas import tpu as pltpu
from jax.sharding import PartitionSpec as P

CENTER = 1.0
HALF_WIDTH = 0.5
HIGHEST = lax.Precision.HIGHEST
NT = (((1,), (1,)), ((), ()))
NN = (((1,), (0,)), ((), ()))
BF16 = jnp.bfloat16
F32 = jnp.float32
VMEM = pl.BlockSpec(memory_space=pltpu.VMEM)
SMEM = pl.BlockSpec(memory_space=pltpu.SMEM)
ANY = pl.BlockSpec(memory_space=pl.ANY)
DEGREE_ROWS = 16


def call(kernel, out_shape, scratch, limit, args, flops=0, smem=0, after=(), aliases={}):
    moved = sum(x.size * x.dtype.itemsize for x in args)
    return pl.pallas_call(
        lambda *refs: kernel(*refs[len(after) :]),
        out_shape=jax.tree.map(lambda x: jax.ShapeDtypeStruct(x.shape, x.dtype), out_shape),
        in_specs=[ANY] * len(after) + [SMEM] * smem + [VMEM] * (len(args) - smem),
        out_specs=jax.tree.map(lambda _: VMEM, out_shape),
        scratch_shapes=scratch,
        input_output_aliases=aliases,
        compiler_params=pltpu.CompilerParams(vmem_limit_bytes=limit * 2**20),
        cost_estimate=pl.CostEstimate(flops=flops, bytes_accessed=moved, transcendentals=0),
    )(*after, *args)


def trade(part, axis, d):
    n = lax.axis_size(axis)
    return lax.ppermute(part, axis, [(i, i ^ d) for i in range(n)])


def exchange(parts, axis, step=1):
    far_first = [trade(part, axis, step * d) for d, part in reversed(list(enumerate(parts, 1)))]
    return far_first[::-1]


def tiles_first(ref, width):
    return [ref[:, k * width : (k + 1) * width] for k in range(ref.shape[1] // width)]


def round_kernel(vec_ref, out_ref):
    for k, piece in enumerate(tiles_first(vec_ref, out_ref.shape[2])):
        out_ref[k] = piece.astype(BF16)


def split_degree(sums):
    high = sums.astype(BF16).astype(F32)
    return jnp.concatenate([high, sums - high], 0).astype(BF16)


def join_degree(payload, group):
    parts = payload[payload.shape[0] - 2 * group :, :].astype(F32)
    return parts[:group] + parts[group:]


def fill(panel, parts, runs):
    for part, places in zip(parts, runs):
        at = 0
        for place, count in places:
            panel[place : place + count, : part.shape[1], :] = part[at : at + count]
            at += count


def table_kernel(group, meta, rows_ref, cols_ref, table):
    rows, cols = rows_ref[...], cols_ref[...]
    apart = lax.div(rows, group) ^ meta[1:2, :]
    halves = lax.rem(apart, 2) * meta[2:3, :] + lax.div(apart, 2)
    inside = lax.rem(rows, group)
    table[0:1, :] = (lax.div(cols, group) ^ meta[0:1, :]) * group + lax.rem(cols, group)
    table[1:2, :] = apart * group + inside
    table[2:3, :] = halves * group + inside


def fetch(source, table, arrived):
    copy = pltpu.make_async_copy(source, table, arrived)
    copy.start()
    return copy


def fill_ones(panel, vectors_n):
    rows = panel.shape[1] - vectors_n
    if rows:
        panel[:, vectors_n:, :] = jnp.ones((panel.shape[0], rows, panel.shape[2]), BF16)


def degree_of(total, start, group, vectors_n):
    return jnp.concatenate(
        [total[start + k, vectors_n : vectors_n + 1, :] for k in range(group)], 0
    )


def hold_kernel(tiles_ref, held_ref):
    held_ref[...] = tiles_ref[...]


def zero_kernel(*refs):
    for ref in refs:
        ref[...] = jnp.zeros_like(ref)


def column_kernel(runs, source, tiles_ref, *refs):
    parts, refs = refs[: len(runs)], refs[len(runs) :]
    _, own_ref, total, *send_refs, panel, table, arrived = refs
    copy = fetch(source, table, arrived)
    group, vectors_n, _ = parts[0].shape
    fill(panel, parts, runs)
    fill_ones(panel, vectors_n)
    copy.wait()
    for t in range(tiles_ref.shape[0]):
        total[table[0, t]] += lax.dot_general(
            panel[table[1, t]], tiles_ref[t], NN, preferred_element_type=F32
        )
    own_ref[...] = total[:group]
    for d, send in enumerate(send_refs, 1):
        round_sums(send, total, d * group, group, vectors_n)


def row_kernel(runs, source, tiles_ref, *refs):
    parts, refs = refs[: len(runs)], refs[len(runs) :]
    _, total, swap_ref, panel, table, arrived = refs
    copy = fetch(source, table, arrived)
    group, vectors_n, _ = parts[0].shape
    half = swap_ref.shape[0]
    fill(panel, parts, runs)
    fill_ones(panel, vectors_n)
    copy.wait()
    for t in range(tiles_ref.shape[0]):
        total[table[2, t]] += lax.dot_general(
            panel[table[0, t]], tiles_ref[t], NT, preferred_element_type=F32
        )
    for d in range(half):
        round_sums(swap_ref.at[d], total, (half + d) * group, group, vectors_n)


def round_sums(send, total, start, group, vectors_n):
    for k in range(group):
        send[k * vectors_n : (k + 1) * vectors_n, :] = total[start + k, :vectors_n, :].astype(BF16)
    if total.shape[1] > vectors_n:
        send[group * vectors_n :, :] = split_degree(degree_of(total, start, group, vectors_n))


def products(tiles, table, col_parts, row_parts, zeros, runs, degree):
    group, vectors_n, width = col_parts[0].shape
    half = len(row_parts) // 2
    rows_n = max(place + count for run in runs[0] for place, count in run) // group
    rows = group * vectors_n + (2 * group if degree else 0)
    height = vectors_n + (DEGREE_ROWS if degree else 0)
    send_shape = jax.ShapeDtypeStruct((rows, width), BF16)
    flops = 2 * tiles.size * vectors_n

    def panel(count):
        return pltpu.VMEM((count * group, height, width), BF16)

    fetched = [pltpu.SMEM(table.shape, table.dtype), pltpu.SemaphoreType.DMA(())]
    col_own, _, *col_send = call(
        functools.partial(column_kernel, runs[1]),
        [jax.ShapeDtypeStruct((group, height, width), F32), zeros[1]] + [send_shape] * (rows_n - 1),
        [panel(2 * half), *fetched],
        24,
        [table, tiles, *row_parts, zeros[1]],
        flops,
        0,
        (),
        {2 + len(row_parts): 1},
    )
    kept, swap = call(
        functools.partial(row_kernel, runs[0]),
        [zeros[0], jax.ShapeDtypeStruct((half, rows, width), BF16)],
        [panel(rows_n), *fetched],
        24,
        [table, tiles, *col_parts, zeros[0]],
        flops,
        0,
        [col_own],
        {3 + len(col_parts): 0},
    )
    return kept, swap, col_own, col_send


def merge_kernel(degree, vectors_n, kept, got, own_ref, *send_refs):
    if degree:
        own_degree, *send_refs = send_refs
    group = own_ref.shape[0]
    for k in range(group):
        rows = slice(k * vectors_n, (k + 1) * vectors_n)
        own_ref[k] = kept[k, :vectors_n, :] + got[0, rows, :].astype(F32)
        for d, send in enumerate(send_refs, 1):
            both = kept[d * group + k, :vectors_n, :] + got[d, rows, :].astype(F32)
            send[rows, :] = both.astype(BF16)
    if degree:
        for d in range(got.shape[0]):
            sums = degree_of(kept, d * group, group, vectors_n) + join_degree(got.at[d], group)
            if d:
                send_refs[d - 1][group * vectors_n :, :] = split_degree(sums)
            else:
                own_degree[...] = sums


def merge(kept, got, vectors_n, degree):
    half, width = got.shape[0], got.shape[2]
    group = kept.shape[0] // (2 * half)
    out_shape = [jax.ShapeDtypeStruct((group, vectors_n, width), F32)]
    if degree:
        out_shape += [jax.ShapeDtypeStruct((group, width), F32)]
    out_shape += [jax.ShapeDtypeStruct(got.shape[1:], BF16)] * (half - 1)
    kernel = functools.partial(merge_kernel, degree, vectors_n)
    return call(kernel, out_shape, [], 24, [kept, got])


def gathered_sum(own, received, k, vectors_n):
    total = own[k, :vectors_n, :]
    rows = slice(k * vectors_n, (k + 1) * vectors_n)
    for part in received:
        total = total + part[rows, :].astype(F32)
    return total


def symmetric_part(row_own, row_refs, col_own, col_refs, k, vectors_n):
    return 0.5 * (
        gathered_sum(row_own, row_refs, k, vectors_n)
        + gathered_sum(col_own, col_refs, k, vectors_n)
    )


def first_kernel(chips_n, vec_ref, row_degree, row_own, col_own, *refs):
    row_refs, refs = refs[: chips_n - 1], refs[chips_n - 1 :]
    col_refs, (first_ref, rounded_ref, degree_ref) = refs[:-3], refs[-3:]
    group, vectors_n, width = rounded_ref.shape
    degree = row_degree[...] + degree_of(col_own, 0, group, vectors_n)
    for part in (*row_refs, *col_refs):
        degree += join_degree(part, group)
    degree = 0.5 * degree
    degree_ref[...] = degree
    for k, vec in enumerate(tiles_first(vec_ref, width)):
        symmetric = symmetric_part(row_own, row_refs, col_own, col_refs, k, vectors_n)
        image = degree[k : k + 1, :] * vec - symmetric
        first = (image - CENTER * vec) / HALF_WIDTH
        first_ref[:, k * width : (k + 1) * width] = first
        rounded_ref[k] = first.astype(BF16)


def filter_kernel(chips_n, start_ref, first_ref, degree_ref, row_own, col_own, *refs):
    row_refs, refs = refs[: chips_n - 1], refs[chips_n - 1 :]
    col_refs, (filtered_ref, rounded_ref) = refs[:-2], refs[-2:]
    _, vectors_n, width = rounded_ref.shape
    for k, vec in enumerate(tiles_first(first_ref, width)):
        symmetric = symmetric_part(row_own, row_refs, col_own, col_refs, k, vectors_n)
        columns = slice(k * width, (k + 1) * width)
        image = degree_ref[k : k + 1, :] * vec - symmetric
        filtered = 2.0 * (image - CENTER * vec) / HALF_WIDTH - start_ref[:, columns]
        filtered_ref[:, columns] = filtered
        rounded_ref[k] = filtered.astype(BF16)


def gram_kernel(filtered_ref, degree_ref, gram_ref, both):
    vectors_n, width = filtered_ref.shape[0], degree_ref.shape[1]
    for k, vec in enumerate(tiles_first(filtered_ref, width)):
        columns = slice(k * width, (k + 1) * width)
        both[:vectors_n, columns] = vec
        both[vectors_n:, columns] = degree_ref[k : k + 1, :] * vec
    gram_ref[...] = lax.dot_general(
        filtered_ref[...], both[...], NT, precision=HIGHEST, preferred_element_type=F32
    )


def half_form_kernel(runs, source, tiles_ref, *refs):
    parts, (out_ref, panel, table, arrived) = refs[:-4], refs[-4:]
    copy = fetch(source, table, arrived)
    width = panel.shape[2]
    fill(panel, parts, runs)
    copy.wait()
    for t in range(tiles_ref.shape[0]):
        out_ref[:, t * width : (t + 1) * width] = lax.dot_general(
            panel[table[1, t]], tiles_ref[t], NN, preferred_element_type=F32
        ).astype(BF16)


def form_kernel(runs, source, left, gram_ref, *refs):
    parts, (out_ref, panel, right, table, arrived) = refs[:-5], refs[-5:]
    copy = fetch(source, table, arrived)
    _, vectors_n, width = panel.shape
    fill(panel, parts, runs)
    copy.wait()
    for t in range(right.shape[1] // width):
        right[:, t * width : (t + 1) * width] = panel[table[0, t]]
    form = lax.dot_general(left[...], right[...], NT, preferred_element_type=F32)
    projected = gram_ref[:, vectors_n:] - 0.5 * (form + form.T)
    row, col = square_index(vectors_n)
    packed = jnp.where(col >= row, gram_ref[:, :vectors_n], projected)
    diagonal = jnp.sum(jnp.where(row == col, projected, 0.0), 0, keepdims=True)
    half = vectors_n // 2
    out_ref[:half] = jnp.concatenate([packed[:half], packed[half:]], 1)
    diagonal = jnp.broadcast_to(diagonal, (8, vectors_n))
    out_ref[half:] = jnp.concatenate([diagonal, jnp.zeros_like(diagonal)], 1)


def square_index(n):
    return tuple(lax.broadcasted_iota(jnp.int32, (n, n), axis) for axis in (0, 1))


def inverse_factor(gram):
    n = gram.shape[0]
    row, col = square_index(n)
    table = jnp.concatenate([gram, jnp.where(row == col, 1.0, 0.0)], 1)
    bands = [table[i : i + 8] for i in range(0, n, 8)]
    shape = (8, 2 * n)
    line = lax.broadcasted_iota(jnp.int32, shape, 0)

    def spread(values, j):
        return jnp.broadcast_to(values[:, j : j + 1], shape)

    def pick(values, i):
        return jnp.broadcast_to(values[i : i + 1, :], shape)

    for at in range(n // 8):
        block = [spread(bands[at], 8 * at + c) for c in range(8)]
        forward, solved = bands[at], bands[at]
        solved_block = list(block)
        for s in range(8):
            scale = 1.0 / pick(block[s], s)
            below = jnp.where(line > s, block[s], 0.0) * scale
            above = jnp.where(line < s, solved_block[s] * scale, 0.0)
            both = below + above
            pivot_row = pick(forward, s)
            forward = forward - below * pivot_row
            solved = solved - both * pivot_row
            for c in range(s + 1, 8):
                pivot = pick(block[c], s)
                block[c] = block[c] - below * pivot
                solved_block[c] = solved_block[c] - both * pivot
        pivots = block[0]
        for s in range(1, 8):
            pivots = jnp.where(line == s, block[s], pivots)
        solved = solved / pivots
        bands[at] = forward / jnp.sqrt(pivots)
        for i in range(at + 1, n // 8):
            update = spread(bands[i], 8 * at) * pick(solved, 0)
            for c in range(1, 8):
                update = update + spread(bands[i], 8 * at + c) * pick(solved, c)
            bands[i] = bands[i] - update
    return jnp.concatenate(bands, 0)[:, n:]


def last_kernel(total_nodes, filtered_ref, *refs):
    (own, *parts), (ritz_ref, rayleigh_ref) = refs[:-2], refs[-2:]
    parts = [own, *parts[::-1]]
    n = filtered_ref.shape[0]
    half = n // 2
    sums = tree_sum([part[...] for part in parts]) * (1.0 / total_nodes)
    packed = jnp.concatenate([sums[:half, :n], sums[:half, n:]], 0)
    row, col = square_index(n)
    upper = jnp.where(col > row, packed, 0.0)
    gram = jnp.where(col >= row, packed, 0.0) + upper.T
    lower = jnp.where(col < row, packed, 0.0)
    diagonal = jnp.broadcast_to(sums[half : half + 1, :n], (n, n))
    projected = lower + lower.T + jnp.where(row == col, diagonal, 0.0)
    inverse = inverse_factor(gram)

    def dot(a, b, dims):
        return lax.dot_general(a, b, dims, precision=HIGHEST, preferred_element_type=F32)

    half_way = dot(inverse, projected, NN)
    rayleigh_ref[...] = dot(half_way, inverse, NT)
    turned = dot(inverse, half_way, NT)
    ritz_ref[...] = dot(turned, dot(inverse, filtered_ref[...], NN), NN)


def tree_sum(parts):
    while len(parts) > 1:
        parts = [a + b for a, b in zip(parts[::2], parts[1::2])]
    return parts[0]


def local(tiles, tile_rows, tile_cols, start):
    tiles, tile_rows, tile_cols = tiles[0, 0], tile_rows[0, 0], tile_cols[0, 0]
    width = tiles.shape[-1]
    vectors_n, own_nodes = start.shape
    rows_n, cols_n = lax.axis_size("row"), lax.axis_size("col")
    chips_n = cols_n // 2
    total_nodes = own_nodes * rows_n * cols_n
    group = own_nodes // width
    spread = (vectors_n, tiles.shape[0] * width)

    rounded_shape = jax.ShapeDtypeStruct((group, vectors_n, width), BF16)
    vector_shape = jax.ShapeDtypeStruct((vectors_n, own_nodes), F32)
    degree_shape = jax.ShapeDtypeStruct((group, width), F32)

    late = 1
    levels = [rows_n >> i for i in range(1, rows_n.bit_length())]
    col_runs = [[(0, group)]]
    for d in levels:
        if len(col_runs) == 1:
            col_runs += [[(d * group, group)]]
            continue
        cut = group - late
        passed = [((p // group ^ d) * group + p % group, n) for run in col_runs[1:] for p, n in run]
        col_runs += [[(d * group, cut)], [(d * group + cut, late), *passed]]
    chip_order = [0, *range(chips_n - 1, 0, -1)]
    row_runs = [[((2 * d + core) * group, group)] for core in range(2) for d in chip_order]
    runs = (col_runs, row_runs)
    def gather(rounded, first=()):
        held = [rounded]
        for d in levels:
            if len(held) == 1:
                held += [trade(rounded, "row", d)]
                continue
            near = trade(rounded[: group - late], "row", d)
            near, *passed = lax.optimization_barrier((near, *held[1:], *first))
            held[1:] = passed[: len(held) - 1]
            held += [near, trade(jnp.concatenate([rounded[group - late :], *held[1:]]), "row", d)]
        chips = [rounded, *exchange([rounded] * (chips_n - 1), "col", 2)[::-1]]
        return held, chips + [trade(chip, "col", 1) for chip in chips]

    def apply(rounded, table, degree, first=()):
        height = vectors_n + (DEGREE_ROWS if degree else 0)
        zeros = call(
            zero_kernel,
            [jax.ShapeDtypeStruct((n * group, height, width), F32) for n in (cols_n, rows_n)],
            [],
            16,
            [],
            4 * total_nodes * vectors_n,
        )
        parts = gather(rounded, (*first, *zeros))
        kept, swap, col_own, col_send = products(tiles, table, *parts, zeros, runs, degree)
        col_got = exchange(col_send, "row")
        row_own, *row_send = merge(kept, trade(swap, "col", 1), vectors_n, degree)
        row_degree = row_send[:1] if degree else []
        row_got = exchange(row_send[len(row_degree) :], "col", 2)[::-1]
        return [*row_degree, row_own, col_own, *row_got, *col_got]

    rounded = call(round_kernel, rounded_shape, [], 16, [start])
    meta = jnp.stack([lax.axis_index("row"), lax.axis_index("col"), chips_n]).astype(jnp.int32)
    meta = jnp.broadcast_to(meta[:, None], (3, tiles.shape[0]))
    table = call(
        functools.partial(table_kernel, group),
        jax.ShapeDtypeStruct((3, tiles.shape[0]), jnp.int32),
        [],
        16,
        [meta, tile_rows[None], tile_cols[None]],
    )
    tiles = call(
        hold_kernel,
        jax.ShapeDtypeStruct(tiles.shape, BF16),
        [],
        16,
        [tiles],
        4 * tiles.size * DEGREE_ROWS,
    )
    first, rounded, degree = call(
        functools.partial(first_kernel, chips_n),
        [vector_shape, rounded_shape, degree_shape],
        [],
        24,
        [start, *apply(rounded, table, True, (table,))],
    )
    filtered, rounded = call(
        functools.partial(filter_kernel, chips_n),
        [vector_shape, rounded_shape],
        [],
        24,
        [start, first, degree, *apply(rounded, table, False)],
    )
    gram = call(
        gram_kernel,
        jax.ShapeDtypeStruct((vectors_n, 2 * vectors_n), F32),
        [pltpu.VMEM((2 * vectors_n, own_nodes), F32)],
        16,
        [filtered, degree],
        24 * vectors_n * vectors_n * own_nodes,
    )
    col_parts, row_parts = gather(rounded, (gram,))
    fetched = [pltpu.SMEM(table.shape, table.dtype), pltpu.SemaphoreType.DMA(())]
    left = call(
        functools.partial(half_form_kernel, runs[1]),
        jax.ShapeDtypeStruct(spread, BF16),
        [pltpu.VMEM((cols_n * group, vectors_n, width), BF16), *fetched],
        24,
        [table, tiles, *row_parts],
        2 * tiles.size * vectors_n,
    )
    sums = call(
        functools.partial(form_kernel, runs[0]),
        jax.ShapeDtypeStruct((vectors_n // 2 + 8, 2 * vectors_n), F32),
        [pltpu.VMEM((rows_n * group, vectors_n, width), BF16), pltpu.VMEM(spread, BF16), *fetched],
        24,
        [table, left, gram, *col_parts],
        2 * vectors_n * spread[0] * spread[1],
    )
    sums = tree_sum([*exchange([sums] * (chips_n - 1), "col", 2)[::-1], sums])
    sums = tree_sum([*exchange([sums] * (rows_n - 1), "row")[::-1], sums])
    return call(
        functools.partial(last_kernel, total_nodes),
        [vector_shape, jax.ShapeDtypeStruct((vectors_n, vectors_n), F32)],
        [],
        24,
        [filtered, sums, trade(sums, "col", 1)],
    )


def solution(mesh):
    placed = (
        P("row", "col", None, None, None),
        P("row", "col", None),
        P("row", "col", None),
        P(None, ("row", "col")),
    )
    return jax.shard_map(
        local, mesh=mesh, in_specs=placed, out_specs=(P(None, ("row", "col")), P()), check_vma=False
    )
```

```python
import functools

import jax
import jax.numpy as jnp
from jax import lax
from jax.experimental import pallas as pl
from jax.experimental.pallas import tpu as pltpu
from jax.sharding import PartitionSpec as P

CENTER = 1.0
HALF_WIDTH = 0.5
HIGHEST = lax.Precision.HIGHEST
NT = (((1,), (1,)), ((), ()))
NN = (((1,), (0,)), ((), ()))
BF16 = jnp.bfloat16
F32 = jnp.float32
VMEM = pl.BlockSpec(memory_space=pltpu.VMEM)
SMEM = pl.BlockSpec(memory_space=pltpu.SMEM)
ANY = pl.BlockSpec(memory_space=pl.ANY)
DEGREE_ROWS = 16


def call(kernel, out_shape, scratch, limit, args, flops=0, smem=0, after=(), aliases={}):
    moved = sum(x.size * x.dtype.itemsize for x in args)
    return pl.pallas_call(
        lambda *refs: kernel(*refs[len(after) :]),
        out_shape=jax.tree.map(lambda x: jax.ShapeDtypeStruct(x.shape, x.dtype), out_shape),
        in_specs=[ANY] * len(after) + [SMEM] * smem + [VMEM] * (len(args) - smem),
        out_specs=jax.tree.map(lambda _: VMEM, out_shape),
        scratch_shapes=scratch,
        input_output_aliases=aliases,
        compiler_params=pltpu.CompilerParams(vmem_limit_bytes=limit * 2**20),
        cost_estimate=pl.CostEstimate(flops=flops, bytes_accessed=moved, transcendentals=0),
    )(*after, *args)


def trade(part, axis, d):
    n = lax.axis_size(axis)
    return lax.ppermute(part, axis, [(i, i ^ d) for i in range(n)])


def exchange(parts, axis, step=1):
    far_first = [trade(part, axis, step * d) for d, part in reversed(list(enumerate(parts, 1)))]
    return far_first[::-1]


def tiles_first(ref, width):
    return [ref[:, k * width : (k + 1) * width] for k in range(ref.shape[1] // width)]


def round_kernel(vec_ref, out_ref):
    for k, piece in enumerate(tiles_first(vec_ref, out_ref.shape[2])):
        out_ref[k] = piece.astype(BF16)


def split_degree(sums):
    high = sums.astype(BF16).astype(F32)
    return jnp.concatenate([high, sums - high], 0).astype(BF16)


def join_degree(payload, group):
    parts = payload[payload.shape[0] - 2 * group :, :].astype(F32)
    return parts[:group] + parts[group:]


def fill(panel, parts, runs):
    for part, places in zip(parts, runs):
        at = 0
        for place, count in places:
            panel[place : place + count, : part.shape[1], :] = part[at : at + count]
            at += count


def table_kernel(group, meta, rows_ref, cols_ref, table):
    rows, cols = rows_ref[...], cols_ref[...]
    apart = lax.div(rows, group) ^ meta[1:2, :]
    halves = lax.rem(apart, 2) * meta[2:3, :] + lax.div(apart, 2)
    inside = lax.rem(rows, group)
    table[0:1, :] = (lax.div(cols, group) ^ meta[0:1, :]) * group + lax.rem(cols, group)
    table[1:2, :] = apart * group + inside
    table[2:3, :] = halves * group + inside


def fetch(source, table, arrived):
    copy = pltpu.make_async_copy(source, table, arrived)
    copy.start()
    return copy


def fill_ones(panel, vectors_n):
    rows = panel.shape[1] - vectors_n
    if rows:
        panel[:, vectors_n:, :] = jnp.ones((panel.shape[0], rows, panel.shape[2]), BF16)


def degree_of(total, start, group, vectors_n):
    return jnp.concatenate(
        [total[start + k, vectors_n : vectors_n + 1, :] for k in range(group)], 0
    )


def hold_kernel(tiles_ref, held_ref):
    held_ref[...] = tiles_ref[...]


def zero_kernel(*refs):
    for ref in refs:
        ref[...] = jnp.zeros_like(ref)


def column_kernel(runs, source, tiles_ref, *refs):
    parts, refs = refs[: len(runs)], refs[len(runs) :]
    _, own_ref, total, *send_refs, panel, table, arrived = refs
    copy = fetch(source, table, arrived)
    group, vectors_n, _ = parts[0].shape
    fill(panel, parts, runs)
    fill_ones(panel, vectors_n)
    copy.wait()
    for t in range(tiles_ref.shape[0]):
        total[table[0, t]] += lax.dot_general(
            panel[table[1, t]], tiles_ref[t], NN, preferred_element_type=F32
        )
    own_ref[...] = total[:group]
    for d, send in enumerate(send_refs, 1):
        round_sums(send, total, d * group, group, vectors_n)


def row_kernel(runs, source, tiles_ref, *refs):
    parts, refs = refs[: len(runs)], refs[len(runs) :]
    _, total, swap_ref, panel, table, arrived = refs
    copy = fetch(source, table, arrived)
    group, vectors_n, _ = parts[0].shape
    half = swap_ref.shape[0]
    fill(panel, parts, runs)
    fill_ones(panel, vectors_n)
    copy.wait()
    for t in range(tiles_ref.shape[0]):
        total[table[2, t]] += lax.dot_general(
            panel[table[0, t]], tiles_ref[t], NT, preferred_element_type=F32
        )
    for d in range(half):
        round_sums(swap_ref.at[d], total, (half + d) * group, group, vectors_n)


def round_sums(send, total, start, group, vectors_n):
    for k in range(group):
        send[k * vectors_n : (k + 1) * vectors_n, :] = total[start + k, :vectors_n, :].astype(BF16)
    if total.shape[1] > vectors_n:
        send[group * vectors_n :, :] = split_degree(degree_of(total, start, group, vectors_n))


def products(tiles, table, col_parts, row_parts, zeros, runs, degree):
    group, vectors_n, width = col_parts[0].shape
    half = len(row_parts) // 2
    rows_n = max(place + count for run in runs[0] for place, count in run) // group
    rows = group * vectors_n + (2 * group if degree else 0)
    height = vectors_n + (DEGREE_ROWS if degree else 0)
    send_shape = jax.ShapeDtypeStruct((rows, width), BF16)
    flops = 2 * tiles.size * vectors_n

    def panel(count):
        return pltpu.VMEM((count * group, height, width), BF16)

    fetched = [pltpu.SMEM(table.shape, table.dtype), pltpu.SemaphoreType.DMA(())]
    col_own, _, *col_send = call(
        functools.partial(column_kernel, runs[1]),
        [jax.ShapeDtypeStruct((group, height, width), F32), zeros[1]] + [send_shape] * (rows_n - 1),
        [panel(2 * half), *fetched],
        24,
        [table, tiles, *row_parts, zeros[1]],
        flops,
        0,
        (),
        {2 + len(row_parts): 1},
    )
    kept, swap = call(
        functools.partial(row_kernel, runs[0]),
        [zeros[0], jax.ShapeDtypeStruct((half, rows, width), BF16)],
        [panel(rows_n), *fetched],
        24,
        [table, tiles, *col_parts, zeros[0]],
        flops,
        0,
        [col_own],
        {3 + len(col_parts): 0},
    )
    return kept, swap, col_own, col_send


def merge_kernel(degree, vectors_n, kept, got, own_ref, *send_refs):
    if degree:
        own_degree, *send_refs = send_refs
    group = own_ref.shape[0]
    for k in range(group):
        rows = slice(k * vectors_n, (k + 1) * vectors_n)
        own_ref[k] = kept[k, :vectors_n, :] + got[0, rows, :].astype(F32)
        for d, send in enumerate(send_refs, 1):
            both = kept[d * group + k, :vectors_n, :] + got[d, rows, :].astype(F32)
            send[rows, :] = both.astype(BF16)
    if degree:
        for d in range(got.shape[0]):
            sums = degree_of(kept, d * group, group, vectors_n) + join_degree(got.at[d], group)
            if d:
                send_refs[d - 1][group * vectors_n :, :] = split_degree(sums)
            else:
                own_degree[...] = sums


def merge(kept, got, vectors_n, degree):
    half, width = got.shape[0], got.shape[2]
    group = kept.shape[0] // (2 * half)
    out_shape = [jax.ShapeDtypeStruct((group, vectors_n, width), F32)]
    if degree:
        out_shape += [jax.ShapeDtypeStruct((group, width), F32)]
    out_shape += [jax.ShapeDtypeStruct(got.shape[1:], BF16)] * (half - 1)
    kernel = functools.partial(merge_kernel, degree, vectors_n)
    return call(kernel, out_shape, [], 24, [kept, got])


def gathered_sum(own, received, k, vectors_n):
    total = own[k, :vectors_n, :]
    rows = slice(k * vectors_n, (k + 1) * vectors_n)
    for part in received:
        total = total + part[rows, :].astype(F32)
    return total


def symmetric_part(row_own, row_refs, col_own, col_refs, k, vectors_n):
    return 0.5 * (
        gathered_sum(row_own, row_refs, k, vectors_n)
        + gathered_sum(col_own, col_refs, k, vectors_n)
    )


def first_kernel(chips_n, vec_ref, row_degree, row_own, col_own, *refs):
    row_refs, refs = refs[: chips_n - 1], refs[chips_n - 1 :]
    col_refs, (first_ref, rounded_ref, degree_ref) = refs[:-3], refs[-3:]
    group, vectors_n, width = rounded_ref.shape
    degree = row_degree[...] + degree_of(col_own, 0, group, vectors_n)
    for part in (*row_refs, *col_refs):
        degree += join_degree(part, group)
    degree = 0.5 * degree
    degree_ref[...] = degree
    for k, vec in enumerate(tiles_first(vec_ref, width)):
        symmetric = symmetric_part(row_own, row_refs, col_own, col_refs, k, vectors_n)
        image = degree[k : k + 1, :] * vec - symmetric
        first = (image - CENTER * vec) / HALF_WIDTH
        first_ref[:, k * width : (k + 1) * width] = first
        rounded_ref[k] = first.astype(BF16)


def filter_kernel(chips_n, start_ref, first_ref, degree_ref, row_own, col_own, *refs):
    row_refs, refs = refs[: chips_n - 1], refs[chips_n - 1 :]
    col_refs, (filtered_ref, rounded_ref) = refs[:-2], refs[-2:]
    _, vectors_n, width = rounded_ref.shape
    for k, vec in enumerate(tiles_first(first_ref, width)):
        symmetric = symmetric_part(row_own, row_refs, col_own, col_refs, k, vectors_n)
        columns = slice(k * width, (k + 1) * width)
        image = degree_ref[k : k + 1, :] * vec - symmetric
        filtered = 2.0 * (image - CENTER * vec) / HALF_WIDTH - start_ref[:, columns]
        filtered_ref[:, columns] = filtered
        rounded_ref[k] = filtered.astype(BF16)


def gram_kernel(filtered_ref, degree_ref, gram_ref, both):
    vectors_n, width = filtered_ref.shape[0], degree_ref.shape[1]
    for k, vec in enumerate(tiles_first(filtered_ref, width)):
        columns = slice(k * width, (k + 1) * width)
        both[:vectors_n, columns] = vec
        both[vectors_n:, columns] = degree_ref[k : k + 1, :] * vec
    gram_ref[...] = lax.dot_general(
        filtered_ref[...], both[...], NT, precision=HIGHEST, preferred_element_type=F32
    )


def half_form_kernel(runs, source, tiles_ref, *refs):
    parts, (out_ref, panel, table, arrived) = refs[:-4], refs[-4:]
    copy = fetch(source, table, arrived)
    width = panel.shape[2]
    fill(panel, parts, runs)
    copy.wait()
    for t in range(tiles_ref.shape[0]):
        out_ref[:, t * width : (t + 1) * width] = lax.dot_general(
            panel[table[1, t]], tiles_ref[t], NN, preferred_element_type=F32
        ).astype(BF16)


def form_kernel(runs, source, left, gram_ref, *refs):
    parts, (out_ref, panel, right, table, arrived) = refs[:-5], refs[-5:]
    copy = fetch(source, table, arrived)
    _, vectors_n, width = panel.shape
    fill(panel, parts, runs)
    copy.wait()
    for t in range(right.shape[1] // width):
        right[:, t * width : (t + 1) * width] = panel[table[0, t]]
    form = lax.dot_general(left[...], right[...], NT, preferred_element_type=F32)
    projected = gram_ref[:, vectors_n:] - 0.5 * (form + form.T)
    row, col = square_index(vectors_n)
    packed = jnp.where(col >= row, gram_ref[:, :vectors_n], projected)
    diagonal = jnp.sum(jnp.where(row == col, projected, 0.0), 0, keepdims=True)
    half = vectors_n // 2
    out_ref[:half] = jnp.concatenate([packed[:half], packed[half:]], 1)
    diagonal = jnp.broadcast_to(diagonal, (8, vectors_n))
    out_ref[half:] = jnp.concatenate([diagonal, jnp.zeros_like(diagonal)], 1)


def square_index(n):
    return tuple(lax.broadcasted_iota(jnp.int32, (n, n), axis) for axis in (0, 1))


def inverse_factor(gram):
    n = gram.shape[0]
    row, col = square_index(n)
    table = jnp.concatenate([gram, jnp.where(row == col, 1.0, 0.0)], 1)
    bands = [table[i : i + 8] for i in range(0, n, 8)]
    shape = (8, 2 * n)
    line = lax.broadcasted_iota(jnp.int32, shape, 0)

    def spread(values, j):
        return jnp.broadcast_to(values[:, j : j + 1], shape)

    def pick(values, i):
        return jnp.broadcast_to(values[i : i + 1, :], shape)

    for at in range(n // 8):
        block = [spread(bands[at], 8 * at + c) for c in range(8)]
        forward, solved = bands[at], bands[at]
        solved_block = list(block)
        for s in range(8):
            scale = 1.0 / pick(block[s], s)
            below = jnp.where(line > s, block[s], 0.0) * scale
            above = jnp.where(line < s, solved_block[s] * scale, 0.0)
            both = below + above
            pivot_row = pick(forward, s)
            forward = forward - below * pivot_row
            solved = solved - both * pivot_row
            for c in range(s + 1, 8):
                pivot = pick(block[c], s)
                block[c] = block[c] - below * pivot
                solved_block[c] = solved_block[c] - both * pivot
        pivots = block[0]
        for s in range(1, 8):
            pivots = jnp.where(line == s, block[s], pivots)
        solved = solved / pivots
        bands[at] = forward / jnp.sqrt(pivots)
        for i in range(at + 1, n // 8):
            update = spread(bands[i], 8 * at) * pick(solved, 0)
            for c in range(1, 8):
                update = update + spread(bands[i], 8 * at + c) * pick(solved, c)
            bands[i] = bands[i] - update
    return jnp.concatenate(bands, 0)[:, n:]


def last_kernel(total_nodes, filtered_ref, *refs):
    (own, *parts), (ritz_ref, rayleigh_ref) = refs[:-2], refs[-2:]
    parts = [own, *parts[::-1]]
    n = filtered_ref.shape[0]
    half = n // 2
    sums = tree_sum([part[...] for part in parts]) * (1.0 / total_nodes)
    packed = jnp.concatenate([sums[:half, :n], sums[:half, n:]], 0)
    row, col = square_index(n)
    upper = jnp.where(col > row, packed, 0.0)
    gram = jnp.where(col >= row, packed, 0.0) + upper.T
    lower = jnp.where(col < row, packed, 0.0)
    diagonal = jnp.broadcast_to(sums[half : half + 1, :n], (n, n))
    projected = lower + lower.T + jnp.where(row == col, diagonal, 0.0)
    inverse = inverse_factor(gram)

    def dot(a, b, dims):
        return lax.dot_general(a, b, dims, precision=HIGHEST, preferred_element_type=F32)

    half_way = dot(inverse, projected, NN)
    rayleigh_ref[...] = dot(half_way, inverse, NT)
    turned = dot(inverse, half_way, NT)
    ritz_ref[...] = dot(turned, dot(inverse, filtered_ref[...], NN), NN)


def tree_sum(parts):
    while len(parts) > 1:
        parts = [a + b for a, b in zip(parts[::2], parts[1::2])]
    return parts[0]


def local(tiles, tile_rows, tile_cols, start):
    tiles, tile_rows, tile_cols = tiles[0, 0], tile_rows[0, 0], tile_cols[0, 0]
    width = tiles.shape[-1]
    vectors_n, own_nodes = start.shape
    rows_n, cols_n = lax.axis_size("row"), lax.axis_size("col")
    chips_n = cols_n // 2
    total_nodes = own_nodes * rows_n * cols_n
    group = own_nodes // width
    spread = (vectors_n, tiles.shape[0] * width)

    rounded_shape = jax.ShapeDtypeStruct((group, vectors_n, width), BF16)
    vector_shape = jax.ShapeDtypeStruct((vectors_n, own_nodes), F32)
    degree_shape = jax.ShapeDtypeStruct((group, width), F32)

    late = 1
    levels = [rows_n >> i for i in range(1, rows_n.bit_length())]
    col_runs = [[(0, group)]]
    for d in levels:
        if len(col_runs) == 1:
            col_runs += [[(d * group, group)]]
            continue
        cut = group - late
        passed = [((p // group ^ d) * group + p % group, n) for run in col_runs[1:] for p, n in run]
        col_runs += [[(d * group, cut)], [(d * group + cut, late), *passed]]
    chip_order = [0, *range(chips_n - 1, 0, -1)]
    row_runs = [[((2 * d + core) * group, group)] for core in range(2) for d in chip_order]
    runs = (col_runs, row_runs)
    def gather(rounded, first=()):
        held = [rounded]
        for d in levels:
            if len(held) == 1:
                held += [trade(rounded, "row", d)]
                continue
            near = trade(rounded[: group - late], "row", d)
            near, *passed = lax.optimization_barrier((near, *held[1:], *first))
            held[1:] = passed[: len(held) - 1]
            held += [near, trade(jnp.concatenate([rounded[group - late :], *held[1:]]), "row", d)]
        chips = [rounded, *exchange([rounded] * (chips_n - 1), "col", 2)[::-1]]
        return held, chips + [trade(chip, "col", 1) for chip in chips]

    def apply(rounded, table, degree, first=()):
        height = vectors_n + (DEGREE_ROWS if degree else 0)
        zeros = call(
            zero_kernel,
            [jax.ShapeDtypeStruct((n * group, height, width), F32) for n in (cols_n, rows_n)],
            [],
            16,
            [],
            4 * total_nodes * vectors_n,
        )
        parts = gather(rounded, (*first, *zeros))
        kept, swap, col_own, col_send = products(tiles, table, *parts, zeros, runs, degree)
        near, *far = exchange(col_send, "row")
        col_got = [near, *far[::-1]]
        row_own, *row_send = merge(kept, trade(swap, "col", 1), vectors_n, degree)
        row_degree = row_send[:1] if degree else []
        row_got = exchange(row_send[len(row_degree) :], "col", 2)[::-1]
        return [*row_degree, row_own, col_own, *row_got, *col_got]

    rounded = call(round_kernel, rounded_shape, [], 16, [start])
    meta = jnp.stack([lax.axis_index("row"), lax.axis_index("col"), chips_n]).astype(jnp.int32)
    meta = jnp.broadcast_to(meta[:, None], (3, tiles.shape[0]))
    table = call(
        functools.partial(table_kernel, group),
        jax.ShapeDtypeStruct((3, tiles.shape[0]), jnp.int32),
        [],
        16,
        [meta, tile_rows[None], tile_cols[None]],
    )
    tiles = call(
        hold_kernel,
        jax.ShapeDtypeStruct(tiles.shape, BF16),
        [],
        16,
        [tiles],
        4 * tiles.size * DEGREE_ROWS,
    )
    first, rounded, degree = call(
        functools.partial(first_kernel, chips_n),
        [vector_shape, rounded_shape, degree_shape],
        [],
        24,
        [start, *apply(rounded, table, True, (table,))],
    )
    filtered, rounded = call(
        functools.partial(filter_kernel, chips_n),
        [vector_shape, rounded_shape],
        [],
        24,
        [start, first, degree, *apply(rounded, table, False)],
    )
    gram = call(
        gram_kernel,
        jax.ShapeDtypeStruct((vectors_n, 2 * vectors_n), F32),
        [pltpu.VMEM((2 * vectors_n, own_nodes), F32)],
        16,
        [filtered, degree],
        24 * vectors_n * vectors_n * own_nodes,
    )
    col_parts, row_parts = gather(rounded, (gram,))
    fetched = [pltpu.SMEM(table.shape, table.dtype), pltpu.SemaphoreType.DMA(())]
    left = call(
        functools.partial(half_form_kernel, runs[1]),
        jax.ShapeDtypeStruct(spread, BF16),
        [pltpu.VMEM((cols_n * group, vectors_n, width), BF16), *fetched],
        24,
        [table, tiles, *row_parts],
        2 * tiles.size * vectors_n,
    )
    sums = call(
        functools.partial(form_kernel, runs[0]),
        jax.ShapeDtypeStruct((vectors_n // 2 + 8, 2 * vectors_n), F32),
        [pltpu.VMEM((rows_n * group, vectors_n, width), BF16), pltpu.VMEM(spread, BF16), *fetched],
        24,
        [table, left, gram, *col_parts],
        2 * vectors_n * spread[0] * spread[1],
    )
    sums = sums + trade(sums, "col", 1)
    sums = tree_sum([*exchange([sums] * (chips_n - 1), "col", 2)[::-1], sums])
    return call(
        functools.partial(last_kernel, total_nodes),
        [vector_shape, jax.ShapeDtypeStruct((vectors_n, vectors_n), F32)],
        [],
        24,
        [filtered, sums, *exchange([sums] * (rows_n - 1), "row")[::-1]],
    )


def solution(mesh):
    placed = (
        P("row", "col", None, None, None),
        P("row", "col", None),
        P("row", "col", None),
        P(None, ("row", "col")),
    )
    return jax.shard_map(
        local, mesh=mesh, in_specs=placed, out_specs=(P(None, ("row", "col")), P()), check_vma=False
    )
```

```python
import functools

import jax
import jax.numpy as jnp
from jax import lax
from jax.experimental import pallas as pl
from jax.experimental.pallas import tpu as pltpu
from jax.sharding import PartitionSpec as P

CENTER = 1.0
HALF_WIDTH = 0.5
HIGHEST = lax.Precision.HIGHEST
NT = (((1,), (1,)), ((), ()))
NN = (((1,), (0,)), ((), ()))
BF16 = jnp.bfloat16
F32 = jnp.float32
VMEM = pl.BlockSpec(memory_space=pltpu.VMEM)
SMEM = pl.BlockSpec(memory_space=pltpu.SMEM)
ANY = pl.BlockSpec(memory_space=pl.ANY)
DEGREE_ROWS = 16


def call(kernel, out_shape, scratch, limit, args, flops=0, smem=0, after=(), aliases={}):
    moved = sum(x.size * x.dtype.itemsize for x in args)
    return pl.pallas_call(
        lambda *refs: kernel(*refs[len(after) :]),
        out_shape=jax.tree.map(lambda x: jax.ShapeDtypeStruct(x.shape, x.dtype), out_shape),
        in_specs=[ANY] * len(after) + [SMEM] * smem + [VMEM] * (len(args) - smem),
        out_specs=jax.tree.map(lambda _: VMEM, out_shape),
        scratch_shapes=scratch,
        input_output_aliases=aliases,
        compiler_params=pltpu.CompilerParams(vmem_limit_bytes=limit * 2**20),
        cost_estimate=pl.CostEstimate(flops=flops, bytes_accessed=moved, transcendentals=0),
    )(*after, *args)


def trade(part, axis, d):
    n = lax.axis_size(axis)
    return lax.ppermute(part, axis, [(i, i ^ d) for i in range(n)])


def exchange(parts, axis, step=1):
    far_first = [trade(part, axis, step * d) for d, part in reversed(list(enumerate(parts, 1)))]
    return far_first[::-1]


def tiles_first(ref, width):
    return [ref[:, k * width : (k + 1) * width] for k in range(ref.shape[1] // width)]


def round_kernel(vec_ref, out_ref):
    for k, piece in enumerate(tiles_first(vec_ref, out_ref.shape[2])):
        out_ref[k] = piece.astype(BF16)


def split_degree(sums):
    high = sums.astype(BF16).astype(F32)
    return jnp.concatenate([high, sums - high], 0).astype(BF16)


def join_degree(payload, group):
    parts = payload[payload.shape[0] - 2 * group :, :].astype(F32)
    return parts[:group] + parts[group:]


def fill(panel, parts, runs):
    for part, places in zip(parts, runs):
        at = 0
        for place, count in places:
            panel[place : place + count, : part.shape[1], :] = part[at : at + count]
            at += count


def table_kernel(group, meta, rows_ref, cols_ref, table):
    rows, cols = rows_ref[...], cols_ref[...]
    apart = lax.div(rows, group) ^ meta[1:2, :]
    halves = lax.rem(apart, 2) * meta[2:3, :] + lax.div(apart, 2)
    inside = lax.rem(rows, group)
    table[0:1, :] = (lax.div(cols, group) ^ meta[0:1, :]) * group + lax.rem(cols, group)
    table[1:2, :] = apart * group + inside
    table[2:3, :] = halves * group + inside


def fetch(source, table, arrived):
    copy = pltpu.make_async_copy(source, table, arrived)
    copy.start()
    return copy


def fill_ones(panel, vectors_n):
    rows = panel.shape[1] - vectors_n
    if rows:
        panel[:, vectors_n:, :] = jnp.ones((panel.shape[0], rows, panel.shape[2]), BF16)


def degree_of(total, start, group, vectors_n):
    return jnp.concatenate(
        [total[start + k, vectors_n : vectors_n + 1, :] for k in range(group)], 0
    )


def hold_kernel(tiles_ref, held_ref):
    held_ref[...] = tiles_ref[...]


def zero_kernel(*refs):
    for ref in refs:
        ref[...] = jnp.zeros_like(ref)


def column_kernel(runs, source, tiles_ref, *refs):
    parts, refs = refs[: len(runs)], refs[len(runs) :]
    _, own_ref, total, *send_refs, panel, table, arrived = refs
    copy = fetch(source, table, arrived)
    group, vectors_n, _ = parts[0].shape
    fill(panel, parts, runs)
    fill_ones(panel, vectors_n)
    copy.wait()
    for t in range(tiles_ref.shape[0]):
        total[table[0, t]] += lax.dot_general(
            panel[table[1, t]], tiles_ref[t], NN, preferred_element_type=F32
        )
    own_ref[...] = total[:group]
    for d, send in enumerate(send_refs, 1):
        round_sums(send, total, d * group, group, vectors_n)


def row_kernel(runs, source, tiles_ref, *refs):
    parts, refs = refs[: len(runs)], refs[len(runs) :]
    _, total, swap_ref, panel, table, arrived = refs
    copy = fetch(source, table, arrived)
    group, vectors_n, _ = parts[0].shape
    half = swap_ref.shape[0]
    fill(panel, parts, runs)
    fill_ones(panel, vectors_n)
    copy.wait()
    for t in range(tiles_ref.shape[0]):
        total[table[2, t]] += lax.dot_general(
            panel[table[0, t]], tiles_ref[t], NT, preferred_element_type=F32
        )
    for d in range(half):
        round_sums(swap_ref.at[d], total, (half + d) * group, group, vectors_n)


def round_sums(send, total, start, group, vectors_n):
    for k in range(group):
        send[k * vectors_n : (k + 1) * vectors_n, :] = total[start + k, :vectors_n, :].astype(BF16)
    if total.shape[1] > vectors_n:
        send[group * vectors_n :, :] = split_degree(degree_of(total, start, group, vectors_n))


def products(tiles, table, col_parts, row_parts, zeros, runs, degree):
    group, vectors_n, width = col_parts[0].shape
    half = len(row_parts) // 2
    rows_n = max(place + count for run in runs[0] for place, count in run) // group
    rows = group * vectors_n + (2 * group if degree else 0)
    height = vectors_n + (DEGREE_ROWS if degree else 0)
    send_shape = jax.ShapeDtypeStruct((rows, width), BF16)
    flops = 2 * tiles.size * vectors_n

    def panel(count):
        return pltpu.VMEM((count * group, height, width), BF16)

    fetched = [pltpu.SMEM(table.shape, table.dtype), pltpu.SemaphoreType.DMA(())]
    col_own, _, *col_send = call(
        functools.partial(column_kernel, runs[1]),
        [jax.ShapeDtypeStruct((group, height, width), F32), zeros[1]] + [send_shape] * (rows_n - 1),
        [panel(2 * half), *fetched],
        24,
        [table, tiles, *row_parts, zeros[1]],
        flops,
        0,
        (),
        {2 + len(row_parts): 1},
    )
    kept, swap = call(
        functools.partial(row_kernel, runs[0]),
        [zeros[0], jax.ShapeDtypeStruct((half, rows, width), BF16)],
        [panel(rows_n), *fetched],
        24,
        [table, tiles, *col_parts, zeros[0]],
        flops,
        0,
        [col_own],
        {3 + len(col_parts): 0},
    )
    return kept, swap, col_own, col_send


def merge_kernel(degree, vectors_n, kept, got, own_ref, *send_refs):
    if degree:
        own_degree, *send_refs = send_refs
    group = own_ref.shape[0]
    for k in range(group):
        rows = slice(k * vectors_n, (k + 1) * vectors_n)
        own_ref[k] = kept[k, :vectors_n, :] + got[0, rows, :].astype(F32)
        for d, send in enumerate(send_refs, 1):
            both = kept[d * group + k, :vectors_n, :] + got[d, rows, :].astype(F32)
            send[rows, :] = both.astype(BF16)
    if degree:
        for d in range(got.shape[0]):
            sums = degree_of(kept, d * group, group, vectors_n) + join_degree(got.at[d], group)
            if d:
                send_refs[d - 1][group * vectors_n :, :] = split_degree(sums)
            else:
                own_degree[...] = sums


def merge(kept, got, vectors_n, degree):
    half, width = got.shape[0], got.shape[2]
    group = kept.shape[0] // (2 * half)
    out_shape = [jax.ShapeDtypeStruct((group, vectors_n, width), F32)]
    if degree:
        out_shape += [jax.ShapeDtypeStruct((group, width), F32)]
    out_shape += [jax.ShapeDtypeStruct(got.shape[1:], BF16)] * (half - 1)
    kernel = functools.partial(merge_kernel, degree, vectors_n)
    return call(kernel, out_shape, [], 24, [kept, got])


def gathered_sum(own, received, k, vectors_n):
    total = own[k, :vectors_n, :]
    rows = slice(k * vectors_n, (k + 1) * vectors_n)
    for part in received:
        total = total + part[rows, :].astype(F32)
    return total


def symmetric_part(row_own, row_refs, col_own, col_refs, k, vectors_n):
    return 0.5 * (
        gathered_sum(row_own, row_refs, k, vectors_n)
        + gathered_sum(col_own, col_refs, k, vectors_n)
    )


def first_kernel(chips_n, vec_ref, row_degree, row_own, col_own, *refs):
    row_refs, refs = refs[: chips_n - 1], refs[chips_n - 1 :]
    col_refs, (first_ref, rounded_ref, degree_ref) = refs[:-3], refs[-3:]
    group, vectors_n, width = rounded_ref.shape
    degree = row_degree[...] + degree_of(col_own, 0, group, vectors_n)
    for part in (*row_refs, *col_refs):
        degree += join_degree(part, group)
    degree = 0.5 * degree
    degree_ref[...] = degree
    for k, vec in enumerate(tiles_first(vec_ref, width)):
        symmetric = symmetric_part(row_own, row_refs, col_own, col_refs, k, vectors_n)
        image = degree[k : k + 1, :] * vec - symmetric
        first = (image - CENTER * vec) / HALF_WIDTH
        first_ref[:, k * width : (k + 1) * width] = first
        rounded_ref[k] = first.astype(BF16)


def filter_kernel(chips_n, start_ref, first_ref, degree_ref, row_own, col_own, *refs):
    row_refs, refs = refs[: chips_n - 1], refs[chips_n - 1 :]
    col_refs, (filtered_ref, rounded_ref) = refs[:-2], refs[-2:]
    _, vectors_n, width = rounded_ref.shape
    for k, vec in enumerate(tiles_first(first_ref, width)):
        symmetric = symmetric_part(row_own, row_refs, col_own, col_refs, k, vectors_n)
        columns = slice(k * width, (k + 1) * width)
        image = degree_ref[k : k + 1, :] * vec - symmetric
        filtered = 2.0 * (image - CENTER * vec) / HALF_WIDTH - start_ref[:, columns]
        filtered_ref[:, columns] = filtered
        rounded_ref[k] = filtered.astype(BF16)


def gram_kernel(filtered_ref, degree_ref, gram_ref, both):
    vectors_n, width = filtered_ref.shape[0], degree_ref.shape[1]
    for k, vec in enumerate(tiles_first(filtered_ref, width)):
        columns = slice(k * width, (k + 1) * width)
        both[:vectors_n, columns] = vec
        both[vectors_n:, columns] = degree_ref[k : k + 1, :] * vec
    gram_ref[...] = lax.dot_general(
        filtered_ref[...], both[...], NT, precision=HIGHEST, preferred_element_type=F32
    )


def half_form_kernel(runs, source, tiles_ref, *refs):
    parts, (out_ref, panel, table, arrived) = refs[:-4], refs[-4:]
    copy = fetch(source, table, arrived)
    width = panel.shape[2]
    fill(panel, parts, runs)
    copy.wait()
    for t in range(tiles_ref.shape[0]):
        out_ref[:, t * width : (t + 1) * width] = lax.dot_general(
            panel[table[1, t]], tiles_ref[t], NN, preferred_element_type=F32
        ).astype(BF16)


def form_kernel(runs, source, left, gram_ref, *refs):
    parts, (out_ref, panel, right, table, arrived) = refs[:-5], refs[-5:]
    copy = fetch(source, table, arrived)
    _, vectors_n, width = panel.shape
    fill(panel, parts, runs)
    copy.wait()
    for t in range(right.shape[1] // width):
        right[:, t * width : (t + 1) * width] = panel[table[0, t]]
    form = lax.dot_general(left[...], right[...], NT, preferred_element_type=F32)
    projected = gram_ref[:, vectors_n:] - 0.5 * (form + form.T)
    row, col = square_index(vectors_n)
    packed = jnp.where(col >= row, gram_ref[:, :vectors_n], projected)
    diagonal = jnp.sum(jnp.where(row == col, projected, 0.0), 0, keepdims=True)
    half = vectors_n // 2
    out_ref[:half] = jnp.concatenate([packed[:half], packed[half:]], 1)
    diagonal = jnp.broadcast_to(diagonal, (8, vectors_n))
    out_ref[half:] = jnp.concatenate([diagonal, jnp.zeros_like(diagonal)], 1)


def square_index(n):
    return tuple(lax.broadcasted_iota(jnp.int32, (n, n), axis) for axis in (0, 1))


def inverse_factor(gram):
    n = gram.shape[0]
    row, col = square_index(n)
    table = jnp.concatenate([gram, jnp.where(row == col, 1.0, 0.0)], 1)
    bands = [table[i : i + 8] for i in range(0, n, 8)]
    shape = (8, 2 * n)
    line = lax.broadcasted_iota(jnp.int32, shape, 0)

    def spread(values, j):
        return jnp.broadcast_to(values[:, j : j + 1], shape)

    def pick(values, i):
        return jnp.broadcast_to(values[i : i + 1, :], shape)

    for at in range(n // 8):
        block = [spread(bands[at], 8 * at + c) for c in range(8)]
        forward, solved = bands[at], bands[at]
        solved_block = list(block)
        for s in range(8):
            scale = 1.0 / pick(block[s], s)
            below = jnp.where(line > s, block[s], 0.0) * scale
            above = jnp.where(line < s, solved_block[s] * scale, 0.0)
            both = below + above
            pivot_row = pick(forward, s)
            forward = forward - below * pivot_row
            solved = solved - both * pivot_row
            for c in range(s + 1, 8):
                pivot = pick(block[c], s)
                block[c] = block[c] - below * pivot
                solved_block[c] = solved_block[c] - both * pivot
        pivots = block[0]
        for s in range(1, 8):
            pivots = jnp.where(line == s, block[s], pivots)
        solved = solved / pivots
        bands[at] = forward / jnp.sqrt(pivots)
        for i in range(at + 1, n // 8):
            update = spread(bands[i], 8 * at) * pick(solved, 0)
            for c in range(1, 8):
                update = update + spread(bands[i], 8 * at + c) * pick(solved, c)
            bands[i] = bands[i] - update
    return jnp.concatenate(bands, 0)[:, n:]


def last_kernel(total_nodes, filtered_ref, *refs):
    (own, *parts), (ritz_ref, rayleigh_ref) = refs[:-2], refs[-2:]
    parts = [own, *parts[::-1]]
    n = filtered_ref.shape[0]
    half = n // 2
    sums = tree_sum([part[...] for part in parts]) * (1.0 / total_nodes)
    packed = jnp.concatenate([sums[:half, :n], sums[:half, n:]], 0)
    row, col = square_index(n)
    upper = jnp.where(col > row, packed, 0.0)
    gram = jnp.where(col >= row, packed, 0.0) + upper.T
    lower = jnp.where(col < row, packed, 0.0)
    diagonal = jnp.broadcast_to(sums[half : half + 1, :n], (n, n))
    projected = lower + lower.T + jnp.where(row == col, diagonal, 0.0)
    inverse = inverse_factor(gram)

    def dot(a, b, dims):
        return lax.dot_general(a, b, dims, precision=HIGHEST, preferred_element_type=F32)

    half_way = dot(inverse, projected, NN)
    rayleigh_ref[...] = dot(half_way, inverse, NT)
    turned = dot(inverse, half_way, NT)
    ritz_ref[...] = dot(turned, dot(inverse, filtered_ref[...], NN), NN)


def tree_sum(parts):
    while len(parts) > 1:
        parts = [a + b for a, b in zip(parts[::2], parts[1::2])]
    return parts[0]


def local(tiles, tile_rows, tile_cols, start):
    tiles, tile_rows, tile_cols = tiles[0, 0], tile_rows[0, 0], tile_cols[0, 0]
    width = tiles.shape[-1]
    vectors_n, own_nodes = start.shape
    rows_n, cols_n = lax.axis_size("row"), lax.axis_size("col")
    chips_n = cols_n // 2
    total_nodes = own_nodes * rows_n * cols_n
    group = own_nodes // width
    spread = (vectors_n, tiles.shape[0] * width)

    rounded_shape = jax.ShapeDtypeStruct((group, vectors_n, width), BF16)
    vector_shape = jax.ShapeDtypeStruct((vectors_n, own_nodes), F32)
    degree_shape = jax.ShapeDtypeStruct((group, width), F32)

    late = 2
    levels = [rows_n >> i for i in range(1, rows_n.bit_length())]
    col_runs = [[(0, group)]]
    for d in levels:
        if len(col_runs) == 1:
            col_runs += [[(d * group, group)]]
            continue
        cut = group - late
        passed = [((p // group ^ d) * group + p % group, n) for run in col_runs[1:] for p, n in run]
        col_runs += [[(d * group, cut)], [(d * group + cut, late), *passed]]
    chip_order = [0, *range(chips_n - 1, 0, -1)]
    row_runs = [[((2 * d + core) * group, group)] for core in range(2) for d in chip_order]
    runs = (col_runs, row_runs)
    def gather(rounded, first=()):
        held = [rounded]
        for d in levels:
            if len(held) == 1:
                held += [trade(rounded, "row", d)]
                continue
            near = trade(rounded[: group - late], "row", d)
            near, *passed = lax.optimization_barrier((near, *held[1:], *first))
            held[1:] = passed[: len(held) - 1]
            held += [near, trade(jnp.concatenate([rounded[group - late :], *held[1:]]), "row", d)]
        chips = [rounded, *exchange([rounded] * (chips_n - 1), "col", 2)[::-1]]
        return held, chips + [trade(chip, "col", 1) for chip in chips]

    def apply(rounded, table, degree, first=()):
        height = vectors_n + (DEGREE_ROWS if degree else 0)
        zeros = call(
            zero_kernel,
            [jax.ShapeDtypeStruct((n * group, height, width), F32) for n in (cols_n, rows_n)],
            [],
            16,
            [],
            4 * total_nodes * vectors_n,
        )
        parts = gather(rounded, (*first, *zeros))
        kept, swap, col_own, col_send = products(tiles, table, *parts, zeros, runs, degree)
        col_got = exchange(col_send, "row")
        row_own, *row_send = merge(kept, trade(swap, "col", 1), vectors_n, degree)
        row_degree = row_send[:1] if degree else []
        row_got = exchange(row_send[len(row_degree) :], "col", 2)[::-1]
        return [*row_degree, row_own, col_own, *row_got, *col_got]

    rounded = call(round_kernel, rounded_shape, [], 16, [start])
    meta = jnp.stack([lax.axis_index("row"), lax.axis_index("col"), chips_n]).astype(jnp.int32)
    meta = jnp.broadcast_to(meta[:, None], (3, tiles.shape[0]))
    table = call(
        functools.partial(table_kernel, group),
        jax.ShapeDtypeStruct((3, tiles.shape[0]), jnp.int32),
        [],
        16,
        [meta, tile_rows[None], tile_cols[None]],
    )
    tiles = call(
        hold_kernel,
        jax.ShapeDtypeStruct(tiles.shape, BF16),
        [],
        16,
        [tiles],
        4 * tiles.size * DEGREE_ROWS,
    )
    first, rounded, degree = call(
        functools.partial(first_kernel, chips_n),
        [vector_shape, rounded_shape, degree_shape],
        [],
        24,
        [start, *apply(rounded, table, True, (table,))],
    )
    filtered, rounded = call(
        functools.partial(filter_kernel, chips_n),
        [vector_shape, rounded_shape],
        [],
        24,
        [start, first, degree, *apply(rounded, table, False)],
    )
    gram = call(
        gram_kernel,
        jax.ShapeDtypeStruct((vectors_n, 2 * vectors_n), F32),
        [pltpu.VMEM((2 * vectors_n, own_nodes), F32)],
        16,
        [filtered, degree],
        24 * vectors_n * vectors_n * own_nodes,
    )
    col_parts, row_parts = gather(rounded, (gram,))
    fetched = [pltpu.SMEM(table.shape, table.dtype), pltpu.SemaphoreType.DMA(())]
    left = call(
        functools.partial(half_form_kernel, runs[1]),
        jax.ShapeDtypeStruct(spread, BF16),
        [pltpu.VMEM((cols_n * group, vectors_n, width), BF16), *fetched],
        24,
        [table, tiles, *row_parts],
        2 * tiles.size * vectors_n,
    )
    sums = call(
        functools.partial(form_kernel, runs[0]),
        jax.ShapeDtypeStruct((vectors_n // 2 + 8, 2 * vectors_n), F32),
        [pltpu.VMEM((rows_n * group, vectors_n, width), BF16), pltpu.VMEM(spread, BF16), *fetched],
        24,
        [table, left, gram, *col_parts],
        2 * vectors_n * spread[0] * spread[1],
    )
    sums = sums + trade(sums, "col", 1)
    sums = tree_sum([*exchange([sums] * (chips_n - 1), "col", 2)[::-1], sums])
    return call(
        functools.partial(last_kernel, total_nodes),
        [vector_shape, jax.ShapeDtypeStruct((vectors_n, vectors_n), F32)],
        [],
        24,
        [filtered, sums, *exchange([sums] * (rows_n - 1), "row")[::-1]],
    )


def solution(mesh):
    placed = (
        P("row", "col", None, None, None),
        P("row", "col", None),
        P("row", "col", None),
        P(None, ("row", "col")),
    )
    return jax.shard_map(
        local, mesh=mesh, in_specs=placed, out_specs=(P(None, ("row", "col")), P()), check_vma=False
    )
```
